128 devices in a mesh: tile: 16 (over x_lo, y, core), sample: 8 (over z, x_hi).
Axes of the slice: x: 4 (x_hi: 2, x_lo: 2; x = x_hi * 2 + x_lo), y: 4, z: 4, core: 2. Of those that a mesh axis runs over, the one named last changes fastest.
Arguments:
- pair: bfloat16 [256, 256, 128], P('tile', 'sample'), may hold values from -30 to 30
- pair_mask: int32 [256, 256], P('tile', 'sample'), may hold values 0 or 1
- tri_in_w: bfloat16 [128, 512], replicated, may hold values from -0.5 to 0.5
- tri_gate_w: bfloat16 [128, 128], replicated, may hold values from -0.5 to 0.5
- tri_out_w: bfloat16 [128, 128], replicated, may hold values from -0.5 to 0.5
- bias_w: bfloat16 [128, 16], replicated, may hold values from -0.5 to 0.5
- atom_feats: bfloat16 [2048, 128], P('tile'), may hold values from -6 to 6
- atom_to_token: int32 [2048], P('tile'), may hold values from 0 to 255, never falling along the last dimension, each value on 1 to 24 neighbouring positions
- atom_w: bfloat16 [128, 768], replicated, may hold values from -0.5 to 0.5
- tokens: bfloat16 [256, 256, 768], P(('tile', 'sample')), may hold values from -40 to 40
- attention_input_weight: bfloat16 [768, 3072], replicated, may hold values from -2 to 2
- attention_output_weight: bfloat16 [768, 768], replicated, may hold values from -0.21875 to 0.21875
- cot_pair: bfloat16 [256, 256, 128], P('tile', 'sample'), may hold values from -6 to 6
- token_output_cotangent: bfloat16 [256, 256, 768], P(('tile', 'sample')), may hold values from -6 to 6
Outputs:
- pair_next: float32 [256, 256, 128], P('tile', 'sample')
- token_output_rows: float32 [256, 256, 768], P(('tile', 'sample'))
- grad_pair: float32 [256, 256, 128], P('tile', 'sample')
- grad_tokens: float32 [256, 256, 768], P(('tile', 'sample'))
- grad_tri_in_w: float32 [128, 512], replicated
- grad_tri_gate_w: float32 [128, 128], replicated
- grad_tri_out_w: float32 [128, 128], replicated
- grad_bias_w: float32 [128, 16], replicated
- grad_atom_w: float32 [128, 768], replicated
- attention_input_weight_gradient: float32 [768, 3072], replicated
- attention_output_weight_gradient: float32 [768, 768], replicated
The draws below stay inside these ranges and needn't reach their ends.
Inputs may be any that keep to these rules, and one draw needn't show every extreme that they name: `atom_to_token`: atoms are in order of their tokens; every token has 1 to 24 atoms.
All inputs are finite; a program needn't handle non-finite values. No bound on the sum of `pair_mask` on one device may be relied on, other than what follows from the above.
Results may differ from the reference program's by a relative error of at most 0.034.
Values may be sent and summed in bfloat16 or wider, within the bound.
A program may use at most 128 MiB of HBM per device.

```python
import math
import jax
import jax.numpy as jnp
import numpy as np
from jax import lax

N = 256
CZ = 128
CH = 128
DT = 768
HEADS = 16
HD = 48
CA = 128
MOST_ATOMS = 24
SAMPLES = 256
ATOMS = 2048
N_TILE = 16


def draw_pair(key, part):
    key = jax.random.fold_in(key, 1)
    keys = jax.random.split(key, 3)
    channel_scale = 0.3 * jnp.exp(jax.random.uniform(keys[0], (CZ,), jnp.float32, 0.0, math.log(10.0)))
    pixel_scale = 0.3 * jnp.exp(jax.random.uniform(keys[1], (N, N, 1), jnp.float32, 0.0, math.log(10.0)))
    values = jax.random.normal(keys[2], (N, N, CZ), jnp.float32) * channel_scale * pixel_scale
    return jnp.clip(values, -30.0, 30.0).astype(jnp.bfloat16)


def draw_tokens(key, part):
    key = jax.random.fold_in(key, 2)
    keys = jax.random.split(key, 3)
    column_scale = 0.3 * jnp.exp(jax.random.uniform(keys[0], (DT,), jnp.float32, 0.0, math.log(10.0)))
    row_scale = 0.3 * jnp.exp(jax.random.uniform(keys[1], (SAMPLES, N, 1), jnp.float32, 0.0, math.log(10.0)))
    values = jax.random.normal(keys[2], (SAMPLES, N, DT), jnp.float32) * column_scale * row_scale
    return jnp.clip(values, -40.0, 40.0).astype(jnp.bfloat16)


def draw_attention_input_weight(key, part):
    key = jax.random.fold_in(key, 3)
    keys = jax.random.split(key, 1)
    values = jax.random.normal(keys[0], (DT, 4 * DT), jnp.float32) / math.sqrt(DT)
    return jnp.clip(values, -2.0, 2.0).astype(jnp.bfloat16)


def touch_ends(drawn, key, least, largest):
    shape = drawn.shape
    spot = [jax.random.randint(jax.random.fold_in(key, axis), (), 0, shape[axis]) for axis in range(len(shape))]
    drawn = drawn.at[tuple(spot)].set(least)
    longest = shape.index(max(shape))
    spot[longest] = (spot[longest] + 1) % shape[longest]
    return drawn.at[tuple(spot)].set(largest)


def steps_of(stream_key, extent, cuts, least, largest):
    def one(axis_at, blocks):
        draws = jax.random.uniform(jax.random.fold_in(jax.random.fold_in(stream_key, 6), axis_at), (blocks,), jnp.float32, least / len(cuts), largest / len(cuts))
        return jnp.repeat(jnp.exp(draws), extent[axis_at] // blocks).reshape((-1,) + (1,) * (len(extent) - axis_at - 1))

    factor_of = one(*cuts[0])
    for cut in cuts[1:]:
        factor_of = factor_of * one(*cut)
    return factor_of


def profile(amount, total, most, slope):
    loads = [(1 << 20) // math.isqrt(standing ** slope) + 1 for standing in range(2, amount + 1)]
    rest, holding = total - most - (amount - 1), [1] * (amount - 1)
    while rest > 0:
        free = [i for i in range(amount - 1) if holding[i] < most]
        whole, remaining = sum([loads[i] for i in free]), rest
        for i in free:
            more = min(most - holding[i], max(1, remaining * loads[i] // whole), rest)
            holding[i] = holding[i] + more
            rest = rest - more
    return np.array([most] + holding)


def uneven(stream_key, count, total, most, slope):
    if count == 2:
        one = jax.random.randint(stream_key, (), max(1, total - most), min(most, total - 1) + 1)
        return jnp.stack([one, total - one])
    lengths = jnp.asarray(profile(count, total, most, slope), jnp.int32)
    pairs = (count - 1) // 2
    source_of, taker = lengths[1:1 + 2 * pairs:2], lengths[2:2 + 2 * pairs:2]
    room = jnp.minimum(source_of - 1, most - taker)
    passed = jax.random.randint(jax.random.fold_in(stream_key, 1), (pairs,), 0, 1 << 20) % (room + 1)
    lengths = lengths.at[1:1 + 2 * pairs:2].set(source_of - passed).at[2:2 + 2 * pairs:2].set(taker + passed)
    return lengths[jax.random.permutation(jax.random.fold_in(stream_key, 2), count)]


def scatter_about(rng, dims, spread, reach, pieces=(), kind=jnp.bfloat16):
    values = spread * jax.random.normal(rng, dims, jnp.float32)
    if pieces:
        values = values * steps_of(rng, dims, pieces, -0.22, 0.18)
    return jnp.clip(values, -reach, reach).astype(kind)


def setup_inputs(seed: int = 0) -> dict:
    arg_keys = jax.random.split(jax.random.key(seed), 15)
    return {
        "pair": draw_pair(jax.random.fold_in(arg_keys[14], 71), 0),
        "pair_mask": touch_ends((jax.random.randint(arg_keys[1], (N, N), 0, 8) < 7).astype(jnp.int32), jax.random.fold_in(arg_keys[1], 1), 0, 1),
        "tri_in_w": scatter_about(arg_keys[2], (CZ, 4 * CH), CZ ** -0.5, 0.5),
        "tri_gate_w": scatter_about(arg_keys[3], (CZ, CZ), CZ ** -0.5, 0.5),
        "tri_out_w": scatter_about(arg_keys[4], (CH, CZ), CH ** -0.5, 0.5),
        "bias_w": scatter_about(arg_keys[5], (CZ, HEADS), CZ ** -0.5, 0.5),
        "atom_feats": scatter_about(arg_keys[6], (ATOMS, CA), 1.0, 6.0, ((0, 16),)),
        "atom_to_token": jnp.searchsorted(jnp.cumsum(uneven(arg_keys[7], N, ATOMS, MOST_ATOMS, 1)), jnp.arange(ATOMS), side="right").astype(jnp.int32),
        "atom_w": scatter_about(arg_keys[8], (CA, DT), CA ** -0.5, 0.5),
        "tokens": draw_tokens(jax.random.fold_in(arg_keys[14], 71), 0),
        "attention_input_weight": draw_attention_input_weight(jax.random.fold_in(arg_keys[14], 71), 0),
        "attention_output_weight": scatter_about(arg_keys[11], (DT, DT), DT ** -0.5, 0.21875),
        "cot_pair": scatter_about(arg_keys[12], (N, N, CZ), 1.0, 6.0, ((0, 16), (1, 8))),
        "token_output_cotangent": scatter_about(arg_keys[13], (SAMPLES, N, DT), 1.0, 6.0, ((0, 128),)),
    }


EPSILON = 1e-05
HIGHEST = lax.Precision.HIGHEST

def norm_parts(values, axis):
    centered = values - lax.optimization_barrier(jnp.mean(values, axis=axis, keepdims=True))
    inverse = lax.rsqrt(lax.optimization_barrier(jnp.mean(centered * centered, axis=axis, keepdims=True)) + EPSILON)
    return (centered * inverse, inverse)

def norm_back(normed, inverse, incoming_gradient, axis):
    first_mean = lax.optimization_barrier(jnp.mean(incoming_gradient, axis=axis, keepdims=True))
    second_mean = lax.optimization_barrier(jnp.mean(incoming_gradient * normed, axis=axis, keepdims=True))
    return (incoming_gradient - first_mean - normed * second_mean) * inverse

def silu_slope(values):
    sigmoid_part = jax.nn.sigmoid(values)
    return sigmoid_part * (1.0 + values * (1.0 - sigmoid_part))

def rounded(values):
    return lax.optimization_barrier(values.astype(jnp.bfloat16)).astype(jnp.float32)

def reference(pair, pair_mask, tri_in_w, tri_gate_w, tri_out_w, bias_w, atom_feats, atom_to_token, atom_w, tokens, attention_input_weight, attention_output_weight, cot_pair, token_output_cotangent):
    block_rows = N // N_TILE
    pair_f = pair.astype(jnp.float32)
    normed_z, inverse_z = norm_parts(pair_f, 2)
    normed_zb = normed_z.astype(jnp.bfloat16)
    normed_zf = normed_zb.astype(jnp.float32)
    projected = jnp.einsum('ijz,zc->ijc', normed_zf, tri_in_w.astype(jnp.float32))
    mask_cells = pair_mask.astype(jnp.float32)[:, :, None]
    gate_left = jax.nn.sigmoid(projected[:, :, 0:CH])
    gate_right = jax.nn.sigmoid(projected[:, :, 2 * CH:3 * CH])
    left_rows = (gate_left * projected[:, :, CH:2 * CH] * mask_cells).astype(jnp.bfloat16)
    right_rows = (gate_right * projected[:, :, 3 * CH:] * mask_cells).astype(jnp.bfloat16)
    left_f = left_rows.astype(jnp.float32)
    right_f = right_rows.astype(jnp.float32)
    product = jnp.einsum('ikc,jkc->ijc', left_f, right_f).astype(jnp.bfloat16)
    normed_p, inverse_p = norm_parts(product.astype(jnp.float32), 2)
    normed_pb = normed_p.astype(jnp.bfloat16)
    linear = jnp.einsum('ijc,cz->ijz', normed_pb.astype(jnp.float32), tri_out_w.astype(jnp.float32))
    tri_gate = jax.nn.sigmoid(jnp.einsum('ijz,zy->ijy', normed_zf, tri_gate_w.astype(jnp.float32)))
    pair_next = pair_f + tri_gate * linear
    normed_n, inverse_n = norm_parts(pair_next, 2)
    normed_nb = normed_n.astype(jnp.bfloat16)
    bias_heads = jnp.einsum('ijz,zh->hij', normed_nb.astype(jnp.float32), bias_w.astype(jnp.float32)).astype(jnp.bfloat16)
    bias_f = bias_heads.astype(jnp.float32)
    atom_pre = jnp.dot(atom_feats, atom_w, preferred_element_type=jnp.float32)
    atom_act = jax.nn.silu(atom_pre)
    token_sums = jax.ops.segment_sum(atom_act, atom_to_token, num_segments=N)
    token_counts = jax.ops.segment_sum(jnp.ones((ATOMS,), jnp.float32), atom_to_token, num_segments=N)
    token_cond = token_sums / token_counts[:, None]
    token_state_rows = tokens.astype(jnp.float32) + token_cond[None]
    normed_h, inverse_h = norm_parts(token_state_rows, 2)
    normalized_hidden_bfloat = normed_h.astype(jnp.bfloat16)
    normalized_hidden_float = normalized_hidden_bfloat.astype(jnp.float32)
    attention_float = attention_input_weight.astype(jnp.float32)
    projected_hidden = jnp.einsum('zut,tw->zuw', normalized_hidden_float, attention_float)
    queries = projected_hidden[:, :, :DT].astype(jnp.bfloat16)
    gate_values = jax.nn.sigmoid(projected_hidden[:, :, DT:2 * DT])
    keys_all = projected_hidden[:, :, 2 * DT:3 * DT].astype(jnp.bfloat16)
    values_all = projected_hidden[:, :, 3 * DT:].astype(jnp.bfloat16)
    score_scale = 1.0 / math.sqrt(HD)
    output_matrix = attention_output_weight.astype(jnp.float32)

    def one_sample(bias_total, inputs):
        query_rows, key_rows, value_rows, gate_row, cot_row = inputs
        query_h = query_rows.astype(jnp.float32).reshape(N, HEADS, HD)
        key_h = key_rows.astype(jnp.float32).reshape(N, HEADS, HD)
        value_h = value_rows.astype(jnp.float32).reshape(N, HEADS, HD)
        scores = jnp.einsum('ihd,jhd->hij', query_h, key_h) * score_scale + bias_f
        top_score = lax.optimization_barrier(jnp.max(scores, axis=2, keepdims=True))
        weights = jnp.exp(scores - top_score)
        attn_probs = weights / lax.optimization_barrier(jnp.sum(weights, axis=2, keepdims=True))
        probs_bf = rounded(attn_probs)
        attended = jnp.einsum('hij,jhd->ihd', probs_bf, value_h).reshape(N, DT)
        gated_row = (gate_row * attended).astype(jnp.bfloat16)
        incoming_gradient = jnp.einsum('ie,de->id', cot_row.astype(jnp.float32), output_matrix)
        d_att = rounded(incoming_gradient * gate_row)
        d_gate = (incoming_gradient * attended * gate_row * (1.0 - gate_row)).astype(jnp.bfloat16)
        d_att_h = d_att.reshape(N, HEADS, HD)
        d_probs = jnp.einsum('ihd,jhd->hij', d_att_h, value_h)
        d_scores = attn_probs * (d_probs - lax.optimization_barrier(jnp.sum(attn_probs * d_probs, axis=2, keepdims=True)))
        d_scores_b = rounded(d_scores)
        d_query = (jnp.einsum('hij,jhd->ihd', d_scores_b, key_h) * score_scale).astype(jnp.bfloat16).reshape(N, DT)
        d_key = (jnp.einsum('hij,ihd->jhd', d_scores_b, query_h) * score_scale).astype(jnp.bfloat16).reshape(N, DT)
        d_value = jnp.einsum('hij,ihd->jhd', probs_bf, d_att_h).astype(jnp.bfloat16).reshape(N, DT)
        return (bias_total + d_scores, (gated_row, d_query, d_gate, d_key, d_value))
    d_bias, stacked = lax.scan(one_sample, jnp.zeros((HEADS, N, N), jnp.float32), (queries, keys_all, values_all, gate_values, token_output_cotangent))
    gated_attention, d_query, d_gate, d_key, d_value = stacked
    gated_attention_float = gated_attention.astype(jnp.float32)
    token_output_rows = token_state_rows + jnp.einsum('zut,tw->zuw', gated_attention_float, output_matrix)
    attention_output_weight_gradient = jnp.einsum('jol,jot->lt', gated_attention_float, token_output_cotangent.astype(jnp.float32))
    every_gradient = jnp.concatenate([d_query, d_gate, d_key, d_value], axis=2).astype(jnp.float32)
    normalized_hidden_gradient = jnp.einsum('xqu,bu->xqb', every_gradient, attention_float)
    attention_input_weight_gradient = jnp.einsum('jol,jot->lt', normalized_hidden_float, every_gradient)
    grad_tokens = token_output_cotangent.astype(jnp.float32) + norm_back(normed_h, inverse_h, normalized_hidden_gradient, 2)
    cond_grad = lax.optimization_barrier(jnp.sum(grad_tokens, axis=0)) / token_counts[:, None]
    d_act = jnp.take(cond_grad, atom_to_token, axis=0) * silu_slope(atom_pre)
    grad_atom_w = jnp.einsum('ac,ad->cd', atom_feats.astype(jnp.float32), d_act, precision=HIGHEST)
    d_normed_n = jnp.einsum('hij,zh->ijz', d_bias, bias_w.astype(jnp.float32), precision=HIGHEST)
    grad_bias_w = jnp.einsum('ijz,hij->zh', normed_nb.astype(jnp.float32), d_bias, precision=HIGHEST)
    d_next = cot_pair.astype(jnp.float32) + norm_back(normed_n, inverse_n, d_normed_n, 2)
    d_linear = (d_next * tri_gate).astype(jnp.bfloat16).astype(jnp.float32)
    d_gate_pre = (d_next * linear * tri_gate * (1.0 - tri_gate)).astype(jnp.bfloat16).astype(jnp.float32)
    grad_tri_out_w = jnp.einsum('ijc,ijz->cz', normed_pb.astype(jnp.float32), d_linear)
    d_normed_p = jnp.einsum('ijz,cz->ijc', d_linear, tri_out_w.astype(jnp.float32))
    d_product = norm_back(normed_p, inverse_p, d_normed_p, 2).astype(jnp.bfloat16).astype(jnp.float32)
    d_left = jnp.einsum('ijc,jkc->ikc', d_product, right_f).astype(jnp.bfloat16).astype(jnp.float32)

    def block_term(total, index):
        start = index * block_rows
        rows_grad = lax.dynamic_slice_in_dim(d_product, start, block_rows, 0)
        rows_left = lax.dynamic_slice_in_dim(left_f, start, block_rows, 0)
        return (total + rounded(jnp.einsum('ijc,ikc->jkc', rows_grad, rows_left)), None)
    d_right_sum = lax.scan(block_term, jnp.zeros((N, N, CH), jnp.float32), jnp.arange(N_TILE, dtype=jnp.int32))[0]
    d_right = d_right_sum.astype(jnp.bfloat16).astype(jnp.float32)
    d_proj = jnp.concatenate([d_left * projected[:, :, CH:2 * CH] * mask_cells * gate_left * (1.0 - gate_left), d_left * gate_left * mask_cells, d_right * projected[:, :, 3 * CH:] * mask_cells * gate_right * (1.0 - gate_right), d_right * gate_right * mask_cells], axis=2).astype(jnp.bfloat16).astype(jnp.float32)
    grad_tri_in_w = jnp.einsum('ijz,ijc->zc', normed_zf, d_proj)
    grad_tri_gate_w = jnp.einsum('ijz,ijy->zy', normed_zf, d_gate_pre)
    d_normed_z = jnp.einsum('ijc,zc->ijz', d_proj, tri_in_w.astype(jnp.float32)) + jnp.einsum('ijy,zy->ijz', d_gate_pre, tri_gate_w.astype(jnp.float32))
    grad_pair = d_next + norm_back(normed_z, inverse_z, d_normed_z, 2)
    return (pair_next, token_output_rows, grad_pair, grad_tokens, grad_tri_in_w, grad_tri_gate_w, grad_tri_out_w, grad_bias_w, grad_atom_w, attention_input_weight_gradient, attention_output_weight_gradient)
```

```python
import functools
import math

import jax
import jax.numpy as jnp
from jax import lax
from jax.experimental import pallas as pl
from jax.experimental.pallas import tpu as pltpu
from jax.sharding import PartitionSpec as P

EPSILON = 1e-05
N_TILE = 16
N_SAMPLE = 8
N_CHIP = 8
MESH = pl.DeviceIdType.MESH
BF16 = jnp.bfloat16
F32 = jnp.float32
HIGHEST = lax.Precision.HIGHEST


def enter(t, s):
    barrier = pltpu.get_barrier_semaphore()
    for k in range(1, N_SAMPLE):
        pl.semaphore_signal(
            barrier, inc=1, device_id=(t, lax.rem(s + k, N_SAMPLE)), device_id_type=MESH
        )
    for k in range(1, N_TILE):
        pl.semaphore_signal(
            barrier, inc=1, device_id=(lax.rem(t + k, N_TILE), s), device_id_type=MESH
        )
    pl.semaphore_wait(barrier, N_SAMPLE + N_TILE - 2)


def wait_bytes(ref, sem):
    pltpu.make_async_copy(ref, ref, sem).wait()


def send(src, dst, send_sem, recv_sem, t, s):
    pltpu.make_async_remote_copy(
        src, dst, send_sem, recv_sem, device_id=(t, s), device_id_type=MESH
    ).start()


def exchange_kernel(x, out, mid, send_sem, recv_sem, local_sem):
    t, s = lax.axis_index("tile"), lax.axis_index("sample")
    enter(t, s)
    for k in range(1, N_SAMPLE):
        d = lax.rem(s + k, N_SAMPLE)
        send(x.at[:, d], mid.at[:, s], send_sem.at[0], recv_sem.at[0], t, d)
    own = pltpu.make_async_copy(x.at[:, s], mid.at[:, s], local_sem)
    own.start()
    own.wait()
    wait_bytes(mid.at[:, pl.ds(0, N_SAMPLE - 1)], recv_sem.at[0])
    for k in range(1, N_TILE):
        d = lax.rem(t + k, N_TILE)
        send(mid.at[d], out.at[t], send_sem.at[1], recv_sem.at[1], d, s)
    own = pltpu.make_async_copy(mid.at[t], out.at[t], local_sem)
    own.start()
    own.wait()
    wait_bytes(out.at[pl.ds(0, N_TILE - 1)], recv_sem.at[1])
    wait_bytes(mid.at[:, pl.ds(0, N_SAMPLE - 1)], send_sem.at[0])
    wait_bytes(out.at[pl.ds(0, N_TILE - 1)], send_sem.at[1])


def exchange(x, collective_id):
    return pl.pallas_call(
        exchange_kernel,
        out_shape=jax.ShapeDtypeStruct(x.shape, x.dtype),
        in_specs=[pl.BlockSpec(memory_space=pltpu.VMEM)],
        out_specs=pl.BlockSpec(memory_space=pltpu.VMEM),
        scratch_shapes=[
            pltpu.VMEM(x.shape, x.dtype),
            pltpu.SemaphoreType.DMA((2,)),
            pltpu.SemaphoreType.DMA((2,)),
            pltpu.SemaphoreType.DMA,
        ],
        compiler_params=pltpu.CompilerParams(
            collective_id=collective_id, has_side_effects=True, vmem_limit_bytes=32 << 20
        ),
    )(x)


def gather_kernel(x, out, send_sem, recv_sem, local_sem):
    t, s = lax.axis_index("tile"), lax.axis_index("sample")
    m, c = t // 2, lax.rem(t, 2)
    other = m * 2 + 1 - c
    enter(t, s)
    own = pltpu.make_async_copy(x, out.at[m, c, s], local_sem)
    own.start()
    for k in range(1, N_SAMPLE):
        send(x, out.at[m, c, s], send_sem.at[0], recv_sem.at[0], t, lax.rem(s + k, N_SAMPLE))
    own.wait()
    wait_bytes(out.at[m, c, pl.ds(0, N_SAMPLE - 1)], recv_sem.at[0])
    block = out.at[m, c]
    send(block, block, send_sem.at[1], recv_sem.at[N_CHIP], other, s)
    for k in range(1, N_CHIP):
        send(block, block, send_sem.at[1], recv_sem.at[k], lax.rem(m + k, N_CHIP) * 2 + c, s)
    for k in range(1, N_CHIP):
        arrived = out.at[lax.rem(m + N_CHIP - k, N_CHIP), c]
        wait_bytes(arrived, recv_sem.at[k])
        send(arrived, arrived, send_sem.at[1], recv_sem.at[N_CHIP], other, s)
    wait_bytes(out.at[:, 0], recv_sem.at[N_CHIP])
    wait_bytes(out.at[0, 0, pl.ds(0, N_SAMPLE - 1)], send_sem.at[0])
    wait_bytes(out.at[:, 0], send_sem.at[1])
    wait_bytes(out.at[pl.ds(0, N_CHIP - 1), 0], send_sem.at[1])


def gather(x, collective_id):
    return pl.pallas_call(
        gather_kernel,
        out_shape=jax.ShapeDtypeStruct((N_CHIP, 2, N_SAMPLE) + x.shape, x.dtype),
        in_specs=[pl.BlockSpec(memory_space=pltpu.VMEM)],
        out_specs=pl.BlockSpec(memory_space=pltpu.VMEM),
        scratch_shapes=[
            pltpu.SemaphoreType.DMA((2,)),
            pltpu.SemaphoreType.DMA((N_CHIP + 1,)),
            pltpu.SemaphoreType.DMA,
        ],
        compiler_params=pltpu.CompilerParams(
            collective_id=collective_id, has_side_effects=True, vmem_limit_bytes=32 << 20
        ),
    )(x)


def scatter_sum_kernel(x, out, pair_sum, by_chip, by_sample, send_sem, recv_sem):
    t, s = lax.axis_index("tile"), lax.axis_index("sample")
    m, c = t // 2, lax.rem(t, 2)
    enter(t, s)
    for k in range(1, N_CHIP + 1):
        d = lax.rem(m + k, N_CHIP)
        send(x.at[d, 1 - c], pair_sum.at[d], send_sem.at[0], recv_sem.at[k], m * 2 + 1 - c, s)
    for k in range(1, N_CHIP + 1):
        d = lax.rem(m + k, N_CHIP)
        wait_bytes(pair_sum.at[d], recv_sem.at[k])
        pair_sum[d] = (pair_sum[d].astype(F32) + x[d, c].astype(F32)).astype(x.dtype)
        if k < N_CHIP:
            send(
                pair_sum.at[d],
                by_chip.at[k - 1],
                send_sem.at[1],
                recv_sem.at[N_CHIP + k],
                d * 2 + c,
                s,
            )
    total = pair_sum[m].astype(F32)
    for k in range(1, N_CHIP):
        wait_bytes(by_chip.at[k - 1], recv_sem.at[N_CHIP + k])
        total = total + by_chip[k - 1].astype(F32)
    pair_sum[m] = total.astype(x.dtype)
    for k in range(1, N_SAMPLE):
        d = lax.rem(s + k, N_SAMPLE)
        send(pair_sum.at[m, d], by_sample.at[k - 1], send_sem.at[2], recv_sem.at[0], t, d)
    wait_bytes(by_sample, recv_sem.at[0])
    out[...] = pair_sum[m, s].astype(F32) + jnp.sum(by_sample[...].astype(F32), axis=0)
    wait_bytes(pair_sum, send_sem.at[0])
    wait_bytes(by_chip, send_sem.at[1])
    wait_bytes(by_sample, send_sem.at[2])


def scatter_sum(x, collective_id):
    block = x.shape[3:]
    return pl.pallas_call(
        scatter_sum_kernel,
        out_shape=jax.ShapeDtypeStruct(block, F32),
        in_specs=[pl.BlockSpec(memory_space=pltpu.VMEM)],
        out_specs=pl.BlockSpec(memory_space=pltpu.VMEM),
        scratch_shapes=[
            pltpu.VMEM((N_CHIP, N_SAMPLE) + block, x.dtype),
            pltpu.VMEM((N_CHIP - 1, N_SAMPLE) + block, x.dtype),
            pltpu.VMEM((N_SAMPLE - 1,) + block, x.dtype),
            pltpu.SemaphoreType.DMA((3,)),
            pltpu.SemaphoreType.DMA((2 * N_CHIP,)),
        ],
        compiler_params=pltpu.CompilerParams(
            collective_id=collective_id, has_side_effects=True, vmem_limit_bytes=32 << 20
        ),
    )(x)


def norm_parts(values, axis):
    centered = values - jnp.mean(values, axis=axis, keepdims=True)
    inverse = lax.rsqrt(jnp.mean(centered * centered, axis=axis, keepdims=True) + EPSILON)
    return (centered * inverse, inverse)


def norm_back(normed, inverse, incoming_gradient, axis):
    first_mean = jnp.mean(incoming_gradient, axis=axis, keepdims=True)
    second_mean = jnp.mean(incoming_gradient * normed, axis=axis, keepdims=True)
    return (incoming_gradient - first_mean - normed * second_mean) * inverse


def silu_slope(values):
    sigmoid_part = jax.nn.sigmoid(values)
    return sigmoid_part * (1.0 + values * (1.0 - sigmoid_part))


def shards(
    pair,
    pair_mask,
    tri_in_w,
    tri_gate_w,
    tri_out_w,
    bias_w,
    atom_feats,
    atom_to_token,
    atom_w,
    tokens,
    attention_input_weight,
    attention_output_weight,
    cot_pair,
    token_output_cotangent,
):
    hidden = tri_in_w.shape[1] // 4
    token_width = attention_input_weight.shape[0]
    head_count = bias_w.shape[1]
    head_size = token_width // head_count
    sample_count = tokens.shape[0]
    total_tokens = tokens.shape[1]
    score_scale = 1.0 / math.sqrt(head_size)
    pair_f = pair.astype(jnp.float32)
    normed_z, inverse_z = norm_parts(pair_f, 2)
    normed_zb = normed_z.astype(jnp.bfloat16)
    projected = jnp.einsum("ijz,zc->cij", normed_zb, tri_in_w, preferred_element_type=jnp.float32)
    mask_rows = pair_mask.astype(jnp.float32)[None]
    gate_left = jax.nn.sigmoid(projected[0:hidden])
    gate_right = jax.nn.sigmoid(projected[2 * hidden : 3 * hidden])
    rows, columns = pair_mask.shape
    blocks = (N_TILE, N_SAMPLE)
    left_local = (gate_left * projected[hidden : 2 * hidden] * mask_rows).astype(BF16)
    right_local = (gate_right * projected[3 * hidden :] * mask_rows).astype(BF16)
    halves = jnp.stack([left_local, right_local], axis=1).astype(F32)
    halves = exchange(halves.reshape(blocks + (8, 128)), 0)
    panels = (
        halves.reshape(blocks + (2, rows, columns))
        .astype(BF16)
        .transpose(2, 0, 3, 1, 4)
        .reshape(2, N_TILE * rows, N_SAMPLE * columns)
    )
    left_panel, right_panel = panels[0], panels[1]
    product_panel = jnp.dot(left_panel, right_panel.T, preferred_element_type=F32).astype(BF16)
    product_blocks = (
        product_panel.reshape(N_TILE, rows, N_SAMPLE, columns)
        .transpose(0, 2, 1, 3)
        .reshape(blocks + (4, 128))
    )
    product = exchange(product_blocks.astype(F32), 1).reshape(hidden, rows, columns)
    normed_p, inverse_p = norm_parts(product, 0)
    normed_pb = normed_p.astype(jnp.bfloat16)
    linear = jnp.einsum("cij,cz->ijz", normed_pb, tri_out_w, preferred_element_type=jnp.float32)
    tri_gate = jax.nn.sigmoid(
        jnp.einsum("ijz,zy->ijy", normed_zb, tri_gate_w, preferred_element_type=jnp.float32)
    )
    pair_next = pair_f + tri_gate * linear
    normed_n, inverse_n = norm_parts(pair_next, 2)
    normed_nb = normed_n.astype(jnp.bfloat16)
    bias_local = jnp.einsum(
        "ijz,zh->hij", normed_nb, bias_w, preferred_element_type=jnp.float32
    ).astype(jnp.bfloat16)
    bias_all = (
        gather(bias_local.reshape(head_count, rows * columns), 2)
        .reshape(N_TILE, N_SAMPLE, head_count, rows, columns)
        .transpose(2, 0, 3, 1, 4)
        .reshape(head_count, N_TILE * rows, N_SAMPLE * columns)
    )
    every_feat = lax.all_gather(atom_feats, "tile", axis=0, tiled=True)
    every_atom = lax.all_gather(atom_to_token, "tile", axis=0, tiled=True)
    atom_pre = jnp.dot(every_feat, atom_w, preferred_element_type=jnp.float32)
    atom_act = jax.nn.silu(atom_pre).astype(BF16)
    token_ids = jnp.arange(total_tokens, dtype=jnp.int32)
    one_hot = (token_ids[:, None] == every_atom[None, :]).astype(BF16)
    token_sums = jnp.dot(one_hot, atom_act, preferred_element_type=F32)
    token_counts = jnp.sum(one_hot.astype(F32), axis=1)
    token_cond = token_sums / token_counts[:, None]
    token_state_rows = tokens.astype(jnp.float32) + token_cond[None]
    normed_h, inverse_h = norm_parts(token_state_rows, 2)
    normalized_hidden_bfloat = normed_h.astype(jnp.bfloat16)
    projected_hidden = jnp.einsum(
        "zut,tw->zuw",
        normalized_hidden_bfloat,
        attention_input_weight,
        preferred_element_type=jnp.float32,
    )
    queries = (
        projected_hidden[:, :, :token_width]
        .astype(jnp.bfloat16)
        .reshape(sample_count, total_tokens, head_count, head_size)
    )
    gate_values = jax.nn.sigmoid(projected_hidden[:, :, token_width : 2 * token_width])
    keys_all = (
        projected_hidden[:, :, 2 * token_width : 3 * token_width]
        .astype(jnp.bfloat16)
        .reshape(sample_count, total_tokens, head_count, head_size)
    )
    values_all = (
        projected_hidden[:, :, 3 * token_width :]
        .astype(jnp.bfloat16)
        .reshape(sample_count, total_tokens, head_count, head_size)
    )
    scores = (
        jnp.einsum("sihd,sjhd->shij", queries, keys_all, preferred_element_type=jnp.float32)
        * score_scale
        + bias_all.astype(jnp.float32)[None]
    )
    top_score = jnp.max(scores, axis=3, keepdims=True)
    weights = jnp.exp(scores - top_score)
    attn_probs = weights / jnp.sum(weights, axis=3, keepdims=True)
    probs_b = attn_probs.astype(jnp.bfloat16)
    attended = jnp.einsum(
        "shij,sjhd->sihd", probs_b, values_all, preferred_element_type=jnp.float32
    ).reshape(sample_count, total_tokens, token_width)
    gated_attention = (gate_values * attended).astype(jnp.bfloat16)
    token_output_rows = token_state_rows + jnp.einsum(
        "zut,tw->zuw", gated_attention, attention_output_weight, preferred_element_type=jnp.float32
    )
    incoming_gradient = jnp.einsum(
        "xqu,bu->xqb",
        token_output_cotangent,
        attention_output_weight,
        preferred_element_type=jnp.float32,
    )
    d_att = (incoming_gradient * gate_values).astype(jnp.bfloat16)
    d_gate = (incoming_gradient * attended * gate_values * (1.0 - gate_values)).astype(jnp.bfloat16)
    d_att_h = d_att.reshape(sample_count, total_tokens, head_count, head_size)
    d_probs = jnp.einsum("sihd,sjhd->shij", d_att_h, values_all, preferred_element_type=jnp.float32)
    d_scores = attn_probs * (d_probs - jnp.sum(attn_probs * d_probs, axis=3, keepdims=True))
    d_scores_b = d_scores.astype(jnp.bfloat16)
    d_query = (
        (
            jnp.einsum("shij,sjhd->sihd", d_scores_b, keys_all, preferred_element_type=jnp.float32)
            * score_scale
        )
        .astype(jnp.bfloat16)
        .reshape(sample_count, total_tokens, token_width)
    )
    d_key = (
        (
            jnp.einsum("shij,sihd->sjhd", d_scores_b, queries, preferred_element_type=jnp.float32)
            * score_scale
        )
        .astype(jnp.bfloat16)
        .reshape(sample_count, total_tokens, token_width)
    )
    d_value = (
        jnp.einsum("shij,sihd->sjhd", probs_b, d_att_h, preferred_element_type=jnp.float32)
        .astype(jnp.bfloat16)
        .reshape(sample_count, total_tokens, token_width)
    )
    bias_term = jnp.sum(d_scores, axis=0)
    bias_blocks = (
        bias_term.astype(BF16)
        .reshape(head_count, N_CHIP, 2, rows, N_SAMPLE, columns)
        .transpose(1, 2, 4, 0, 3, 5)
        .reshape(N_CHIP, 2, N_SAMPLE, head_count, rows * columns)
    )
    bias_grad = scatter_sum(bias_blocks, 3).reshape(head_count, rows, columns)
    every_gradient = jnp.concatenate([d_query, d_gate, d_key, d_value], axis=2)
    normalized_hidden_gradient = jnp.einsum(
        "xqu,bu->xqb", every_gradient, attention_input_weight, preferred_element_type=jnp.float32
    )
    attention_input_weight_gradient = jnp.einsum(
        "jol,jot->lt", normalized_hidden_bfloat, every_gradient, preferred_element_type=jnp.float32
    )
    attention_output_weight_gradient = jnp.einsum(
        "jol,jot->lt", gated_attention, token_output_cotangent, preferred_element_type=jnp.float32
    )
    grad_tokens = token_output_cotangent.astype(jnp.float32) + norm_back(
        normed_h, inverse_h, normalized_hidden_gradient, 2
    )
    cond_grad = (jnp.sum(grad_tokens, axis=0) / token_counts[:, None]).astype(BF16)
    d_act = lax.dot_general(
        one_hot, cond_grad, (((0,), (0,)), ((), ())), preferred_element_type=F32
    ) * silu_slope(atom_pre)
    grad_atom_w = lax.dot_general(
        every_feat, d_act.astype(BF16), (((0,), (0,)), ((), ())), preferred_element_type=F32
    )
    d_normed_n = jnp.einsum("hij,zh->ijz", bias_grad, bias_w.astype(jnp.float32), precision=HIGHEST)
    grad_bias_w = jnp.einsum(
        "ijz,hij->zh", normed_nb.astype(jnp.float32), bias_grad, precision=HIGHEST
    )
    d_next = cot_pair.astype(jnp.float32) + norm_back(normed_n, inverse_n, d_normed_n, 2)
    d_linear = (d_next * tri_gate).astype(jnp.bfloat16)
    d_gate_pre = (d_next * linear * tri_gate * (1.0 - tri_gate)).astype(jnp.bfloat16)
    grad_tri_out_w = jnp.einsum(
        "cij,ijz->cz", normed_pb, d_linear, preferred_element_type=jnp.float32
    )
    d_normed_p = jnp.einsum("ijz,cz->cij", d_linear, tri_out_w, preferred_element_type=jnp.float32)
    d_product = norm_back(normed_p, inverse_p, d_normed_p, 0).astype(jnp.bfloat16)
    d_product_panel = (
        exchange(d_product.astype(F32).reshape(blocks + (4, 128)), 4)
        .reshape(blocks + (rows, columns))
        .astype(BF16)
        .transpose(0, 2, 1, 3)
        .reshape(N_TILE * rows, N_SAMPLE * columns)
    )
    d_left_panel = jnp.dot(d_product_panel, right_panel, preferred_element_type=F32)
    d_right_panel = jnp.dot(d_product_panel.T, left_panel, preferred_element_type=F32)
    d_halves = (
        jnp.stack([d_left_panel, d_right_panel])
        .reshape(2, N_TILE, rows, N_SAMPLE, columns)
        .transpose(1, 3, 0, 2, 4)
        .reshape(blocks + (8, 128))
    )
    d_halves = exchange(d_halves, 5).reshape(hidden, 2, rows, columns)
    d_left, d_right = d_halves[:, 0], d_halves[:, 1]
    d_proj = jnp.concatenate(
        [
            d_left * projected[hidden : 2 * hidden] * mask_rows * gate_left * (1.0 - gate_left),
            d_left * gate_left * mask_rows,
            d_right * projected[3 * hidden :] * mask_rows * gate_right * (1.0 - gate_right),
            d_right * gate_right * mask_rows,
        ],
        axis=0,
    ).astype(jnp.bfloat16)
    grad_tri_in_w = jnp.einsum("ijz,cij->zc", normed_zb, d_proj, preferred_element_type=jnp.float32)
    grad_tri_gate_w = jnp.einsum(
        "ijz,ijy->zy", normed_zb, d_gate_pre, preferred_element_type=jnp.float32
    )
    d_normed_z = jnp.einsum(
        "cij,zc->ijz", d_proj, tri_in_w, preferred_element_type=jnp.float32
    ) + jnp.einsum("ijy,zy->ijz", d_gate_pre, tri_gate_w, preferred_element_type=jnp.float32)
    grad_pair = d_next + norm_back(normed_z, inverse_z, d_normed_z, 2)
    axes = ("tile", "sample")
    grad_in_w, grad_out_w = lax.psum(
        (
            attention_input_weight_gradient.astype(BF16),
            attention_output_weight_gradient.astype(BF16),
        ),
        axes,
    )
    summed = lax.psum(
        (grad_tri_in_w, grad_tri_gate_w, grad_tri_out_w, grad_bias_w, grad_atom_w), axes
    ) + (grad_in_w.astype(F32), grad_out_w.astype(F32))
    return (pair_next, token_output_rows, grad_pair, grad_tokens) + summed


def solution(mesh):
    in_specs = (
        P("tile", "sample", None),
        P("tile", "sample"),
        P(),
        P(),
        P(),
        P(),
        P("tile", None),
        P("tile"),
        P(),
        P(("tile", "sample"), None, None),
        P(),
        P(),
        P("tile", "sample", None),
        P(("tile", "sample"), None, None),
    )
    out_specs = (
        P("tile", "sample", None),
        P(("tile", "sample"), None, None),
        P("tile", "sample", None),
        P(("tile", "sample"), None, None),
        P(),
        P(),
        P(),
        P(),
        P(),
        P(),
        P(),
    )
    return jax.shard_map(shards, mesh=mesh, in_specs=in_specs, out_specs=out_specs, check_vma=False)
```

```python
import functools
import math

import jax
import jax.numpy as jnp
from jax import lax
from jax.experimental import pallas as pl
from jax.experimental.pallas import tpu as pltpu
from jax.sharding import PartitionSpec as P

EPSILON = 1e-05
N_TILE = 16
N_SAMPLE = 8
N_CHIP = 8
MESH = pl.DeviceIdType.MESH
BF16 = jnp.bfloat16
F32 = jnp.float32
HIGHEST = lax.Precision.HIGHEST


def enter(t, s):
    barrier = pltpu.get_barrier_semaphore()
    for k in range(1, N_SAMPLE):
        pl.semaphore_signal(
            barrier, inc=1, device_id=(t, lax.rem(s + k, N_SAMPLE)), device_id_type=MESH
        )
    for k in range(1, N_TILE):
        pl.semaphore_signal(
            barrier, inc=1, device_id=(lax.rem(t + k, N_TILE), s), device_id_type=MESH
        )
    pl.semaphore_wait(barrier, N_SAMPLE + N_TILE - 2)


def wait_bytes(ref, sem):
    pltpu.make_async_copy(ref, ref, sem).wait()


def send(src, dst, send_sem, recv_sem, t, s):
    pltpu.make_async_remote_copy(
        src, dst, send_sem, recv_sem, device_id=(t, s), device_id_type=MESH
    ).start()


def exchange_kernel(x, out, mid, send_sem, recv_sem, local_sem):
    t, s = lax.axis_index("tile"), lax.axis_index("sample")
    enter(t, s)
    for k in range(1, N_SAMPLE):
        d = lax.rem(s + k, N_SAMPLE)
        send(x.at[:, d], mid.at[:, s], send_sem.at[0], recv_sem.at[0], t, d)
    own = pltpu.make_async_copy(x.at[:, s], mid.at[:, s], local_sem)
    own.start()
    own.wait()
    wait_bytes(mid.at[:, pl.ds(0, N_SAMPLE - 1)], recv_sem.at[0])
    for k in range(1, N_TILE):
        d = lax.rem(t + k, N_TILE)
        send(mid.at[d], out.at[t], send_sem.at[1], recv_sem.at[1], d, s)
    own = pltpu.make_async_copy(mid.at[t], out.at[t], local_sem)
    own.start()
    own.wait()
    wait_bytes(out.at[pl.ds(0, N_TILE - 1)], recv_sem.at[1])
    wait_bytes(mid.at[:, pl.ds(0, N_SAMPLE - 1)], send_sem.at[0])
    wait_bytes(out.at[pl.ds(0, N_TILE - 1)], send_sem.at[1])


def exchange(x, collective_id):
    return pl.pallas_call(
        exchange_kernel,
        out_shape=jax.ShapeDtypeStruct(x.shape, x.dtype),
        in_specs=[pl.BlockSpec(memory_space=pltpu.VMEM)],
        out_specs=pl.BlockSpec(memory_space=pltpu.VMEM),
        scratch_shapes=[
            pltpu.VMEM(x.shape, x.dtype),
            pltpu.SemaphoreType.DMA((2,)),
            pltpu.SemaphoreType.DMA((2,)),
            pltpu.SemaphoreType.DMA,
        ],
        compiler_params=pltpu.CompilerParams(
            collective_id=collective_id, has_side_effects=True, vmem_limit_bytes=32 << 20
        ),
    )(x)


def exchange_and_gather_kernel(
    x, feats, atoms, out, every_feat, every_atom, mid, send_sem, recv_sem, local_sem, far_sem
):
    t, s = lax.axis_index("tile"), lax.axis_index("sample")
    enter(t, s)
    for k in range(1, N_SAMPLE):
        d = lax.rem(s + k, N_SAMPLE)
        send(x.at[:, d], mid.at[:, s], send_sem.at[0], recv_sem.at[0], t, d)
    for k in range(1, N_TILE):
        d = lax.rem(t + k, N_TILE)
        send(feats, every_feat.at[t], far_sem.at[0], far_sem.at[1], d, s)
        send(atoms, every_atom.at[t], far_sem.at[2], far_sem.at[3], d, s)
    every_feat[t] = feats[...]
    every_atom[t] = atoms[...]
    own = pltpu.make_async_copy(x.at[:, s], mid.at[:, s], local_sem)
    own.start()
    own.wait()
    wait_bytes(mid.at[:, pl.ds(0, N_SAMPLE - 1)], recv_sem.at[0])
    for k in range(1, N_TILE):
        d = lax.rem(t + k, N_TILE)
        send(mid.at[d], out.at[t], send_sem.at[1], recv_sem.at[1], d, s)
    own = pltpu.make_async_copy(mid.at[t], out.at[t], local_sem)
    own.start()
    own.wait()
    wait_bytes(out.at[pl.ds(0, N_TILE - 1)], recv_sem.at[1])
    wait_bytes(mid.at[:, pl.ds(0, N_SAMPLE - 1)], send_sem.at[0])
    wait_bytes(out.at[pl.ds(0, N_TILE - 1)], send_sem.at[1])
    for i in (0, 1):
        wait_bytes(every_feat.at[pl.ds(0, N_TILE - 1)], far_sem.at[i])
        wait_bytes(every_atom.at[pl.ds(0, N_TILE - 1)], far_sem.at[2 + i])


def exchange_and_gather(x, feats, atoms, collective_id):
    return pl.pallas_call(
        exchange_and_gather_kernel,
        out_shape=(
            jax.ShapeDtypeStruct(x.shape, x.dtype),
            jax.ShapeDtypeStruct((N_TILE,) + feats.shape, feats.dtype),
            jax.ShapeDtypeStruct((N_TILE,) + atoms.shape, atoms.dtype),
        ),
        in_specs=[pl.BlockSpec(memory_space=pltpu.VMEM)] * 3,
        out_specs=[pl.BlockSpec(memory_space=pltpu.VMEM)] * 3,
        scratch_shapes=[
            pltpu.VMEM(x.shape, x.dtype),
            pltpu.SemaphoreType.DMA((2,)),
            pltpu.SemaphoreType.DMA((2,)),
            pltpu.SemaphoreType.DMA,
            pltpu.SemaphoreType.DMA((4,)),
        ],
        compiler_params=pltpu.CompilerParams(
            collective_id=collective_id, has_side_effects=True, vmem_limit_bytes=32 << 20
        ),
    )(x, feats, atoms)


def gather_kernel(x, out, send_sem, recv_sem, local_sem):
    t, s = lax.axis_index("tile"), lax.axis_index("sample")
    m, c = t // 2, lax.rem(t, 2)
    other = m * 2 + 1 - c
    enter(t, s)
    own = pltpu.make_async_copy(x, out.at[m, c, s], local_sem)
    own.start()
    for k in range(1, N_SAMPLE):
        send(x, out.at[m, c, s], send_sem.at[0], recv_sem.at[0], t, lax.rem(s + k, N_SAMPLE))
    own.wait()
    wait_bytes(out.at[m, c, pl.ds(0, N_SAMPLE - 1)], recv_sem.at[0])
    block = out.at[m, c]
    send(block, block, send_sem.at[1], recv_sem.at[N_CHIP], other, s)
    for k in range(1, N_CHIP):
        send(block, block, send_sem.at[1], recv_sem.at[k], lax.rem(m + k, N_CHIP) * 2 + c, s)
    for k in range(1, N_CHIP):
        arrived = out.at[lax.rem(m + N_CHIP - k, N_CHIP), c]
        wait_bytes(arrived, recv_sem.at[k])
        send(arrived, arrived, send_sem.at[1], recv_sem.at[N_CHIP], other, s)
    wait_bytes(out.at[:, 0], recv_sem.at[N_CHIP])
    wait_bytes(out.at[0, 0, pl.ds(0, N_SAMPLE - 1)], send_sem.at[0])
    wait_bytes(out.at[:, 0], send_sem.at[1])
    wait_bytes(out.at[pl.ds(0, N_CHIP - 1), 0], send_sem.at[1])


def gather(x, collective_id):
    return pl.pallas_call(
        gather_kernel,
        out_shape=jax.ShapeDtypeStruct((N_CHIP, 2, N_SAMPLE) + x.shape, x.dtype),
        in_specs=[pl.BlockSpec(memory_space=pltpu.VMEM)],
        out_specs=pl.BlockSpec(memory_space=pltpu.VMEM),
        scratch_shapes=[
            pltpu.SemaphoreType.DMA((2,)),
            pltpu.SemaphoreType.DMA((N_CHIP + 1,)),
            pltpu.SemaphoreType.DMA,
        ],
        compiler_params=pltpu.CompilerParams(
            collective_id=collective_id, has_side_effects=True, vmem_limit_bytes=32 << 20
        ),
    )(x)


def scatter_sum_kernel(x, out, pair_sum, by_chip, by_sample, send_sem, recv_sem):
    t, s = lax.axis_index("tile"), lax.axis_index("sample")
    m, c = t // 2, lax.rem(t, 2)
    enter(t, s)
    for k in range(1, N_CHIP + 1):
        d = lax.rem(m + k, N_CHIP)
        send(x.at[d, 1 - c], pair_sum.at[d], send_sem.at[0], recv_sem.at[k], m * 2 + 1 - c, s)
    for k in range(1, N_CHIP + 1):
        d = lax.rem(m + k, N_CHIP)
        wait_bytes(pair_sum.at[d], recv_sem.at[k])
        pair_sum[d] = (pair_sum[d].astype(F32) + x[d, c].astype(F32)).astype(x.dtype)
        if k < N_CHIP:
            send(
                pair_sum.at[d],
                by_chip.at[k - 1],
                send_sem.at[1],
                recv_sem.at[N_CHIP + k],
                d * 2 + c,
                s,
            )
    total = pair_sum[m].astype(F32)
    for k in range(1, N_CHIP):
        wait_bytes(by_chip.at[k - 1], recv_sem.at[N_CHIP + k])
        total = total + by_chip[k - 1].astype(F32)
    pair_sum[m] = total.astype(x.dtype)
    for k in range(1, N_SAMPLE):
        d = lax.rem(s + k, N_SAMPLE)
        send(pair_sum.at[m, d], by_sample.at[k - 1], send_sem.at[2], recv_sem.at[0], t, d)
    wait_bytes(by_sample, recv_sem.at[0])
    out[...] = pair_sum[m, s].astype(F32) + jnp.sum(by_sample[...].astype(F32), axis=0)
    wait_bytes(pair_sum, send_sem.at[0])
    wait_bytes(by_chip, send_sem.at[1])
    wait_bytes(by_sample, send_sem.at[2])


def scatter_sum(x, collective_id):
    block = x.shape[3:]
    return pl.pallas_call(
        scatter_sum_kernel,
        out_shape=jax.ShapeDtypeStruct(block, F32),
        in_specs=[pl.BlockSpec(memory_space=pltpu.VMEM)],
        out_specs=pl.BlockSpec(memory_space=pltpu.VMEM),
        scratch_shapes=[
            pltpu.VMEM((N_CHIP, N_SAMPLE) + block, x.dtype),
            pltpu.VMEM((N_CHIP - 1, N_SAMPLE) + block, x.dtype),
            pltpu.VMEM((N_SAMPLE - 1,) + block, x.dtype),
            pltpu.SemaphoreType.DMA((3,)),
            pltpu.SemaphoreType.DMA((2 * N_CHIP,)),
        ],
        compiler_params=pltpu.CompilerParams(
            collective_id=collective_id, has_side_effects=True, vmem_limit_bytes=32 << 20
        ),
    )(x)


QUARTER = 208
PADDED = 256
WIDTH = 640


def reduce_kernel(
    left_in,
    right_in,
    left_out,
    right_out,
    small,
    full,
    mine,
    theirs,
    from_core,
    part1,
    sum1,
    part2,
    sum2,
    part3,
    sum3,
    send_sem,
    recv_sem,
):
    t, s = lax.axis_index("tile"), lax.axis_index("sample")
    core = lax.rem(t, 2)
    place = [lax.rem(s, 2) * 2 + t // 8, lax.rem(t // 2, 4), s // 2]

    def device(where, c):
        return (lax.rem(where[0], 2) * 8 + where[1] * 2 + c, where[2] * 2 + where[0] // 2)

    def peer(axis, k):
        where = list(place)
        where[axis] = lax.rem(place[axis] + k, 4)
        return where[axis], device(where, core)

    partner = device(place, 1 - core)
    barrier = pltpu.get_barrier_semaphore()
    others = [partner] + [peer(axis, k)[1] for axis in range(3) for k in range(1, 4)]
    for other in others:
        pl.semaphore_signal(barrier, inc=1, device_id=other, device_id_type=MESH)

    def form(g, c, target):
        wide = pl.ds(pl.multiple_of(g * 1024 + c * 512, 512), 512)
        narrow = pl.ds(pl.multiple_of(g * 256 + c * 128, 128), 128)
        chunk = pl.ds(pl.multiple_of(g * WIDTH, 128), WIDTH)

        @pl.loop(0, 4)
        def _(a):
            rows = pl.ds(pl.multiple_of(a * 192, 64), 192)
            target[g, a, pl.ds(0, 192), pl.ds(0, 512)] = jnp.dot(
                left_in[rows, :], right_in[:, wide], preferred_element_type=F32
            ).astype(BF16)
            target[g, a, pl.ds(0, 192), pl.ds(512, 128)] = jnp.dot(
                left_out[rows, :], right_out[:, narrow], preferred_element_type=F32
            ).astype(BF16)
            target[g, a, pl.ds(192, 16), :] = small[
                pl.ds(pl.multiple_of(c * 64 + a * 16, 16), 16), chunk
            ]

    def add(count, store, *terms):
        @pl.loop(0, count)
        def _(r):
            rows = pl.ds(pl.multiple_of(r * 16, 16), 16)
            total = terms[0](rows).astype(F32)
            for term in terms[1:]:
                total = total + term(rows).astype(F32)
            store(rows, total.astype(BF16))

    for g in range(3):
        form(g, 1 - core, theirs)
        if g == 0:
            pl.semaphore_wait(barrier, len(others))
        send(theirs.at[g], from_core.at[g], send_sem.at[0], recv_sem.at[g, 0], *partner)
    for g in range(3):
        form(g, core, mine)
        wait_bytes(from_core.at[g], recv_sem.at[g, 0])
        for a in range(4):

            def put(rows, total, g=g, a=a):
                mine[g, a, rows, :] = total

            add(
                QUARTER // 16,
                put,
                lambda rows, g=g, a=a: mine[g, a, rows, :],
                lambda rows, g=g, a=a: from_core[g, a, rows, :],
            )
        for k in range(1, 4):
            d, to = peer(g, k)
            send(mine.at[g, d], part1.at[g, k - 1], send_sem.at[1], recv_sem.at[g, 1], *to)
    for g in range(3):
        p1 = place[g]
        wait_bytes(part1.at[g], recv_sem.at[g, 1])

        def put(rows, total, g=g):
            sum1[g, rows, :] = total

        add(
            QUARTER // 16,
            put,
            lambda rows, g=g, p1=p1: mine[g, p1, rows, :],
            *[lambda rows, g=g, k=k: part1[g, k, rows, :] for k in range(3)],
        )
        sum1[g, pl.ds(QUARTER, PADDED - QUARTER), :] = jnp.zeros((PADDED - QUARTER, WIDTH), BF16)
        for k in range(1, 4):
            d, to = peer((g + 1) % 3, k)
            rows = pl.ds(pl.multiple_of(d * 64, 64), 64)
            send(sum1.at[g, rows], part2.at[g, k - 1], send_sem.at[2], recv_sem.at[g, 2], *to)
    for g in range(3):
        first = place[(g + 1) % 3] * 64
        wait_bytes(part2.at[g], recv_sem.at[g, 2])
        rows = pl.ds(pl.multiple_of(first, 64), 64)
        total = sum1[g, rows, :].astype(F32)
        for k in range(3):
            total = total + part2[g, k].astype(F32)
        sum2[g] = total.astype(BF16)
        for k in range(1, 4):
            d, to = peer((g + 2) % 3, k)
            rows = pl.ds(pl.multiple_of(d * 16, 16), 16)
            send(sum2.at[g, rows], part3.at[g, k - 1], send_sem.at[3], recv_sem.at[g, 3], *to)
    for g in range(3):
        p1, p2, p3 = place[g], place[(g + 1) % 3], place[(g + 2) % 3]
        wait_bytes(part3.at[g], recv_sem.at[g, 3])
        total = sum2[g, pl.ds(pl.multiple_of(p3 * 16, 16), 16), :].astype(F32)
        for k in range(3):
            total = total + part3[g, k].astype(F32)
        rows = pl.ds(pl.multiple_of(p2 * 64 + p3 * 16, 16), 16)
        full[g, core, p1, rows, :] = total.astype(BF16)
        block = full.at[g, core, p1, rows]
        for k in range(1, 4):
            _, to = peer((g + 2) % 3, k)
            send(block, block, send_sem.at[4], recv_sem.at[g, 4], *to)
    for g in range(3):
        p1, p2 = place[g], place[(g + 1) % 3]
        wait_bytes(full.at[g, core, p1, pl.ds(0, 48)], recv_sem.at[g, 4])
        block = full.at[g, core, p1, pl.ds(pl.multiple_of(p2 * 64, 64), 64)]
        for k in range(1, 4):
            _, to = peer((g + 1) % 3, k)
            send(block, block, send_sem.at[5], recv_sem.at[g, 5], *to)
    for g in range(3):
        p1 = place[g]
        wait_bytes(full.at[g, core, p1, pl.ds(0, 192)], recv_sem.at[g, 5])
        block = full.at[g, core, p1, pl.ds(0, QUARTER)]
        for k in range(1, 4):
            _, to = peer(g, k)
            send(block, block, send_sem.at[6], recv_sem.at[g, 6], *to)
        send(block, block, send_sem.at[7], recv_sem.at[g, 7], *partner)
    for g in range(3):
        wait_bytes(full.at[g, core, pl.ds(0, 3), pl.ds(0, QUARTER)], recv_sem.at[g, 6])
        for k in range(1, 4):
            block = full.at[g, core, lax.rem(place[g] + k, 4), pl.ds(0, QUARTER)]
            send(block, block, send_sem.at[7], recv_sem.at[g, 7], *partner)
    for g in range(3):
        wait_bytes(full.at[g, 0, :, pl.ds(0, QUARTER)], recv_sem.at[g, 7])
    wait_bytes(theirs, send_sem.at[0])
    wait_bytes(part1, send_sem.at[1])
    wait_bytes(part2, send_sem.at[2])
    wait_bytes(part3, send_sem.at[3])
    wait_bytes(part3, send_sem.at[4])
    wait_bytes(part2, send_sem.at[5])
    wait_bytes(part1, send_sem.at[6])
    wait_bytes(theirs, send_sem.at[7])


def reduce_all(left_in, right_in, left_out, right_out, small, collective_id):
    chunk = (3, 4, QUARTER, WIDTH)
    return pl.pallas_call(
        reduce_kernel,
        out_shape=jax.ShapeDtypeStruct((3, 2, 4, PADDED, WIDTH), BF16),
        in_specs=[pl.BlockSpec(memory_space=pltpu.VMEM)] * 5,
        out_specs=pl.BlockSpec(memory_space=pltpu.VMEM),
        scratch_shapes=[
            pltpu.VMEM(chunk, BF16),
            pltpu.VMEM(chunk, BF16),
            pltpu.VMEM(chunk, BF16),
            pltpu.VMEM((3, 3, QUARTER, WIDTH), BF16),
            pltpu.VMEM((3, PADDED, WIDTH), BF16),
            pltpu.VMEM((3, 3, 64, WIDTH), BF16),
            pltpu.VMEM((3, 64, WIDTH), BF16),
            pltpu.VMEM((3, 3, 16, WIDTH), BF16),
            pltpu.VMEM((3, 16, WIDTH), BF16),
            pltpu.SemaphoreType.DMA((8,)),
            pltpu.SemaphoreType.DMA((3, 8)),
        ],
        compiler_params=pltpu.CompilerParams(
            collective_id=collective_id, has_side_effects=True, vmem_limit_bytes=48 << 20
        ),
    )(left_in, right_in, left_out, right_out, small)


def norm_parts(values, axis):
    centered = values - jnp.mean(values, axis=axis, keepdims=True)
    inverse = lax.rsqrt(jnp.mean(centered * centered, axis=axis, keepdims=True) + EPSILON)
    return (centered * inverse, inverse)


def norm_back(normed, inverse, incoming_gradient, axis):
    first_mean = jnp.mean(incoming_gradient, axis=axis, keepdims=True)
    second_mean = jnp.mean(incoming_gradient * normed, axis=axis, keepdims=True)
    return (incoming_gradient - first_mean - normed * second_mean) * inverse


def silu_slope(values):
    sigmoid_part = jax.nn.sigmoid(values)
    return sigmoid_part * (1.0 + values * (1.0 - sigmoid_part))


def shards(
    pair,
    pair_mask,
    tri_in_w,
    tri_gate_w,
    tri_out_w,
    bias_w,
    atom_feats,
    atom_to_token,
    atom_w,
    tokens,
    attention_input_weight,
    attention_output_weight,
    cot_pair,
    token_output_cotangent,
):
    hidden = tri_in_w.shape[1] // 4
    token_width = attention_input_weight.shape[0]
    head_count = bias_w.shape[1]
    head_size = token_width // head_count
    sample_count = tokens.shape[0]
    total_tokens = tokens.shape[1]
    score_scale = 1.0 / math.sqrt(head_size)
    pair_f = pair.astype(jnp.float32)
    normed_z, inverse_z = norm_parts(pair_f, 2)
    normed_zb = normed_z.astype(jnp.bfloat16)
    projected = jnp.einsum("ijz,zc->cij", normed_zb, tri_in_w, preferred_element_type=jnp.float32)
    mask_rows = pair_mask.astype(jnp.float32)[None]
    gate_left = jax.nn.sigmoid(projected[0:hidden])
    gate_right = jax.nn.sigmoid(projected[2 * hidden : 3 * hidden])
    rows, columns = pair_mask.shape
    blocks = (N_TILE, N_SAMPLE)
    left_local = (gate_left * projected[hidden : 2 * hidden] * mask_rows).astype(BF16)
    right_local = (gate_right * projected[3 * hidden :] * mask_rows).astype(BF16)
    halves = jnp.stack([left_local, right_local], axis=1).astype(F32)
    halves, every_feat, every_atom = exchange_and_gather(
        halves.reshape(blocks + (8, 128)), atom_feats, atom_to_token[None], 0
    )
    every_feat = every_feat.reshape(-1, atom_feats.shape[1])
    every_atom = every_atom.reshape(-1)
    panels = (
        halves.reshape(blocks + (2, rows, columns))
        .astype(BF16)
        .transpose(2, 0, 3, 1, 4)
        .reshape(2, N_TILE * rows, N_SAMPLE * columns)
    )
    left_panel, right_panel = panels[0], panels[1]
    product_panel = jnp.dot(left_panel, right_panel.T, preferred_element_type=F32).astype(BF16)
    product_blocks = (
        product_panel.reshape(N_TILE, rows, N_SAMPLE, columns)
        .transpose(0, 2, 1, 3)
        .reshape(blocks + (4, 128))
    )
    product = exchange(product_blocks.astype(F32), 1).reshape(hidden, rows, columns)
    normed_p, inverse_p = norm_parts(product, 0)
    normed_pb = normed_p.astype(jnp.bfloat16)
    linear = jnp.einsum("cij,cz->ijz", normed_pb, tri_out_w, preferred_element_type=jnp.float32)
    tri_gate = jax.nn.sigmoid(
        jnp.einsum("ijz,zy->ijy", normed_zb, tri_gate_w, preferred_element_type=jnp.float32)
    )
    pair_next = pair_f + tri_gate * linear
    normed_n, inverse_n = norm_parts(pair_next, 2)
    normed_nb = normed_n.astype(jnp.bfloat16)
    bias_local = jnp.einsum(
        "ijz,zh->hij", normed_nb, bias_w, preferred_element_type=jnp.float32
    ).astype(jnp.bfloat16)
    bias_all = (
        gather(bias_local.reshape(head_count, rows * columns), 2)
        .reshape(N_TILE, N_SAMPLE, head_count, rows, columns)
        .transpose(2, 0, 3, 1, 4)
        .reshape(head_count, N_TILE * rows, N_SAMPLE * columns)
    )
    atom_pre = jnp.dot(every_feat, atom_w, preferred_element_type=jnp.float32)
    atom_act = jax.nn.silu(atom_pre).astype(BF16)
    token_ids = jnp.arange(total_tokens, dtype=jnp.int32)
    one_hot = (token_ids[:, None] == every_atom[None, :]).astype(BF16)
    token_sums = jnp.dot(one_hot, atom_act, preferred_element_type=F32)
    token_counts = jnp.sum(one_hot.astype(F32), axis=1)
    token_cond = token_sums / token_counts[:, None]
    token_state_rows = tokens.astype(jnp.float32) + token_cond[None]
    normed_h, inverse_h = norm_parts(token_state_rows, 2)
    normalized_hidden_bfloat = normed_h.astype(jnp.bfloat16)
    projected_hidden = jnp.einsum(
        "zut,tw->zuw",
        normalized_hidden_bfloat,
        attention_input_weight,
        preferred_element_type=jnp.float32,
    )
    queries = (
        projected_hidden[:, :, :token_width]
        .astype(jnp.bfloat16)
        .reshape(sample_count, total_tokens, head_count, head_size)
    )
    gate_values = jax.nn.sigmoid(projected_hidden[:, :, token_width : 2 * token_width])
    keys_all = (
        projected_hidden[:, :, 2 * token_width : 3 * token_width]
        .astype(jnp.bfloat16)
        .reshape(sample_count, total_tokens, head_count, head_size)
    )
    values_all = (
        projected_hidden[:, :, 3 * token_width :]
        .astype(jnp.bfloat16)
        .reshape(sample_count, total_tokens, head_count, head_size)
    )
    scores = (
        jnp.einsum("sihd,sjhd->shij", queries, keys_all, preferred_element_type=jnp.float32)
        * score_scale
        + bias_all.astype(jnp.float32)[None]
    )
    top_score = jnp.max(scores, axis=3, keepdims=True)
    weights = jnp.exp(scores - top_score)
    attn_probs = weights / jnp.sum(weights, axis=3, keepdims=True)
    probs_b = attn_probs.astype(jnp.bfloat16)
    attended = jnp.einsum(
        "shij,sjhd->sihd", probs_b, values_all, preferred_element_type=jnp.float32
    ).reshape(sample_count, total_tokens, token_width)
    gated_attention = (gate_values * attended).astype(jnp.bfloat16)
    token_output_rows = token_state_rows + jnp.einsum(
        "zut,tw->zuw", gated_attention, attention_output_weight, preferred_element_type=jnp.float32
    )
    incoming_gradient = jnp.einsum(
        "xqu,bu->xqb",
        token_output_cotangent,
        attention_output_weight,
        preferred_element_type=jnp.float32,
    )
    d_att = (incoming_gradient * gate_values).astype(jnp.bfloat16)
    d_gate = (incoming_gradient * attended * gate_values * (1.0 - gate_values)).astype(jnp.bfloat16)
    d_att_h = d_att.reshape(sample_count, total_tokens, head_count, head_size)
    d_probs = jnp.einsum("sihd,sjhd->shij", d_att_h, values_all, preferred_element_type=jnp.float32)
    d_scores = attn_probs * (d_probs - jnp.sum(attn_probs * d_probs, axis=3, keepdims=True))
    d_scores_b = d_scores.astype(jnp.bfloat16)
    d_query = (
        (
            jnp.einsum("shij,sjhd->sihd", d_scores_b, keys_all, preferred_element_type=jnp.float32)
            * score_scale
        )
        .astype(jnp.bfloat16)
        .reshape(sample_count, total_tokens, token_width)
    )
    d_key = (
        (
            jnp.einsum("shij,sihd->sjhd", d_scores_b, queries, preferred_element_type=jnp.float32)
            * score_scale
        )
        .astype(jnp.bfloat16)
        .reshape(sample_count, total_tokens, token_width)
    )
    d_value = (
        jnp.einsum("shij,sihd->sjhd", probs_b, d_att_h, preferred_element_type=jnp.float32)
        .astype(jnp.bfloat16)
        .reshape(sample_count, total_tokens, token_width)
    )
    bias_term = jnp.sum(d_scores, axis=0)
    bias_blocks = (
        bias_term.astype(BF16)
        .reshape(head_count, N_CHIP, 2, rows, N_SAMPLE, columns)
        .transpose(1, 2, 4, 0, 3, 5)
        .reshape(N_CHIP, 2, N_SAMPLE, head_count, rows * columns)
    )
    bias_grad = scatter_sum(bias_blocks, 3).reshape(head_count, rows, columns)
    every_gradient = jnp.concatenate([d_query, d_gate, d_key, d_value], axis=2)
    normalized_hidden_gradient = jnp.einsum(
        "xqu,bu->xqb", every_gradient, attention_input_weight, preferred_element_type=jnp.float32
    )
    grad_tokens = token_output_cotangent.astype(jnp.float32) + norm_back(
        normed_h, inverse_h, normalized_hidden_gradient, 2
    )
    cond_grad = (jnp.sum(grad_tokens, axis=0) / token_counts[:, None]).astype(BF16)
    d_act = lax.dot_general(
        one_hot, cond_grad, (((0,), (0,)), ((), ())), preferred_element_type=F32
    ) * silu_slope(atom_pre)
    grad_atom_w = lax.dot_general(
        every_feat, d_act.astype(BF16), (((0,), (0,)), ((), ())), preferred_element_type=F32
    )
    d_normed_n = jnp.einsum("hij,zh->ijz", bias_grad, bias_w.astype(jnp.float32), precision=HIGHEST)
    grad_bias_w = jnp.einsum(
        "ijz,hij->zh", normed_nb.astype(jnp.float32), bias_grad, precision=HIGHEST
    )
    d_next = cot_pair.astype(jnp.float32) + norm_back(normed_n, inverse_n, d_normed_n, 2)
    d_linear = (d_next * tri_gate).astype(jnp.bfloat16)
    d_gate_pre = (d_next * linear * tri_gate * (1.0 - tri_gate)).astype(jnp.bfloat16)
    grad_tri_out_w = jnp.einsum(
        "cij,ijz->cz", normed_pb, d_linear, preferred_element_type=jnp.float32
    )
    d_normed_p = jnp.einsum("ijz,cz->cij", d_linear, tri_out_w, preferred_element_type=jnp.float32)
    d_product = norm_back(normed_p, inverse_p, d_normed_p, 0).astype(jnp.bfloat16)
    d_product_panel = (
        exchange(d_product.astype(F32).reshape(blocks + (4, 128)), 4)
        .reshape(blocks + (rows, columns))
        .astype(BF16)
        .transpose(0, 2, 1, 3)
        .reshape(N_TILE * rows, N_SAMPLE * columns)
    )
    d_left_panel = jnp.dot(d_product_panel, right_panel, preferred_element_type=F32)
    d_right_panel = jnp.dot(d_product_panel.T, left_panel, preferred_element_type=F32)
    d_halves = (
        jnp.stack([d_left_panel, d_right_panel])
        .reshape(2, N_TILE, rows, N_SAMPLE, columns)
        .transpose(1, 3, 0, 2, 4)
        .reshape(blocks + (8, 128))
    )
    d_halves = exchange(d_halves, 5).reshape(hidden, 2, rows, columns)
    d_left, d_right = d_halves[:, 0], d_halves[:, 1]
    d_proj = jnp.concatenate(
        [
            d_left * projected[hidden : 2 * hidden] * mask_rows * gate_left * (1.0 - gate_left),
            d_left * gate_left * mask_rows,
            d_right * projected[3 * hidden :] * mask_rows * gate_right * (1.0 - gate_right),
            d_right * gate_right * mask_rows,
        ],
        axis=0,
    ).astype(jnp.bfloat16)
    grad_tri_in_w = jnp.einsum("ijz,cij->zc", normed_zb, d_proj, preferred_element_type=jnp.float32)
    grad_tri_gate_w = jnp.einsum(
        "ijz,ijy->zy", normed_zb, d_gate_pre, preferred_element_type=jnp.float32
    )
    d_normed_z = jnp.einsum(
        "cij,zc->ijz", d_proj, tri_in_w, preferred_element_type=jnp.float32
    ) + jnp.einsum("ijy,zy->ijz", d_gate_pre, tri_gate_w, preferred_element_type=jnp.float32)
    grad_pair = d_next + norm_back(normed_z, inverse_z, d_normed_z, 2)
    small = jnp.concatenate(
        [
            grad_tri_in_w,
            grad_tri_gate_w,
            grad_tri_out_w,
            grad_bias_w,
            jnp.zeros((hidden, 128 - head_count), F32),
            grad_atom_w,
            jnp.zeros((hidden, 3 * WIDTH - 4 * hidden - 3 * 128 - token_width), F32),
        ],
        axis=1,
    ).astype(BF16)
    full = reduce_all(
        normalized_hidden_bfloat.reshape(-1, token_width).T,
        every_gradient.reshape(-1, 4 * token_width),
        gated_attention.reshape(-1, token_width).T,
        token_output_cotangent.reshape(-1, token_width),
        small,
        6,
    )
    small_sum = (
        full[:, :, :, 192:QUARTER].transpose(1, 2, 3, 0, 4).reshape(hidden, 3 * WIDTH).astype(F32)
    )
    at = 4 * hidden
    summed = (
        small_sum[:, :at],
        small_sum[:, at : at + 128],
        small_sum[:, at + 128 : at + 256],
        small_sum[:, at + 256 : at + 256 + head_count],
        small_sum[:, at + 384 : at + 384 + token_width],
        full[:, :, :, :192, :512]
        .transpose(2, 3, 0, 1, 4)
        .reshape(token_width, 4 * token_width)
        .astype(F32),
        full[:, :, :, :192, 512:]
        .transpose(2, 3, 0, 1, 4)
        .reshape(token_width, token_width)
        .astype(F32),
    )
    return (pair_next, token_output_rows, grad_pair, grad_tokens) + summed


def solution(mesh):
    in_specs = (
        P("tile", "sample", None),
        P("tile", "sample"),
        P(),
        P(),
        P(),
        P(),
        P("tile", None),
        P("tile"),
        P(),
        P(("tile", "sample"), None, None),
        P(),
        P(),
        P("tile", "sample", None),
        P(("tile", "sample"), None, None),
    )
    out_specs = (
        P("tile", "sample", None),
        P(("tile", "sample"), None, None),
        P("tile", "sample", None),
        P(("tile", "sample"), None, None),
        P(),
        P(),
        P(),
        P(),
        P(),
        P(),
        P(),
    )
    return jax.shard_map(shards, mesh=mesh, in_specs=in_specs, out_specs=out_specs, check_vma=False)
```

```python
import functools
import math

import jax
import jax.numpy as jnp
from jax import lax
from jax.experimental import pallas as pl
from jax.experimental.pallas import tpu as pltpu
from jax.sharding import PartitionSpec as P

EPSILON = 1e-05
N_TILE = 16
N_SAMPLE = 8
N_CHIP = 8
MESH = pl.DeviceIdType.MESH
BF16 = jnp.bfloat16
F32 = jnp.float32
HIGHEST = lax.Precision.HIGHEST


def enter(t, s):
    barrier = pltpu.get_barrier_semaphore()
    for k in range(1, N_SAMPLE):
        pl.semaphore_signal(
            barrier, inc=1, device_id=(t, lax.rem(s + k, N_SAMPLE)), device_id_type=MESH
        )
    for k in range(1, N_TILE):
        pl.semaphore_signal(
            barrier, inc=1, device_id=(lax.rem(t + k, N_TILE), s), device_id_type=MESH
        )
    pl.semaphore_wait(barrier, N_SAMPLE + N_TILE - 2)


def wait_bytes(ref, sem):
    pltpu.make_async_copy(ref, ref, sem).wait()


def send(src, dst, send_sem, recv_sem, t, s):
    pltpu.make_async_remote_copy(
        src, dst, send_sem, recv_sem, device_id=(t, s), device_id_type=MESH
    ).start()


def exchange_kernel(x, out, mid, send_sem, recv_sem, local_sem):
    t, s = lax.axis_index("tile"), lax.axis_index("sample")
    enter(t, s)
    for k in range(1, N_SAMPLE):
        d = lax.rem(s + k, N_SAMPLE)
        send(x.at[:, d], mid.at[:, s], send_sem.at[0], recv_sem.at[0], t, d)
    own = pltpu.make_async_copy(x.at[:, s], mid.at[:, s], local_sem)
    own.start()
    own.wait()
    wait_bytes(mid.at[:, pl.ds(0, N_SAMPLE - 1)], recv_sem.at[0])
    for k in range(1, N_TILE):
        d = lax.rem(t + k, N_TILE)
        send(mid.at[d], out.at[t], send_sem.at[1], recv_sem.at[1], d, s)
    own = pltpu.make_async_copy(mid.at[t], out.at[t], local_sem)
    own.start()
    own.wait()
    wait_bytes(out.at[pl.ds(0, N_TILE - 1)], recv_sem.at[1])
    wait_bytes(mid.at[:, pl.ds(0, N_SAMPLE - 1)], send_sem.at[0])
    wait_bytes(out.at[pl.ds(0, N_TILE - 1)], send_sem.at[1])


def exchange(x, collective_id):
    return pl.pallas_call(
        exchange_kernel,
        out_shape=jax.ShapeDtypeStruct(x.shape, x.dtype),
        in_specs=[pl.BlockSpec(memory_space=pltpu.VMEM)],
        out_specs=pl.BlockSpec(memory_space=pltpu.VMEM),
        scratch_shapes=[
            pltpu.VMEM(x.shape, x.dtype),
            pltpu.SemaphoreType.DMA((2,)),
            pltpu.SemaphoreType.DMA((2,)),
            pltpu.SemaphoreType.DMA,
        ],
        compiler_params=pltpu.CompilerParams(
            collective_id=collective_id, has_side_effects=True, vmem_limit_bytes=32 << 20
        ),
    )(x)


def exchange_and_gather_kernel(
    x, feats, atoms, out, every_feat, every_atom, mid, send_sem, recv_sem, local_sem, far_sem
):
    t, s = lax.axis_index("tile"), lax.axis_index("sample")
    enter(t, s)
    for k in range(1, N_SAMPLE):
        d = lax.rem(s + k, N_SAMPLE)
        send(x.at[:, d], mid.at[:, s], send_sem.at[0], recv_sem.at[0], t, d)
    for k in range(1, N_TILE):
        d = lax.rem(t + k, N_TILE)
        send(feats, every_feat.at[t], far_sem.at[0], far_sem.at[1], d, s)
        send(atoms, every_atom.at[t], far_sem.at[2], far_sem.at[3], d, s)
    every_feat[t] = feats[...]
    every_atom[t] = atoms[...]
    own = pltpu.make_async_copy(x.at[:, s], mid.at[:, s], local_sem)
    own.start()
    own.wait()
    wait_bytes(mid.at[:, pl.ds(0, N_SAMPLE - 1)], recv_sem.at[0])
    for k in range(1, N_TILE):
        d = lax.rem(t + k, N_TILE)
        send(mid.at[d], out.at[t], send_sem.at[1], recv_sem.at[1], d, s)
    own = pltpu.make_async_copy(mid.at[t], out.at[t], local_sem)
    own.start()
    own.wait()
    wait_bytes(out.at[pl.ds(0, N_TILE - 1)], recv_sem.at[1])
    wait_bytes(mid.at[:, pl.ds(0, N_SAMPLE - 1)], send_sem.at[0])
    wait_bytes(out.at[pl.ds(0, N_TILE - 1)], send_sem.at[1])
    for i in (0, 1):
        wait_bytes(every_feat.at[pl.ds(0, N_TILE - 1)], far_sem.at[i])
        wait_bytes(every_atom.at[pl.ds(0, N_TILE - 1)], far_sem.at[2 + i])


def exchange_and_gather(x, feats, atoms, collective_id):
    return pl.pallas_call(
        exchange_and_gather_kernel,
        out_shape=(
            jax.ShapeDtypeStruct(x.shape, x.dtype),
            jax.ShapeDtypeStruct((N_TILE,) + feats.shape, feats.dtype),
            jax.ShapeDtypeStruct((N_TILE,) + atoms.shape, atoms.dtype),
        ),
        in_specs=[pl.BlockSpec(memory_space=pltpu.VMEM)] * 3,
        out_specs=[pl.BlockSpec(memory_space=pltpu.VMEM)] * 3,
        scratch_shapes=[
            pltpu.VMEM(x.shape, x.dtype),
            pltpu.SemaphoreType.DMA((2,)),
            pltpu.SemaphoreType.DMA((2,)),
            pltpu.SemaphoreType.DMA,
            pltpu.SemaphoreType.DMA((4,)),
        ],
        compiler_params=pltpu.CompilerParams(
            collective_id=collective_id, has_side_effects=True, vmem_limit_bytes=32 << 20
        ),
    )(x, feats, atoms)


def gather_kernel(x, out, send_sem, recv_sem, local_sem):
    t, s = lax.axis_index("tile"), lax.axis_index("sample")
    m, c = t // 2, lax.rem(t, 2)
    other = m * 2 + 1 - c
    enter(t, s)
    own = pltpu.make_async_copy(x, out.at[m, c, s], local_sem)
    own.start()
    for k in range(1, N_SAMPLE):
        send(x, out.at[m, c, s], send_sem.at[0], recv_sem.at[0], t, lax.rem(s + k, N_SAMPLE))
    own.wait()
    wait_bytes(out.at[m, c, pl.ds(0, N_SAMPLE - 1)], recv_sem.at[0])
    block = out.at[m, c]
    send(block, block, send_sem.at[1], recv_sem.at[N_CHIP], other, s)
    for k in range(1, N_CHIP):
        send(block, block, send_sem.at[1], recv_sem.at[k], lax.rem(m + k, N_CHIP) * 2 + c, s)
    for k in range(1, N_CHIP):
        arrived = out.at[lax.rem(m + N_CHIP - k, N_CHIP), c]
        wait_bytes(arrived, recv_sem.at[k])
        send(arrived, arrived, send_sem.at[1], recv_sem.at[N_CHIP], other, s)
    wait_bytes(out.at[:, 0], recv_sem.at[N_CHIP])
    wait_bytes(out.at[0, 0, pl.ds(0, N_SAMPLE - 1)], send_sem.at[0])
    wait_bytes(out.at[:, 0], send_sem.at[1])
    wait_bytes(out.at[pl.ds(0, N_CHIP - 1), 0], send_sem.at[1])


def gather(x, collective_id):
    return pl.pallas_call(
        gather_kernel,
        out_shape=jax.ShapeDtypeStruct((N_CHIP, 2, N_SAMPLE) + x.shape, x.dtype),
        in_specs=[pl.BlockSpec(memory_space=pltpu.VMEM)],
        out_specs=pl.BlockSpec(memory_space=pltpu.VMEM),
        scratch_shapes=[
            pltpu.SemaphoreType.DMA((2,)),
            pltpu.SemaphoreType.DMA((N_CHIP + 1,)),
            pltpu.SemaphoreType.DMA,
        ],
        compiler_params=pltpu.CompilerParams(
            collective_id=collective_id, has_side_effects=True, vmem_limit_bytes=32 << 20
        ),
    )(x)


def scatter_sum_kernel(x, out, pair_sum, by_chip, by_sample, send_sem, recv_sem):
    t, s = lax.axis_index("tile"), lax.axis_index("sample")
    m, c = t // 2, lax.rem(t, 2)
    enter(t, s)
    for k in range(1, N_CHIP + 1):
        d = lax.rem(m + k, N_CHIP)
        send(x.at[d, 1 - c], pair_sum.at[d], send_sem.at[0], recv_sem.at[k], m * 2 + 1 - c, s)
    for k in range(1, N_CHIP + 1):
        d = lax.rem(m + k, N_CHIP)
        wait_bytes(pair_sum.at[d], recv_sem.at[k])
        pair_sum[d] = (pair_sum[d].astype(F32) + x[d, c].astype(F32)).astype(x.dtype)
        if k < N_CHIP:
            send(
                pair_sum.at[d],
                by_chip.at[k - 1],
                send_sem.at[1],
                recv_sem.at[N_CHIP + k],
                d * 2 + c,
                s,
            )
    total = pair_sum[m].astype(F32)
    for k in range(1, N_CHIP):
        wait_bytes(by_chip.at[k - 1], recv_sem.at[N_CHIP + k])
        total = total + by_chip[k - 1].astype(F32)
    pair_sum[m] = total.astype(x.dtype)
    for k in range(1, N_SAMPLE):
        d = lax.rem(s + k, N_SAMPLE)
        send(pair_sum.at[m, d], by_sample.at[k - 1], send_sem.at[2], recv_sem.at[0], t, d)
    wait_bytes(by_sample, recv_sem.at[0])
    out[...] = pair_sum[m, s].astype(F32) + jnp.sum(by_sample[...].astype(F32), axis=0)
    wait_bytes(pair_sum, send_sem.at[0])
    wait_bytes(by_chip, send_sem.at[1])
    wait_bytes(by_sample, send_sem.at[2])


def scatter_sum(x, collective_id):
    block = x.shape[3:]
    return pl.pallas_call(
        scatter_sum_kernel,
        out_shape=jax.ShapeDtypeStruct(block, F32),
        in_specs=[pl.BlockSpec(memory_space=pltpu.VMEM)],
        out_specs=pl.BlockSpec(memory_space=pltpu.VMEM),
        scratch_shapes=[
            pltpu.VMEM((N_CHIP, N_SAMPLE) + block, x.dtype),
            pltpu.VMEM((N_CHIP - 1, N_SAMPLE) + block, x.dtype),
            pltpu.VMEM((N_SAMPLE - 1,) + block, x.dtype),
            pltpu.SemaphoreType.DMA((3,)),
            pltpu.SemaphoreType.DMA((2 * N_CHIP,)),
        ],
        compiler_params=pltpu.CompilerParams(
            collective_id=collective_id, has_side_effects=True, vmem_limit_bytes=32 << 20
        ),
    )(x)


def dot(a, b):
    return jnp.dot(a, b, preferred_element_type=F32)


def dot_t(a, b):
    return lax.dot_general(a, b, (((1,), (1,)), ((), ())), preferred_element_type=F32)


def t_dot(a, b):
    return lax.dot_general(a, b, (((0,), (0,)), ((), ())), preferred_element_type=F32)


HEAD = 48
GROUP = 4
LANES = 32


def attention_kernel(q, k, v, gate, up, bias, gated, d_every, d_bias, bias_rows, bias_total):
    tokens = bias_rows.shape[1]
    scale = 1.0 / math.sqrt(HEAD)
    group_of = lax.broadcasted_iota(jnp.int32, (tokens, 128), 1) // LANES

    for half in range(2):
        parts = [
            bias[:, :, half * 4 + i, 0].reshape(tokens, 128).astype(F32) for i in range(4)
        ]
        for h in range(GROUP):
            row = parts[0] if h == 0 else pltpu.roll(parts[0], (-h) % 4 * LANES, 1)
            for i in range(1, 4):
                shift = (i - h) % 4 * LANES
                moved = pltpu.roll(parts[i], shift, 1) if shift else parts[i]
                row = jnp.where(group_of == i, moved, row)
            bias_rows[h, :, pl.ds(half * 128, 128)] = row

    @pl.loop(0, GROUP)
    def _(h):
        rows = pl.ds(pl.multiple_of(h * HEAD, 16), HEAD)
        for sample in range(2):
            columns = pl.ds(sample * tokens, tokens)
            qh, kh, vh = q[rows, columns], k[rows, columns], v[rows, columns]
            scores = t_dot(qh, kh) * scale + bias_rows[h]
            weights = jnp.exp(scores - jnp.max(scores, axis=1, keepdims=True))
            probs = weights * (1.0 / jnp.sum(weights, axis=1, keepdims=True))
            probs_b = probs.astype(BF16)
            attended = dot_t(vh, probs_b)
            gate_h, up_h = gate[rows, columns], up[rows, columns]
            gated[rows, columns] = (gate_h * attended).astype(BF16)
            d_att = (up_h * gate_h).astype(BF16)
            d_every[1, rows, columns] = (up_h * attended * gate_h * (1.0 - gate_h)).astype(BF16)
            d_probs = t_dot(d_att, vh)
            inner = jnp.sum(probs * d_probs, axis=1, keepdims=True)
            d_scores = probs * (d_probs - inner)
            d_scores_b = d_scores.astype(BF16)
            d_every[0, rows, columns] = (dot_t(kh, d_scores_b) * scale).astype(BF16)
            d_every[2, rows, columns] = (dot(qh, d_scores_b) * scale).astype(BF16)
            d_every[3, rows, columns] = dot(d_att, probs_b).astype(BF16)
            if sample == 0:
                bias_total[h] = d_scores
            else:
                bias_total[h] = bias_total[h] + d_scores

    for half in range(2):
        parts = [bias_total[h, :, pl.ds(half * 128, 128)] for h in range(GROUP)]
        for i in range(4):
            row = parts[0] if i == 0 else pltpu.roll(parts[0], (-i) % 4 * LANES, 1)
            for h in range(1, GROUP):
                shift = (h - i) % 4 * LANES
                moved = pltpu.roll(parts[h], shift, 1) if shift else parts[h]
                row = jnp.where(group_of == h, moved, row)
            d_bias[:, :, half * 4 + i, 0] = row.astype(BF16).reshape(N_CHIP, 2, 16, 128)


def attention(q, k, v, gate, up, bias):
    width, columns = q.shape
    tokens = columns // 2
    block = GROUP * HEAD
    feature = pl.BlockSpec((block, columns), lambda i: (i, 0))
    of_bias = pl.BlockSpec((N_CHIP, 2, N_SAMPLE, 1, 16, 128), lambda i: (0, 0, 0, i, 0, 0))
    return pl.pallas_call(
        attention_kernel,
        grid=(width // block,),
        in_specs=[feature] * 5 + [of_bias],
        out_specs=[feature, pl.BlockSpec((4, block, columns), lambda i: (0, i, 0)), of_bias],
        out_shape=[
            jax.ShapeDtypeStruct((width, columns), BF16),
            jax.ShapeDtypeStruct((4, width, columns), BF16),
            jax.ShapeDtypeStruct(bias.shape, BF16),
        ],
        scratch_shapes=[
            pltpu.VMEM((GROUP, tokens, tokens), F32),
            pltpu.VMEM((GROUP, tokens, tokens), F32),
        ],
        compiler_params=pltpu.CompilerParams(vmem_limit_bytes=40 << 20),
    )(q, k, v, gate, up, bias)


QUARTER = 208
PADDED = 256
WIDTH = 640


def reduce_kernel(
    left_in,
    right_in,
    left_out,
    right_out,
    small,
    in_sum,
    out_sum,
    small_sum,
    full,
    other,
    mine,
    theirs,
    from_core,
    part1,
    sum1,
    part2,
    sum2,
    part3,
    sum3,
    send_sem,
    recv_sem,
):
    t, s = lax.axis_index("tile"), lax.axis_index("sample")
    core = lax.rem(t, 2)
    place = [lax.rem(s, 2) * 2 + t // 8, lax.rem(t // 2, 4), s // 2]

    def device(where, c):
        return (lax.rem(where[0], 2) * 8 + where[1] * 2 + c, where[2] * 2 + where[0] // 2)

    def peer(axis, k):
        where = list(place)
        where[axis] = lax.rem(place[axis] + k, 4)
        return where[axis], device(where, core)

    partner = device(place, 1 - core)
    barrier = pltpu.get_barrier_semaphore()
    others = [partner] + [peer(axis, k)[1] for axis in range(3) for k in range(1, 4)]
    for to in others:
        pl.semaphore_signal(barrier, inc=1, device_id=to, device_id_type=MESH)

    def form(g, c, target):
        wide = pl.ds(pl.multiple_of(g * 1024 + c * 512, 512), 512)
        narrow = pl.ds(pl.multiple_of(g * 256 + c * 128, 128), 128)
        chunk = pl.ds(pl.multiple_of(g * WIDTH, 128), WIDTH)

        @pl.loop(0, 4)
        def _(a):
            rows = pl.ds(pl.multiple_of(a * 192, 64), 192)
            target[g, a, pl.ds(0, 192), pl.ds(0, 512)] = dot_t(
                left_in[rows, :], right_in[wide, :]
            ).astype(BF16)
            target[g, a, pl.ds(0, 192), pl.ds(512, 128)] = jnp.dot(
                left_out[rows, :], right_out[:, narrow], preferred_element_type=F32
            ).astype(BF16)
            target[g, a, pl.ds(192, 16), :] = small[
                pl.ds(pl.multiple_of(c * 64 + a * 16, 16), 16), chunk
            ]

    def add(count, store, *terms):
        @pl.loop(0, count)
        def _(r):
            rows = pl.ds(pl.multiple_of(r * 16, 16), 16)
            total = terms[0](rows).astype(F32)
            for term in terms[1:]:
                total = total + term(rows).astype(F32)
            store(rows, total.astype(BF16))

    for g in range(3):
        form(g, 1 - core, theirs)
        if g == 0:
            pl.semaphore_wait(barrier, len(others))
        send(theirs.at[g], from_core.at[g], send_sem.at[0], recv_sem.at[g, 0], *partner)
    for g in range(3):
        form(g, core, mine)
        wait_bytes(from_core.at[g], recv_sem.at[g, 0])
        for a in range(4):

            def put(rows, total, g=g, a=a):
                mine[g, a, rows, :] = total

            add(
                QUARTER // 16,
                put,
                lambda rows, g=g, a=a: mine[g, a, rows, :],
                lambda rows, g=g, a=a: from_core[g, a, rows, :],
            )
        for k in range(1, 4):
            d, to = peer(g, k)
            send(mine.at[g, d], part1.at[g, k - 1], send_sem.at[1], recv_sem.at[g, 1], *to)
    for g in range(3):
        p1 = place[g]
        wait_bytes(part1.at[g], recv_sem.at[g, 1])

        def put(rows, total, g=g):
            sum1[g, rows, :] = total

        add(
            QUARTER // 16,
            put,
            lambda rows, g=g, p1=p1: mine[g, p1, rows, :],
            *[lambda rows, g=g, k=k: part1[g, k, rows, :] for k in range(3)],
        )
        sum1[g, pl.ds(QUARTER, PADDED - QUARTER), :] = jnp.zeros((PADDED - QUARTER, WIDTH), BF16)
        for k in range(1, 4):
            d, to = peer((g + 1) % 3, k)
            rows = pl.ds(pl.multiple_of(d * 64, 64), 64)
            send(sum1.at[g, rows], part2.at[g, k - 1], send_sem.at[2], recv_sem.at[g, 2], *to)
    for g in range(3):
        first = place[(g + 1) % 3] * 64
        wait_bytes(part2.at[g], recv_sem.at[g, 2])
        rows = pl.ds(pl.multiple_of(first, 64), 64)
        total = sum1[g, rows, :].astype(F32)
        for k in range(3):
            total = total + part2[g, k].astype(F32)
        sum2[g] = total.astype(BF16)
        for k in range(1, 4):
            d, to = peer((g + 2) % 3, k)
            rows = pl.ds(pl.multiple_of(d * 16, 16), 16)
            send(sum2.at[g, rows], part3.at[g, k - 1], send_sem.at[3], recv_sem.at[g, 3], *to)
    for g in range(3):
        p1, p2, p3 = place[g], place[(g + 1) % 3], place[(g + 2) % 3]
        wait_bytes(part3.at[g], recv_sem.at[g, 3])
        total = sum2[g, pl.ds(pl.multiple_of(p3 * 16, 16), 16), :].astype(F32)
        for k in range(3):
            total = total + part3[g, k].astype(F32)
        rows = pl.ds(pl.multiple_of(p2 * 64 + p3 * 16, 16), 16)
        full[g, p1, rows, :] = total.astype(BF16)
        block = full.at[g, p1, rows]
        for k in range(1, 4):
            _, to = peer((g + 2) % 3, k)
            send(block, block, send_sem.at[4], recv_sem.at[g, 4], *to)
    for g in range(3):
        p1, p2 = place[g], place[(g + 1) % 3]
        wait_bytes(full.at[g, p1, pl.ds(0, 48)], recv_sem.at[g, 4])
        block = full.at[g, p1, pl.ds(pl.multiple_of(p2 * 64, 64), 64)]
        for k in range(1, 4):
            _, to = peer((g + 1) % 3, k)
            send(block, block, send_sem.at[5], recv_sem.at[g, 5], *to)
    for g in range(3):
        p1 = place[g]
        wait_bytes(full.at[g, p1, pl.ds(0, 192)], recv_sem.at[g, 5])
        block = full.at[g, p1, pl.ds(0, QUARTER)]
        for k in range(1, 4):
            _, to = peer(g, k)
            send(block, block, send_sem.at[6], recv_sem.at[g, 6], *to)
        send(block, other.at[g, p1], send_sem.at[7], recv_sem.at[g, 7], *partner)

    def unpack(source, g, c):
        wide = pl.ds(pl.multiple_of(g * 1024 + c * 512, 512), 512)
        narrow = pl.ds(pl.multiple_of(g * 256 + c * 128, 128), 128)

        @pl.loop(0, 4)
        def _(a):
            @pl.loop(0, 12)
            def _(r):
                rows = pl.ds(pl.multiple_of(r * 16, 16), 16)
                place_rows = pl.ds(pl.multiple_of(a * 192 + r * 16, 16), 16)
                in_sum[place_rows, wide] = source[g, a, rows, pl.ds(0, 512)]
                out_sum[place_rows, narrow] = source[g, a, rows, pl.ds(512, 128)]

            small_sum[pl.ds(pl.multiple_of(c * 64 + a * 16, 16), 16), pl.ds(g * WIDTH, WIDTH)] = source[
                g, a, pl.ds(192, 16), :
            ]

    for g in range(3):
        wait_bytes(full.at[g, pl.ds(0, 3), pl.ds(0, QUARTER)], recv_sem.at[g, 6])
        for k in range(1, 4):
            p1 = lax.rem(place[g] + k, 4)
            block = full.at[g, p1, pl.ds(0, QUARTER)]
            send(block, other.at[g, p1], send_sem.at[7], recv_sem.at[g, 7], *partner)
        unpack(full, g, core)
    for g in range(3):
        wait_bytes(other.at[g], recv_sem.at[g, 7])
        unpack(other, g, 1 - core)
    wait_bytes(theirs, send_sem.at[0])
    wait_bytes(part1, send_sem.at[1])
    wait_bytes(part2, send_sem.at[2])
    wait_bytes(part3, send_sem.at[3])
    wait_bytes(part3, send_sem.at[4])
    wait_bytes(part2, send_sem.at[5])
    wait_bytes(part1, send_sem.at[6])
    wait_bytes(theirs, send_sem.at[7])


def reduce_all(left_in, right_in, left_out, right_out, small, collective_id):
    chunk = (3, 4, QUARTER, WIDTH)
    return pl.pallas_call(
        reduce_kernel,
        out_shape=(
            jax.ShapeDtypeStruct((768, 3072), BF16),
            jax.ShapeDtypeStruct((768, 768), BF16),
            jax.ShapeDtypeStruct((128, 3 * WIDTH), BF16),
        ),
        in_specs=[pl.BlockSpec(memory_space=pltpu.VMEM)] * 5,
        out_specs=[pl.BlockSpec(memory_space=pltpu.VMEM)] * 3,
        scratch_shapes=[
            pltpu.VMEM((3, 4, PADDED, WIDTH), BF16),
            pltpu.VMEM(chunk, BF16),
            pltpu.VMEM(chunk, BF16),
            pltpu.VMEM(chunk, BF16),
            pltpu.VMEM(chunk, BF16),
            pltpu.VMEM((3, 3, QUARTER, WIDTH), BF16),
            pltpu.VMEM((3, PADDED, WIDTH), BF16),
            pltpu.VMEM((3, 3, 64, WIDTH), BF16),
            pltpu.VMEM((3, 64, WIDTH), BF16),
            pltpu.VMEM((3, 3, 16, WIDTH), BF16),
            pltpu.VMEM((3, 16, WIDTH), BF16),
            pltpu.SemaphoreType.DMA((8,)),
            pltpu.SemaphoreType.DMA((3, 8)),
        ],
        compiler_params=pltpu.CompilerParams(
            collective_id=collective_id, has_side_effects=True, vmem_limit_bytes=48 << 20
        ),
    )(left_in, right_in, left_out, right_out, small)


def norm_parts(values, axis):
    centered = values - jnp.mean(values, axis=axis, keepdims=True)
    inverse = lax.rsqrt(jnp.mean(centered * centered, axis=axis, keepdims=True) + EPSILON)
    return (centered * inverse, inverse)


def norm_back(normed, inverse, incoming_gradient, axis):
    first_mean = jnp.mean(incoming_gradient, axis=axis, keepdims=True)
    second_mean = jnp.mean(incoming_gradient * normed, axis=axis, keepdims=True)
    return (incoming_gradient - first_mean - normed * second_mean) * inverse


def silu_slope(values):
    sigmoid_part = jax.nn.sigmoid(values)
    return sigmoid_part * (1.0 + values * (1.0 - sigmoid_part))


def shards(
    pair,
    pair_mask,
    tri_in_w,
    tri_gate_w,
    tri_out_w,
    bias_w,
    atom_feats,
    atom_to_token,
    atom_w,
    tokens,
    attention_input_weight,
    attention_output_weight,
    cot_pair,
    token_output_cotangent,
):
    hidden = tri_in_w.shape[1] // 4
    token_width = attention_input_weight.shape[0]
    head_count = bias_w.shape[1]
    total_tokens = tokens.shape[1]
    pair_f = pair.astype(jnp.float32)
    normed_z, inverse_z = norm_parts(pair_f, 2)
    normed_zb = normed_z.astype(jnp.bfloat16)
    projected = jnp.einsum("ijz,zc->cij", normed_zb, tri_in_w, preferred_element_type=jnp.float32)
    mask_rows = pair_mask.astype(jnp.float32)[None]
    gate_left = jax.nn.sigmoid(projected[0:hidden])
    gate_right = jax.nn.sigmoid(projected[2 * hidden : 3 * hidden])
    rows, columns = pair_mask.shape
    blocks = (N_TILE, N_SAMPLE)
    left_local = (gate_left * projected[hidden : 2 * hidden] * mask_rows).astype(BF16)
    right_local = (gate_right * projected[3 * hidden :] * mask_rows).astype(BF16)
    halves = jnp.stack([left_local, right_local], axis=1).astype(F32)
    halves, every_feat, every_atom = exchange_and_gather(
        halves.reshape(blocks + (8, 128)), atom_feats, atom_to_token[None], 0
    )
    every_feat = every_feat.reshape(-1, atom_feats.shape[1])
    every_atom = every_atom.reshape(-1)
    panels = (
        halves.reshape(blocks + (2, rows, columns))
        .astype(BF16)
        .transpose(2, 0, 3, 1, 4)
        .reshape(2, N_TILE * rows, N_SAMPLE * columns)
    )
    left_panel, right_panel = panels[0], panels[1]
    product_panel = jnp.dot(left_panel, right_panel.T, preferred_element_type=F32).astype(BF16)
    product_blocks = (
        product_panel.reshape(N_TILE, rows, N_SAMPLE, columns)
        .transpose(0, 2, 1, 3)
        .reshape(blocks + (4, 128))
    )
    product = exchange(product_blocks.astype(F32), 1).reshape(hidden, rows, columns)
    normed_p, inverse_p = norm_parts(product, 0)
    normed_pb = normed_p.astype(jnp.bfloat16)
    linear = jnp.einsum("cij,cz->ijz", normed_pb, tri_out_w, preferred_element_type=jnp.float32)
    tri_gate = jax.nn.sigmoid(
        jnp.einsum("ijz,zy->ijy", normed_zb, tri_gate_w, preferred_element_type=jnp.float32)
    )
    pair_next = pair_f + tri_gate * linear
    normed_n, inverse_n = norm_parts(pair_next, 2)
    normed_nb = normed_n.astype(jnp.bfloat16)
    bias_local = jnp.einsum(
        "ijz,zh->hij", normed_nb, bias_w, preferred_element_type=jnp.float32
    ).astype(jnp.bfloat16)
    bias_all = gather(
        bias_local.reshape(head_count // GROUP, GROUP, rows, columns)
        .transpose(0, 2, 1, 3)
        .reshape(head_count // GROUP, rows, GROUP * columns),
        2,
    )
    atom_pre = jnp.dot(every_feat, atom_w, preferred_element_type=jnp.float32)
    atom_act = jax.nn.silu(atom_pre).astype(BF16)
    token_ids = jnp.arange(total_tokens, dtype=jnp.int32)
    one_hot = (token_ids[:, None] == every_atom[None, :]).astype(BF16)
    token_sums = jnp.dot(one_hot, atom_act, preferred_element_type=F32)
    token_counts = jnp.sum(one_hot.astype(F32), axis=1)
    token_cond = token_sums / token_counts[:, None]
    token_state_rows = tokens.astype(jnp.float32) + token_cond[None]
    normed_h, inverse_h = norm_parts(token_state_rows, 2)
    normalized_hidden_bfloat = normed_h.astype(jnp.bfloat16)
    hidden_t = normalized_hidden_bfloat.reshape(-1, token_width).T
    cot_rows = token_output_cotangent.reshape(-1, token_width)

    def project(block):
        weight = attention_input_weight[:, block * token_width : (block + 1) * token_width]
        return t_dot(weight, hidden_t)

    gated_t, d_every_t, bias_blocks = attention(
        project(0).astype(BF16),
        project(2).astype(BF16),
        project(3).astype(BF16),
        jax.nn.sigmoid(project(1)),
        dot_t(attention_output_weight, cot_rows),
        bias_all,
    )
    d_every_t = d_every_t.reshape(4 * token_width, -1)
    token_output_rows = token_state_rows + t_dot(gated_t, attention_output_weight).reshape(
        token_state_rows.shape
    )
    bias_grad = (
        scatter_sum(bias_blocks, 3)
        .reshape(head_count // GROUP, rows, GROUP, columns)
        .transpose(0, 2, 1, 3)
        .reshape(head_count, rows, columns)
    )
    normalized_hidden_gradient = lax.dot_general(
        d_every_t, attention_input_weight, (((0,), (1,)), ((), ())), preferred_element_type=F32
    ).reshape(token_state_rows.shape)
    grad_tokens = token_output_cotangent.astype(jnp.float32) + norm_back(
        normed_h, inverse_h, normalized_hidden_gradient, 2
    )
    cond_grad = (jnp.sum(grad_tokens, axis=0) / token_counts[:, None]).astype(BF16)
    d_act = lax.dot_general(
        one_hot, cond_grad, (((0,), (0,)), ((), ())), preferred_element_type=F32
    ) * silu_slope(atom_pre)
    grad_atom_w = lax.dot_general(
        every_feat, d_act.astype(BF16), (((0,), (0,)), ((), ())), preferred_element_type=F32
    )
    d_normed_n = jnp.einsum("hij,zh->ijz", bias_grad, bias_w.astype(jnp.float32), precision=HIGHEST)
    grad_bias_w = jnp.einsum(
        "ijz,hij->zh", normed_nb.astype(jnp.float32), bias_grad, precision=HIGHEST
    )
    d_next = cot_pair.astype(jnp.float32) + norm_back(normed_n, inverse_n, d_normed_n, 2)
    d_linear = (d_next * tri_gate).astype(jnp.bfloat16)
    d_gate_pre = (d_next * linear * tri_gate * (1.0 - tri_gate)).astype(jnp.bfloat16)
    grad_tri_out_w = jnp.einsum(
        "cij,ijz->cz", normed_pb, d_linear, preferred_element_type=jnp.float32
    )
    d_normed_p = jnp.einsum("ijz,cz->cij", d_linear, tri_out_w, preferred_element_type=jnp.float32)
    d_product = norm_back(normed_p, inverse_p, d_normed_p, 0).astype(jnp.bfloat16)
    d_product_panel = (
        exchange(d_product.astype(F32).reshape(blocks + (4, 128)), 4)
        .reshape(blocks + (rows, columns))
        .astype(BF16)
        .transpose(0, 2, 1, 3)
        .reshape(N_TILE * rows, N_SAMPLE * columns)
    )
    d_left_panel = jnp.dot(d_product_panel, right_panel, preferred_element_type=F32)
    d_right_panel = jnp.dot(d_product_panel.T, left_panel, preferred_element_type=F32)
    d_halves = (
        jnp.stack([d_left_panel, d_right_panel])
        .reshape(2, N_TILE, rows, N_SAMPLE, columns)
        .transpose(1, 3, 0, 2, 4)
        .reshape(blocks + (8, 128))
    )
    d_halves = exchange(d_halves, 5).reshape(hidden, 2, rows, columns)
    d_left, d_right = d_halves[:, 0], d_halves[:, 1]
    d_proj = jnp.concatenate(
        [
            d_left * projected[hidden : 2 * hidden] * mask_rows * gate_left * (1.0 - gate_left),
            d_left * gate_left * mask_rows,
            d_right * projected[3 * hidden :] * mask_rows * gate_right * (1.0 - gate_right),
            d_right * gate_right * mask_rows,
        ],
        axis=0,
    ).astype(jnp.bfloat16)
    grad_tri_in_w = jnp.einsum("ijz,cij->zc", normed_zb, d_proj, preferred_element_type=jnp.float32)
    grad_tri_gate_w = jnp.einsum(
        "ijz,ijy->zy", normed_zb, d_gate_pre, preferred_element_type=jnp.float32
    )
    d_normed_z = jnp.einsum(
        "cij,zc->ijz", d_proj, tri_in_w, preferred_element_type=jnp.float32
    ) + jnp.einsum("ijy,zy->ijz", d_gate_pre, tri_gate_w, preferred_element_type=jnp.float32)
    grad_pair = d_next + norm_back(normed_z, inverse_z, d_normed_z, 2)
    small = jnp.concatenate(
        [
            grad_tri_in_w,
            grad_tri_gate_w,
            grad_tri_out_w,
            grad_bias_w,
            jnp.zeros((hidden, 128 - head_count), F32),
            grad_atom_w,
            jnp.zeros((hidden, 3 * WIDTH - 4 * hidden - 3 * 128 - token_width), F32),
        ],
        axis=1,
    ).astype(BF16)
    in_sum, out_sum, small_sum = reduce_all(hidden_t, d_every_t, gated_t, cot_rows, small, 6)
    small_sum = small_sum.astype(F32)
    at = 4 * hidden
    summed = (
        small_sum[:, :at],
        small_sum[:, at : at + 128],
        small_sum[:, at + 128 : at + 256],
        small_sum[:, at + 256 : at + 256 + head_count],
        small_sum[:, at + 384 : at + 384 + token_width],
        in_sum.astype(F32),
        out_sum.astype(F32),
    )
    return (pair_next, token_output_rows, grad_pair, grad_tokens) + summed


def solution(mesh):
    in_specs = (
        P("tile", "sample", None),
        P("tile", "sample"),
        P(),
        P(),
        P(),
        P(),
        P("tile", None),
        P("tile"),
        P(),
        P(("tile", "sample"), None, None),
        P(),
        P(),
        P("tile", "sample", None),
        P(("tile", "sample"), None, None),
    )
    out_specs = (
        P("tile", "sample", None),
        P(("tile", "sample"), None, None),
        P("tile", "sample", None),
        P(("tile", "sample"), None, None),
        P(),
        P(),
        P(),
        P(),
        P(),
        P(),
        P(),
    )
    return jax.shard_map(shards, mesh=mesh, in_specs=in_specs, out_specs=out_specs, check_vma=False)
```

```python
import functools
import math

import jax
import jax.numpy as jnp
from jax import lax
from jax.experimental import pallas as pl
from jax.experimental.pallas import tpu as pltpu
from jax.sharding import PartitionSpec as P

EPSILON = 1e-05
N_TILE = 16
N_SAMPLE = 8
N_CHIP = 8
MESH = pl.DeviceIdType.MESH
BF16 = jnp.bfloat16
F32 = jnp.float32
HIGHEST = lax.Precision.HIGHEST


def enter(t, s):
    barrier = pltpu.get_barrier_semaphore()
    for k in range(1, N_SAMPLE):
        pl.semaphore_signal(
            barrier, inc=1, device_id=(t, lax.rem(s + k, N_SAMPLE)), device_id_type=MESH
        )
    for k in range(1, N_TILE):
        pl.semaphore_signal(
            barrier, inc=1, device_id=(lax.rem(t + k, N_TILE), s), device_id_type=MESH
        )
    pl.semaphore_wait(barrier, N_SAMPLE + N_TILE - 2)


def wait_bytes(ref, sem):
    pltpu.make_async_copy(ref, ref, sem).wait()


def send(src, dst, send_sem, recv_sem, t, s):
    pltpu.make_async_remote_copy(
        src, dst, send_sem, recv_sem, device_id=(t, s), device_id_type=MESH
    ).start()


def exchange_kernel(x, out, mid, send_sem, recv_sem, local_sem):
    t, s = lax.axis_index("tile"), lax.axis_index("sample")
    enter(t, s)
    for k in range(1, N_SAMPLE):
        d = lax.rem(s + k, N_SAMPLE)
        send(x.at[:, d], mid.at[:, s], send_sem.at[0], recv_sem.at[0], t, d)
    own = pltpu.make_async_copy(x.at[:, s], mid.at[:, s], local_sem)
    own.start()
    own.wait()
    wait_bytes(mid.at[:, pl.ds(0, N_SAMPLE - 1)], recv_sem.at[0])
    for k in range(1, N_TILE):
        d = lax.rem(t + k, N_TILE)
        send(mid.at[d], out.at[t], send_sem.at[1], recv_sem.at[1], d, s)
    own = pltpu.make_async_copy(mid.at[t], out.at[t], local_sem)
    own.start()
    own.wait()
    wait_bytes(out.at[pl.ds(0, N_TILE - 1)], recv_sem.at[1])
    wait_bytes(mid.at[:, pl.ds(0, N_SAMPLE - 1)], send_sem.at[0])
    wait_bytes(out.at[pl.ds(0, N_TILE - 1)], send_sem.at[1])


def exchange(x, collective_id):
    return pl.pallas_call(
        exchange_kernel,
        out_shape=jax.ShapeDtypeStruct(x.shape, x.dtype),
        in_specs=[pl.BlockSpec(memory_space=pltpu.VMEM)],
        out_specs=pl.BlockSpec(memory_space=pltpu.VMEM),
        scratch_shapes=[
            pltpu.VMEM(x.shape, x.dtype),
            pltpu.SemaphoreType.DMA((2,)),
            pltpu.SemaphoreType.DMA((2,)),
            pltpu.SemaphoreType.DMA,
        ],
        compiler_params=pltpu.CompilerParams(
            collective_id=collective_id, has_side_effects=True, vmem_limit_bytes=32 << 20
        ),
    )(x)


def dot(a, b):
    return jnp.dot(a, b, preferred_element_type=F32)


def dot_t(a, b):
    return lax.dot_general(a, b, (((1,), (1,)), ((), ())), preferred_element_type=F32)


def t_dot(a, b):
    return lax.dot_general(a, b, (((0,), (0,)), ((), ())), preferred_element_type=F32)


HEAD = 48
GROUP = 4
LANES = 32


def place_lanes(parts, first):
    group_of = lax.broadcasted_iota(jnp.int32, parts[0].shape, 1) // LANES
    result = None
    for i in range(4):
        shift = (i - first) % 4 * LANES
        moved = pltpu.roll(parts[i], shift, 1) if shift else parts[i]
        result = moved if result is None else jnp.where(group_of == i, moved, result)
    return result


def panel_of(arrived, first, step, panel):
    for part in range(4):
        rows = [
            arrived[part, pl.ds(first + s * (step // 8), 16, stride=step), :] for s in range(8)
        ]
        for i in range(4):
            for half in range(2):
                panel[half, pl.ds(part * 4 + i, 16, stride=16), :] = place_lanes(
                    rows[half * 4 : half * 4 + 4], i
                )


def blocks_of(panel, store):
    for half in range(2):
        for part in range(4):
            rows = [panel[half, pl.ds(part * 4 + i, 16, stride=16), :] for i in range(4)]
            for q in range(4):
                store(half * 4 + q, pl.ds(part * 128, 128), place_lanes(rows, q))


def split_lanes(values, ref):
    for part in range(ref.shape[0]):
        ref[part] = values[:, part * 128 : part * 128 + 128]


def joined(ref):
    return jnp.concatenate([ref[0], ref[1]], axis=1)


def norm_rows(values, axis):
    centered = values - jnp.mean(values, axis=axis, keepdims=True)
    inverse = lax.rsqrt(jnp.mean(centered * centered, axis=axis, keepdims=True) + EPSILON)
    return centered * inverse, inverse


def sigmoid(values):
    return 1.0 / (1.0 + jnp.exp(-values))


def pair_forward_kernel(
    pair,
    mask,
    in_w_t,
    gate_w,
    out_w,
    bias_w_t,
    feats,
    atoms,
    pair_next,
    bias,
    left,
    right,
    product,
    every_feat,
    every_atom,
    x1,
    mid,
    mid_rows,
    x2,
    arrived,
    arrived_rows,
    panel,
    x3,
    back,
    back_rows,
    x4,
    packed,
    mine,
    send_sem,
    recv_sem,
):
    t, s = lax.axis_index("tile"), lax.axis_index("sample")
    m, c = t // 2, lax.rem(t, 2)
    barrier = pltpu.get_barrier_semaphore()
    tile_peers = [lax.rem(t + k, N_TILE) for k in range(1, N_TILE)]
    sample_peers = [lax.rem(s + k, N_SAMPLE) for k in range(1, N_SAMPLE)]
    for d in sample_peers:
        pl.semaphore_signal(barrier, inc=1, device_id=(t, d), device_id_type=MESH)
    for d in tile_peers:
        pl.semaphore_signal(barrier, inc=1, device_id=(d, s), device_id_type=MESH)

    normed_z = norm_rows(pair[...].astype(F32), 1)[0].astype(BF16)

    def project(block):
        return dot_t(in_w_t[pl.ds(block * 128, 128), :], normed_z)

    for side in range(2):
        value = (sigmoid(project(2 * side)) * project(2 * side + 1) * mask[...]).astype(BF16)
        for d in range(N_SAMPLE):
            x1[d, side] = value[d * 16 : d * 16 + 16]
    pl.semaphore_wait(barrier, N_SAMPLE + N_TILE - 2)
    for d in sample_peers:
        send(x1.at[d], mid.at[s], send_sem.at[0], recv_sem.at[0], t, d)
    for d in tile_peers:
        send(feats, every_feat.at[t], send_sem.at[1], recv_sem.at[1], d, s)
        send(atoms, every_atom.at[t], send_sem.at[2], recv_sem.at[2], d, s)
    every_feat[t] = feats[...]
    every_atom[t] = atoms[...]
    mid[s] = x1[s]
    tri_gate = sigmoid(dot(normed_z, gate_w[...]))
    wait_bytes(mid.at[pl.ds(0, N_SAMPLE - 1)], recv_sem.at[0])
    split_lanes(mid[...].reshape(256, 512).astype(F32), mid_rows)
    for d in range(N_TILE):
        for part in range(4):
            x2[d, :, pl.ds(part * 128, 128)] = mid_rows[part, pl.ds(d, 16, stride=16), :].astype(
                BF16
            )
    for d in tile_peers:
        send(x2.at[d], arrived.at[t], send_sem.at[3], recv_sem.at[3], d, s)
    arrived[t] = x2[t]
    wait_bytes(arrived.at[pl.ds(0, N_TILE - 1)], recv_sem.at[3])
    split_lanes(arrived[...].reshape(256, 512).astype(F32), arrived_rows)
    panel_of(arrived_rows, 0, 16, panel)
    left[...] = joined(panel).astype(BF16)
    panel_of(arrived_rows, 1, 16, panel)
    right[...] = joined(panel).astype(BF16)
    x3[...] = dot_t(left[...], right[...]).astype(BF16).reshape(N_TILE, 16, 256)
    for d in tile_peers:
        send(x3.at[d], back.at[t], send_sem.at[4], recv_sem.at[4], d, s)
    back[t] = x3[t]
    wait_bytes(back.at[pl.ds(0, N_TILE - 1)], recv_sem.at[4])
    split_lanes(back[...].reshape(256, 256).astype(F32), back_rows)

    def store(d, lanes, rows):
        x4[d, :, lanes] = rows.astype(BF16)

    blocks_of(back_rows, store)
    for d in sample_peers:
        send(x4.at[d], product.at[s], send_sem.at[5], recv_sem.at[5], t, d)
    product[s] = x4[s]
    wait_bytes(product.at[pl.ds(0, N_SAMPLE - 1)], recv_sem.at[5])
    normed_p = norm_rows(product[...].reshape(128, 512).astype(F32), 0)[0].astype(BF16)
    linear = t_dot(normed_p, out_w[...])
    following = pair[...].astype(F32) + tri_gate * linear
    pair_next[...] = following
    normed_n = norm_rows(following, 1)[0].astype(BF16)
    head_rows = dot_t(bias_w_t[...], normed_n)
    split_lanes(head_rows, packed)
    for part in range(4):
        rows = [packed[part, pl.ds(h, 4, stride=4), :] for h in range(4)]
        for i in range(4):
            mine[:, part * 4 + i] = place_lanes(rows, i)
    bias[m, c, s] = mine[...].astype(BF16)

    own = bias.at[m, c, s]
    for d in sample_peers:
        send(own, own, send_sem.at[6], recv_sem.at[6], t, d)
    wait_bytes(bias.at[m, c, pl.ds(0, N_SAMPLE - 1)], recv_sem.at[6])
    block = bias.at[m, c]
    other = m * 2 + 1 - c
    for k in range(1, N_CHIP):
        send(block, block, send_sem.at[7], recv_sem.at[7 + k], lax.rem(m + k, N_CHIP) * 2 + c, s)
    send(block, block, send_sem.at[8], recv_sem.at[7], other, s)
    for k in range(1, N_CHIP):
        came = bias.at[lax.rem(m + N_CHIP - k, N_CHIP), c]
        wait_bytes(came, recv_sem.at[7 + k])
        send(came, came, send_sem.at[8], recv_sem.at[7], other, s)
    wait_bytes(bias.at[:, 0], recv_sem.at[7])
    wait_bytes(every_feat.at[pl.ds(0, N_TILE - 1)], recv_sem.at[1])
    wait_bytes(every_atom.at[pl.ds(0, N_TILE - 1)], recv_sem.at[2])
    wait_bytes(mid.at[pl.ds(0, N_SAMPLE - 1)], send_sem.at[0])
    wait_bytes(every_feat.at[pl.ds(0, N_TILE - 1)], send_sem.at[1])
    wait_bytes(every_atom.at[pl.ds(0, N_TILE - 1)], send_sem.at[2])
    wait_bytes(arrived.at[pl.ds(0, N_TILE - 1)], send_sem.at[3])
    wait_bytes(back.at[pl.ds(0, N_TILE - 1)], send_sem.at[4])
    wait_bytes(product.at[pl.ds(0, N_SAMPLE - 1)], send_sem.at[5])
    wait_bytes(bias.at[m, c, pl.ds(0, N_SAMPLE - 1)], send_sem.at[6])
    wait_bytes(bias.at[pl.ds(0, N_CHIP - 1), 0], send_sem.at[7])
    wait_bytes(bias.at[:, 0], send_sem.at[8])


def pair_forward(pair, mask, in_w_t, gate_w, out_w, bias_w_t, feats, atoms, collective_id):
    vmem = pl.BlockSpec(memory_space=pltpu.VMEM)
    return pl.pallas_call(
        pair_forward_kernel,
        out_shape=[
            jax.ShapeDtypeStruct(pair.shape, F32),
            jax.ShapeDtypeStruct((N_CHIP, 2, N_SAMPLE, 4, 16, 128), BF16),
            jax.ShapeDtypeStruct((256, 256), BF16),
            jax.ShapeDtypeStruct((256, 256), BF16),
            jax.ShapeDtypeStruct((N_SAMPLE, 16, 512), BF16),
            jax.ShapeDtypeStruct((N_TILE,) + feats.shape, feats.dtype),
            jax.ShapeDtypeStruct((N_TILE,) + atoms.shape, atoms.dtype),
        ],
        in_specs=[vmem] * 8,
        out_specs=[vmem] * 7,
        scratch_shapes=[
            pltpu.VMEM((N_SAMPLE, 2, 16, 512), BF16),
            pltpu.VMEM((N_SAMPLE, 2, 16, 512), BF16),
            pltpu.VMEM((4, 256, 128), F32),
            pltpu.VMEM((N_TILE, 16, 512), BF16),
            pltpu.VMEM((N_TILE, 16, 512), BF16),
            pltpu.VMEM((4, 256, 128), F32),
            pltpu.VMEM((2, 256, 128), F32),
            pltpu.VMEM((N_TILE, 16, 256), BF16),
            pltpu.VMEM((N_TILE, 16, 256), BF16),
            pltpu.VMEM((2, 256, 128), F32),
            pltpu.VMEM((N_SAMPLE, 16, 512), BF16),
            pltpu.VMEM((4, 16, 128), F32),
            pltpu.VMEM((4, 16, 128), F32),
            pltpu.SemaphoreType.DMA((9,)),
            pltpu.SemaphoreType.DMA((15,)),
        ],
        compiler_params=pltpu.CompilerParams(
            collective_id=collective_id, has_side_effects=True, vmem_limit_bytes=40 << 20
        ),
    )(pair, mask, in_w_t, gate_w, out_w, bias_w_t, feats, atoms)


def scatter_sum_kernel(x, out, pair_sum, by_chip, by_sample, send_sem, recv_sem):
    t, s = lax.axis_index("tile"), lax.axis_index("sample")
    m, c = t // 2, lax.rem(t, 2)
    enter(t, s)
    for k in range(1, N_CHIP + 1):
        d = lax.rem(m + k, N_CHIP)
        send(x.at[d, 1 - c], pair_sum.at[d], send_sem.at[0], recv_sem.at[k], m * 2 + 1 - c, s)
    for k in range(1, N_CHIP + 1):
        d = lax.rem(m + k, N_CHIP)
        wait_bytes(pair_sum.at[d], recv_sem.at[k])
        pair_sum[d] = (pair_sum[d].astype(F32) + x[d, c].astype(F32)).astype(x.dtype)
        if k < N_CHIP:
            send(
                pair_sum.at[d],
                by_chip.at[k - 1],
                send_sem.at[1],
                recv_sem.at[N_CHIP + k],
                d * 2 + c,
                s,
            )
    total = pair_sum[m].astype(F32)
    for k in range(1, N_CHIP):
        wait_bytes(by_chip.at[k - 1], recv_sem.at[N_CHIP + k])
        total = total + by_chip[k - 1].astype(F32)
    pair_sum[m] = total.astype(x.dtype)
    for k in range(1, N_SAMPLE):
        d = lax.rem(s + k, N_SAMPLE)
        send(pair_sum.at[m, d], by_sample.at[k - 1], send_sem.at[2], recv_sem.at[0], t, d)
    wait_bytes(by_sample, recv_sem.at[0])
    out[...] = pair_sum[m, s].astype(F32) + jnp.sum(by_sample[...].astype(F32), axis=0)
    wait_bytes(pair_sum, send_sem.at[0])
    wait_bytes(by_chip, send_sem.at[1])
    wait_bytes(by_sample, send_sem.at[2])


def scatter_sum(x, collective_id):
    block = x.shape[3:]
    return pl.pallas_call(
        scatter_sum_kernel,
        out_shape=jax.ShapeDtypeStruct(block, F32),
        in_specs=[pl.BlockSpec(memory_space=pltpu.VMEM)],
        out_specs=pl.BlockSpec(memory_space=pltpu.VMEM),
        scratch_shapes=[
            pltpu.VMEM((N_CHIP, N_SAMPLE) + block, x.dtype),
            pltpu.VMEM((N_CHIP - 1, N_SAMPLE) + block, x.dtype),
            pltpu.VMEM((N_SAMPLE - 1,) + block, x.dtype),
            pltpu.SemaphoreType.DMA((3,)),
            pltpu.SemaphoreType.DMA((2 * N_CHIP,)),
        ],
        compiler_params=pltpu.CompilerParams(
            collective_id=collective_id, has_side_effects=True, vmem_limit_bytes=32 << 20
        ),
    )(x)


def attention_kernel(q, k, v, gate, up, bias, gated, d_every, d_bias, bias_rows, bias_total):
    tokens = bias_rows.shape[1]
    scale = 1.0 / math.sqrt(HEAD)
    group_of = lax.broadcasted_iota(jnp.int32, (tokens, 128), 1) // LANES

    for half in range(2):
        parts = [
            bias[:, :, half * 4 + i, 0].reshape(tokens, 128).astype(F32) for i in range(4)
        ]
        for h in range(GROUP):
            row = parts[0] if h == 0 else pltpu.roll(parts[0], (-h) % 4 * LANES, 1)
            for i in range(1, 4):
                shift = (i - h) % 4 * LANES
                moved = pltpu.roll(parts[i], shift, 1) if shift else parts[i]
                row = jnp.where(group_of == i, moved, row)
            bias_rows[h, :, pl.ds(half * 128, 128)] = row

    @pl.loop(0, GROUP)
    def _(h):
        rows = pl.ds(pl.multiple_of(h * HEAD, 16), HEAD)
        for sample in range(2):
            columns = pl.ds(sample * tokens, tokens)
            qh, kh, vh = q[rows, columns], k[rows, columns], v[rows, columns]
            scores = t_dot(qh, kh) * scale + bias_rows[h]
            weights = jnp.exp(scores - jnp.max(scores, axis=1, keepdims=True))
            probs = weights * (1.0 / jnp.sum(weights, axis=1, keepdims=True))
            probs_b = probs.astype(BF16)
            attended = dot_t(vh, probs_b)
            gate_h, up_h = gate[rows, columns], up[rows, columns]
            gated[rows, columns] = (gate_h * attended).astype(BF16)
            d_att = (up_h * gate_h).astype(BF16)
            d_every[1, rows, columns] = (up_h * attended * gate_h * (1.0 - gate_h)).astype(BF16)
            d_probs = t_dot(d_att, vh)
            inner = jnp.sum(probs * d_probs, axis=1, keepdims=True)
            d_scores = probs * (d_probs - inner)
            d_scores_b = d_scores.astype(BF16)
            d_every[0, rows, columns] = (dot_t(kh, d_scores_b) * scale).astype(BF16)
            d_every[2, rows, columns] = (dot(qh, d_scores_b) * scale).astype(BF16)
            d_every[3, rows, columns] = dot(d_att, probs_b).astype(BF16)
            if sample == 0:
                bias_total[h] = d_scores
            else:
                bias_total[h] = bias_total[h] + d_scores

    for half in range(2):
        parts = [bias_total[h, :, pl.ds(half * 128, 128)] for h in range(GROUP)]
        for i in range(4):
            row = parts[0] if i == 0 else pltpu.roll(parts[0], (-i) % 4 * LANES, 1)
            for h in range(1, GROUP):
                shift = (h - i) % 4 * LANES
                moved = pltpu.roll(parts[h], shift, 1) if shift else parts[h]
                row = jnp.where(group_of == h, moved, row)
            d_bias[:, :, half * 4 + i, 0] = row.astype(BF16).reshape(N_CHIP, 2, 16, 128)


def attention(q, k, v, gate, up, bias):
    width, columns = q.shape
    tokens = columns // 2
    block = GROUP * HEAD
    feature = pl.BlockSpec((block, columns), lambda i: (i, 0))
    of_bias = pl.BlockSpec((N_CHIP, 2, N_SAMPLE, 1, 16, 128), lambda i: (0, 0, 0, i, 0, 0))
    return pl.pallas_call(
        attention_kernel,
        grid=(width // block,),
        in_specs=[feature] * 5 + [of_bias],
        out_specs=[feature, pl.BlockSpec((4, block, columns), lambda i: (0, i, 0)), of_bias],
        out_shape=[
            jax.ShapeDtypeStruct((width, columns), BF16),
            jax.ShapeDtypeStruct((4, width, columns), BF16),
            jax.ShapeDtypeStruct(bias.shape, BF16),
        ],
        scratch_shapes=[
            pltpu.VMEM((GROUP, tokens, tokens), F32),
            pltpu.VMEM((GROUP, tokens, tokens), F32),
        ],
        compiler_params=pltpu.CompilerParams(vmem_limit_bytes=40 << 20),
    )(q, k, v, gate, up, bias)


QUARTER = 208
PADDED = 256
WIDTH = 640


def reduce_kernel(
    left_in,
    right_in,
    left_out,
    right_out,
    small,
    in_sum,
    out_sum,
    small_sum,
    full,
    other,
    mine,
    theirs,
    from_core,
    part1,
    sum1,
    part2,
    sum2,
    part3,
    sum3,
    send_sem,
    recv_sem,
):
    t, s = lax.axis_index("tile"), lax.axis_index("sample")
    core = lax.rem(t, 2)
    place = [lax.rem(s, 2) * 2 + t // 8, lax.rem(t // 2, 4), s // 2]

    def device(where, c):
        return (lax.rem(where[0], 2) * 8 + where[1] * 2 + c, where[2] * 2 + where[0] // 2)

    def peer(axis, k):
        where = list(place)
        where[axis] = lax.rem(place[axis] + k, 4)
        return where[axis], device(where, core)

    partner = device(place, 1 - core)
    barrier = pltpu.get_barrier_semaphore()
    others = [partner] + [peer(axis, k)[1] for axis in range(3) for k in range(1, 4)]
    for to in others:
        pl.semaphore_signal(barrier, inc=1, device_id=to, device_id_type=MESH)

    def form(g, c, target):
        wide = pl.ds(pl.multiple_of(g * 1024 + c * 512, 512), 512)
        narrow = pl.ds(pl.multiple_of(g * 256 + c * 128, 128), 128)
        chunk = pl.ds(pl.multiple_of(g * WIDTH, 128), WIDTH)

        @pl.loop(0, 4)
        def _(a):
            rows = pl.ds(pl.multiple_of(a * 192, 64), 192)
            target[g, a, pl.ds(0, 192), pl.ds(0, 512)] = dot_t(
                left_in[rows, :], right_in[wide, :]
            ).astype(BF16)
            target[g, a, pl.ds(0, 192), pl.ds(512, 128)] = jnp.dot(
                left_out[rows, :], right_out[:, narrow], preferred_element_type=F32
            ).astype(BF16)
            target[g, a, pl.ds(192, 16), :] = small[
                pl.ds(pl.multiple_of(c * 64 + a * 16, 16), 16), chunk
            ]

    def add(count, store, *terms):
        @pl.loop(0, count)
        def _(r):
            rows = pl.ds(pl.multiple_of(r * 16, 16), 16)
            total = terms[0](rows).astype(F32)
            for term in terms[1:]:
                total = total + term(rows).astype(F32)
            store(rows, total.astype(BF16))

    for g in range(3):
        form(g, 1 - core, theirs)
        if g == 0:
            pl.semaphore_wait(barrier, len(others))
        send(theirs.at[g], from_core.at[g], send_sem.at[0], recv_sem.at[g, 0], *partner)
    for g in range(3):
        form(g, core, mine)
        wait_bytes(from_core.at[g], recv_sem.at[g, 0])
        for a in range(4):

            def put(rows, total, g=g, a=a):
                mine[g, a, rows, :] = total

            add(
                QUARTER // 16,
                put,
                lambda rows, g=g, a=a: mine[g, a, rows, :],
                lambda rows, g=g, a=a: from_core[g, a, rows, :],
            )
        for k in range(1, 4):
            d, to = peer(g, k)
            send(mine.at[g, d], part1.at[g, k - 1], send_sem.at[1], recv_sem.at[g, 1], *to)
    for g in range(3):
        p1 = place[g]
        wait_bytes(part1.at[g], recv_sem.at[g, 1])

        def put(rows, total, g=g):
            sum1[g, rows, :] = total

        add(
            QUARTER // 16,
            put,
            lambda rows, g=g, p1=p1: mine[g, p1, rows, :],
            *[lambda rows, g=g, k=k: part1[g, k, rows, :] for k in range(3)],
        )
        sum1[g, pl.ds(QUARTER, PADDED - QUARTER), :] = jnp.zeros((PADDED - QUARTER, WIDTH), BF16)
        for k in range(1, 4):
            d, to = peer((g + 1) % 3, k)
            rows = pl.ds(pl.multiple_of(d * 64, 64), 64)
            send(sum1.at[g, rows], part2.at[g, k - 1], send_sem.at[2], recv_sem.at[g, 2], *to)
    for g in range(3):
        first = place[(g + 1) % 3] * 64
        wait_bytes(part2.at[g], recv_sem.at[g, 2])
        rows = pl.ds(pl.multiple_of(first, 64), 64)
        total = sum1[g, rows, :].astype(F32)
        for k in range(3):
            total = total + part2[g, k].astype(F32)
        sum2[g] = total.astype(BF16)
        for k in range(1, 4):
            d, to = peer((g + 2) % 3, k)
            rows = pl.ds(pl.multiple_of(d * 16, 16), 16)
            send(sum2.at[g, rows], part3.at[g, k - 1], send_sem.at[3], recv_sem.at[g, 3], *to)
    for g in range(3):
        p1, p2, p3 = place[g], place[(g + 1) % 3], place[(g + 2) % 3]
        wait_bytes(part3.at[g], recv_sem.at[g, 3])
        total = sum2[g, pl.ds(pl.multiple_of(p3 * 16, 16), 16), :].astype(F32)
        for k in range(3):
            total = total + part3[g, k].astype(F32)
        rows = pl.ds(pl.multiple_of(p2 * 64 + p3 * 16, 16), 16)
        full[g, p1, rows, :] = total.astype(BF16)
        block = full.at[g, p1, rows]
        for k in range(1, 4):
            _, to = peer((g + 2) % 3, k)
            send(block, block, send_sem.at[4], recv_sem.at[g, 4], *to)
    for g in range(3):
        p1, p2 = place[g], place[(g + 1) % 3]
        wait_bytes(full.at[g, p1, pl.ds(0, 48)], recv_sem.at[g, 4])
        block = full.at[g, p1, pl.ds(pl.multiple_of(p2 * 64, 64), 64)]
        for k in range(1, 4):
            _, to = peer((g + 1) % 3, k)
            send(block, block, send_sem.at[5], recv_sem.at[g, 5], *to)
    for g in range(3):
        p1 = place[g]
        wait_bytes(full.at[g, p1, pl.ds(0, 192)], recv_sem.at[g, 5])
        block = full.at[g, p1, pl.ds(0, QUARTER)]
        for k in range(1, 4):
            _, to = peer(g, k)
            send(block, block, send_sem.at[6], recv_sem.at[g, 6], *to)
        send(block, other.at[g, p1], send_sem.at[7], recv_sem.at[g, 7], *partner)

    def unpack(source, g, c):
        wide = pl.ds(pl.multiple_of(g * 1024 + c * 512, 512), 512)
        narrow = pl.ds(pl.multiple_of(g * 256 + c * 128, 128), 128)

        @pl.loop(0, 4)
        def _(a):
            @pl.loop(0, 12)
            def _(r):
                rows = pl.ds(pl.multiple_of(r * 16, 16), 16)
                place_rows = pl.ds(pl.multiple_of(a * 192 + r * 16, 16), 16)
                in_sum[place_rows, wide] = source[g, a, rows, pl.ds(0, 512)]
                out_sum[place_rows, narrow] = source[g, a, rows, pl.ds(512, 128)]

            small_sum[pl.ds(pl.multiple_of(c * 64 + a * 16, 16), 16), pl.ds(g * WIDTH, WIDTH)] = source[
                g, a, pl.ds(192, 16), :
            ]

    for g in range(3):
        wait_bytes(full.at[g, pl.ds(0, 3), pl.ds(0, QUARTER)], recv_sem.at[g, 6])
        for k in range(1, 4):
            p1 = lax.rem(place[g] + k, 4)
            block = full.at[g, p1, pl.ds(0, QUARTER)]
            send(block, other.at[g, p1], send_sem.at[7], recv_sem.at[g, 7], *partner)
        unpack(full, g, core)
    for g in range(3):
        wait_bytes(other.at[g], recv_sem.at[g, 7])
        unpack(other, g, 1 - core)
    wait_bytes(theirs, send_sem.at[0])
    wait_bytes(part1, send_sem.at[1])
    wait_bytes(part2, send_sem.at[2])
    wait_bytes(part3, send_sem.at[3])
    wait_bytes(part3, send_sem.at[4])
    wait_bytes(part2, send_sem.at[5])
    wait_bytes(part1, send_sem.at[6])
    wait_bytes(theirs, send_sem.at[7])


def reduce_all(left_in, right_in, left_out, right_out, small, collective_id):
    chunk = (3, 4, QUARTER, WIDTH)
    return pl.pallas_call(
        reduce_kernel,
        out_shape=(
            jax.ShapeDtypeStruct((768, 3072), BF16),
            jax.ShapeDtypeStruct((768, 768), BF16),
            jax.ShapeDtypeStruct((128, 3 * WIDTH), BF16),
        ),
        in_specs=[pl.BlockSpec(memory_space=pltpu.VMEM)] * 5,
        out_specs=[pl.BlockSpec(memory_space=pltpu.VMEM)] * 3,
        scratch_shapes=[
            pltpu.VMEM((3, 4, PADDED, WIDTH), BF16),
            pltpu.VMEM(chunk, BF16),
            pltpu.VMEM(chunk, BF16),
            pltpu.VMEM(chunk, BF16),
            pltpu.VMEM(chunk, BF16),
            pltpu.VMEM((3, 3, QUARTER, WIDTH), BF16),
            pltpu.VMEM((3, PADDED, WIDTH), BF16),
            pltpu.VMEM((3, 3, 64, WIDTH), BF16),
            pltpu.VMEM((3, 64, WIDTH), BF16),
            pltpu.VMEM((3, 3, 16, WIDTH), BF16),
            pltpu.VMEM((3, 16, WIDTH), BF16),
            pltpu.SemaphoreType.DMA((8,)),
            pltpu.SemaphoreType.DMA((3, 8)),
        ],
        compiler_params=pltpu.CompilerParams(
            collective_id=collective_id, has_side_effects=True, vmem_limit_bytes=48 << 20
        ),
    )(left_in, right_in, left_out, right_out, small)


def norm_parts(values, axis):
    centered = values - jnp.mean(values, axis=axis, keepdims=True)
    inverse = lax.rsqrt(jnp.mean(centered * centered, axis=axis, keepdims=True) + EPSILON)
    return (centered * inverse, inverse)


def norm_back(normed, inverse, incoming_gradient, axis):
    first_mean = jnp.mean(incoming_gradient, axis=axis, keepdims=True)
    second_mean = jnp.mean(incoming_gradient * normed, axis=axis, keepdims=True)
    return (incoming_gradient - first_mean - normed * second_mean) * inverse


def silu_slope(values):
    sigmoid_part = jax.nn.sigmoid(values)
    return sigmoid_part * (1.0 + values * (1.0 - sigmoid_part))


def shards(
    pair,
    pair_mask,
    tri_in_w,
    tri_gate_w,
    tri_out_w,
    bias_w,
    atom_feats,
    atom_to_token,
    atom_w,
    tokens,
    attention_input_weight,
    attention_output_weight,
    cot_pair,
    token_output_cotangent,
):
    hidden = tri_in_w.shape[1] // 4
    token_width = attention_input_weight.shape[0]
    head_count = bias_w.shape[1]
    total_tokens = tokens.shape[1]
    pair_f = pair.astype(jnp.float32)
    normed_z, inverse_z = norm_parts(pair_f, 2)
    normed_zb = normed_z.astype(jnp.bfloat16)
    projected = jnp.einsum("ijz,zc->cij", normed_zb, tri_in_w, preferred_element_type=jnp.float32)
    mask_rows = pair_mask.astype(jnp.float32)[None]
    gate_left = jax.nn.sigmoid(projected[0:hidden])
    gate_right = jax.nn.sigmoid(projected[2 * hidden : 3 * hidden])
    rows, columns = pair_mask.shape
    blocks = (N_TILE, N_SAMPLE)
    following, bias_all, left_panel, right_panel, product, every_feat, every_atom = pair_forward(
        pair.reshape(-1, hidden),
        pair_mask.astype(F32).reshape(1, -1),
        tri_in_w.T,
        tri_gate_w,
        tri_out_w,
        bias_w.T,
        atom_feats,
        atom_to_token[None],
        0,
    )
    every_feat = every_feat.reshape(-1, atom_feats.shape[1])
    every_atom = every_atom.reshape(-1)
    product = product.reshape(hidden, rows, columns).astype(F32)
    normed_p, inverse_p = norm_parts(product, 0)
    normed_pb = normed_p.astype(jnp.bfloat16)
    linear = jnp.einsum("cij,cz->ijz", normed_pb, tri_out_w, preferred_element_type=jnp.float32)
    tri_gate = jax.nn.sigmoid(
        jnp.einsum("ijz,zy->ijy", normed_zb, tri_gate_w, preferred_element_type=jnp.float32)
    )
    pair_next = following.reshape(pair.shape)
    normed_n, inverse_n = norm_parts(pair_next, 2)
    normed_nb = normed_n.astype(jnp.bfloat16)
    atom_pre = jnp.dot(every_feat, atom_w, preferred_element_type=jnp.float32)
    atom_act = jax.nn.silu(atom_pre).astype(BF16)
    token_ids = jnp.arange(total_tokens, dtype=jnp.int32)
    one_hot = (token_ids[:, None] == every_atom[None, :]).astype(BF16)
    token_sums = jnp.dot(one_hot, atom_act, preferred_element_type=F32)
    token_counts = jnp.sum(one_hot.astype(F32), axis=1)
    token_cond = token_sums / token_counts[:, None]
    token_state_rows = tokens.astype(jnp.float32) + token_cond[None]
    normed_h, inverse_h = norm_parts(token_state_rows, 2)
    normalized_hidden_bfloat = normed_h.astype(jnp.bfloat16)
    hidden_t = normalized_hidden_bfloat.reshape(-1, token_width).T
    cot_rows = token_output_cotangent.reshape(-1, token_width)

    def project(block):
        weight = attention_input_weight[:, block * token_width : (block + 1) * token_width]
        return t_dot(weight, hidden_t)

    gated_t, d_every_t, bias_blocks = attention(
        project(0).astype(BF16),
        project(2).astype(BF16),
        project(3).astype(BF16),
        jax.nn.sigmoid(project(1)),
        dot_t(attention_output_weight, cot_rows),
        bias_all,
    )
    d_every_t = d_every_t.reshape(4 * token_width, -1)
    token_output_rows = token_state_rows + t_dot(gated_t, attention_output_weight).reshape(
        token_state_rows.shape
    )
    bias_grad = (
        scatter_sum(bias_blocks, 3)
        .reshape(head_count // GROUP, rows, GROUP, columns)
        .transpose(0, 2, 1, 3)
        .reshape(head_count, rows, columns)
    )
    normalized_hidden_gradient = lax.dot_general(
        d_every_t, attention_input_weight, (((0,), (1,)), ((), ())), preferred_element_type=F32
    ).reshape(token_state_rows.shape)
    grad_tokens = token_output_cotangent.astype(jnp.float32) + norm_back(
        normed_h, inverse_h, normalized_hidden_gradient, 2
    )
    cond_grad = (jnp.sum(grad_tokens, axis=0) / token_counts[:, None]).astype(BF16)
    d_act = lax.dot_general(
        one_hot, cond_grad, (((0,), (0,)), ((), ())), preferred_element_type=F32
    ) * silu_slope(atom_pre)
    grad_atom_w = lax.dot_general(
        every_feat, d_act.astype(BF16), (((0,), (0,)), ((), ())), preferred_element_type=F32
    )
    d_normed_n = jnp.einsum("hij,zh->ijz", bias_grad, bias_w.astype(jnp.float32), precision=HIGHEST)
    grad_bias_w = jnp.einsum(
        "ijz,hij->zh", normed_nb.astype(jnp.float32), bias_grad, precision=HIGHEST
    )
    d_next = cot_pair.astype(jnp.float32) + norm_back(normed_n, inverse_n, d_normed_n, 2)
    d_linear = (d_next * tri_gate).astype(jnp.bfloat16)
    d_gate_pre = (d_next * linear * tri_gate * (1.0 - tri_gate)).astype(jnp.bfloat16)
    grad_tri_out_w = jnp.einsum(
        "cij,ijz->cz", normed_pb, d_linear, preferred_element_type=jnp.float32
    )
    d_normed_p = jnp.einsum("ijz,cz->cij", d_linear, tri_out_w, preferred_element_type=jnp.float32)
    d_product = norm_back(normed_p, inverse_p, d_normed_p, 0).astype(jnp.bfloat16)

    def by_owner(values):
        return values.reshape((N_SAMPLE, N_TILE) + values.shape[1:]).swapaxes(0, 1)

    d_product_panel = (
        exchange(by_owner(d_product.astype(F32)).reshape(blocks + (4, 128)), 4)
        .reshape(blocks + (rows, columns))
        .astype(BF16)
        .transpose(0, 2, 1, 3)
        .reshape(N_TILE * rows, N_SAMPLE * columns)
    )
    d_left_panel = jnp.dot(d_product_panel, right_panel, preferred_element_type=F32)
    d_right_panel = jnp.dot(d_product_panel.T, left_panel, preferred_element_type=F32)
    d_halves = (
        jnp.stack([d_left_panel, d_right_panel])
        .reshape(2, N_TILE, rows, N_SAMPLE, columns)
        .transpose(1, 3, 0, 2, 4)
        .reshape(blocks + (8, 128))
    )
    d_halves = (
        exchange(d_halves, 5)
        .reshape(blocks + (2, rows, columns))
        .transpose(1, 0, 2, 3, 4)
        .reshape(hidden, 2, rows, columns)
    )
    d_left, d_right = d_halves[:, 0], d_halves[:, 1]
    d_proj = jnp.concatenate(
        [
            d_left * projected[hidden : 2 * hidden] * mask_rows * gate_left * (1.0 - gate_left),
            d_left * gate_left * mask_rows,
            d_right * projected[3 * hidden :] * mask_rows * gate_right * (1.0 - gate_right),
            d_right * gate_right * mask_rows,
        ],
        axis=0,
    ).astype(jnp.bfloat16)
    grad_tri_in_w = jnp.einsum("ijz,cij->zc", normed_zb, d_proj, preferred_element_type=jnp.float32)
    grad_tri_gate_w = jnp.einsum(
        "ijz,ijy->zy", normed_zb, d_gate_pre, preferred_element_type=jnp.float32
    )
    d_normed_z = jnp.einsum(
        "cij,zc->ijz", d_proj, tri_in_w, preferred_element_type=jnp.float32
    ) + jnp.einsum("ijy,zy->ijz", d_gate_pre, tri_gate_w, preferred_element_type=jnp.float32)
    grad_pair = d_next + norm_back(normed_z, inverse_z, d_normed_z, 2)
    small = jnp.concatenate(
        [
            grad_tri_in_w,
            grad_tri_gate_w,
            grad_tri_out_w,
            grad_bias_w,
            jnp.zeros((hidden, 128 - head_count), F32),
            grad_atom_w,
            jnp.zeros((hidden, 3 * WIDTH - 4 * hidden - 3 * 128 - token_width), F32),
        ],
        axis=1,
    ).astype(BF16)
    in_sum, out_sum, small_sum = reduce_all(hidden_t, d_every_t, gated_t, cot_rows, small, 6)
    small_sum = small_sum.astype(F32)
    at = 4 * hidden
    summed = (
        small_sum[:, :at],
        small_sum[:, at : at + 128],
        small_sum[:, at + 128 : at + 256],
        small_sum[:, at + 256 : at + 256 + head_count],
        small_sum[:, at + 384 : at + 384 + token_width],
        in_sum.astype(F32),
        out_sum.astype(F32),
    )
    return (pair_next, token_output_rows, grad_pair, grad_tokens) + summed


def solution(mesh):
    in_specs = (
        P("tile", "sample", None),
        P("tile", "sample"),
        P(),
        P(),
        P(),
        P(),
        P("tile", None),
        P("tile"),
        P(),
        P(("tile", "sample"), None, None),
        P(),
        P(),
        P("tile", "sample", None),
        P(("tile", "sample"), None, None),
    )
    out_specs = (
        P("tile", "sample", None),
        P(("tile", "sample"), None, None),
        P("tile", "sample", None),
        P(("tile", "sample"), None, None),
        P(),
        P(),
        P(),
        P(),
        P(),
        P(),
        P(),
    )
    return jax.shard_map(shards, mesh=mesh, in_specs=in_specs, out_specs=out_specs, check_vma=False)
```

```python
import functools
import math

import jax
import jax.numpy as jnp
from jax import lax
from jax.experimental import pallas as pl
from jax.experimental.pallas import tpu as pltpu
from jax.sharding import PartitionSpec as P

EPSILON = 1e-05
N_TILE = 16
N_SAMPLE = 8
N_CHIP = 8
MESH = pl.DeviceIdType.MESH
BF16 = jnp.bfloat16
F32 = jnp.float32
HIGHEST = lax.Precision.HIGHEST


def wait_bytes(ref, sem):
    pltpu.make_async_copy(ref, ref, sem).wait()


def send(src, dst, send_sem, recv_sem, t, s):
    pltpu.make_async_remote_copy(
        src, dst, send_sem, recv_sem, device_id=(t, s), device_id_type=MESH
    ).start()


def dot(a, b):
    return jnp.dot(a, b, preferred_element_type=F32)


def dot_t(a, b):
    return lax.dot_general(a, b, (((1,), (1,)), ((), ())), preferred_element_type=F32)


def t_dot(a, b):
    return lax.dot_general(a, b, (((0,), (0,)), ((), ())), preferred_element_type=F32)


HEAD = 48
GROUP = 4
LANES = 32


def place_lanes(parts, first):
    group_of = lax.broadcasted_iota(jnp.int32, parts[0].shape, 1) // LANES
    result = None
    for i in range(4):
        shift = (i - first) % 4 * LANES
        moved = pltpu.roll(parts[i], shift, 1) if shift else parts[i]
        result = moved if result is None else jnp.where(group_of == i, moved, result)
    return result


def panel_of(arrived, first, step, panel):
    for part in range(4):
        rows = [
            arrived[part, pl.ds(first + s * (step // 8), 16, stride=step), :] for s in range(8)
        ]
        for i in range(4):
            for half in range(2):
                panel[half, pl.ds(part * 4 + i, 16, stride=16), :] = place_lanes(
                    rows[half * 4 : half * 4 + 4], i
                )


def blocks_of(panel, store):
    for half in range(2):
        for part in range(4):
            rows = [panel[half, pl.ds(part * 4 + i, 16, stride=16), :] for i in range(4)]
            for q in range(4):
                store(half * 4 + q, pl.ds(part * 128, 128), place_lanes(rows, q))


def split_lanes(values, ref):
    for part in range(ref.shape[0]):
        ref[part] = values[:, part * 128 : part * 128 + 128]


def joined(ref):
    return jnp.concatenate([ref[0], ref[1]], axis=1)


def norm_rows(values, axis):
    centered = values - jnp.mean(values, axis=axis, keepdims=True)
    inverse = lax.rsqrt(jnp.mean(centered * centered, axis=axis, keepdims=True) + EPSILON)
    return centered * inverse, inverse


def sigmoid(values):
    return 1.0 / (1.0 + jnp.exp(-values))


def pair_forward_kernel(
    pair,
    mask,
    in_w_t,
    gate_w,
    out_w,
    bias_w_t,
    feats,
    atoms,
    pair_next,
    bias,
    left,
    right,
    product,
    every_feat,
    every_atom,
    x1,
    mid,
    mid_rows,
    x2,
    arrived,
    arrived_rows,
    panel,
    x3,
    back,
    back_rows,
    x4,
    packed,
    mine,
    send_sem,
    recv_sem,
):
    t, s = lax.axis_index("tile"), lax.axis_index("sample")
    m, c = t // 2, lax.rem(t, 2)
    barrier = pltpu.get_barrier_semaphore()
    tile_peers = [lax.rem(t + k, N_TILE) for k in range(1, N_TILE)]
    sample_peers = [lax.rem(s + k, N_SAMPLE) for k in range(1, N_SAMPLE)]
    for d in sample_peers:
        pl.semaphore_signal(barrier, inc=1, device_id=(t, d), device_id_type=MESH)
    for d in tile_peers:
        pl.semaphore_signal(barrier, inc=1, device_id=(d, s), device_id_type=MESH)

    normed_z = norm_rows(pair[...].astype(F32), 1)[0].astype(BF16)

    def project(block):
        return dot_t(in_w_t[pl.ds(block * 128, 128), :], normed_z)

    for side in range(2):
        value = (sigmoid(project(2 * side)) * project(2 * side + 1) * mask[...]).astype(BF16)
        for d in range(N_SAMPLE):
            x1[d, side] = value[d * 16 : d * 16 + 16]
    pl.semaphore_wait(barrier, N_SAMPLE + N_TILE - 2)
    for d in sample_peers:
        send(x1.at[d], mid.at[s], send_sem.at[0], recv_sem.at[0], t, d)
    for d in tile_peers:
        send(feats, every_feat.at[t], send_sem.at[1], recv_sem.at[1], d, s)
        send(atoms, every_atom.at[t], send_sem.at[2], recv_sem.at[2], d, s)
    every_feat[t] = feats[...]
    every_atom[t] = atoms[...]
    mid[s] = x1[s]
    tri_gate = sigmoid(dot(normed_z, gate_w[...]))
    wait_bytes(mid.at[pl.ds(0, N_SAMPLE - 1)], recv_sem.at[0])
    split_lanes(mid[...].reshape(256, 512).astype(F32), mid_rows)
    for d in range(N_TILE):
        for part in range(4):
            x2[d, :, pl.ds(part * 128, 128)] = mid_rows[part, pl.ds(d, 16, stride=16), :].astype(
                BF16
            )
    for d in tile_peers:
        send(x2.at[d], arrived.at[t], send_sem.at[3], recv_sem.at[3], d, s)
    arrived[t] = x2[t]
    wait_bytes(arrived.at[pl.ds(0, N_TILE - 1)], recv_sem.at[3])
    split_lanes(arrived[...].reshape(256, 512).astype(F32), arrived_rows)
    panel_of(arrived_rows, 0, 16, panel)
    left[...] = joined(panel).astype(BF16)
    panel_of(arrived_rows, 1, 16, panel)
    right[...] = joined(panel).astype(BF16)
    x3[...] = dot_t(left[...], right[...]).astype(BF16).reshape(N_TILE, 16, 256)
    for d in tile_peers:
        send(x3.at[d], back.at[t], send_sem.at[4], recv_sem.at[4], d, s)
    back[t] = x3[t]
    wait_bytes(back.at[pl.ds(0, N_TILE - 1)], recv_sem.at[4])
    split_lanes(back[...].reshape(256, 256).astype(F32), back_rows)

    def store(d, lanes, rows):
        x4[d, :, lanes] = rows.astype(BF16)

    blocks_of(back_rows, store)
    for d in sample_peers:
        send(x4.at[d], product.at[s], send_sem.at[5], recv_sem.at[5], t, d)
    product[s] = x4[s]
    wait_bytes(product.at[pl.ds(0, N_SAMPLE - 1)], recv_sem.at[5])
    normed_p = norm_rows(product[...].reshape(128, 512).astype(F32), 0)[0].astype(BF16)
    linear = t_dot(normed_p, out_w[...])
    following = pair[...].astype(F32) + tri_gate * linear
    pair_next[...] = following
    normed_n = norm_rows(following, 1)[0].astype(BF16)
    head_rows = dot_t(bias_w_t[...], normed_n)
    split_lanes(head_rows, packed)
    for part in range(4):
        rows = [packed[part, pl.ds(h, 4, stride=4), :] for h in range(4)]
        for i in range(4):
            mine[:, part * 4 + i] = place_lanes(rows, i)
    bias[m, c, s] = mine[...].astype(BF16)

    own = bias.at[m, c, s]
    for d in sample_peers:
        send(own, own, send_sem.at[6], recv_sem.at[6], t, d)
    wait_bytes(bias.at[m, c, pl.ds(0, N_SAMPLE - 1)], recv_sem.at[6])
    block = bias.at[m, c]
    other = m * 2 + 1 - c
    for k in range(1, N_CHIP):
        send(block, block, send_sem.at[7], recv_sem.at[7 + k], lax.rem(m + k, N_CHIP) * 2 + c, s)
    send(block, block, send_sem.at[8], recv_sem.at[7], other, s)
    for k in range(1, N_CHIP):
        came = bias.at[lax.rem(m + N_CHIP - k, N_CHIP), c]
        wait_bytes(came, recv_sem.at[7 + k])
        send(came, came, send_sem.at[8], recv_sem.at[7], other, s)
    wait_bytes(bias.at[:, 0], recv_sem.at[7])
    wait_bytes(every_feat.at[pl.ds(0, N_TILE - 1)], recv_sem.at[1])
    wait_bytes(every_atom.at[pl.ds(0, N_TILE - 1)], recv_sem.at[2])
    wait_bytes(mid.at[pl.ds(0, N_SAMPLE - 1)], send_sem.at[0])
    wait_bytes(every_feat.at[pl.ds(0, N_TILE - 1)], send_sem.at[1])
    wait_bytes(every_atom.at[pl.ds(0, N_TILE - 1)], send_sem.at[2])
    wait_bytes(arrived.at[pl.ds(0, N_TILE - 1)], send_sem.at[3])
    wait_bytes(back.at[pl.ds(0, N_TILE - 1)], send_sem.at[4])
    wait_bytes(product.at[pl.ds(0, N_SAMPLE - 1)], send_sem.at[5])
    wait_bytes(bias.at[m, c, pl.ds(0, N_SAMPLE - 1)], send_sem.at[6])
    wait_bytes(bias.at[pl.ds(0, N_CHIP - 1), 0], send_sem.at[7])
    wait_bytes(bias.at[:, 0], send_sem.at[8])


def pair_forward(pair, mask, in_w_t, gate_w, out_w, bias_w_t, feats, atoms, collective_id):
    vmem = pl.BlockSpec(memory_space=pltpu.VMEM)
    return pl.pallas_call(
        pair_forward_kernel,
        out_shape=[
            jax.ShapeDtypeStruct(pair.shape, F32),
            jax.ShapeDtypeStruct((N_CHIP, 2, N_SAMPLE, 4, 16, 128), BF16),
            jax.ShapeDtypeStruct((256, 256), BF16),
            jax.ShapeDtypeStruct((256, 256), BF16),
            jax.ShapeDtypeStruct((N_SAMPLE, 16, 512), BF16),
            jax.ShapeDtypeStruct((N_TILE,) + feats.shape, feats.dtype),
            jax.ShapeDtypeStruct((N_TILE,) + atoms.shape, atoms.dtype),
        ],
        in_specs=[vmem] * 8,
        out_specs=[vmem] * 7,
        scratch_shapes=[
            pltpu.VMEM((N_SAMPLE, 2, 16, 512), BF16),
            pltpu.VMEM((N_SAMPLE, 2, 16, 512), BF16),
            pltpu.VMEM((4, 256, 128), F32),
            pltpu.VMEM((N_TILE, 16, 512), BF16),
            pltpu.VMEM((N_TILE, 16, 512), BF16),
            pltpu.VMEM((4, 256, 128), F32),
            pltpu.VMEM((2, 256, 128), F32),
            pltpu.VMEM((N_TILE, 16, 256), BF16),
            pltpu.VMEM((N_TILE, 16, 256), BF16),
            pltpu.VMEM((2, 256, 128), F32),
            pltpu.VMEM((N_SAMPLE, 16, 512), BF16),
            pltpu.VMEM((4, 16, 128), F32),
            pltpu.VMEM((4, 16, 128), F32),
            pltpu.SemaphoreType.DMA((9,)),
            pltpu.SemaphoreType.DMA((15,)),
        ],
        compiler_params=pltpu.CompilerParams(
            collective_id=collective_id, has_side_effects=True, vmem_limit_bytes=40 << 20
        ),
    )(pair, mask, in_w_t, gate_w, out_w, bias_w_t, feats, atoms)


def attention_kernel(q, k, v, gate, up, bias, gated, d_every, d_bias, bias_rows, bias_total):
    tokens = bias_rows.shape[1]
    scale = 1.0 / math.sqrt(HEAD)
    group_of = lax.broadcasted_iota(jnp.int32, (tokens, 128), 1) // LANES

    for half in range(2):
        parts = [
            bias[:, :, half * 4 + i, 0].reshape(tokens, 128).astype(F32) for i in range(4)
        ]
        for h in range(GROUP):
            row = parts[0] if h == 0 else pltpu.roll(parts[0], (-h) % 4 * LANES, 1)
            for i in range(1, 4):
                shift = (i - h) % 4 * LANES
                moved = pltpu.roll(parts[i], shift, 1) if shift else parts[i]
                row = jnp.where(group_of == i, moved, row)
            bias_rows[h, :, pl.ds(half * 128, 128)] = row

    @pl.loop(0, GROUP)
    def _(h):
        rows = pl.ds(pl.multiple_of(h * HEAD, 16), HEAD)
        for sample in range(2):
            columns = pl.ds(sample * tokens, tokens)
            qh, kh, vh = q[rows, columns], k[rows, columns], v[rows, columns]
            scores = t_dot(qh, kh) * scale + bias_rows[h]
            weights = jnp.exp(scores - jnp.max(scores, axis=1, keepdims=True))
            probs = weights * (1.0 / jnp.sum(weights, axis=1, keepdims=True))
            probs_b = probs.astype(BF16)
            attended = dot_t(vh, probs_b)
            gate_h, up_h = gate[rows, columns], up[rows, columns]
            gated[rows, columns] = (gate_h * attended).astype(BF16)
            d_att = (up_h * gate_h).astype(BF16)
            d_every[1, rows, columns] = (up_h * attended * gate_h * (1.0 - gate_h)).astype(BF16)
            d_probs = t_dot(d_att, vh)
            inner = jnp.sum(probs * d_probs, axis=1, keepdims=True)
            d_scores = probs * (d_probs - inner)
            d_scores_b = d_scores.astype(BF16)
            d_every[0, rows, columns] = (dot_t(kh, d_scores_b) * scale).astype(BF16)
            d_every[2, rows, columns] = (dot(qh, d_scores_b) * scale).astype(BF16)
            d_every[3, rows, columns] = dot(d_att, probs_b).astype(BF16)
            if sample == 0:
                bias_total[h] = d_scores
            else:
                bias_total[h] = bias_total[h] + d_scores

    for half in range(2):
        parts = [bias_total[h, :, pl.ds(half * 128, 128)] for h in range(GROUP)]
        for i in range(4):
            row = parts[0] if i == 0 else pltpu.roll(parts[0], (-i) % 4 * LANES, 1)
            for h in range(1, GROUP):
                shift = (h - i) % 4 * LANES
                moved = pltpu.roll(parts[h], shift, 1) if shift else parts[h]
                row = jnp.where(group_of == h, moved, row)
            d_bias[:, :, half * 4 + i, 0] = row.astype(BF16).reshape(N_CHIP, 2, 16, 128)


def attention(q, k, v, gate, up, bias):
    width, columns = q.shape
    tokens = columns // 2
    block = GROUP * HEAD
    feature = pl.BlockSpec((block, columns), lambda i: (i, 0))
    of_bias = pl.BlockSpec((N_CHIP, 2, N_SAMPLE, 1, 16, 128), lambda i: (0, 0, 0, i, 0, 0))
    return pl.pallas_call(
        attention_kernel,
        grid=(width // block,),
        in_specs=[feature] * 5 + [of_bias],
        out_specs=[feature, pl.BlockSpec((4, block, columns), lambda i: (0, i, 0)), of_bias],
        out_shape=[
            jax.ShapeDtypeStruct((width, columns), BF16),
            jax.ShapeDtypeStruct((4, width, columns), BF16),
            jax.ShapeDtypeStruct(bias.shape, BF16),
        ],
        scratch_shapes=[
            pltpu.VMEM((GROUP, tokens, tokens), F32),
            pltpu.VMEM((GROUP, tokens, tokens), F32),
        ],
        compiler_params=pltpu.CompilerParams(vmem_limit_bytes=40 << 20),
    )(q, k, v, gate, up, bias)


ROWS = 192
WIDTH = 640
SMALL = 2048


def norm_back_rows(normed, inverse, incoming, axis):
    first = jnp.mean(incoming, axis=axis, keepdims=True)
    second = jnp.mean(incoming * normed, axis=axis, keepdims=True)
    return (incoming - first - normed * second) * inverse


def backward_kernel(
    d_bias,
    pair,
    mask,
    in_w_t,
    gate_w,
    out_w,
    bias_w_t,
    following,
    product,
    left,
    right,
    cot_pair,
    atom_grad,
    left_in,
    right_in,
    left_out,
    right_out,
    grad_pair,
    in_sum,
    out_sum,
    small_sum,
    pair_sum,
    by_chip,
    by_sample,
    bias_block,
    head_rows,
    coefficient,
    keep,
    keep_p,
    x1,
    mid,
    mid_rows,
    x2,
    arrived,
    arrived_rows,
    panel,
    x3,
    back,
    back_rows,
    x4,
    final,
    small,
    small_part,
    small_mid,
    small_last,
    theirs,
    mine,
    from_core,
    part1,
    sum1,
    part2,
    sum2,
    part3,
    full,
    other,
    send_sem,
    recv_sem,
    chip_sem,
    w_send,
    w_recv,
):
    t, s = lax.axis_index("tile"), lax.axis_index("sample")
    m, core = t // 2, lax.rem(t, 2)
    partner_t = m * 2 + 1 - core
    place = [lax.rem(s, 2) * 2 + t // 8, lax.rem(t // 2, 4), s // 2]
    tile_peers = [lax.rem(t + k, N_TILE) for k in range(1, N_TILE)]
    sample_peers = [lax.rem(s + k, N_SAMPLE) for k in range(1, N_SAMPLE)]

    def peer(axis, k):
        where = list(place)
        where[axis] = lax.rem(place[axis] + k, 4)
        x, y, z = where
        return where[axis], (lax.rem(x, 2) * 8 + y * 2 + core, z * 2 + x // 2)

    barrier = pltpu.get_barrier_semaphore()
    for d in sample_peers:
        pl.semaphore_signal(barrier, inc=1, device_id=(t, d), device_id_type=MESH)
    for d in tile_peers:
        pl.semaphore_signal(barrier, inc=1, device_id=(d, s), device_id_type=MESH)
    diagonal = (lax.rem(t + 8, N_TILE), s + 1 - 2 * lax.rem(s, 2))
    pl.semaphore_signal(barrier, inc=1, device_id=diagonal, device_id_type=MESH)

    def form(g, c, target):
        wide = pl.ds(pl.multiple_of(g * 1024 + c * 512, 512), 512)
        narrow = pl.ds(pl.multiple_of(g * 256 + c * 128, 128), 128)

        @pl.loop(0, 4)
        def _(a):
            rows = pl.ds(pl.multiple_of(a * ROWS, 64), ROWS)
            target[g, a, :, pl.ds(0, 512)] = dot_t(left_in[rows, :], right_in[wide, :]).astype(BF16)
            target[g, a, :, pl.ds(512, 128)] = dot(left_out[rows, :], right_out[:, narrow]).astype(
                BF16
            )

    def form_theirs(g):
        form(g, 1 - core, theirs)
        send(theirs.at[g], from_core.at[g], w_send.at[0], w_recv.at[g, 0], partner_t, s)

    def form_mine(g):
        form(g, core, mine)

    def add_cores(g):
        wait_bytes(from_core.at[g], w_recv.at[g, 0])

        @pl.loop(0, 4)
        def _(a):
            @pl.loop(0, ROWS // 16)
            def _(r):
                rows = pl.ds(pl.multiple_of(r * 16, 16), 16)
                total = mine[g, a, rows, :].astype(F32) + from_core[g, a, rows, :].astype(F32)
                mine[g, a, rows, :] = total.astype(BF16)

        for k in range(1, 4):
            d, to = peer(g, k)
            send(mine.at[g, d], part1.at[g, k - 1], w_send.at[1], w_recv.at[g, 1], *to)

    def add_first(g):
        p1 = place[g]
        wait_bytes(part1.at[g], w_recv.at[g, 1])

        @pl.loop(0, ROWS // 16)
        def _(r):
            rows = pl.ds(pl.multiple_of(r * 16, 16), 16)
            total = mine[g, p1, rows, :].astype(F32)
            for k in range(3):
                total = total + part1[g, k, rows, :].astype(F32)
            sum1[g, rows, :] = total.astype(BF16)

        for k in range(1, 4):
            d, to = peer((g + 1) % 3, k)
            rows = pl.ds(pl.multiple_of(d * 48, 16), 48)
            send(sum1.at[g, rows], part2.at[g, k - 1], w_send.at[2], w_recv.at[g, 2], *to)

    def add_second(g):
        p2, p3 = place[(g + 1) % 3], place[(g + 2) % 3]
        wait_bytes(part2.at[g], w_recv.at[g, 2])
        total = sum1[g, pl.ds(pl.multiple_of(p2 * 48, 16), 48), :].astype(F32)
        for k in range(3):
            total = total + part2[g, k].astype(F32)
        sum2[g] = total.astype(BF16)
        for k in range(1, 4):
            _, to = peer((g + 2) % 3, k)
            send(sum2.at[g], part3.at[g, p3], w_send.at[3], w_recv.at[g, 3], *to)
        part3[g, p3] = sum2[g]

    def add_third(g):
        p1, p2 = place[g], place[(g + 1) % 3]
        wait_bytes(part3.at[g, pl.ds(0, 3)], w_recv.at[g, 3])
        total = part3[g, 0].astype(F32)
        for k in range(1, 4):
            total = total + part3[g, k].astype(F32)
        rows = pl.ds(pl.multiple_of(p2 * 48, 16), 48)
        full[g, p1, rows, :] = total.astype(BF16)
        block = full.at[g, p1, rows]
        for k in range(1, 4):
            _, to = peer((g + 1) % 3, k)
            send(block, block, w_send.at[4], w_recv.at[g, 4], *to)

    def gather_second(g):
        p1 = place[g]
        wait_bytes(full.at[g, p1, pl.ds(0, 144)], w_recv.at[g, 4])
        block = full.at[g, p1]
        for k in range(1, 4):
            _, to = peer(g, k)
            send(block, block, w_send.at[5], w_recv.at[g, 5], *to)
        send(block, other.at[g, p1], w_send.at[6], w_recv.at[g, 6], partner_t, s)

    def unpack(source, g, c):
        wide = pl.ds(pl.multiple_of(g * 1024 + c * 512, 512), 512)
        narrow = pl.ds(pl.multiple_of(g * 256 + c * 128, 128), 128)

        @pl.loop(0, 4)
        def _(a):
            @pl.loop(0, ROWS // 16)
            def _(r):
                rows = pl.ds(pl.multiple_of(r * 16, 16), 16)
                to_rows = pl.ds(pl.multiple_of(a * ROWS + r * 16, 16), 16)
                in_sum[to_rows, wide] = source[g, a, rows, pl.ds(0, 512)]
                out_sum[to_rows, narrow] = source[g, a, rows, pl.ds(512, 128)]

    def gather_first(g):
        wait_bytes(full.at[g, pl.ds(0, 3)], w_recv.at[g, 5])
        for k in range(1, 4):
            p1 = lax.rem(place[g] + k, 4)
            send(full.at[g, p1], other.at[g, p1], w_send.at[6], w_recv.at[g, 6], partner_t, s)

    pl.semaphore_wait(barrier, N_SAMPLE + N_TILE - 1)
    for k in range(1, N_CHIP + 1):
        d = lax.rem(m + k, N_CHIP)
        send(d_bias.at[d, 1 - core], pair_sum.at[d], send_sem.at[0], chip_sem.at[k - 1], partner_t, s)

    keep[0], inverse_z = norm_rows(pair[...].astype(F32), 1)
    normed_z = keep[0].astype(BF16)

    def project(block):
        return dot_t(in_w_t[pl.ds(block * 128, 128), :], normed_z)

    for side in range(2):
        gate_side = sigmoid(project(2 * side))
        masked = gate_side * mask[...]
        coefficient[2 * side] = masked * (1.0 - gate_side) * project(2 * side + 1)
        coefficient[2 * side + 1] = masked
    keep[1] = sigmoid(dot(normed_z, gate_w[...]))
    keep_p[...], inverse_p = norm_rows(product[...].reshape(128, 512).astype(F32), 0)
    normed_p = keep_p[...].astype(BF16)
    keep[2] = t_dot(normed_p, out_w[...])
    keep[3], inverse_n = norm_rows(following[...], 1)
    normed_n = keep[3].astype(BF16)

    for k in range(1, N_CHIP + 1):
        d = lax.rem(m + k, N_CHIP)
        wait_bytes(pair_sum.at[d], chip_sem.at[k - 1])
        pair_sum[d] = (pair_sum[d].astype(F32) + d_bias[d, core].astype(F32)).astype(BF16)
        if k < N_CHIP:
            send(
                pair_sum.at[d],
                by_chip.at[k - 1],
                send_sem.at[1],
                chip_sem.at[N_CHIP + k - 1],
                d * 2 + core,
                s,
            )
    for g in range(3):
        form_theirs(g)
    form_mine(0)
    total = pair_sum[m].astype(F32)
    for k in range(1, N_CHIP):
        wait_bytes(by_chip.at[k - 1], chip_sem.at[N_CHIP + k - 1])
        total = total + by_chip[k - 1].astype(F32)
    pair_sum[m] = total.astype(BF16)
    for k in range(1, N_SAMPLE):
        send(
            pair_sum.at[m, sample_peers[k - 1]],
            by_sample.at[k - 1],
            send_sem.at[2],
            recv_sem.at[2],
            t,
            sample_peers[k - 1],
        )
    form_mine(1)
    wait_bytes(by_sample, recv_sem.at[2])
    bias_block[...] = pair_sum[m, s].astype(F32) + jnp.sum(by_sample[...].astype(F32), axis=0)

    for part in range(4):
        rows = [bias_block[:, part * 4 + i] for i in range(4)]
        for h in range(4):
            head_rows[part, pl.ds(h, 4, stride=4), :] = place_lanes(rows, h)
    d_heads = jnp.concatenate([head_rows[part] for part in range(4)], axis=1)
    high = d_heads.astype(BF16)
    low = (d_heads - high.astype(F32)).astype(BF16)
    d_normed_n = t_dot(high, bias_w_t[...]) + t_dot(low, bias_w_t[...])
    small[...] = jnp.zeros((128, SMALL), BF16)
    small[pl.ds(0, 16), pl.ds(1536, 128)] = (dot(high, normed_n) + dot(low, normed_n)).astype(BF16)
    small[:, pl.ds(768, 768)] = atom_grad[...]
    d_next = cot_pair[...].astype(F32) + norm_back_rows(keep[3], inverse_n, d_normed_n, 1)
    tri_gate = keep[1]
    d_linear = (d_next * tri_gate).astype(BF16)
    d_gate = (d_next * keep[2] * tri_gate * (1.0 - tri_gate)).astype(BF16)
    keep[4] = d_next
    d_product = norm_back_rows(keep_p[...], inverse_p, dot_t(out_w[...], d_linear), 0).astype(BF16)
    for d in range(N_SAMPLE):
        x1[d] = d_product[d * 16 : d * 16 + 16]
    for d in sample_peers:
        send(x1.at[d], mid.at[s], send_sem.at[3], recv_sem.at[3], t, d)
    mid[s] = x1[s]
    small[:, pl.ds(512, 128)] = t_dot(normed_z, d_gate).astype(BF16)
    small[:, pl.ds(640, 128)] = dot(normed_p, d_linear).astype(BF16)
    keep[5] = dot_t(d_gate, gate_w[...])
    add_cores(0)
    wait_bytes(mid.at[pl.ds(0, N_SAMPLE - 1)], recv_sem.at[3])
    split_lanes(mid[...].reshape(128, 512).astype(F32), mid_rows)
    for d in range(N_TILE):
        for part in range(4):
            x2[d, :, pl.ds(part * 128, 128)] = mid_rows[part, pl.ds(d, 8, stride=16), :]
    for d in tile_peers:
        send(x2.at[d], arrived.at[t], send_sem.at[4], recv_sem.at[4], d, s)
    arrived[t] = x2[t]
    add_cores(1)
    form_mine(2)
    wait_bytes(arrived.at[pl.ds(0, N_TILE - 1)], recv_sem.at[4])
    split_lanes(arrived[...].reshape(128, 512), arrived_rows)
    panel_of(arrived_rows, 0, 8, panel)
    d_panel = joined(panel).astype(BF16)
    x3[:, 0] = dot(d_panel, right[...]).astype(BF16).reshape(N_TILE, 16, 256)
    x3[:, 1] = t_dot(d_panel, left[...]).astype(BF16).reshape(N_TILE, 16, 256)
    for d in tile_peers:
        send(x3.at[d], back.at[t], send_sem.at[5], recv_sem.at[5], d, s)
    back[t] = x3[t]
    add_cores(2)
    wait_bytes(back.at[pl.ds(0, N_TILE - 1)], recv_sem.at[5])
    for side in range(2):
        split_lanes(back[:, side].reshape(256, 256).astype(F32), back_rows)

        def store(d, lanes, rows, side=side):
            x4[d, side, :, lanes] = rows.astype(BF16)

        blocks_of(back_rows, store)
    for d in sample_peers:
        send(x4.at[d], final.at[s], send_sem.at[6], recv_sem.at[6], t, d)
    final[s] = x4[s]
    add_first(0)
    wait_bytes(final.at[pl.ds(0, N_SAMPLE - 1)], recv_sem.at[6])
    d_normed_z = keep[5]
    for block in range(4):
        incoming = final[:, block // 2].reshape(128, 512).astype(F32)
        d_proj = (incoming * coefficient[block]).astype(BF16)
        small[:, pl.ds(block * 128, 128)] = dot(d_proj, normed_z).astype(BF16)
        d_normed_z = d_normed_z + t_dot(d_proj, in_w_t[pl.ds(block * 128, 128), :])
    for k in range(1, N_SAMPLE):
        d = sample_peers[k - 1]
        rows = pl.ds(pl.multiple_of(d * 16, 16), 16)
        send(small.at[rows], small_part.at[k - 1], send_sem.at[7], recv_sem.at[7], t, d)
    grad_pair[...] = keep[4] + norm_back_rows(keep[0], inverse_z, d_normed_z, 1)
    add_first(1)
    add_first(2)
    wait_bytes(small_part, recv_sem.at[7])
    own = pl.ds(pl.multiple_of(s * 16, 16), 16)
    total = small[own, :].astype(F32)
    for k in range(N_SAMPLE - 1):
        total = total + small_part[k].astype(F32)
    small_mid[...] = total.astype(BF16)
    for k in range(1, N_TILE):
        d = tile_peers[k - 1]
        lanes = pl.ds(pl.multiple_of(d * 128, 128), 128)
        send(small_mid.at[:, lanes], small_last.at[k - 1], send_sem.at[8], recv_sem.at[8], d, s)
    for g in range(3):
        add_second(g)
    wait_bytes(small_last, recv_sem.at[8])
    lanes = pl.ds(pl.multiple_of(t * 128, 128), 128)
    total = small_mid[:, lanes].astype(F32)
    for k in range(N_TILE - 1):
        total = total + small_last[k].astype(F32)
    small_sum[own, lanes] = total.astype(BF16)
    block = small_sum.at[own, lanes]
    for d in tile_peers:
        send(block, block, send_sem.at[9], recv_sem.at[9], d, s)
    for g in range(3):
        add_third(g)
    wait_bytes(small_last, recv_sem.at[9])
    block = small_sum.at[own]
    for d in sample_peers:
        send(block, block, send_sem.at[10], recv_sem.at[10], t, d)
    for g in range(3):
        gather_second(g)
    for g in range(3):
        gather_first(g)
        unpack(full, g, core)
    wait_bytes(small_part, recv_sem.at[10])
    for g in range(3):
        wait_bytes(other.at[g], w_recv.at[g, 6])
        unpack(other, g, 1 - core)

    wait_bytes(pair_sum, send_sem.at[0])
    wait_bytes(by_chip, send_sem.at[1])
    wait_bytes(by_sample, send_sem.at[2])
    wait_bytes(mid.at[pl.ds(0, N_SAMPLE - 1)], send_sem.at[3])
    wait_bytes(arrived.at[pl.ds(0, N_TILE - 1)], send_sem.at[4])
    wait_bytes(back.at[pl.ds(0, N_TILE - 1)], send_sem.at[5])
    wait_bytes(final.at[pl.ds(0, N_SAMPLE - 1)], send_sem.at[6])
    wait_bytes(small_part, send_sem.at[7])
    wait_bytes(small_last, send_sem.at[8])
    wait_bytes(small_last, send_sem.at[9])
    wait_bytes(small_part, send_sem.at[10])
    wait_bytes(theirs, w_send.at[0])
    wait_bytes(part1, w_send.at[1])
    wait_bytes(part2, w_send.at[2])
    wait_bytes(part3.at[:, pl.ds(0, 3)], w_send.at[3])
    wait_bytes(part2, w_send.at[4])
    wait_bytes(part1, w_send.at[5])
    wait_bytes(theirs, w_send.at[6])


def backward(collective_id, *operands):
    vmem = pl.BlockSpec(memory_space=pltpu.VMEM)
    chunk = (3, 4, ROWS, WIDTH)
    block = (4, 16, 128)
    return pl.pallas_call(
        backward_kernel,
        out_shape=[
            jax.ShapeDtypeStruct((512, 128), F32),
            jax.ShapeDtypeStruct((768, 3072), BF16),
            jax.ShapeDtypeStruct((768, 768), BF16),
            jax.ShapeDtypeStruct((128, SMALL), BF16),
        ],
        in_specs=[vmem] * len(operands),
        out_specs=[vmem] * 4,
        scratch_shapes=[
            pltpu.VMEM((N_CHIP, N_SAMPLE) + block, BF16),
            pltpu.VMEM((N_CHIP - 1, N_SAMPLE) + block, BF16),
            pltpu.VMEM((N_SAMPLE - 1,) + block, BF16),
            pltpu.VMEM(block, F32),
            pltpu.VMEM((4, 16, 128), F32),
            pltpu.VMEM((4, 128, 512), F32),
            pltpu.VMEM((6, 512, 128), F32),
            pltpu.VMEM((128, 512), F32),
            pltpu.VMEM((N_SAMPLE, 16, 512), BF16),
            pltpu.VMEM((N_SAMPLE, 16, 512), BF16),
            pltpu.VMEM((4, 128, 128), F32),
            pltpu.VMEM((N_TILE, 8, 512), F32),
            pltpu.VMEM((N_TILE, 8, 512), F32),
            pltpu.VMEM((4, 128, 128), F32),
            pltpu.VMEM((2, 256, 128), F32),
            pltpu.VMEM((N_TILE, 2, 16, 256), BF16),
            pltpu.VMEM((N_TILE, 2, 16, 256), BF16),
            pltpu.VMEM((2, 256, 128), F32),
            pltpu.VMEM((N_SAMPLE, 2, 16, 512), BF16),
            pltpu.VMEM((N_SAMPLE, 2, 16, 512), BF16),
            pltpu.VMEM((128, SMALL), BF16),
            pltpu.VMEM((N_SAMPLE - 1, 16, SMALL), BF16),
            pltpu.VMEM((16, SMALL), BF16),
            pltpu.VMEM((N_TILE - 1, 16, 128), BF16),
            pltpu.VMEM(chunk, BF16),
            pltpu.VMEM(chunk, BF16),
            pltpu.VMEM(chunk, BF16),
            pltpu.VMEM((3, 3, ROWS, WIDTH), BF16),
            pltpu.VMEM((3, ROWS, WIDTH), BF16),
            pltpu.VMEM((3, 3, 48, WIDTH), BF16),
            pltpu.VMEM((3, 48, WIDTH), BF16),
            pltpu.VMEM((3, 4, 48, WIDTH), BF16),
            pltpu.VMEM(chunk, BF16),
            pltpu.VMEM(chunk, BF16),
            pltpu.SemaphoreType.DMA((11,)),
            pltpu.SemaphoreType.DMA((11,)),
            pltpu.SemaphoreType.DMA((15,)),
            pltpu.SemaphoreType.DMA((7,)),
            pltpu.SemaphoreType.DMA((3, 7)),
        ],
        compiler_params=pltpu.CompilerParams(
            collective_id=collective_id, has_side_effects=True, vmem_limit_bytes=56 << 20
        ),
    )(*operands)


def norm_parts(values, axis):
    centered = values - jnp.mean(values, axis=axis, keepdims=True)
    inverse = lax.rsqrt(jnp.mean(centered * centered, axis=axis, keepdims=True) + EPSILON)
    return (centered * inverse, inverse)


def norm_back(normed, inverse, incoming_gradient, axis):
    first_mean = jnp.mean(incoming_gradient, axis=axis, keepdims=True)
    second_mean = jnp.mean(incoming_gradient * normed, axis=axis, keepdims=True)
    return (incoming_gradient - first_mean - normed * second_mean) * inverse


def silu_slope(values):
    sigmoid_part = jax.nn.sigmoid(values)
    return sigmoid_part * (1.0 + values * (1.0 - sigmoid_part))


def shards(
    pair,
    pair_mask,
    tri_in_w,
    tri_gate_w,
    tri_out_w,
    bias_w,
    atom_feats,
    atom_to_token,
    atom_w,
    tokens,
    attention_input_weight,
    attention_output_weight,
    cot_pair,
    token_output_cotangent,
):
    hidden = tri_in_w.shape[1] // 4
    token_width = attention_input_weight.shape[0]
    head_count = bias_w.shape[1]
    total_tokens = tokens.shape[1]
    pair_rows = pair.reshape(-1, hidden)
    mask_row = pair_mask.astype(F32).reshape(1, -1)
    in_w_t, bias_w_t = tri_in_w.T, bias_w.T
    following, bias_all, left_panel, right_panel, product, every_feat, every_atom = pair_forward(
        pair_rows,
        mask_row,
        in_w_t,
        tri_gate_w,
        tri_out_w,
        bias_w_t,
        atom_feats,
        atom_to_token[None],
        0,
    )
    every_feat = every_feat.reshape(-1, atom_feats.shape[1])
    every_atom = every_atom.reshape(-1)
    atom_pre = jnp.dot(every_feat, atom_w, preferred_element_type=jnp.float32)
    atom_act = jax.nn.silu(atom_pre).astype(BF16)
    token_ids = jnp.arange(total_tokens, dtype=jnp.int32)
    one_hot = (token_ids[:, None] == every_atom[None, :]).astype(BF16)
    token_sums = jnp.dot(one_hot, atom_act, preferred_element_type=F32)
    token_counts = jnp.sum(one_hot.astype(F32), axis=1)
    token_cond = token_sums / token_counts[:, None]
    token_state_rows = tokens.astype(jnp.float32) + token_cond[None]
    normed_h, inverse_h = norm_parts(token_state_rows, 2)
    normalized_hidden_bfloat = normed_h.astype(jnp.bfloat16)
    hidden_t = normalized_hidden_bfloat.reshape(-1, token_width).T
    cot_rows = token_output_cotangent.reshape(-1, token_width)

    def project(block):
        weight = attention_input_weight[:, block * token_width : (block + 1) * token_width]
        return t_dot(weight, hidden_t)

    gated_t, d_every_t, bias_blocks = attention(
        project(0).astype(BF16),
        project(2).astype(BF16),
        project(3).astype(BF16),
        jax.nn.sigmoid(project(1)),
        dot_t(attention_output_weight, cot_rows),
        bias_all,
    )
    d_every_t = d_every_t.reshape(4 * token_width, -1)
    token_output_rows = token_state_rows + t_dot(gated_t, attention_output_weight).reshape(
        token_state_rows.shape
    )
    normalized_hidden_gradient = lax.dot_general(
        d_every_t, attention_input_weight, (((0,), (1,)), ((), ())), preferred_element_type=F32
    ).reshape(token_state_rows.shape)
    grad_tokens = token_output_cotangent.astype(jnp.float32) + norm_back(
        normed_h, inverse_h, normalized_hidden_gradient, 2
    )
    cond_grad = (jnp.sum(grad_tokens, axis=0) / token_counts[:, None]).astype(BF16)
    d_act = lax.dot_general(
        one_hot, cond_grad, (((0,), (0,)), ((), ())), preferred_element_type=F32
    ) * silu_slope(atom_pre)
    grad_atom_w = lax.dot_general(
        every_feat, d_act.astype(BF16), (((0,), (0,)), ((), ())), preferred_element_type=F32
    )
    grad_pair, in_sum, out_sum, small_sum = backward(
        1,
        bias_blocks,
        pair_rows,
        mask_row,
        in_w_t,
        tri_gate_w,
        tri_out_w,
        bias_w_t,
        following,
        product,
        left_panel,
        right_panel,
        cot_pair.reshape(-1, hidden),
        grad_atom_w.astype(BF16),
        hidden_t,
        d_every_t,
        gated_t,
        cot_rows,
    )
    small_sum = small_sum.astype(F32)
    at = 4 * hidden
    summed = (
        small_sum[:, :at].reshape(hidden, 4, hidden).transpose(2, 1, 0).reshape(hidden, at),
        small_sum[:, at : at + hidden],
        small_sum[:, at + hidden : at + 2 * hidden],
        small_sum[:head_count, at + 2 * hidden + token_width :][:, :hidden].T,
        small_sum[:, at + 2 * hidden : at + 2 * hidden + token_width],
        in_sum.astype(F32),
        out_sum.astype(F32),
    )
    pair_next, grad_pair = following.reshape(pair.shape), grad_pair.reshape(pair.shape)
    return (pair_next, token_output_rows, grad_pair, grad_tokens) + summed


def solution(mesh):
    in_specs = (
        P("tile", "sample", None),
        P("tile", "sample"),
        P(),
        P(),
        P(),
        P(),
        P("tile", None),
        P("tile"),
        P(),
        P(("tile", "sample"), None, None),
        P(),
        P(),
        P("tile", "sample", None),
        P(("tile", "sample"), None, None),
    )
    out_specs = (
        P("tile", "sample", None),
        P(("tile", "sample"), None, None),
        P("tile", "sample", None),
        P(("tile", "sample"), None, None),
        P(),
        P(),
        P(),
        P(),
        P(),
        P(),
        P(),
    )
    return jax.shard_map(shards, mesh=mesh, in_specs=in_specs, out_specs=out_specs, check_vma=False)
```

```python
import functools
import math

import jax
import jax.numpy as jnp
from jax import lax
from jax.experimental import pallas as pl
from jax.experimental.pallas import tpu as pltpu
from jax.sharding import PartitionSpec as P

EPSILON = 1e-05
N_TILE = 16
N_SAMPLE = 8
N_CHIP = 8
MESH = pl.DeviceIdType.MESH
BF16 = jnp.bfloat16
F32 = jnp.float32
HIGHEST = lax.Precision.HIGHEST


def wait_bytes(ref, sem):
    pltpu.make_async_copy(ref, ref, sem).wait()


def send(src, dst, send_sem, recv_sem, t, s):
    pltpu.make_async_remote_copy(
        src, dst, send_sem, recv_sem, device_id=(t, s), device_id_type=MESH
    ).start()


def dot(a, b):
    return jnp.dot(a, b, preferred_element_type=F32)


def dot_t(a, b):
    return lax.dot_general(a, b, (((1,), (1,)), ((), ())), preferred_element_type=F32)


def t_dot(a, b):
    return lax.dot_general(a, b, (((0,), (0,)), ((), ())), preferred_element_type=F32)


HEAD = 48
GROUP = 4
LANES = 32


def place_lanes(parts, first):
    group_of = lax.broadcasted_iota(jnp.int32, parts[0].shape, 1) // LANES
    result = None
    for i in range(4):
        shift = (i - first) % 4 * LANES
        moved = pltpu.roll(parts[i], shift, 1) if shift else parts[i]
        result = moved if result is None else jnp.where(group_of == i, moved, result)
    return result


def panel_of(arrived, first, step, panel):
    for part in range(4):
        rows = [
            arrived[part, pl.ds(first + s * (step // 8), 16, stride=step), :] for s in range(8)
        ]
        for i in range(4):
            for half in range(2):
                panel[half, pl.ds(part * 4 + i, 16, stride=16), :] = place_lanes(
                    rows[half * 4 : half * 4 + 4], i
                )


def blocks_of(panel, store):
    for half in range(2):
        for part in range(4):
            rows = [panel[half, pl.ds(part * 4 + i, 16, stride=16), :] for i in range(4)]
            for q in range(4):
                store(half * 4 + q, pl.ds(part * 128, 128), place_lanes(rows, q))


def split_lanes(values, ref):
    for part in range(ref.shape[0]):
        ref[part] = values[:, part * 128 : part * 128 + 128]


def joined(ref):
    return jnp.concatenate([ref[0], ref[1]], axis=1)


def norm_rows(values, axis):
    centered = values - jnp.mean(values, axis=axis, keepdims=True)
    inverse = lax.rsqrt(jnp.mean(centered * centered, axis=axis, keepdims=True) + EPSILON)
    return centered * inverse, inverse


def sigmoid(values):
    return 1.0 / (1.0 + jnp.exp(-values))


def pair_forward_kernel(
    pair,
    mask,
    in_w_t,
    gate_w,
    out_w,
    bias_w_t,
    feats,
    atoms,
    pair_next,
    bias,
    left,
    right,
    product,
    every_feat,
    every_atom,
    x1,
    mid,
    mid_rows,
    x2,
    arrived,
    arrived_rows,
    panel,
    x3,
    back,
    back_rows,
    x4,
    packed,
    mine,
    send_sem,
    recv_sem,
):
    t, s = lax.axis_index("tile"), lax.axis_index("sample")
    m, c = t // 2, lax.rem(t, 2)
    barrier = pltpu.get_barrier_semaphore()
    tile_peers = [lax.rem(t + k, N_TILE) for k in range(1, N_TILE)]
    sample_peers = [lax.rem(s + k, N_SAMPLE) for k in range(1, N_SAMPLE)]
    for d in sample_peers:
        pl.semaphore_signal(barrier, inc=1, device_id=(t, d), device_id_type=MESH)
    for d in tile_peers:
        pl.semaphore_signal(barrier, inc=1, device_id=(d, s), device_id_type=MESH)

    normed_z = norm_rows(pair[...].astype(F32), 1)[0].astype(BF16)

    def project(block):
        return dot_t(in_w_t[pl.ds(block * 128, 128), :], normed_z)

    for side in range(2):
        value = (sigmoid(project(2 * side)) * project(2 * side + 1) * mask[...]).astype(BF16)
        for d in range(N_SAMPLE):
            x1[d, side] = value[d * 16 : d * 16 + 16]
    pl.semaphore_wait(barrier, N_SAMPLE + N_TILE - 2)
    for d in sample_peers:
        send(x1.at[d], mid.at[s], send_sem.at[0], recv_sem.at[0], t, d)
    for d in tile_peers:
        send(feats, every_feat.at[t], send_sem.at[1], recv_sem.at[1], d, s)
        send(atoms, every_atom.at[t], send_sem.at[2], recv_sem.at[2], d, s)
    every_feat[t] = feats[...]
    every_atom[t] = atoms[...]
    mid[s] = x1[s]
    tri_gate = sigmoid(dot(normed_z, gate_w[...]))
    wait_bytes(mid.at[pl.ds(0, N_SAMPLE - 1)], recv_sem.at[0])
    split_lanes(mid[...].reshape(256, 512).astype(F32), mid_rows)
    for d in range(N_TILE):
        for part in range(4):
            x2[d, :, pl.ds(part * 128, 128)] = mid_rows[part, pl.ds(d, 16, stride=16), :].astype(
                BF16
            )
    for d in tile_peers:
        send(x2.at[d], arrived.at[t], send_sem.at[3], recv_sem.at[3], d, s)
    arrived[t] = x2[t]
    wait_bytes(arrived.at[pl.ds(0, N_TILE - 1)], recv_sem.at[3])
    split_lanes(arrived[...].reshape(256, 512).astype(F32), arrived_rows)
    panel_of(arrived_rows, 0, 16, panel)
    left[...] = joined(panel).astype(BF16)
    panel_of(arrived_rows, 1, 16, panel)
    right[...] = joined(panel).astype(BF16)
    x3[...] = dot_t(left[...], right[...]).astype(BF16).reshape(N_TILE, 16, 256)
    for d in tile_peers:
        send(x3.at[d], back.at[t], send_sem.at[4], recv_sem.at[4], d, s)
    back[t] = x3[t]
    wait_bytes(back.at[pl.ds(0, N_TILE - 1)], recv_sem.at[4])
    split_lanes(back[...].reshape(256, 256).astype(F32), back_rows)

    def store(d, lanes, rows):
        x4[d, :, lanes] = rows.astype(BF16)

    blocks_of(back_rows, store)
    for d in sample_peers:
        send(x4.at[d], product.at[s], send_sem.at[5], recv_sem.at[5], t, d)
    product[s] = x4[s]
    wait_bytes(product.at[pl.ds(0, N_SAMPLE - 1)], recv_sem.at[5])
    normed_p = norm_rows(product[...].reshape(128, 512).astype(F32), 0)[0].astype(BF16)
    linear = t_dot(normed_p, out_w[...])
    following = pair[...].astype(F32) + tri_gate * linear
    pair_next[...] = following
    normed_n = norm_rows(following, 1)[0].astype(BF16)
    head_rows = dot_t(bias_w_t[...], normed_n)
    split_lanes(head_rows, packed)
    for part in range(4):
        rows = [packed[part, pl.ds(h, 4, stride=4), :] for h in range(4)]
        for i in range(4):
            mine[:, part * 4 + i] = place_lanes(rows, i)
    bias[m, c, s] = mine[...].astype(BF16)

    own = bias.at[m, c, s]
    for d in sample_peers:
        send(own, own, send_sem.at[6], recv_sem.at[6], t, d)
    wait_bytes(bias.at[m, c, pl.ds(0, N_SAMPLE - 1)], recv_sem.at[6])
    block = bias.at[m, c]
    other = m * 2 + 1 - c
    for k in range(1, N_CHIP):
        send(block, block, send_sem.at[7], recv_sem.at[7 + k], lax.rem(m + k, N_CHIP) * 2 + c, s)
    send(block, block, send_sem.at[8], recv_sem.at[7], other, s)
    for k in range(1, N_CHIP):
        came = bias.at[lax.rem(m + N_CHIP - k, N_CHIP), c]
        wait_bytes(came, recv_sem.at[7 + k])
        send(came, came, send_sem.at[8], recv_sem.at[7], other, s)
    wait_bytes(bias.at[:, 0], recv_sem.at[7])
    wait_bytes(every_feat.at[pl.ds(0, N_TILE - 1)], recv_sem.at[1])
    wait_bytes(every_atom.at[pl.ds(0, N_TILE - 1)], recv_sem.at[2])
    wait_bytes(mid.at[pl.ds(0, N_SAMPLE - 1)], send_sem.at[0])
    wait_bytes(every_feat.at[pl.ds(0, N_TILE - 1)], send_sem.at[1])
    wait_bytes(every_atom.at[pl.ds(0, N_TILE - 1)], send_sem.at[2])
    wait_bytes(arrived.at[pl.ds(0, N_TILE - 1)], send_sem.at[3])
    wait_bytes(back.at[pl.ds(0, N_TILE - 1)], send_sem.at[4])
    wait_bytes(product.at[pl.ds(0, N_SAMPLE - 1)], send_sem.at[5])
    wait_bytes(bias.at[m, c, pl.ds(0, N_SAMPLE - 1)], send_sem.at[6])
    wait_bytes(bias.at[pl.ds(0, N_CHIP - 1), 0], send_sem.at[7])
    wait_bytes(bias.at[:, 0], send_sem.at[8])


def pair_forward(pair, mask, in_w_t, gate_w, out_w, bias_w_t, feats, atoms, collective_id):
    vmem = pl.BlockSpec(memory_space=pltpu.VMEM)
    return pl.pallas_call(
        pair_forward_kernel,
        out_shape=[
            jax.ShapeDtypeStruct(pair.shape, F32),
            jax.ShapeDtypeStruct((N_CHIP, 2, N_SAMPLE, 4, 16, 128), BF16),
            jax.ShapeDtypeStruct((256, 256), BF16),
            jax.ShapeDtypeStruct((256, 256), BF16),
            jax.ShapeDtypeStruct((N_SAMPLE, 16, 512), BF16),
            jax.ShapeDtypeStruct((N_TILE,) + feats.shape, feats.dtype),
            jax.ShapeDtypeStruct((N_TILE,) + atoms.shape, atoms.dtype),
        ],
        in_specs=[vmem] * 8,
        out_specs=[vmem] * 7,
        scratch_shapes=[
            pltpu.VMEM((N_SAMPLE, 2, 16, 512), BF16),
            pltpu.VMEM((N_SAMPLE, 2, 16, 512), BF16),
            pltpu.VMEM((4, 256, 128), F32),
            pltpu.VMEM((N_TILE, 16, 512), BF16),
            pltpu.VMEM((N_TILE, 16, 512), BF16),
            pltpu.VMEM((4, 256, 128), F32),
            pltpu.VMEM((2, 256, 128), F32),
            pltpu.VMEM((N_TILE, 16, 256), BF16),
            pltpu.VMEM((N_TILE, 16, 256), BF16),
            pltpu.VMEM((2, 256, 128), F32),
            pltpu.VMEM((N_SAMPLE, 16, 512), BF16),
            pltpu.VMEM((4, 16, 128), F32),
            pltpu.VMEM((4, 16, 128), F32),
            pltpu.SemaphoreType.DMA((9,)),
            pltpu.SemaphoreType.DMA((15,)),
        ],
        compiler_params=pltpu.CompilerParams(
            collective_id=collective_id, has_side_effects=True, vmem_limit_bytes=40 << 20
        ),
    )(pair, mask, in_w_t, gate_w, out_w, bias_w_t, feats, atoms)


def attention_kernel(q, k, v, gate, up, bias, gated, d_every, d_bias, bias_rows, bias_total):
    tokens = bias_rows.shape[1]
    scale = 1.0 / math.sqrt(HEAD)
    group_of = lax.broadcasted_iota(jnp.int32, (tokens, 128), 1) // LANES

    for half in range(2):
        parts = [
            bias[:, :, half * 4 + i, 0].reshape(tokens, 128).astype(F32) for i in range(4)
        ]
        for h in range(GROUP):
            row = parts[0] if h == 0 else pltpu.roll(parts[0], (-h) % 4 * LANES, 1)
            for i in range(1, 4):
                shift = (i - h) % 4 * LANES
                moved = pltpu.roll(parts[i], shift, 1) if shift else parts[i]
                row = jnp.where(group_of == i, moved, row)
            bias_rows[h, :, pl.ds(half * 128, 128)] = row

    @pl.loop(0, GROUP)
    def _(h):
        rows = pl.ds(pl.multiple_of(h * HEAD, 16), HEAD)
        for sample in range(2):
            columns = pl.ds(sample * tokens, tokens)
            qh, kh, vh = q[rows, columns], k[rows, columns], v[rows, columns]
            scores = t_dot(qh, kh) * scale + bias_rows[h]
            weights = jnp.exp(scores - jnp.max(scores, axis=1, keepdims=True))
            probs = weights * (1.0 / jnp.sum(weights, axis=1, keepdims=True))
            probs_b = probs.astype(BF16)
            attended = dot_t(vh, probs_b)
            gate_h, up_h = gate[rows, columns], up[rows, columns]
            gated[rows, columns] = (gate_h * attended).astype(BF16)
            d_att = (up_h * gate_h).astype(BF16)
            d_every[1, rows, columns] = (up_h * attended * gate_h * (1.0 - gate_h)).astype(BF16)
            d_probs = t_dot(d_att, vh)
            inner = jnp.sum(probs * d_probs, axis=1, keepdims=True)
            d_scores = probs * (d_probs - inner)
            d_scores_b = d_scores.astype(BF16)
            d_every[0, rows, columns] = (dot_t(kh, d_scores_b) * scale).astype(BF16)
            d_every[2, rows, columns] = (dot(qh, d_scores_b) * scale).astype(BF16)
            d_every[3, rows, columns] = dot(d_att, probs_b).astype(BF16)
            if sample == 0:
                bias_total[h] = d_scores
            else:
                bias_total[h] = bias_total[h] + d_scores

    for half in range(2):
        parts = [bias_total[h, :, pl.ds(half * 128, 128)] for h in range(GROUP)]
        for i in range(4):
            row = parts[0] if i == 0 else pltpu.roll(parts[0], (-i) % 4 * LANES, 1)
            for h in range(1, GROUP):
                shift = (h - i) % 4 * LANES
                moved = pltpu.roll(parts[h], shift, 1) if shift else parts[h]
                row = jnp.where(group_of == h, moved, row)
            d_bias[:, :, half * 4 + i, 0] = row.astype(BF16).reshape(N_CHIP, 2, 16, 128)


def attention(q, k, v, gate, up, bias):
    width, columns = q.shape
    tokens = columns // 2
    block = GROUP * HEAD
    feature = pl.BlockSpec((block, columns), lambda i: (i, 0))
    of_bias = pl.BlockSpec((N_CHIP, 2, N_SAMPLE, 1, 16, 128), lambda i: (0, 0, 0, i, 0, 0))
    return pl.pallas_call(
        attention_kernel,
        grid=(width // block,),
        in_specs=[feature] * 5 + [of_bias],
        out_specs=[feature, pl.BlockSpec((4, block, columns), lambda i: (0, i, 0)), of_bias],
        out_shape=[
            jax.ShapeDtypeStruct((width, columns), BF16),
            jax.ShapeDtypeStruct((4, width, columns), BF16),
            jax.ShapeDtypeStruct(bias.shape, BF16),
        ],
        scratch_shapes=[
            pltpu.VMEM((GROUP, tokens, tokens), F32),
            pltpu.VMEM((GROUP, tokens, tokens), F32),
        ],
        compiler_params=pltpu.CompilerParams(vmem_limit_bytes=40 << 20),
    )(q, k, v, gate, up, bias)


ROWS = 192
WIDTH = 640
SMALL = 1152


def norm_back_rows(normed, inverse, incoming, axis):
    first = jnp.mean(incoming, axis=axis, keepdims=True)
    second = jnp.mean(incoming * normed, axis=axis, keepdims=True)
    return (incoming - first - normed * second) * inverse


def backward_kernel(
    d_bias,
    pair,
    mask,
    in_w_t,
    gate_w,
    out_w,
    bias_w_t,
    following,
    product,
    left,
    right,
    cot_pair,
    left_in,
    right_in,
    left_out,
    right_out,
    in_w,
    inverse_h,
    counts,
    feats,
    atoms,
    atom_w,
    grad_pair,
    grad_tokens,
    in_sum,
    out_sum,
    small_sum,
    tri_sum,
    pair_sum,
    by_chip,
    by_sample,
    bias_block,
    head_rows,
    coefficient,
    keep,
    keep_p,
    x1,
    mid,
    mid_rows,
    x2,
    arrived,
    arrived_rows,
    panel,
    x3,
    back,
    back_rows,
    x4,
    final,
    small,
    small_part,
    small_mid,
    small_last,
    tri,
    tri_part,
    tri_all,
    theirs,
    mine,
    from_core,
    part1,
    sum1,
    part2,
    sum2,
    part3,
    full,
    other,
    d_hidden,
    cond_grad,
    atom_grad,
    send_sem,
    recv_sem,
    chip_sem,
    w_send,
    w_recv,
):
    t, s = lax.axis_index("tile"), lax.axis_index("sample")
    m, core = t // 2, lax.rem(t, 2)
    partner_t = m * 2 + 1 - core
    place = [lax.rem(s, 2) * 2 + t // 8, lax.rem(t // 2, 4), s // 2]
    tile_peers = [lax.rem(t + k, N_TILE) for k in range(1, N_TILE)]
    sample_peers = [lax.rem(s + k, N_SAMPLE) for k in range(1, N_SAMPLE)]

    def peer(axis, k):
        where = list(place)
        where[axis] = lax.rem(place[axis] + k, 4)
        x, y, z = where
        return where[axis], (lax.rem(x, 2) * 8 + y * 2 + core, z * 2 + x // 2)

    barrier = pltpu.get_barrier_semaphore()
    for d in sample_peers:
        pl.semaphore_signal(barrier, inc=1, device_id=(t, d), device_id_type=MESH)
    for d in tile_peers:
        pl.semaphore_signal(barrier, inc=1, device_id=(d, s), device_id_type=MESH)
    diagonal = (lax.rem(t + 8, N_TILE), s + 1 - 2 * lax.rem(s, 2))
    pl.semaphore_signal(barrier, inc=1, device_id=diagonal, device_id_type=MESH)

    def form(g, c, target):
        wide = pl.ds(pl.multiple_of(g * 1024 + c * 512, 512), 512)
        narrow = pl.ds(pl.multiple_of(g * 256 + c * 128, 128), 128)

        @pl.loop(0, 4)
        def _(a):
            rows = pl.ds(pl.multiple_of(a * ROWS, 64), ROWS)
            target[g, a, :, pl.ds(0, 512)] = dot_t(left_in[rows, :], right_in[wide, :]).astype(BF16)
            target[g, a, :, pl.ds(512, 128)] = dot(left_out[rows, :], right_out[:, narrow]).astype(
                BF16
            )

    def form_theirs(g):
        form(g, 1 - core, theirs)
        send(theirs.at[g], from_core.at[g], w_send.at[0], w_recv.at[g, 0], partner_t, s)

    def form_mine(g):
        form(g, core, mine)

    def add_cores(g):
        wait_bytes(from_core.at[g], w_recv.at[g, 0])

        @pl.loop(0, 4)
        def _(a):
            @pl.loop(0, ROWS // 16)
            def _(r):
                rows = pl.ds(pl.multiple_of(r * 16, 16), 16)
                total = mine[g, a, rows, :].astype(F32) + from_core[g, a, rows, :].astype(F32)
                mine[g, a, rows, :] = total.astype(BF16)

        for k in range(1, 4):
            d, to = peer(g, k)
            send(mine.at[g, d], part1.at[g, k - 1], w_send.at[1], w_recv.at[g, 1], *to)

    def add_first(g):
        p1 = place[g]
        wait_bytes(part1.at[g], w_recv.at[g, 1])

        @pl.loop(0, ROWS // 16)
        def _(r):
            rows = pl.ds(pl.multiple_of(r * 16, 16), 16)
            total = mine[g, p1, rows, :].astype(F32)
            for k in range(3):
                total = total + part1[g, k, rows, :].astype(F32)
            sum1[g, rows, :] = total.astype(BF16)

        for k in range(1, 4):
            d, to = peer((g + 1) % 3, k)
            rows = pl.ds(pl.multiple_of(d * 48, 16), 48)
            send(sum1.at[g, rows], part2.at[g, k - 1], w_send.at[2], w_recv.at[g, 2], *to)

    def add_second(g):
        p2, p3 = place[(g + 1) % 3], place[(g + 2) % 3]
        wait_bytes(part2.at[g], w_recv.at[g, 2])
        total = sum1[g, pl.ds(pl.multiple_of(p2 * 48, 16), 48), :].astype(F32)
        for k in range(3):
            total = total + part2[g, k].astype(F32)
        sum2[g] = total.astype(BF16)
        for k in range(1, 4):
            _, to = peer((g + 2) % 3, k)
            send(sum2.at[g], part3.at[g, p3], w_send.at[3], w_recv.at[g, 3], *to)
        part3[g, p3] = sum2[g]

    def add_third(g):
        p1, p2 = place[g], place[(g + 1) % 3]
        wait_bytes(part3.at[g, pl.ds(0, 3)], w_recv.at[g, 3])
        total = part3[g, 0].astype(F32)
        for k in range(1, 4):
            total = total + part3[g, k].astype(F32)
        rows = pl.ds(pl.multiple_of(p2 * 48, 16), 48)
        full[g, p1, rows, :] = total.astype(BF16)
        block = full.at[g, p1, rows]
        for k in range(1, 4):
            _, to = peer((g + 1) % 3, k)
            send(block, block, w_send.at[4], w_recv.at[g, 4], *to)

    def gather_second(g):
        p1 = place[g]
        wait_bytes(full.at[g, p1, pl.ds(0, 144)], w_recv.at[g, 4])
        block = full.at[g, p1]
        for k in range(1, 4):
            _, to = peer(g, k)
            send(block, block, w_send.at[5], w_recv.at[g, 5], *to)
        send(block, other.at[g, p1], w_send.at[6], w_recv.at[g, 6], partner_t, s)

    def unpack(source, g, c):
        wide = pl.ds(pl.multiple_of(g * 1024 + c * 512, 512), 512)
        narrow = pl.ds(pl.multiple_of(g * 256 + c * 128, 128), 128)

        @pl.loop(0, 4)
        def _(a):
            @pl.loop(0, ROWS // 16)
            def _(r):
                rows = pl.ds(pl.multiple_of(r * 16, 16), 16)
                to_rows = pl.ds(pl.multiple_of(a * ROWS + r * 16, 16), 16)
                in_sum[to_rows, wide] = source[g, a, rows, pl.ds(0, 512)]
                out_sum[to_rows, narrow] = source[g, a, rows, pl.ds(512, 128)]

    def gather_first(g):
        wait_bytes(full.at[g, pl.ds(0, 3)], w_recv.at[g, 5])
        for k in range(1, 4):
            p1 = lax.rem(place[g] + k, 4)
            send(full.at[g, p1], other.at[g, p1], w_send.at[6], w_recv.at[g, 6], partner_t, s)

    def token_product():
        @pl.loop(0, 2)
        def _(a):
            rows = pl.ds(pl.multiple_of(a * 384, 128), 384)
            d_hidden[rows, :] = dot(in_w[rows, :], right_in[...])

    def token_norm():
        @pl.loop(0, 4)
        def _(a):
            lanes = pl.ds(pl.multiple_of(a * 128, 128), 128)
            back_t = norm_back_rows(
                left_in[:, lanes].astype(F32), inverse_h[:, lanes], d_hidden[:, lanes], 0
            )
            grad_tokens[lanes, :] = right_out[lanes, :].astype(F32) + back_t.T

        both = grad_tokens[pl.ds(0, 256), :] + grad_tokens[pl.ds(256, 256), :]
        cond_grad[...] = (both / counts[...]).astype(BF16)

    def atom_sums():
        atom_grad[...] = jnp.zeros_like(atom_grad)

        @pl.loop(0, atoms.shape[0])
        def _(a):
            feat = feats[a]
            pre = dot(feat, atom_w[...])
            part = sigmoid(pre)
            token = lax.broadcasted_iota(jnp.int32, (256, atoms.shape[2]), 0)
            one_hot = jnp.where(token == atoms[a], 1.0, 0.0).astype(BF16)
            d_act = t_dot(one_hot, cond_grad[...]) * (part * (1.0 + pre * (1.0 - part)))
            atom_grad[...] += t_dot(feat, d_act.astype(BF16))

        small[:, pl.ds(0, 768)] = atom_grad[...].astype(BF16)

    token_product()
    pl.semaphore_wait(barrier, N_SAMPLE + N_TILE - 1)
    for k in range(1, N_CHIP + 1):
        d = lax.rem(m + k, N_CHIP)
        send(d_bias.at[d, 1 - core], pair_sum.at[d], send_sem.at[0], chip_sem.at[k - 1], partner_t, s)
    form_theirs(0)

    keep[0], inverse_z = norm_rows(pair[...].astype(F32), 1)
    normed_z = keep[0].astype(BF16)

    def project(block):
        return dot_t(in_w_t[pl.ds(block * 128, 128), :], normed_z)

    for side in range(2):
        gate_side = sigmoid(project(2 * side))
        masked = gate_side * mask[...]
        coefficient[2 * side] = masked * (1.0 - gate_side) * project(2 * side + 1)
        coefficient[2 * side + 1] = masked
    for k in range(1, N_CHIP + 1):
        d = lax.rem(m + k, N_CHIP)
        wait_bytes(pair_sum.at[d], chip_sem.at[k - 1])
        pair_sum[d] = (pair_sum[d].astype(F32) + d_bias[d, core].astype(F32)).astype(BF16)
        if k < N_CHIP:
            send(
                pair_sum.at[d],
                by_chip.at[k - 1],
                send_sem.at[1],
                chip_sem.at[N_CHIP + k - 1],
                d * 2 + core,
                s,
            )
    form_theirs(1)
    form_theirs(2)
    keep[1] = sigmoid(dot(normed_z, gate_w[...]))
    keep_p[...], inverse_p = norm_rows(product[...].reshape(128, 512).astype(F32), 0)
    normed_p = keep_p[...].astype(BF16)
    keep[2] = t_dot(normed_p, out_w[...])
    keep[3], inverse_n = norm_rows(following[...], 1)
    normed_n = keep[3].astype(BF16)
    small[...] = jnp.zeros((128, SMALL), BF16)
    small_mid[...] = jnp.zeros((16, N_TILE * 128), BF16)
    form_mine(0)
    form_mine(1)
    total = pair_sum[m].astype(F32)
    for k in range(1, N_CHIP):
        wait_bytes(by_chip.at[k - 1], chip_sem.at[N_CHIP + k - 1])
        total = total + by_chip[k - 1].astype(F32)
    pair_sum[m] = total.astype(BF16)
    for k in range(1, N_SAMPLE):
        send(
            pair_sum.at[m, sample_peers[k - 1]],
            by_sample.at[k - 1],
            send_sem.at[2],
            recv_sem.at[2],
            t,
            sample_peers[k - 1],
        )
    add_cores(0)
    form_mine(2)
    add_cores(1)
    wait_bytes(by_sample, recv_sem.at[2])
    bias_block[...] = pair_sum[m, s].astype(F32) + jnp.sum(by_sample[...].astype(F32), axis=0)

    for part in range(4):
        rows = [bias_block[:, part * 4 + i] for i in range(4)]
        for h in range(4):
            head_rows[part, pl.ds(h, 4, stride=4), :] = place_lanes(rows, h)
    d_heads = jnp.concatenate([head_rows[part] for part in range(4)], axis=1)
    high = d_heads.astype(BF16)
    low = (d_heads - high.astype(F32)).astype(BF16)
    d_normed_n = t_dot(high, bias_w_t[...]) + t_dot(low, bias_w_t[...])
    d_next = cot_pair[...].astype(F32) + norm_back_rows(keep[3], inverse_n, d_normed_n, 1)
    tri_gate = keep[1]
    d_linear = (d_next * tri_gate).astype(BF16)
    d_product = norm_back_rows(keep_p[...], inverse_p, dot_t(out_w[...], d_linear), 0).astype(BF16)
    for d in range(N_SAMPLE):
        x1[d] = d_product[d * 16 : d * 16 + 16]
    for d in sample_peers:
        send(x1.at[d], mid.at[s], send_sem.at[3], recv_sem.at[3], t, d)
    mid[s] = x1[s]
    d_gate = (d_next * keep[2] * tri_gate * (1.0 - tri_gate)).astype(BF16)
    keep[4] = d_next
    small[:, pl.ds(768, 128)] = t_dot(normed_z, d_gate).astype(BF16)
    small[:, pl.ds(896, 128)] = dot(normed_p, d_linear).astype(BF16)
    small[pl.ds(0, 16), pl.ds(1024, 128)] = (dot(high, normed_n) + dot(low, normed_n)).astype(BF16)
    keep[5] = dot_t(d_gate, gate_w[...])
    add_cores(2)
    token_norm()
    wait_bytes(mid.at[pl.ds(0, N_SAMPLE - 1)], recv_sem.at[3])
    split_lanes(mid[...].reshape(128, 512).astype(F32), mid_rows)
    for d in range(N_TILE):
        for part in range(4):
            x2[d, :, pl.ds(part * 128, 128)] = mid_rows[part, pl.ds(d, 8, stride=16), :]
    for d in tile_peers:
        send(x2.at[d], arrived.at[t], send_sem.at[4], recv_sem.at[4], d, s)
    arrived[t] = x2[t]
    atom_sums()
    wait_bytes(arrived.at[pl.ds(0, N_TILE - 1)], recv_sem.at[4])
    split_lanes(arrived[...].reshape(128, 512), arrived_rows)
    panel_of(arrived_rows, 0, 8, panel)
    d_panel = joined(panel).astype(BF16)
    x3[:, 0] = dot(d_panel, right[...]).astype(BF16).reshape(N_TILE, 16, 256)
    x3[:, 1] = t_dot(d_panel, left[...]).astype(BF16).reshape(N_TILE, 16, 256)
    for d in tile_peers:
        send(x3.at[d], back.at[t], send_sem.at[5], recv_sem.at[5], d, s)
    back[t] = x3[t]
    for k in range(1, N_SAMPLE):
        d = sample_peers[k - 1]
        rows = pl.ds(pl.multiple_of(d * 16, 16), 16)
        send(small.at[rows], small_part.at[k - 1], send_sem.at[7], recv_sem.at[7], t, d)
    own = pl.ds(pl.multiple_of(s * 16, 16), 16)
    add_first(0)
    add_first(1)
    wait_bytes(back.at[pl.ds(0, N_TILE - 1)], recv_sem.at[5])
    for side in range(2):
        split_lanes(back[:, side].reshape(256, 256).astype(F32), back_rows)

        def store(d, lanes, rows, side=side):
            x4[d, side, :, lanes] = rows.astype(BF16)

        blocks_of(back_rows, store)
    for d in sample_peers:
        send(x4.at[d], final.at[s], send_sem.at[6], recv_sem.at[6], t, d)
    final[s] = x4[s]
    add_first(2)
    wait_bytes(small_part, recv_sem.at[7])
    total = small[own, :].astype(F32)
    for k in range(N_SAMPLE - 1):
        total = total + small_part[k].astype(F32)
    small_mid[:, pl.ds(0, SMALL)] = total.astype(BF16)
    for k in range(1, N_TILE):
        d = tile_peers[k - 1]
        lanes = pl.ds(pl.multiple_of(d * 128, 128), 128)
        send(small_mid.at[:, lanes], small_last.at[k - 1], send_sem.at[8], recv_sem.at[8], d, s)
    add_second(0)
    add_second(1)
    wait_bytes(final.at[pl.ds(0, N_SAMPLE - 1)], recv_sem.at[6])
    d_normed_z = keep[5]
    for block in range(4):
        incoming = final[:, block // 2].reshape(128, 512).astype(F32)
        d_proj = (incoming * coefficient[block]).astype(BF16)
        tri[:, pl.ds(block * 128, 128)] = dot(d_proj, normed_z).astype(BF16)
        d_normed_z = d_normed_z + t_dot(d_proj, in_w_t[pl.ds(block * 128, 128), :])
    for k in range(1, N_SAMPLE):
        d = sample_peers[k - 1]
        rows = pl.ds(pl.multiple_of(d * 16, 16), 16)
        send(tri.at[rows], tri_part.at[k - 1], send_sem.at[11], recv_sem.at[11], t, d)
    add_second(2)
    grad_pair[...] = keep[4] + norm_back_rows(keep[0], inverse_z, d_normed_z, 1)
    wait_bytes(small_last, recv_sem.at[8])
    lanes = pl.ds(pl.multiple_of(t * 128, 128), 128)
    total = small_mid[:, lanes].astype(F32)
    for k in range(N_TILE - 1):
        total = total + small_last[k].astype(F32)
    small_sum[own, lanes] = total.astype(BF16)
    block = small_sum.at[own, lanes]
    for d in tile_peers:
        send(block, block, send_sem.at[9], recv_sem.at[9], d, s)
    add_third(0)
    add_third(1)
    wait_bytes(tri_part, recv_sem.at[11])
    total = tri[own, :].astype(F32)
    for k in range(N_SAMPLE - 1):
        total = total + tri_part[k].astype(F32)
    tri_all[t] = total.astype(BF16)
    for d in tile_peers:
        send(tri_all.at[t], tri_all.at[t], send_sem.at[12], recv_sem.at[12], d, s)
    add_third(2)
    gather_second(0)
    gather_second(1)
    wait_bytes(tri_all.at[pl.ds(0, N_TILE - 1)], recv_sem.at[12])
    tri_sum[own, :] = jnp.sum(tri_all[...].astype(F32), axis=0).astype(BF16)
    for d in sample_peers:
        send(tri_sum.at[own], tri_sum.at[own], send_sem.at[13], recv_sem.at[13], t, d)
    gather_second(2)
    wait_bytes(small_last, recv_sem.at[9])
    known = small_sum.at[own, pl.ds(0, SMALL)]
    for d in sample_peers:
        send(known, known, send_sem.at[10], recv_sem.at[10], t, d)
    for g in range(3):
        gather_first(g)
        unpack(full, g, core)
    wait_bytes(small_part, recv_sem.at[10])
    wait_bytes(tri_part, recv_sem.at[13])
    for g in range(3):
        wait_bytes(other.at[g], w_recv.at[g, 6])
        unpack(other, g, 1 - core)

    wait_bytes(pair_sum, send_sem.at[0])
    wait_bytes(by_chip, send_sem.at[1])
    wait_bytes(by_sample, send_sem.at[2])
    wait_bytes(mid.at[pl.ds(0, N_SAMPLE - 1)], send_sem.at[3])
    wait_bytes(arrived.at[pl.ds(0, N_TILE - 1)], send_sem.at[4])
    wait_bytes(back.at[pl.ds(0, N_TILE - 1)], send_sem.at[5])
    wait_bytes(final.at[pl.ds(0, N_SAMPLE - 1)], send_sem.at[6])
    wait_bytes(small_part, send_sem.at[7])
    wait_bytes(small_last, send_sem.at[8])
    wait_bytes(small_last, send_sem.at[9])
    wait_bytes(small_part, send_sem.at[10])
    wait_bytes(tri_part, send_sem.at[11])
    wait_bytes(tri_all.at[pl.ds(0, N_TILE - 1)], send_sem.at[12])
    wait_bytes(tri_part, send_sem.at[13])
    wait_bytes(theirs, w_send.at[0])
    wait_bytes(part1, w_send.at[1])
    wait_bytes(part2, w_send.at[2])
    wait_bytes(part3.at[:, pl.ds(0, 3)], w_send.at[3])
    wait_bytes(part2, w_send.at[4])
    wait_bytes(part1, w_send.at[5])
    wait_bytes(theirs, w_send.at[6])


def backward(collective_id, *operands):
    vmem = pl.BlockSpec(memory_space=pltpu.VMEM)
    chunk = (3, 4, ROWS, WIDTH)
    block = (4, 16, 128)
    return pl.pallas_call(
        backward_kernel,
        out_shape=[
            jax.ShapeDtypeStruct((512, 128), F32),
            jax.ShapeDtypeStruct((512, 768), F32),
            jax.ShapeDtypeStruct((768, 3072), BF16),
            jax.ShapeDtypeStruct((768, 768), BF16),
            jax.ShapeDtypeStruct((128, N_TILE * 128), BF16),
            jax.ShapeDtypeStruct((128, 512), BF16),
        ],
        in_specs=[vmem] * len(operands),
        out_specs=[vmem] * 6,
        scratch_shapes=[
            pltpu.VMEM((N_CHIP, N_SAMPLE) + block, BF16),
            pltpu.VMEM((N_CHIP - 1, N_SAMPLE) + block, BF16),
            pltpu.VMEM((N_SAMPLE - 1,) + block, BF16),
            pltpu.VMEM(block, F32),
            pltpu.VMEM((4, 16, 128), F32),
            pltpu.VMEM((4, 128, 512), F32),
            pltpu.VMEM((6, 512, 128), F32),
            pltpu.VMEM((128, 512), F32),
            pltpu.VMEM((N_SAMPLE, 16, 512), BF16),
            pltpu.VMEM((N_SAMPLE, 16, 512), BF16),
            pltpu.VMEM((4, 128, 128), F32),
            pltpu.VMEM((N_TILE, 8, 512), F32),
            pltpu.VMEM((N_TILE, 8, 512), F32),
            pltpu.VMEM((4, 128, 128), F32),
            pltpu.VMEM((2, 256, 128), F32),
            pltpu.VMEM((N_TILE, 2, 16, 256), BF16),
            pltpu.VMEM((N_TILE, 2, 16, 256), BF16),
            pltpu.VMEM((2, 256, 128), F32),
            pltpu.VMEM((N_SAMPLE, 2, 16, 512), BF16),
            pltpu.VMEM((N_SAMPLE, 2, 16, 512), BF16),
            pltpu.VMEM((128, SMALL), BF16),
            pltpu.VMEM((N_SAMPLE - 1, 16, SMALL), BF16),
            pltpu.VMEM((16, N_TILE * 128), BF16),
            pltpu.VMEM((N_TILE - 1, 16, 128), BF16),
            pltpu.VMEM((128, 512), BF16),
            pltpu.VMEM((N_SAMPLE - 1, 16, 512), BF16),
            pltpu.VMEM((N_TILE, 16, 512), BF16),
            pltpu.VMEM(chunk, BF16),
            pltpu.VMEM(chunk, BF16),
            pltpu.VMEM(chunk, BF16),
            pltpu.VMEM((3, 3, ROWS, WIDTH), BF16),
            pltpu.VMEM((3, ROWS, WIDTH), BF16),
            pltpu.VMEM((3, 3, 48, WIDTH), BF16),
            pltpu.VMEM((3, 48, WIDTH), BF16),
            pltpu.VMEM((3, 4, 48, WIDTH), BF16),
            pltpu.VMEM(chunk, BF16),
            pltpu.VMEM(chunk, BF16),
            pltpu.VMEM((768, 512), F32),
            pltpu.VMEM((256, 768), BF16),
            pltpu.VMEM((128, 768), F32),
            pltpu.SemaphoreType.DMA((14,)),
            pltpu.SemaphoreType.DMA((14,)),
            pltpu.SemaphoreType.DMA((15,)),
            pltpu.SemaphoreType.DMA((7,)),
            pltpu.SemaphoreType.DMA((3, 7)),
        ],
        compiler_params=pltpu.CompilerParams(
            collective_id=collective_id, has_side_effects=True, vmem_limit_bytes=60 << 20
        ),
    )(*operands)


def norm_parts(values, axis):
    centered = values - jnp.mean(values, axis=axis, keepdims=True)
    inverse = lax.rsqrt(jnp.mean(centered * centered, axis=axis, keepdims=True) + EPSILON)
    return (centered * inverse, inverse)


def norm_back(normed, inverse, incoming_gradient, axis):
    first_mean = jnp.mean(incoming_gradient, axis=axis, keepdims=True)
    second_mean = jnp.mean(incoming_gradient * normed, axis=axis, keepdims=True)
    return (incoming_gradient - first_mean - normed * second_mean) * inverse


def silu_slope(values):
    sigmoid_part = jax.nn.sigmoid(values)
    return sigmoid_part * (1.0 + values * (1.0 - sigmoid_part))


def shards(
    pair,
    pair_mask,
    tri_in_w,
    tri_gate_w,
    tri_out_w,
    bias_w,
    atom_feats,
    atom_to_token,
    atom_w,
    tokens,
    attention_input_weight,
    attention_output_weight,
    cot_pair,
    token_output_cotangent,
):
    hidden = tri_in_w.shape[1] // 4
    token_width = attention_input_weight.shape[0]
    head_count = bias_w.shape[1]
    total_tokens = tokens.shape[1]
    pair_rows = pair.reshape(-1, hidden)
    mask_row = pair_mask.astype(F32).reshape(1, -1)
    in_w_t, bias_w_t = tri_in_w.T, bias_w.T
    following, bias_all, left_panel, right_panel, product, every_feat, every_atom = pair_forward(
        pair_rows,
        mask_row,
        in_w_t,
        tri_gate_w,
        tri_out_w,
        bias_w_t,
        atom_feats,
        atom_to_token[None],
        0,
    )
    every_feat = every_feat.reshape(-1, atom_feats.shape[1])
    every_atom = every_atom.reshape(-1)
    atom_pre = jnp.dot(every_feat, atom_w, preferred_element_type=jnp.float32)
    atom_act = jax.nn.silu(atom_pre).astype(BF16)
    token_ids = jnp.arange(total_tokens, dtype=jnp.int32)
    one_hot = (token_ids[:, None] == every_atom[None, :]).astype(BF16)
    token_sums = jnp.dot(one_hot, atom_act, preferred_element_type=F32)
    token_counts = jnp.sum(one_hot.astype(F32), axis=1)
    token_cond = token_sums / token_counts[:, None]
    token_state_rows = tokens.astype(jnp.float32) + token_cond[None]
    normed_h, inverse_h = norm_parts(token_state_rows, 2)
    normalized_hidden_bfloat = normed_h.astype(jnp.bfloat16)
    hidden_t = normalized_hidden_bfloat.reshape(-1, token_width).T
    cot_rows = token_output_cotangent.reshape(-1, token_width)

    def project(block):
        weight = attention_input_weight[:, block * token_width : (block + 1) * token_width]
        return t_dot(weight, hidden_t)

    gated_t, d_every_t, bias_blocks = attention(
        project(0).astype(BF16),
        project(2).astype(BF16),
        project(3).astype(BF16),
        jax.nn.sigmoid(project(1)),
        dot_t(attention_output_weight, cot_rows),
        bias_all,
    )
    d_every_t = d_every_t.reshape(4 * token_width, -1)
    token_output_rows = token_state_rows + t_dot(gated_t, attention_output_weight).reshape(
        token_state_rows.shape
    )
    grad_pair, grad_tokens, in_sum, out_sum, small_sum, tri_sum = backward(
        1,
        bias_blocks,
        pair_rows,
        mask_row,
        in_w_t,
        tri_gate_w,
        tri_out_w,
        bias_w_t,
        following,
        product,
        left_panel,
        right_panel,
        cot_pair.reshape(-1, hidden),
        hidden_t,
        d_every_t,
        gated_t,
        cot_rows,
        attention_input_weight,
        inverse_h.reshape(1, -1),
        token_counts[:, None],
        every_feat.reshape(8, -1, every_feat.shape[1]),
        every_atom.reshape(8, 1, -1),
        atom_w,
    )
    grad_tokens = grad_tokens.reshape(tokens.shape)
    small_sum = small_sum.astype(F32)
    at = token_width
    summed = (
        tri_sum.astype(F32)
        .reshape(hidden, 4, hidden)
        .transpose(2, 1, 0)
        .reshape(hidden, 4 * hidden),
        small_sum[:, at : at + hidden],
        small_sum[:, at + hidden : at + 2 * hidden],
        small_sum[:head_count, at + 2 * hidden : at + 3 * hidden].T,
        small_sum[:, :at],
        in_sum.astype(F32),
        out_sum.astype(F32),
    )
    pair_next, grad_pair = following.reshape(pair.shape), grad_pair.reshape(pair.shape)
    return (pair_next, token_output_rows, grad_pair, grad_tokens) + summed


def solution(mesh):
    in_specs = (
        P("tile", "sample", None),
        P("tile", "sample"),
        P(),
        P(),
        P(),
        P(),
        P("tile", None),
        P("tile"),
        P(),
        P(("tile", "sample"), None, None),
        P(),
        P(),
        P("tile", "sample", None),
        P(("tile", "sample"), None, None),
    )
    out_specs = (
        P("tile", "sample", None),
        P(("tile", "sample"), None, None),
        P("tile", "sample", None),
        P(("tile", "sample"), None, None),
        P(),
        P(),
        P(),
        P(),
        P(),
        P(),
        P(),
    )
    return jax.shard_map(shards, mesh=mesh, in_specs=in_specs, out_specs=out_specs, check_vma=False)
```

```python
import functools
import math

import jax
import jax.numpy as jnp
from jax import lax
from jax.experimental import pallas as pl
from jax.experimental.pallas import tpu as pltpu
from jax.sharding import PartitionSpec as P

EPSILON = 1e-05
N_TILE = 16
N_SAMPLE = 8
N_CHIP = 8
MESH = pl.DeviceIdType.MESH
BF16 = jnp.bfloat16
F32 = jnp.float32
HIGHEST = lax.Precision.HIGHEST


def wait_bytes(ref, sem):
    pltpu.make_async_copy(ref, ref, sem).wait()


def send(src, dst, send_sem, recv_sem, t, s):
    pltpu.make_async_remote_copy(
        src, dst, send_sem, recv_sem, device_id=(t, s), device_id_type=MESH
    ).start()


def dot(a, b):
    return jnp.dot(a, b, preferred_element_type=F32)


def dot_t(a, b):
    return lax.dot_general(a, b, (((1,), (1,)), ((), ())), preferred_element_type=F32)


def t_dot(a, b):
    return lax.dot_general(a, b, (((0,), (0,)), ((), ())), preferred_element_type=F32)


HEAD = 48
GROUP = 4
LANES = 32


def fetching(kernel, count):
    def run(*refs):
        sources, rest, buffers, sem = refs[:count], refs[count : -count - 1], refs[-count - 1 : -1], refs[-1]
        copies = [
            pltpu.make_async_copy(source, buffer, sem.at[i])
            for i, (source, buffer) in enumerate(zip(sources, buffers))
        ]
        for copy in copies:
            copy.start()

        def need(*which):
            for i in which:
                copies[i].wait()

        kernel(need, *buffers, *rest)

    return run


def fetch_scratch(operands):
    return [pltpu.VMEM(x.shape, x.dtype) for x in operands] + [
        pltpu.SemaphoreType.DMA((len(operands),))
    ]


def place_lanes(parts, first):
    group_of = lax.broadcasted_iota(jnp.int32, parts[0].shape, 1) // LANES
    result = None
    for i in range(4):
        shift = (i - first) % 4 * LANES
        moved = pltpu.roll(parts[i], shift, 1) if shift else parts[i]
        result = moved if result is None else jnp.where(group_of == i, moved, result)
    return result


def panel_of(arrived, first, step, panel):
    for part in range(4):
        rows = [
            arrived[part, pl.ds(first + s * (step // 8), 16, stride=step), :] for s in range(8)
        ]
        for i in range(4):
            for half in range(2):
                panel[half, pl.ds(part * 4 + i, 16, stride=16), :] = place_lanes(
                    rows[half * 4 : half * 4 + 4], i
                )


def blocks_of(panel, store):
    for half in range(2):
        for part in range(4):
            rows = [panel[half, pl.ds(part * 4 + i, 16, stride=16), :] for i in range(4)]
            for q in range(4):
                store(half * 4 + q, pl.ds(part * 128, 128), place_lanes(rows, q))


def split_lanes(values, ref):
    for part in range(ref.shape[0]):
        ref[part] = values[:, part * 128 : part * 128 + 128]


def joined(ref):
    return jnp.concatenate([ref[0], ref[1]], axis=1)


def norm_rows(values, axis):
    centered = values - jnp.mean(values, axis=axis, keepdims=True)
    inverse = lax.rsqrt(jnp.mean(centered * centered, axis=axis, keepdims=True) + EPSILON)
    return centered * inverse, inverse


def sigmoid(values):
    return 1.0 / (1.0 + jnp.exp(-values))


def forward_kernel(
    need,
    pair,
    in_w_t,
    mask,
    feats,
    atoms,
    gate_w,
    out_w,
    bias_w_t,
    atom_w,
    tokens,
    in_w,
    pair_next,
    bias,
    left,
    right,
    product,
    every_feat,
    every_atom,
    token_cond,
    counts,
    hidden_t,
    inverse_h,
    q,
    k_out,
    v,
    gate,
    x1,
    mid,
    mid_rows,
    x2,
    arrived,
    arrived_rows,
    panel,
    x3,
    back,
    back_rows,
    x4,
    packed,
    mine,
    send_sem,
    recv_sem,
):
    t, s = lax.axis_index("tile"), lax.axis_index("sample")
    m, c = t // 2, lax.rem(t, 2)
    barrier = pltpu.get_barrier_semaphore()
    tile_peers = [lax.rem(t + k, N_TILE) for k in range(1, N_TILE)]
    sample_peers = [lax.rem(s + k, N_SAMPLE) for k in range(1, N_SAMPLE)]
    for d in sample_peers:
        pl.semaphore_signal(barrier, inc=1, device_id=(t, d), device_id_type=MESH)
    for d in tile_peers:
        pl.semaphore_signal(barrier, inc=1, device_id=(d, s), device_id_type=MESH)

    def token_sums():
        token_cond[...] = jnp.zeros_like(token_cond)
        counts[...] = jnp.zeros_like(counts)

        @pl.loop(0, N_TILE)
        def _(a):
            pre = dot(every_feat[a], atom_w[...])
            token = lax.broadcasted_iota(jnp.int32, (256, 128), 0)
            one_hot = jnp.where(token == every_atom[a], 1.0, 0.0)
            token_cond[...] += dot(one_hot.astype(BF16), (pre * sigmoid(pre)).astype(BF16))
            counts[...] += jnp.sum(one_hot, axis=1, keepdims=True)

        token_cond[...] = token_cond[...] / counts[...]

    def token_norm():
        @pl.loop(0, 4)
        def _(a):
            lanes = pl.ds(pl.multiple_of(a * 128, 128), 128)
            of_token = pl.ds(pl.multiple_of(lax.rem(a, 2) * 128, 128), 128)
            state = tokens[lanes, :].astype(F32) + token_cond[of_token, :]
            normed, inverse = norm_rows(state.T, 0)
            hidden_t[:, lanes] = normed.astype(BF16)
            inverse_h[:, lanes] = inverse

    def token_project(block, out):
        @pl.loop(0, 3)
        def _(a):
            rows = pl.ds(pl.multiple_of(a * 256, 256), 256)
            columns = pl.ds(pl.multiple_of(block * 768 + a * 256, 256), 256)
            result = t_dot(in_w[:, columns], hidden_t[...])
            out[rows, :] = (sigmoid(result) if block == 1 else result).astype(out.dtype)

    need(0)
    normed_z = norm_rows(pair[...].astype(F32), 1)[0].astype(BF16)
    need(1, 2)

    def project(block):
        return dot_t(in_w_t[pl.ds(block * 128, 128), :], normed_z)

    for side in range(2):
        value = (sigmoid(project(2 * side)) * project(2 * side + 1) * mask[...]).astype(BF16)
        for d in range(N_SAMPLE):
            x1[d, side] = value[d * 16 : d * 16 + 16]
    need(3, 4)
    pl.semaphore_wait(barrier, N_SAMPLE + N_TILE - 2)
    for d in sample_peers:
        send(x1.at[d], mid.at[s], send_sem.at[0], recv_sem.at[0], t, d)
    for d in tile_peers:
        send(feats, every_feat.at[t], send_sem.at[1], recv_sem.at[1], d, s)
        send(atoms, every_atom.at[t], send_sem.at[2], recv_sem.at[2], d, s)
    every_feat[t] = feats[...]
    every_atom[t] = atoms[...]
    mid[s] = x1[s]
    need(5, 6, 7, 8, 9, 10)
    tri_gate = sigmoid(dot(normed_z, gate_w[...]))
    wait_bytes(mid.at[pl.ds(0, N_SAMPLE - 1)], recv_sem.at[0])
    split_lanes(mid[...].reshape(256, 512).astype(F32), mid_rows)
    for d in range(N_TILE):
        for part in range(4):
            x2[d, :, pl.ds(part * 128, 128)] = mid_rows[part, pl.ds(d, 16, stride=16), :].astype(
                BF16
            )
    for d in tile_peers:
        send(x2.at[d], arrived.at[t], send_sem.at[3], recv_sem.at[3], d, s)
    arrived[t] = x2[t]
    wait_bytes(every_feat.at[pl.ds(0, N_TILE - 1)], recv_sem.at[1])
    wait_bytes(every_atom.at[pl.ds(0, N_TILE - 1)], recv_sem.at[2])
    token_sums()
    wait_bytes(arrived.at[pl.ds(0, N_TILE - 1)], recv_sem.at[3])
    split_lanes(arrived[...].reshape(256, 512).astype(F32), arrived_rows)
    panel_of(arrived_rows, 0, 16, panel)
    left[...] = joined(panel).astype(BF16)
    panel_of(arrived_rows, 1, 16, panel)
    right[...] = joined(panel).astype(BF16)
    x3[...] = dot_t(left[...], right[...]).astype(BF16).reshape(N_TILE, 16, 256)
    for d in tile_peers:
        send(x3.at[d], back.at[t], send_sem.at[4], recv_sem.at[4], d, s)
    back[t] = x3[t]
    token_norm()
    wait_bytes(back.at[pl.ds(0, N_TILE - 1)], recv_sem.at[4])
    split_lanes(back[...].reshape(256, 256).astype(F32), back_rows)

    def store(d, lanes, rows):
        x4[d, :, lanes] = rows.astype(BF16)

    blocks_of(back_rows, store)
    for d in sample_peers:
        send(x4.at[d], product.at[s], send_sem.at[5], recv_sem.at[5], t, d)
    product[s] = x4[s]
    token_project(0, q)
    wait_bytes(product.at[pl.ds(0, N_SAMPLE - 1)], recv_sem.at[5])
    normed_p = norm_rows(product[...].reshape(128, 512).astype(F32), 0)[0].astype(BF16)
    linear = t_dot(normed_p, out_w[...])
    following = pair[...].astype(F32) + tri_gate * linear
    pair_next[...] = following
    normed_n = norm_rows(following, 1)[0].astype(BF16)
    head_rows = dot_t(bias_w_t[...], normed_n)
    split_lanes(head_rows, packed)
    for part in range(4):
        rows = [packed[part, pl.ds(h, 4, stride=4), :] for h in range(4)]
        for i in range(4):
            mine[:, part * 4 + i] = place_lanes(rows, i)
    bias[m, c, s] = mine[...].astype(BF16)

    own = bias.at[m, c, s]
    for d in sample_peers:
        send(own, own, send_sem.at[6], recv_sem.at[6], t, d)
    token_project(2, k_out)
    wait_bytes(bias.at[m, c, pl.ds(0, N_SAMPLE - 1)], recv_sem.at[6])
    block = bias.at[m, c]
    other = m * 2 + 1 - c
    for k in range(1, N_CHIP):
        send(block, block, send_sem.at[7], recv_sem.at[7 + k], lax.rem(m + k, N_CHIP) * 2 + c, s)
    send(block, block, send_sem.at[8], recv_sem.at[7], other, s)
    token_project(3, v)
    token_project(1, gate)
    for k in range(1, N_CHIP):
        came = bias.at[lax.rem(m + N_CHIP - k, N_CHIP), c]
        wait_bytes(came, recv_sem.at[7 + k])
        send(came, came, send_sem.at[8], recv_sem.at[7], other, s)
    wait_bytes(bias.at[:, 0], recv_sem.at[7])
    wait_bytes(mid.at[pl.ds(0, N_SAMPLE - 1)], send_sem.at[0])
    wait_bytes(every_feat.at[pl.ds(0, N_TILE - 1)], send_sem.at[1])
    wait_bytes(every_atom.at[pl.ds(0, N_TILE - 1)], send_sem.at[2])
    wait_bytes(arrived.at[pl.ds(0, N_TILE - 1)], send_sem.at[3])
    wait_bytes(back.at[pl.ds(0, N_TILE - 1)], send_sem.at[4])
    wait_bytes(product.at[pl.ds(0, N_SAMPLE - 1)], send_sem.at[5])
    wait_bytes(bias.at[m, c, pl.ds(0, N_SAMPLE - 1)], send_sem.at[6])
    wait_bytes(bias.at[pl.ds(0, N_CHIP - 1), 0], send_sem.at[7])
    wait_bytes(bias.at[:, 0], send_sem.at[8])


def forward(collective_id, *operands):
    vmem = pl.BlockSpec(memory_space=pltpu.VMEM)
    feats, atoms = operands[3:5]
    return pl.pallas_call(
        fetching(forward_kernel, len(operands)),
        out_shape=[
            jax.ShapeDtypeStruct((512, 128), F32),
            jax.ShapeDtypeStruct((N_CHIP, 2, N_SAMPLE, 4, 16, 128), BF16),
            jax.ShapeDtypeStruct((256, 256), BF16),
            jax.ShapeDtypeStruct((256, 256), BF16),
            jax.ShapeDtypeStruct((N_SAMPLE, 16, 512), BF16),
            jax.ShapeDtypeStruct((N_TILE,) + feats.shape, feats.dtype),
            jax.ShapeDtypeStruct((N_TILE,) + atoms.shape, atoms.dtype),
            jax.ShapeDtypeStruct((256, 768), F32),
            jax.ShapeDtypeStruct((256, 1), F32),
            jax.ShapeDtypeStruct((768, 512), BF16),
            jax.ShapeDtypeStruct((1, 512), F32),
            jax.ShapeDtypeStruct((768, 512), BF16),
            jax.ShapeDtypeStruct((768, 512), BF16),
            jax.ShapeDtypeStruct((768, 512), BF16),
            jax.ShapeDtypeStruct((768, 512), F32),
        ],
        in_specs=[pl.BlockSpec(memory_space=pl.ANY)] * len(operands),
        out_specs=[vmem] * 15,
        scratch_shapes=[
            pltpu.VMEM((N_SAMPLE, 2, 16, 512), BF16),
            pltpu.VMEM((N_SAMPLE, 2, 16, 512), BF16),
            pltpu.VMEM((4, 256, 128), F32),
            pltpu.VMEM((N_TILE, 16, 512), BF16),
            pltpu.VMEM((N_TILE, 16, 512), BF16),
            pltpu.VMEM((4, 256, 128), F32),
            pltpu.VMEM((2, 256, 128), F32),
            pltpu.VMEM((N_TILE, 16, 256), BF16),
            pltpu.VMEM((N_TILE, 16, 256), BF16),
            pltpu.VMEM((2, 256, 128), F32),
            pltpu.VMEM((N_SAMPLE, 16, 512), BF16),
            pltpu.VMEM((4, 16, 128), F32),
            pltpu.VMEM((4, 16, 128), F32),
            pltpu.SemaphoreType.DMA((9,)),
            pltpu.SemaphoreType.DMA((15,)),
        ]
        + fetch_scratch(operands),
        compiler_params=pltpu.CompilerParams(
            collective_id=collective_id, has_side_effects=True, vmem_limit_bytes=40 << 20
        ),
    )(*operands)


def attention_kernel(q, k, v, gate, up, bias, gated, d_every, d_bias, bias_rows, bias_total):
    tokens = bias_rows.shape[1]
    scale = 1.0 / math.sqrt(HEAD)
    group_of = lax.broadcasted_iota(jnp.int32, (tokens, 128), 1) // LANES

    for half in range(2):
        parts = [
            bias[:, :, half * 4 + i, 0].reshape(tokens, 128).astype(F32) for i in range(4)
        ]
        for h in range(GROUP):
            row = parts[0] if h == 0 else pltpu.roll(parts[0], (-h) % 4 * LANES, 1)
            for i in range(1, 4):
                shift = (i - h) % 4 * LANES
                moved = pltpu.roll(parts[i], shift, 1) if shift else parts[i]
                row = jnp.where(group_of == i, moved, row)
            bias_rows[h, :, pl.ds(half * 128, 128)] = row

    @pl.loop(0, GROUP)
    def _(h):
        rows = pl.ds(pl.multiple_of(h * HEAD, 16), HEAD)
        for sample in range(2):
            columns = pl.ds(sample * tokens, tokens)
            qh, kh, vh = q[rows, columns], k[rows, columns], v[rows, columns]
            scores = t_dot(qh, kh) * scale + bias_rows[h]
            weights = jnp.exp(scores - jnp.max(scores, axis=1, keepdims=True))
            probs = weights * (1.0 / jnp.sum(weights, axis=1, keepdims=True))
            probs_b = probs.astype(BF16)
            attended = dot_t(vh, probs_b)
            gate_h, up_h = gate[rows, columns], up[rows, columns]
            gated[rows, columns] = (gate_h * attended).astype(BF16)
            d_att = (up_h * gate_h).astype(BF16)
            d_every[1, rows, columns] = (up_h * attended * gate_h * (1.0 - gate_h)).astype(BF16)
            d_probs = t_dot(d_att, vh)
            inner = jnp.sum(probs * d_probs, axis=1, keepdims=True)
            d_scores = probs * (d_probs - inner)
            d_scores_b = d_scores.astype(BF16)
            d_every[0, rows, columns] = (dot_t(kh, d_scores_b) * scale).astype(BF16)
            d_every[2, rows, columns] = (dot(qh, d_scores_b) * scale).astype(BF16)
            d_every[3, rows, columns] = dot(d_att, probs_b).astype(BF16)
            if sample == 0:
                bias_total[h] = d_scores
            else:
                bias_total[h] = bias_total[h] + d_scores

    for half in range(2):
        parts = [bias_total[h, :, pl.ds(half * 128, 128)] for h in range(GROUP)]
        for i in range(4):
            row = parts[0] if i == 0 else pltpu.roll(parts[0], (-i) % 4 * LANES, 1)
            for h in range(1, GROUP):
                shift = (h - i) % 4 * LANES
                moved = pltpu.roll(parts[h], shift, 1) if shift else parts[h]
                row = jnp.where(group_of == h, moved, row)
            d_bias[:, :, half * 4 + i, 0] = row.astype(BF16).reshape(N_CHIP, 2, 16, 128)


def attention(q, k, v, gate, up, bias):
    width, columns = q.shape
    tokens = columns // 2
    block = GROUP * HEAD
    feature = pl.BlockSpec((block, columns), lambda i: (i, 0))
    of_bias = pl.BlockSpec((N_CHIP, 2, N_SAMPLE, 1, 16, 128), lambda i: (0, 0, 0, i, 0, 0))
    return pl.pallas_call(
        attention_kernel,
        grid=(width // block,),
        in_specs=[feature] * 5 + [of_bias],
        out_specs=[feature, pl.BlockSpec((4, block, columns), lambda i: (0, i, 0)), of_bias],
        out_shape=[
            jax.ShapeDtypeStruct((width, columns), BF16),
            jax.ShapeDtypeStruct((4, width, columns), BF16),
            jax.ShapeDtypeStruct(bias.shape, BF16),
        ],
        scratch_shapes=[
            pltpu.VMEM((GROUP, tokens, tokens), F32),
            pltpu.VMEM((GROUP, tokens, tokens), F32),
        ],
        compiler_params=pltpu.CompilerParams(vmem_limit_bytes=40 << 20),
    )(q, k, v, gate, up, bias)


ROWS = 192
WIDTH = 640
SMALL = 1152


def norm_back_rows(normed, inverse, incoming, axis):
    first = jnp.mean(incoming, axis=axis, keepdims=True)
    second = jnp.mean(incoming * normed, axis=axis, keepdims=True)
    return (incoming - first - normed * second) * inverse


def backward_kernel(
    need,
    d_bias,
    right_in,
    in_w,
    left_in,
    left_out,
    right_out,
    pair,
    in_w_t,
    mask,
    gate_w,
    out_w,
    bias_w_t,
    following,
    product,
    left,
    right,
    cot_pair,
    inverse_h,
    counts,
    feats,
    atoms,
    atom_w,
    grad_pair,
    grad_tokens,
    in_sum,
    out_sum,
    small_sum,
    tri_sum,
    pair_sum,
    by_chip,
    by_sample,
    bias_block,
    head_rows,
    coefficient,
    keep,
    keep_p,
    x1,
    mid,
    mid_rows,
    x2,
    arrived,
    arrived_rows,
    panel,
    x3,
    back,
    back_rows,
    x4,
    final,
    small,
    small_part,
    small_mid,
    small_last,
    tri,
    tri_part,
    tri_all,
    theirs,
    mine,
    from_core,
    part1,
    sum1,
    part2,
    sum2,
    part3,
    full,
    other,
    d_hidden,
    cond_grad,
    atom_grad,
    send_sem,
    recv_sem,
    chip_sem,
    w_send,
    w_recv,
):
    t, s = lax.axis_index("tile"), lax.axis_index("sample")
    m, core = t // 2, lax.rem(t, 2)
    partner_t = m * 2 + 1 - core
    place = [lax.rem(s, 2) * 2 + t // 8, lax.rem(t // 2, 4), s // 2]
    tile_peers = [lax.rem(t + k, N_TILE) for k in range(1, N_TILE)]
    sample_peers = [lax.rem(s + k, N_SAMPLE) for k in range(1, N_SAMPLE)]

    def peer(axis, k):
        where = list(place)
        where[axis] = lax.rem(place[axis] + k, 4)
        x, y, z = where
        return where[axis], (lax.rem(x, 2) * 8 + y * 2 + core, z * 2 + x // 2)

    barrier = pltpu.get_barrier_semaphore()
    for d in sample_peers:
        pl.semaphore_signal(barrier, inc=1, device_id=(t, d), device_id_type=MESH)
    for d in tile_peers:
        pl.semaphore_signal(barrier, inc=1, device_id=(d, s), device_id_type=MESH)
    diagonal = (lax.rem(t + 8, N_TILE), s + 1 - 2 * lax.rem(s, 2))
    pl.semaphore_signal(barrier, inc=1, device_id=diagonal, device_id_type=MESH)

    def form(g, c, target):
        wide = pl.ds(pl.multiple_of(g * 1024 + c * 512, 512), 512)
        narrow = pl.ds(pl.multiple_of(g * 256 + c * 128, 128), 128)

        @pl.loop(0, 4)
        def _(a):
            rows = pl.ds(pl.multiple_of(a * ROWS, 64), ROWS)
            target[g, a, :, pl.ds(0, 512)] = dot_t(left_in[rows, :], right_in[wide, :]).astype(BF16)
            target[g, a, :, pl.ds(512, 128)] = dot(left_out[rows, :], right_out[:, narrow]).astype(
                BF16
            )

    def form_theirs(g):
        form(g, 1 - core, theirs)
        send(theirs.at[g], from_core.at[g], w_send.at[0], w_recv.at[g, 0], partner_t, s)

    def form_mine(g):
        form(g, core, mine)

    def add_cores(g):
        wait_bytes(from_core.at[g], w_recv.at[g, 0])

        @pl.loop(0, 4)
        def _(a):
            @pl.loop(0, ROWS // 16)
            def _(r):
                rows = pl.ds(pl.multiple_of(r * 16, 16), 16)
                total = mine[g, a, rows, :].astype(F32) + from_core[g, a, rows, :].astype(F32)
                mine[g, a, rows, :] = total.astype(BF16)

        for k in range(1, 4):
            d, to = peer(g, k)
            send(mine.at[g, d], part1.at[g, k - 1], w_send.at[1], w_recv.at[g, 1], *to)

    def add_first(g):
        p1 = place[g]
        wait_bytes(part1.at[g], w_recv.at[g, 1])

        @pl.loop(0, ROWS // 16)
        def _(r):
            rows = pl.ds(pl.multiple_of(r * 16, 16), 16)
            total = mine[g, p1, rows, :].astype(F32)
            for k in range(3):
                total = total + part1[g, k, rows, :].astype(F32)
            sum1[g, rows, :] = total.astype(BF16)

        for k in range(1, 4):
            d, to = peer((g + 1) % 3, k)
            rows = pl.ds(pl.multiple_of(d * 48, 16), 48)
            send(sum1.at[g, rows], part2.at[g, k - 1], w_send.at[2], w_recv.at[g, 2], *to)

    def add_second(g):
        p2, p3 = place[(g + 1) % 3], place[(g + 2) % 3]
        wait_bytes(part2.at[g], w_recv.at[g, 2])
        total = sum1[g, pl.ds(pl.multiple_of(p2 * 48, 16), 48), :].astype(F32)
        for k in range(3):
            total = total + part2[g, k].astype(F32)
        sum2[g] = total.astype(BF16)
        for k in range(1, 4):
            _, to = peer((g + 2) % 3, k)
            send(sum2.at[g], part3.at[g, p3], w_send.at[3], w_recv.at[g, 3], *to)
        part3[g, p3] = sum2[g]

    def add_third(g):
        p1, p2 = place[g], place[(g + 1) % 3]
        wait_bytes(part3.at[g, pl.ds(0, 3)], w_recv.at[g, 3])
        total = part3[g, 0].astype(F32)
        for k in range(1, 4):
            total = total + part3[g, k].astype(F32)
        rows = pl.ds(pl.multiple_of(p2 * 48, 16), 48)
        full[g, p1, rows, :] = total.astype(BF16)
        block = full.at[g, p1, rows]
        for k in range(1, 4):
            _, to = peer((g + 1) % 3, k)
            send(block, block, w_send.at[4], w_recv.at[g, 4], *to)

    def gather_second(g):
        p1 = place[g]
        wait_bytes(full.at[g, p1, pl.ds(0, 144)], w_recv.at[g, 4])
        block = full.at[g, p1]
        for k in range(1, 4):
            _, to = peer(g, k)
            send(block, block, w_send.at[5], w_recv.at[g, 5], *to)
        send(block, other.at[g, p1], w_send.at[6], w_recv.at[g, 6], partner_t, s)

    def unpack(source, g, c):
        wide = pl.ds(pl.multiple_of(g * 1024 + c * 512, 512), 512)
        narrow = pl.ds(pl.multiple_of(g * 256 + c * 128, 128), 128)

        @pl.loop(0, 4)
        def _(a):
            @pl.loop(0, ROWS // 16)
            def _(r):
                rows = pl.ds(pl.multiple_of(r * 16, 16), 16)
                to_rows = pl.ds(pl.multiple_of(a * ROWS + r * 16, 16), 16)
                in_sum[to_rows, wide] = source[g, a, rows, pl.ds(0, 512)]
                out_sum[to_rows, narrow] = source[g, a, rows, pl.ds(512, 128)]

    def gather_first(g):
        wait_bytes(full.at[g, pl.ds(0, 3)], w_recv.at[g, 5])
        for k in range(1, 4):
            p1 = lax.rem(place[g] + k, 4)
            send(full.at[g, p1], other.at[g, p1], w_send.at[6], w_recv.at[g, 6], partner_t, s)

    def token_product():
        @pl.loop(0, 2)
        def _(a):
            rows = pl.ds(pl.multiple_of(a * 384, 128), 384)
            d_hidden[rows, :] = dot(in_w[rows, :], right_in[...])

    def token_norm():
        @pl.loop(0, 4)
        def _(a):
            lanes = pl.ds(pl.multiple_of(a * 128, 128), 128)
            back_t = norm_back_rows(
                left_in[:, lanes].astype(F32), inverse_h[:, lanes], d_hidden[:, lanes], 0
            )
            grad_tokens[lanes, :] = right_out[lanes, :].astype(F32) + back_t.T

        both = grad_tokens[pl.ds(0, 256), :] + grad_tokens[pl.ds(256, 256), :]
        cond_grad[...] = (both / counts[...]).astype(BF16)

    def atom_sums():
        atom_grad[...] = jnp.zeros_like(atom_grad)

        @pl.loop(0, atoms.shape[0])
        def _(a):
            feat = feats[a]
            pre = dot(feat, atom_w[...])
            part = sigmoid(pre)
            token = lax.broadcasted_iota(jnp.int32, (256, atoms.shape[2]), 0)
            one_hot = jnp.where(token == atoms[a], 1.0, 0.0).astype(BF16)
            d_act = t_dot(one_hot, cond_grad[...]) * (part * (1.0 + pre * (1.0 - part)))
            atom_grad[...] += t_dot(feat, d_act.astype(BF16))

        small[:, pl.ds(0, 768)] = atom_grad[...].astype(BF16)

    need(1, 2)
    token_product()
    need(0)
    pl.semaphore_wait(barrier, N_SAMPLE + N_TILE - 1)
    for k in range(1, N_CHIP + 1):
        d = lax.rem(m + k, N_CHIP)
        send(d_bias.at[d, 1 - core], pair_sum.at[d], send_sem.at[0], chip_sem.at[k - 1], partner_t, s)
    need(3, 4, 5)
    form_theirs(0)

    need(*range(6, 22))
    keep[0], inverse_z = norm_rows(pair[...].astype(F32), 1)
    normed_z = keep[0].astype(BF16)

    def project(block):
        return dot_t(in_w_t[pl.ds(block * 128, 128), :], normed_z)

    for side in range(2):
        gate_side = sigmoid(project(2 * side))
        masked = gate_side * mask[...]
        coefficient[2 * side] = masked * (1.0 - gate_side) * project(2 * side + 1)
        coefficient[2 * side + 1] = masked
    for k in range(1, N_CHIP + 1):
        d = lax.rem(m + k, N_CHIP)
        wait_bytes(pair_sum.at[d], chip_sem.at[k - 1])
        pair_sum[d] = (pair_sum[d].astype(F32) + d_bias[d, core].astype(F32)).astype(BF16)
        if k < N_CHIP:
            send(
                pair_sum.at[d],
                by_chip.at[k - 1],
                send_sem.at[1],
                chip_sem.at[N_CHIP + k - 1],
                d * 2 + core,
                s,
            )
    form_theirs(1)
    form_theirs(2)
    keep[1] = sigmoid(dot(normed_z, gate_w[...]))
    keep_p[...], inverse_p = norm_rows(product[...].reshape(128, 512).astype(F32), 0)
    normed_p = keep_p[...].astype(BF16)
    keep[2] = t_dot(normed_p, out_w[...])
    keep[3], inverse_n = norm_rows(following[...], 1)
    normed_n = keep[3].astype(BF16)
    small[...] = jnp.zeros((128, SMALL), BF16)
    small_mid[...] = jnp.zeros((16, N_TILE * 128), BF16)
    form_mine(0)
    form_mine(1)
    total = pair_sum[m].astype(F32)
    for k in range(1, N_CHIP):
        wait_bytes(by_chip.at[k - 1], chip_sem.at[N_CHIP + k - 1])
        total = total + by_chip[k - 1].astype(F32)
    pair_sum[m] = total.astype(BF16)
    for k in range(1, N_SAMPLE):
        send(
            pair_sum.at[m, sample_peers[k - 1]],
            by_sample.at[k - 1],
            send_sem.at[2],
            recv_sem.at[2],
            t,
            sample_peers[k - 1],
        )
    add_cores(0)
    form_mine(2)
    add_cores(1)
    wait_bytes(by_sample, recv_sem.at[2])
    bias_block[...] = pair_sum[m, s].astype(F32) + jnp.sum(by_sample[...].astype(F32), axis=0)

    for part in range(4):
        rows = [bias_block[:, part * 4 + i] for i in range(4)]
        for h in range(4):
            head_rows[part, pl.ds(h, 4, stride=4), :] = place_lanes(rows, h)
    d_heads = jnp.concatenate([head_rows[part] for part in range(4)], axis=1)
    high = d_heads.astype(BF16)
    low = (d_heads - high.astype(F32)).astype(BF16)
    d_normed_n = t_dot(high, bias_w_t[...]) + t_dot(low, bias_w_t[...])
    d_next = cot_pair[...].astype(F32) + norm_back_rows(keep[3], inverse_n, d_normed_n, 1)
    tri_gate = keep[1]
    d_linear = (d_next * tri_gate).astype(BF16)
    d_product = norm_back_rows(keep_p[...], inverse_p, dot_t(out_w[...], d_linear), 0).astype(BF16)
    for d in range(N_SAMPLE):
        x1[d] = d_product[d * 16 : d * 16 + 16]
    for d in sample_peers:
        send(x1.at[d], mid.at[s], send_sem.at[3], recv_sem.at[3], t, d)
    mid[s] = x1[s]
    d_gate = (d_next * keep[2] * tri_gate * (1.0 - tri_gate)).astype(BF16)
    keep[4] = d_next
    small[:, pl.ds(768, 128)] = t_dot(normed_z, d_gate).astype(BF16)
    small[:, pl.ds(896, 128)] = dot(normed_p, d_linear).astype(BF16)
    small[pl.ds(0, 16), pl.ds(1024, 128)] = (dot(high, normed_n) + dot(low, normed_n)).astype(BF16)
    keep[5] = dot_t(d_gate, gate_w[...])
    add_cores(2)
    token_norm()
    wait_bytes(mid.at[pl.ds(0, N_SAMPLE - 1)], recv_sem.at[3])
    split_lanes(mid[...].reshape(128, 512).astype(F32), mid_rows)
    for d in range(N_TILE):
        for part in range(4):
            x2[d, :, pl.ds(part * 128, 128)] = mid_rows[part, pl.ds(d, 8, stride=16), :]
    for d in tile_peers:
        send(x2.at[d], arrived.at[t], send_sem.at[4], recv_sem.at[4], d, s)
    arrived[t] = x2[t]
    atom_sums()
    wait_bytes(arrived.at[pl.ds(0, N_TILE - 1)], recv_sem.at[4])
    split_lanes(arrived[...].reshape(128, 512), arrived_rows)
    panel_of(arrived_rows, 0, 8, panel)
    d_panel = joined(panel).astype(BF16)
    x3[:, 0] = dot(d_panel, right[...]).astype(BF16).reshape(N_TILE, 16, 256)
    x3[:, 1] = t_dot(d_panel, left[...]).astype(BF16).reshape(N_TILE, 16, 256)
    for d in tile_peers:
        send(x3.at[d], back.at[t], send_sem.at[5], recv_sem.at[5], d, s)
    back[t] = x3[t]
    for k in range(1, N_SAMPLE):
        d = sample_peers[k - 1]
        rows = pl.ds(pl.multiple_of(d * 16, 16), 16)
        send(small.at[rows], small_part.at[k - 1], send_sem.at[7], recv_sem.at[7], t, d)
    own = pl.ds(pl.multiple_of(s * 16, 16), 16)
    add_first(0)
    add_first(1)
    wait_bytes(back.at[pl.ds(0, N_TILE - 1)], recv_sem.at[5])
    for side in range(2):
        split_lanes(back[:, side].reshape(256, 256).astype(F32), back_rows)

        def store(d, lanes, rows, side=side):
            x4[d, side, :, lanes] = rows.astype(BF16)

        blocks_of(back_rows, store)
    for d in sample_peers:
        send(x4.at[d], final.at[s], send_sem.at[6], recv_sem.at[6], t, d)
    final[s] = x4[s]
    add_first(2)
    wait_bytes(small_part, recv_sem.at[7])
    total = small[own, :].astype(F32)
    for k in range(N_SAMPLE - 1):
        total = total + small_part[k].astype(F32)
    small_mid[:, pl.ds(0, SMALL)] = total.astype(BF16)
    for k in range(1, N_TILE):
        d = tile_peers[k - 1]
        lanes = pl.ds(pl.multiple_of(d * 128, 128), 128)
        send(small_mid.at[:, lanes], small_last.at[k - 1], send_sem.at[8], recv_sem.at[8], d, s)
    add_second(0)
    add_second(1)
    wait_bytes(final.at[pl.ds(0, N_SAMPLE - 1)], recv_sem.at[6])
    d_normed_z = keep[5]
    for block in range(4):
        incoming = final[:, block // 2].reshape(128, 512).astype(F32)
        d_proj = (incoming * coefficient[block]).astype(BF16)
        tri[:, pl.ds(block * 128, 128)] = dot(d_proj, normed_z).astype(BF16)
        d_normed_z = d_normed_z + t_dot(d_proj, in_w_t[pl.ds(block * 128, 128), :])
    for k in range(1, N_SAMPLE):
        d = sample_peers[k - 1]
        rows = pl.ds(pl.multiple_of(d * 16, 16), 16)
        send(tri.at[rows], tri_part.at[k - 1], send_sem.at[11], recv_sem.at[11], t, d)
    add_second(2)
    grad_pair[...] = keep[4] + norm_back_rows(keep[0], inverse_z, d_normed_z, 1)
    wait_bytes(small_last, recv_sem.at[8])
    lanes = pl.ds(pl.multiple_of(t * 128, 128), 128)
    total = small_mid[:, lanes].astype(F32)
    for k in range(N_TILE - 1):
        total = total + small_last[k].astype(F32)
    small_sum[own, lanes] = total.astype(BF16)
    block = small_sum.at[own, lanes]
    for d in tile_peers:
        send(block, block, send_sem.at[9], recv_sem.at[9], d, s)
    add_third(0)
    add_third(1)
    wait_bytes(tri_part, recv_sem.at[11])
    total = tri[own, :].astype(F32)
    for k in range(N_SAMPLE - 1):
        total = total + tri_part[k].astype(F32)
    tri_all[t] = total.astype(BF16)
    for d in tile_peers:
        send(tri_all.at[t], tri_all.at[t], send_sem.at[12], recv_sem.at[12], d, s)
    add_third(2)
    gather_second(0)
    gather_second(1)
    wait_bytes(tri_all.at[pl.ds(0, N_TILE - 1)], recv_sem.at[12])
    tri_sum[own, :] = jnp.sum(tri_all[...].astype(F32), axis=0).astype(BF16)
    for d in sample_peers:
        send(tri_sum.at[own], tri_sum.at[own], send_sem.at[13], recv_sem.at[13], t, d)
    gather_second(2)
    wait_bytes(small_last, recv_sem.at[9])
    known = small_sum.at[own, pl.ds(0, SMALL)]
    for d in sample_peers:
        send(known, known, send_sem.at[10], recv_sem.at[10], t, d)
    for g in range(3):
        gather_first(g)
        unpack(full, g, core)
    wait_bytes(small_part, recv_sem.at[10])
    wait_bytes(tri_part, recv_sem.at[13])
    for g in range(3):
        wait_bytes(other.at[g], w_recv.at[g, 6])
        unpack(other, g, 1 - core)

    wait_bytes(pair_sum, send_sem.at[0])
    wait_bytes(by_chip, send_sem.at[1])
    wait_bytes(by_sample, send_sem.at[2])
    wait_bytes(mid.at[pl.ds(0, N_SAMPLE - 1)], send_sem.at[3])
    wait_bytes(arrived.at[pl.ds(0, N_TILE - 1)], send_sem.at[4])
    wait_bytes(back.at[pl.ds(0, N_TILE - 1)], send_sem.at[5])
    wait_bytes(final.at[pl.ds(0, N_SAMPLE - 1)], send_sem.at[6])
    wait_bytes(small_part, send_sem.at[7])
    wait_bytes(small_last, send_sem.at[8])
    wait_bytes(small_last, send_sem.at[9])
    wait_bytes(small_part, send_sem.at[10])
    wait_bytes(tri_part, send_sem.at[11])
    wait_bytes(tri_all.at[pl.ds(0, N_TILE - 1)], send_sem.at[12])
    wait_bytes(tri_part, send_sem.at[13])
    wait_bytes(theirs, w_send.at[0])
    wait_bytes(part1, w_send.at[1])
    wait_bytes(part2, w_send.at[2])
    wait_bytes(part3.at[:, pl.ds(0, 3)], w_send.at[3])
    wait_bytes(part2, w_send.at[4])
    wait_bytes(part1, w_send.at[5])
    wait_bytes(theirs, w_send.at[6])


def backward(collective_id, *operands):
    vmem = pl.BlockSpec(memory_space=pltpu.VMEM)
    chunk = (3, 4, ROWS, WIDTH)
    block = (4, 16, 128)
    return pl.pallas_call(
        fetching(backward_kernel, len(operands)),
        out_shape=[
            jax.ShapeDtypeStruct((512, 128), F32),
            jax.ShapeDtypeStruct((512, 768), F32),
            jax.ShapeDtypeStruct((768, 3072), BF16),
            jax.ShapeDtypeStruct((768, 768), BF16),
            jax.ShapeDtypeStruct((128, N_TILE * 128), BF16),
            jax.ShapeDtypeStruct((128, 512), BF16),
        ],
        in_specs=[pl.BlockSpec(memory_space=pl.ANY)] * len(operands),
        out_specs=[vmem] * 6,
        scratch_shapes=[
            pltpu.VMEM((N_CHIP, N_SAMPLE) + block, BF16),
            pltpu.VMEM((N_CHIP - 1, N_SAMPLE) + block, BF16),
            pltpu.VMEM((N_SAMPLE - 1,) + block, BF16),
            pltpu.VMEM(block, F32),
            pltpu.VMEM((4, 16, 128), F32),
            pltpu.VMEM((4, 128, 512), F32),
            pltpu.VMEM((6, 512, 128), F32),
            pltpu.VMEM((128, 512), F32),
            pltpu.VMEM((N_SAMPLE, 16, 512), BF16),
            pltpu.VMEM((N_SAMPLE, 16, 512), BF16),
            pltpu.VMEM((4, 128, 128), F32),
            pltpu.VMEM((N_TILE, 8, 512), F32),
            pltpu.VMEM((N_TILE, 8, 512), F32),
            pltpu.VMEM((4, 128, 128), F32),
            pltpu.VMEM((2, 256, 128), F32),
            pltpu.VMEM((N_TILE, 2, 16, 256), BF16),
            pltpu.VMEM((N_TILE, 2, 16, 256), BF16),
            pltpu.VMEM((2, 256, 128), F32),
            pltpu.VMEM((N_SAMPLE, 2, 16, 512), BF16),
            pltpu.VMEM((N_SAMPLE, 2, 16, 512), BF16),
            pltpu.VMEM((128, SMALL), BF16),
            pltpu.VMEM((N_SAMPLE - 1, 16, SMALL), BF16),
            pltpu.VMEM((16, N_TILE * 128), BF16),
            pltpu.VMEM((N_TILE - 1, 16, 128), BF16),
            pltpu.VMEM((128, 512), BF16),
            pltpu.VMEM((N_SAMPLE - 1, 16, 512), BF16),
            pltpu.VMEM((N_TILE, 16, 512), BF16),
            pltpu.VMEM(chunk, BF16),
            pltpu.VMEM(chunk, BF16),
            pltpu.VMEM(chunk, BF16),
            pltpu.VMEM((3, 3, ROWS, WIDTH), BF16),
            pltpu.VMEM((3, ROWS, WIDTH), BF16),
            pltpu.VMEM((3, 3, 48, WIDTH), BF16),
            pltpu.VMEM((3, 48, WIDTH), BF16),
            pltpu.VMEM((3, 4, 48, WIDTH), BF16),
            pltpu.VMEM(chunk, BF16),
            pltpu.VMEM(chunk, BF16),
            pltpu.VMEM((768, 512), F32),
            pltpu.VMEM((256, 768), BF16),
            pltpu.VMEM((128, 768), F32),
            pltpu.SemaphoreType.DMA((14,)),
            pltpu.SemaphoreType.DMA((14,)),
            pltpu.SemaphoreType.DMA((15,)),
            pltpu.SemaphoreType.DMA((7,)),
            pltpu.SemaphoreType.DMA((3, 7)),
        ]
        + fetch_scratch(operands),
        compiler_params=pltpu.CompilerParams(
            collective_id=collective_id, has_side_effects=True, vmem_limit_bytes=60 << 20
        ),
    )(*operands)


def widen_kernel(wide, narrow, wide_out, narrow_out):
    wide_out[...] = wide[...].astype(F32)
    narrow_out[...] = narrow[...].astype(F32)


def widen(wide, narrow):
    steps = 6
    specs = [
        pl.BlockSpec((x.shape[0] // steps, x.shape[1]), lambda i: (i, 0)) for x in (wide, narrow)
    ]
    return pl.pallas_call(
        widen_kernel,
        grid=(steps,),
        in_specs=specs,
        out_specs=specs,
        out_shape=[jax.ShapeDtypeStruct(x.shape, F32) for x in (wide, narrow)],
        compiler_params=pltpu.CompilerParams(vmem_limit_bytes=32 << 20),
    )(wide, narrow)


def shards(
    pair,
    pair_mask,
    tri_in_w,
    tri_gate_w,
    tri_out_w,
    bias_w,
    atom_feats,
    atom_to_token,
    atom_w,
    tokens,
    attention_input_weight,
    attention_output_weight,
    cot_pair,
    token_output_cotangent,
):
    hidden = tri_in_w.shape[1] // 4
    token_width = attention_input_weight.shape[0]
    head_count = bias_w.shape[1]
    total_tokens = tokens.shape[1]
    pair_rows = pair.reshape(-1, hidden)
    mask_row = pair_mask.astype(F32).reshape(1, -1)
    in_w_t, bias_w_t = tri_in_w.T, bias_w.T
    token_rows = tokens.reshape(-1, token_width)
    cot_rows = token_output_cotangent.reshape(-1, token_width)
    (
        following,
        bias_all,
        left_panel,
        right_panel,
        product,
        every_feat,
        every_atom,
        token_cond,
        token_counts,
        hidden_t,
        inverse_h,
        queries,
        keys_all,
        values_all,
        gate_values,
    ) = forward(
        0,
        pair_rows,
        in_w_t,
        mask_row,
        atom_feats,
        atom_to_token[None],
        tri_gate_w,
        tri_out_w,
        bias_w_t,
        atom_w,
        token_rows,
        attention_input_weight,
    )
    gated_t, d_every_t, bias_blocks = attention(
        queries,
        keys_all,
        values_all,
        gate_values,
        dot_t(attention_output_weight, cot_rows),
        bias_all,
    )
    d_every_t = d_every_t.reshape(4 * token_width, -1)
    token_output_rows = (
        tokens.astype(F32)
        + token_cond[None]
        + t_dot(gated_t, attention_output_weight).reshape(tokens.shape)
    )
    grad_pair, grad_tokens, in_sum, out_sum, small_sum, tri_sum = backward(
        1,
        bias_blocks,
        d_every_t,
        attention_input_weight,
        hidden_t,
        gated_t,
        cot_rows,
        pair_rows,
        in_w_t,
        mask_row,
        tri_gate_w,
        tri_out_w,
        bias_w_t,
        following,
        product,
        left_panel,
        right_panel,
        cot_pair.reshape(-1, hidden),
        inverse_h,
        token_counts,
        every_feat,
        every_atom,
        atom_w,
    )
    grad_tokens = grad_tokens.reshape(tokens.shape)
    small_sum = small_sum.astype(F32)
    at = token_width
    summed = (
        tri_sum.astype(F32)
        .reshape(hidden, 4, hidden)
        .transpose(2, 1, 0)
        .reshape(hidden, 4 * hidden),
        small_sum[:, at : at + hidden],
        small_sum[:, at + hidden : at + 2 * hidden],
        small_sum[:head_count, at + 2 * hidden : at + 3 * hidden].T,
        small_sum[:, :at],
        *widen(in_sum, out_sum),
    )
    pair_next, grad_pair = following.reshape(pair.shape), grad_pair.reshape(pair.shape)
    return (pair_next, token_output_rows, grad_pair, grad_tokens) + summed


def solution(mesh):
    in_specs = (
        P("tile", "sample", None),
        P("tile", "sample"),
        P(),
        P(),
        P(),
        P(),
        P("tile", None),
        P("tile"),
        P(),
        P(("tile", "sample"), None, None),
        P(),
        P(),
        P("tile", "sample", None),
        P(("tile", "sample"), None, None),
    )
    out_specs = (
        P("tile", "sample", None),
        P(("tile", "sample"), None, None),
        P("tile", "sample", None),
        P(("tile", "sample"), None, None),
        P(),
        P(),
        P(),
        P(),
        P(),
        P(),
        P(),
    )
    return jax.shard_map(shards, mesh=mesh, in_specs=in_specs, out_specs=out_specs, check_vma=False)
```

```python
import functools
import math

import jax
import jax.numpy as jnp
from jax import lax
from jax.experimental import pallas as pl
from jax.experimental.pallas import tpu as pltpu
from jax.sharding import PartitionSpec as P

EPSILON = 1e-05
N_TILE = 16
N_SAMPLE = 8
N_CHIP = 8
MESH = pl.DeviceIdType.MESH
BF16 = jnp.bfloat16
F32 = jnp.float32
HIGHEST = lax.Precision.HIGHEST


def wait_bytes(ref, sem):
    pltpu.make_async_copy(ref, ref, sem).wait()


def send(src, dst, send_sem, recv_sem, t, s):
    pltpu.make_async_remote_copy(
        src, dst, send_sem, recv_sem, device_id=(t, s), device_id_type=MESH
    ).start()


def dot(a, b):
    return jnp.dot(a, b, preferred_element_type=F32)


def dot_t(a, b):
    return lax.dot_general(a, b, (((1,), (1,)), ((), ())), preferred_element_type=F32)


def t_dot(a, b):
    return lax.dot_general(a, b, (((0,), (0,)), ((), ())), preferred_element_type=F32)


HEAD = 48
GROUP = 4
LANES = 32


def fetching(kernel, count):
    def run(*refs):
        sources, rest, buffers, sem = refs[:count], refs[count : -count - 1], refs[-count - 1 : -1], refs[-1]
        copies = [
            pltpu.make_async_copy(source, buffer, sem.at[i])
            for i, (source, buffer) in enumerate(zip(sources, buffers))
        ]
        for copy in copies:
            copy.start()

        def need(*which):
            for i in which:
                copies[i].wait()

        kernel(need, *buffers, *rest)

    return run


def fetch_scratch(operands):
    return [pltpu.VMEM(x.shape, x.dtype) for x in operands] + [
        pltpu.SemaphoreType.DMA((len(operands),))
    ]


def place_lanes(parts, first):
    group_of = lax.broadcasted_iota(jnp.int32, parts[0].shape, 1) // LANES
    result = None
    for i in range(4):
        shift = (i - first) % 4 * LANES
        moved = pltpu.roll(parts[i], shift, 1) if shift else parts[i]
        result = moved if result is None else jnp.where(group_of == i, moved, result)
    return result


def panel_of(arrived, first, step, panel):
    for part in range(4):
        rows = [
            arrived[part, pl.ds(first + s * (step // 8), 16, stride=step), :] for s in range(8)
        ]
        for i in range(4):
            for half in range(2):
                panel[half, pl.ds(part * 4 + i, 16, stride=16), :] = place_lanes(
                    rows[half * 4 : half * 4 + 4], i
                )


def blocks_of(panel, store):
    for half in range(2):
        for part in range(4):
            rows = [panel[half, pl.ds(part * 4 + i, 16, stride=16), :] for i in range(4)]
            for q in range(4):
                store(half * 4 + q, pl.ds(part * 128, 128), place_lanes(rows, q))


def split_lanes(values, ref):
    for part in range(ref.shape[0]):
        ref[part] = values[:, part * 128 : part * 128 + 128]


def joined(ref):
    return jnp.concatenate([ref[0], ref[1]], axis=1)


def norm_rows(values, axis):
    centered = values - jnp.mean(values, axis=axis, keepdims=True)
    inverse = lax.rsqrt(jnp.mean(centered * centered, axis=axis, keepdims=True) + EPSILON)
    return centered * inverse, inverse


def sigmoid(values):
    return 1.0 / (1.0 + jnp.exp(-values))


def attend(group, q, k, v, gate, up, bias, gated, d_every, d_bias, bias_rows, bias_total):
    tokens = bias_rows.shape[1]
    scale = 1.0 / math.sqrt(HEAD)
    group_of = lax.broadcasted_iota(jnp.int32, (tokens, 128), 1) // LANES

    for half in range(2):
        parts = [
            bias[:, :, half * 4 + i, group].reshape(tokens, 128).astype(F32) for i in range(4)
        ]
        for h in range(GROUP):
            row = parts[0] if h == 0 else pltpu.roll(parts[0], (-h) % 4 * LANES, 1)
            for i in range(1, 4):
                shift = (i - h) % 4 * LANES
                moved = pltpu.roll(parts[i], shift, 1) if shift else parts[i]
                row = jnp.where(group_of == i, moved, row)
            bias_rows[h, :, pl.ds(half * 128, 128)] = row

    @pl.loop(0, GROUP)
    def _(h):
        rows = pl.ds(pl.multiple_of(group * GROUP * HEAD + h * HEAD, 16), HEAD)
        for sample in range(2):
            columns = pl.ds(sample * tokens, tokens)
            qh, kh, vh = q[rows, columns], k[rows, columns], v[rows, columns]
            scores = t_dot(qh, kh) * scale + bias_rows[h]
            weights = jnp.exp(scores - jnp.max(scores, axis=1, keepdims=True))
            probs = weights * (1.0 / jnp.sum(weights, axis=1, keepdims=True))
            probs_b = probs.astype(BF16)
            attended = dot_t(vh, probs_b)
            gate_h, up_h = gate[rows, columns], up[rows, columns]
            gated[rows, columns] = (gate_h * attended).astype(BF16)
            d_att = (up_h * gate_h).astype(BF16)
            d_every[1, rows, columns] = (up_h * attended * gate_h * (1.0 - gate_h)).astype(BF16)
            d_probs = t_dot(d_att, vh)
            inner = jnp.sum(probs * d_probs, axis=1, keepdims=True)
            d_scores = probs * (d_probs - inner)
            d_scores_b = d_scores.astype(BF16)
            d_every[0, rows, columns] = (dot_t(kh, d_scores_b) * scale).astype(BF16)
            d_every[2, rows, columns] = (dot(qh, d_scores_b) * scale).astype(BF16)
            d_every[3, rows, columns] = dot(d_att, probs_b).astype(BF16)
            if sample == 0:
                bias_total[h] = d_scores
            else:
                bias_total[h] = bias_total[h] + d_scores

    for half in range(2):
        parts = [bias_total[h, :, pl.ds(half * 128, 128)] for h in range(GROUP)]
        for i in range(4):
            row = parts[0] if i == 0 else pltpu.roll(parts[0], (-i) % 4 * LANES, 1)
            for h in range(1, GROUP):
                shift = (h - i) % 4 * LANES
                moved = pltpu.roll(parts[h], shift, 1) if shift else parts[h]
                row = jnp.where(group_of == h, moved, row)
            d_bias[:, :, half * 4 + i, group] = row.astype(BF16).reshape(N_CHIP, 2, 16, 128)


def forward_kernel(
    need,
    pair,
    in_w_t,
    mask,
    feats,
    atoms,
    gate_w,
    out_w,
    bias_w_t,
    atom_w,
    tokens,
    in_w,
    up,
    pair_next,
    left,
    right,
    product,
    every_feat,
    every_atom,
    token_cond,
    counts,
    hidden_t,
    inverse_h,
    gated,
    d_every,
    bias_block,
    x1,
    mid,
    mid_rows,
    x2,
    arrived,
    arrived_rows,
    panel,
    x3,
    back,
    back_rows,
    x4,
    packed,
    mine,
    bias,
    q,
    keys,
    v,
    gate,
    bias_rows,
    bias_total,
    d_bias,
    pair_sum,
    by_chip,
    by_sample,
    send_sem,
    recv_sem,
    chip_in,
    core_in,
    core_back,
    chip_back,
):
    t, s = lax.axis_index("tile"), lax.axis_index("sample")
    m, c = t // 2, lax.rem(t, 2)
    barrier = pltpu.get_barrier_semaphore()
    tile_peers = [lax.rem(t + k, N_TILE) for k in range(1, N_TILE)]
    sample_peers = [lax.rem(s + k, N_SAMPLE) for k in range(1, N_SAMPLE)]
    for d in sample_peers:
        pl.semaphore_signal(barrier, inc=1, device_id=(t, d), device_id_type=MESH)
    for d in tile_peers:
        pl.semaphore_signal(barrier, inc=1, device_id=(d, s), device_id_type=MESH)

    def token_sums():
        token_cond[...] = jnp.zeros_like(token_cond)
        counts[...] = jnp.zeros_like(counts)

        @pl.loop(0, N_TILE)
        def _(a):
            pre = dot(every_feat[a], atom_w[...])
            token = lax.broadcasted_iota(jnp.int32, (256, 128), 0)
            one_hot = jnp.where(token == every_atom[a], 1.0, 0.0)
            token_cond[...] += dot(one_hot.astype(BF16), (pre * sigmoid(pre)).astype(BF16))
            counts[...] += jnp.sum(one_hot, axis=1, keepdims=True)

        token_cond[...] = token_cond[...] / counts[...]

    def token_norm():
        @pl.loop(0, 4)
        def _(a):
            lanes = pl.ds(pl.multiple_of(a * 128, 128), 128)
            of_token = pl.ds(pl.multiple_of(lax.rem(a, 2) * 128, 128), 128)
            state = tokens[lanes, :].astype(F32) + token_cond[of_token, :]
            normed, inverse = norm_rows(state.T, 0)
            hidden_t[:, lanes] = normed.astype(BF16)
            inverse_h[:, lanes] = inverse

    def token_project(block, out):
        @pl.loop(0, 3)
        def _(a):
            rows = pl.ds(pl.multiple_of(a * 256, 256), 256)
            columns = pl.ds(pl.multiple_of(block * 768 + a * 256, 256), 256)
            result = t_dot(in_w[:, columns], hidden_t[...])
            out[rows, :] = (sigmoid(result) if block == 1 else result).astype(out.dtype)

    need(0)
    normed_z = norm_rows(pair[...].astype(F32), 1)[0].astype(BF16)
    need(1, 2)

    def project(block):
        return dot_t(in_w_t[pl.ds(block * 128, 128), :], normed_z)

    for side in range(2):
        value = (sigmoid(project(2 * side)) * project(2 * side + 1) * mask[...]).astype(BF16)
        for d in range(N_SAMPLE):
            x1[d, side] = value[d * 16 : d * 16 + 16]
    need(3, 4)
    pl.semaphore_wait(barrier, N_SAMPLE + N_TILE - 2)
    for d in sample_peers:
        send(x1.at[d], mid.at[s], send_sem.at[0], recv_sem.at[0], t, d)
    for d in tile_peers:
        send(feats, every_feat.at[t], send_sem.at[1], recv_sem.at[1], d, s)
        send(atoms, every_atom.at[t], send_sem.at[2], recv_sem.at[2], d, s)
    every_feat[t] = feats[...]
    every_atom[t] = atoms[...]
    mid[s] = x1[s]
    need(5, 6, 7, 8, 9, 10, 11)
    tri_gate = sigmoid(dot(normed_z, gate_w[...]))
    wait_bytes(mid.at[pl.ds(0, N_SAMPLE - 1)], recv_sem.at[0])
    split_lanes(mid[...].reshape(256, 512).astype(F32), mid_rows)
    for d in range(N_TILE):
        for part in range(4):
            x2[d, :, pl.ds(part * 128, 128)] = mid_rows[part, pl.ds(d, 16, stride=16), :].astype(
                BF16
            )
    for d in tile_peers:
        send(x2.at[d], arrived.at[t], send_sem.at[3], recv_sem.at[3], d, s)
    arrived[t] = x2[t]
    wait_bytes(every_feat.at[pl.ds(0, N_TILE - 1)], recv_sem.at[1])
    wait_bytes(every_atom.at[pl.ds(0, N_TILE - 1)], recv_sem.at[2])
    token_sums()
    wait_bytes(arrived.at[pl.ds(0, N_TILE - 1)], recv_sem.at[3])
    split_lanes(arrived[...].reshape(256, 512).astype(F32), arrived_rows)
    panel_of(arrived_rows, 0, 16, panel)
    left[...] = joined(panel).astype(BF16)
    panel_of(arrived_rows, 1, 16, panel)
    right[...] = joined(panel).astype(BF16)
    x3[...] = dot_t(left[...], right[...]).astype(BF16).reshape(N_TILE, 16, 256)
    for d in tile_peers:
        send(x3.at[d], back.at[t], send_sem.at[4], recv_sem.at[4], d, s)
    back[t] = x3[t]
    token_norm()
    wait_bytes(back.at[pl.ds(0, N_TILE - 1)], recv_sem.at[4])
    split_lanes(back[...].reshape(256, 256).astype(F32), back_rows)

    def store(d, lanes, rows):
        x4[d, :, lanes] = rows.astype(BF16)

    blocks_of(back_rows, store)
    for d in sample_peers:
        send(x4.at[d], product.at[s], send_sem.at[5], recv_sem.at[5], t, d)
    product[s] = x4[s]
    token_project(0, q)
    wait_bytes(product.at[pl.ds(0, N_SAMPLE - 1)], recv_sem.at[5])
    normed_p = norm_rows(product[...].reshape(128, 512).astype(F32), 0)[0].astype(BF16)
    linear = t_dot(normed_p, out_w[...])
    following = pair[...].astype(F32) + tri_gate * linear
    pair_next[...] = following
    normed_n = norm_rows(following, 1)[0].astype(BF16)
    head_rows = dot_t(bias_w_t[...], normed_n)
    split_lanes(head_rows, packed)
    for part in range(4):
        rows = [packed[part, pl.ds(h, 4, stride=4), :] for h in range(4)]
        for i in range(4):
            mine[:, part * 4 + i] = place_lanes(rows, i)
    bias[m, c, s] = mine[...].astype(BF16)

    own = bias.at[m, c, s]
    for d in sample_peers:
        send(own, own, send_sem.at[6], recv_sem.at[6], t, d)
    token_project(2, keys)
    wait_bytes(bias.at[m, c, pl.ds(0, N_SAMPLE - 1)], recv_sem.at[6])
    other = m * 2 + 1 - c
    for g in range(4):
        for k in range(1, N_CHIP):
            d = lax.rem(m + k, N_CHIP) * 2 + c
            send(bias.at[m, c, :, g], bias.at[m, c, :, g], send_sem.at[7], chip_in.at[g], d, s)
    token_project(3, v)
    token_project(1, gate)

    def pass_bias(g):
        wait_bytes(bias.at[pl.ds(0, N_CHIP - 1), 0, :, g], chip_in.at[g])
        send(bias.at[:, c, :, g], bias.at[:, c, :, g], send_sem.at[8], core_in.at[g], other, s)

    def add_cores(g):
        wait_bytes(pair_sum.at[:, :, g], core_back.at[g])
        for k in range(1, N_CHIP + 1):
            d = lax.rem(m + k, N_CHIP)
            total = pair_sum[d, :, g].astype(F32) + d_bias[d, c, :, g].astype(F32)
            pair_sum[d, :, g] = total.astype(BF16)
            if k < N_CHIP:
                send(
                    pair_sum.at[d, :, g],
                    by_chip.at[k - 1, :, g],
                    send_sem.at[10],
                    chip_back.at[g],
                    d * 2 + c,
                    s,
                )

    def add_chips(g):
        wait_bytes(by_chip.at[:, :, g], chip_back.at[g])
        total = pair_sum[m, :, g].astype(F32)
        for k in range(N_CHIP - 1):
            total = total + by_chip[k, :, g].astype(F32)
        pair_sum[m, :, g] = total.astype(BF16)
        for k in range(1, N_SAMPLE):
            d = sample_peers[k - 1]
            send(
                pair_sum.at[m, d, g], by_sample.at[k - 1, g], send_sem.at[11], recv_sem.at[7], t, d
            )

    pass_bias(0)
    pass_bias(1)

    @pl.loop(0, 4)
    def _(g):
        wait_bytes(bias.at[:, 0, :, g], core_in.at[g])
        attend(g, q, keys, v, gate, up, bias, gated, d_every, d_bias, bias_rows, bias_total)
        send(d_bias.at[:, 1 - c, :, g], pair_sum.at[:, :, g], send_sem.at[9], core_back.at[g], other, s)

        @pl.when(g < 2)
        def _():
            pass_bias(g + 2)

        @pl.when(g >= 1)
        def _():
            add_cores(g - 1)

        @pl.when(g >= 2)
        def _():
            add_chips(g - 2)

    add_cores(3)
    add_chips(2)
    add_chips(3)
    wait_bytes(by_sample, recv_sem.at[7])
    bias_block[...] = pair_sum[m, s].astype(F32) + jnp.sum(by_sample[...].astype(F32), axis=0)
    wait_bytes(mid.at[pl.ds(0, N_SAMPLE - 1)], send_sem.at[0])
    wait_bytes(every_feat.at[pl.ds(0, N_TILE - 1)], send_sem.at[1])
    wait_bytes(every_atom.at[pl.ds(0, N_TILE - 1)], send_sem.at[2])
    wait_bytes(arrived.at[pl.ds(0, N_TILE - 1)], send_sem.at[3])
    wait_bytes(back.at[pl.ds(0, N_TILE - 1)], send_sem.at[4])
    wait_bytes(product.at[pl.ds(0, N_SAMPLE - 1)], send_sem.at[5])
    wait_bytes(bias.at[m, c, pl.ds(0, N_SAMPLE - 1)], send_sem.at[6])
    wait_bytes(bias.at[pl.ds(0, N_CHIP - 1), 0], send_sem.at[7])
    wait_bytes(bias.at[:, 0], send_sem.at[8])
    wait_bytes(pair_sum, send_sem.at[9])
    wait_bytes(by_chip, send_sem.at[10])
    wait_bytes(by_sample, send_sem.at[11])


def forward(collective_id, *operands):
    vmem = pl.BlockSpec(memory_space=pltpu.VMEM)
    feats, atoms = operands[3:5]
    return pl.pallas_call(
        fetching(forward_kernel, len(operands)),
        out_shape=[
            jax.ShapeDtypeStruct((512, 128), F32),
            jax.ShapeDtypeStruct((256, 256), BF16),
            jax.ShapeDtypeStruct((256, 256), BF16),
            jax.ShapeDtypeStruct((N_SAMPLE, 16, 512), BF16),
            jax.ShapeDtypeStruct((N_TILE,) + feats.shape, feats.dtype),
            jax.ShapeDtypeStruct((N_TILE,) + atoms.shape, atoms.dtype),
            jax.ShapeDtypeStruct((256, 768), F32),
            jax.ShapeDtypeStruct((256, 1), F32),
            jax.ShapeDtypeStruct((768, 512), BF16),
            jax.ShapeDtypeStruct((1, 512), F32),
            jax.ShapeDtypeStruct((768, 512), BF16),
            jax.ShapeDtypeStruct((4, 768, 512), BF16),
            jax.ShapeDtypeStruct((4, 16, 128), F32),
        ],
        in_specs=[pl.BlockSpec(memory_space=pl.ANY)] * len(operands),
        out_specs=[vmem] * 13,
        scratch_shapes=[
            pltpu.VMEM((N_SAMPLE, 2, 16, 512), BF16),
            pltpu.VMEM((N_SAMPLE, 2, 16, 512), BF16),
            pltpu.VMEM((4, 256, 128), F32),
            pltpu.VMEM((N_TILE, 16, 512), BF16),
            pltpu.VMEM((N_TILE, 16, 512), BF16),
            pltpu.VMEM((4, 256, 128), F32),
            pltpu.VMEM((2, 256, 128), F32),
            pltpu.VMEM((N_TILE, 16, 256), BF16),
            pltpu.VMEM((N_TILE, 16, 256), BF16),
            pltpu.VMEM((2, 256, 128), F32),
            pltpu.VMEM((N_SAMPLE, 16, 512), BF16),
            pltpu.VMEM((4, 16, 128), F32),
            pltpu.VMEM((4, 16, 128), F32),
            pltpu.VMEM((N_CHIP, 2, N_SAMPLE, 4, 16, 128), BF16),
            pltpu.VMEM((768, 512), BF16),
            pltpu.VMEM((768, 512), BF16),
            pltpu.VMEM((768, 512), BF16),
            pltpu.VMEM((768, 512), F32),
            pltpu.VMEM((GROUP, 256, 256), F32),
            pltpu.VMEM((GROUP, 256, 256), F32),
            pltpu.VMEM((N_CHIP, 2, N_SAMPLE, 4, 16, 128), BF16),
            pltpu.VMEM((N_CHIP, N_SAMPLE, 4, 16, 128), BF16),
            pltpu.VMEM((N_CHIP - 1, N_SAMPLE, 4, 16, 128), BF16),
            pltpu.VMEM((N_SAMPLE - 1, 4, 16, 128), BF16),
            pltpu.SemaphoreType.DMA((12,)),
            pltpu.SemaphoreType.DMA((8,)),
            pltpu.SemaphoreType.DMA((4,)),
            pltpu.SemaphoreType.DMA((4,)),
            pltpu.SemaphoreType.DMA((4,)),
            pltpu.SemaphoreType.DMA((4,)),
        ]
        + fetch_scratch(operands),
        compiler_params=pltpu.CompilerParams(
            collective_id=collective_id, has_side_effects=True, vmem_limit_bytes=60 << 20
        ),
    )(*operands)


ROWS = 192
WIDTH = 640
SMALL = 1152


def norm_back_rows(normed, inverse, incoming, axis):
    first = jnp.mean(incoming, axis=axis, keepdims=True)
    second = jnp.mean(incoming * normed, axis=axis, keepdims=True)
    return (incoming - first - normed * second) * inverse


def backward_kernel(
    need,
    bias_block,
    right_in,
    in_w,
    left_in,
    left_out,
    right_out,
    pair,
    in_w_t,
    mask,
    gate_w,
    out_w,
    bias_w_t,
    following,
    product,
    left,
    right,
    cot_pair,
    inverse_h,
    counts,
    feats,
    atoms,
    atom_w,
    grad_pair,
    grad_tokens,
    in_sum,
    out_sum,
    small_sum,
    tri_sum,
    head_rows,
    coefficient,
    keep,
    keep_p,
    x1,
    mid,
    mid_rows,
    x2,
    arrived,
    arrived_rows,
    panel,
    x3,
    back,
    back_rows,
    x4,
    final,
    small,
    small_part,
    small_mid,
    small_last,
    tri,
    tri_part,
    tri_all,
    theirs,
    mine,
    from_core,
    part1,
    sum1,
    part2,
    sum2,
    part3,
    full,
    other,
    d_hidden,
    cond_grad,
    atom_grad,
    send_sem,
    recv_sem,
    w_send,
    w_recv,
):
    t, s = lax.axis_index("tile"), lax.axis_index("sample")
    m, core = t // 2, lax.rem(t, 2)
    partner_t = m * 2 + 1 - core
    place = [lax.rem(s, 2) * 2 + t // 8, lax.rem(t // 2, 4), s // 2]
    tile_peers = [lax.rem(t + k, N_TILE) for k in range(1, N_TILE)]
    sample_peers = [lax.rem(s + k, N_SAMPLE) for k in range(1, N_SAMPLE)]

    def peer(axis, k):
        where = list(place)
        where[axis] = lax.rem(place[axis] + k, 4)
        x, y, z = where
        return where[axis], (lax.rem(x, 2) * 8 + y * 2 + core, z * 2 + x // 2)

    barrier = pltpu.get_barrier_semaphore()
    for d in sample_peers:
        pl.semaphore_signal(barrier, inc=1, device_id=(t, d), device_id_type=MESH)
    for d in tile_peers:
        pl.semaphore_signal(barrier, inc=1, device_id=(d, s), device_id_type=MESH)
    diagonal = (lax.rem(t + 8, N_TILE), s + 1 - 2 * lax.rem(s, 2))
    pl.semaphore_signal(barrier, inc=1, device_id=diagonal, device_id_type=MESH)

    def form(g, c, target):
        wide = pl.ds(pl.multiple_of(g * 1024 + c * 512, 512), 512)
        narrow = pl.ds(pl.multiple_of(g * 256 + c * 128, 128), 128)

        @pl.loop(0, 4)
        def _(a):
            rows = pl.ds(pl.multiple_of(a * ROWS, 64), ROWS)
            target[g, a, :, pl.ds(0, 512)] = dot_t(left_in[rows, :], right_in[wide, :]).astype(BF16)
            target[g, a, :, pl.ds(512, 128)] = dot(left_out[rows, :], right_out[:, narrow]).astype(
                BF16
            )

    def form_theirs(g):
        form(g, 1 - core, theirs)
        send(theirs.at[g], from_core.at[g], w_send.at[0], w_recv.at[g, 0], partner_t, s)

    def form_mine(g):
        form(g, core, mine)

    def add_cores(g):
        wait_bytes(from_core.at[g], w_recv.at[g, 0])

        @pl.loop(0, 4)
        def _(a):
            @pl.loop(0, ROWS // 16)
            def _(r):
                rows = pl.ds(pl.multiple_of(r * 16, 16), 16)
                total = mine[g, a, rows, :].astype(F32) + from_core[g, a, rows, :].astype(F32)
                mine[g, a, rows, :] = total.astype(BF16)

        for k in range(1, 4):
            d, to = peer(g, k)
            send(mine.at[g, d], part1.at[g, k - 1], w_send.at[1], w_recv.at[g, 1], *to)

    def add_first(g):
        p1 = place[g]
        wait_bytes(part1.at[g], w_recv.at[g, 1])

        @pl.loop(0, ROWS // 16)
        def _(r):
            rows = pl.ds(pl.multiple_of(r * 16, 16), 16)
            total = mine[g, p1, rows, :].astype(F32)
            for k in range(3):
                total = total + part1[g, k, rows, :].astype(F32)
            sum1[g, rows, :] = total.astype(BF16)

        for k in range(1, 4):
            d, to = peer((g + 1) % 3, k)
            rows = pl.ds(pl.multiple_of(d * 48, 16), 48)
            send(sum1.at[g, rows], part2.at[g, k - 1], w_send.at[2], w_recv.at[g, 2], *to)

    def add_second(g):
        p2, p3 = place[(g + 1) % 3], place[(g + 2) % 3]
        wait_bytes(part2.at[g], w_recv.at[g, 2])
        total = sum1[g, pl.ds(pl.multiple_of(p2 * 48, 16), 48), :].astype(F32)
        for k in range(3):
            total = total + part2[g, k].astype(F32)
        sum2[g] = total.astype(BF16)
        for k in range(1, 4):
            _, to = peer((g + 2) % 3, k)
            send(sum2.at[g], part3.at[g, p3], w_send.at[3], w_recv.at[g, 3], *to)
        part3[g, p3] = sum2[g]

    def add_third(g):
        p1, p2 = place[g], place[(g + 1) % 3]
        wait_bytes(part3.at[g, pl.ds(0, 3)], w_recv.at[g, 3])
        total = part3[g, 0].astype(F32)
        for k in range(1, 4):
            total = total + part3[g, k].astype(F32)
        rows = pl.ds(pl.multiple_of(p2 * 48, 16), 48)
        full[g, p1, rows, :] = total.astype(BF16)
        block = full.at[g, p1, rows]
        for k in range(1, 4):
            _, to = peer((g + 1) % 3, k)
            send(block, block, w_send.at[4], w_recv.at[g, 4], *to)

    def gather_second(g):
        p1 = place[g]
        wait_bytes(full.at[g, p1, pl.ds(0, 144)], w_recv.at[g, 4])
        block = full.at[g, p1]
        for k in range(1, 4):
            _, to = peer(g, k)
            send(block, block, w_send.at[5], w_recv.at[g, 5], *to)
        send(block, other.at[g, p1], w_send.at[6], w_recv.at[g, 6], partner_t, s)

    def unpack(source, g, c):
        wide = pl.ds(pl.multiple_of(g * 1024 + c * 512, 512), 512)
        narrow = pl.ds(pl.multiple_of(g * 256 + c * 128, 128), 128)

        @pl.loop(0, 4)
        def _(a):
            @pl.loop(0, ROWS // 16)
            def _(r):
                rows = pl.ds(pl.multiple_of(r * 16, 16), 16)
                to_rows = pl.ds(pl.multiple_of(a * ROWS + r * 16, 16), 16)
                in_sum[to_rows, wide] = source[g, a, rows, pl.ds(0, 512)]
                out_sum[to_rows, narrow] = source[g, a, rows, pl.ds(512, 128)]

    def gather_first(g):
        wait_bytes(full.at[g, pl.ds(0, 3)], w_recv.at[g, 5])
        for k in range(1, 4):
            p1 = lax.rem(place[g] + k, 4)
            send(full.at[g, p1], other.at[g, p1], w_send.at[6], w_recv.at[g, 6], partner_t, s)

    def token_product():
        @pl.loop(0, 2)
        def _(a):
            rows = pl.ds(pl.multiple_of(a * 384, 128), 384)
            d_hidden[rows, :] = dot(in_w[rows, :], right_in[...])

    def token_norm():
        @pl.loop(0, 4)
        def _(a):
            lanes = pl.ds(pl.multiple_of(a * 128, 128), 128)
            back_t = norm_back_rows(
                left_in[:, lanes].astype(F32), inverse_h[:, lanes], d_hidden[:, lanes], 0
            )
            grad_tokens[lanes, :] = right_out[lanes, :].astype(F32) + back_t.T

        both = grad_tokens[pl.ds(0, 256), :] + grad_tokens[pl.ds(256, 256), :]
        cond_grad[...] = (both / counts[...]).astype(BF16)

    def atom_sums():
        atom_grad[...] = jnp.zeros_like(atom_grad)

        @pl.loop(0, atoms.shape[0])
        def _(a):
            feat = feats[a]
            pre = dot(feat, atom_w[...])
            part = sigmoid(pre)
            token = lax.broadcasted_iota(jnp.int32, (256, atoms.shape[2]), 0)
            one_hot = jnp.where(token == atoms[a], 1.0, 0.0).astype(BF16)
            d_act = t_dot(one_hot, cond_grad[...]) * (part * (1.0 + pre * (1.0 - part)))
            atom_grad[...] += t_dot(feat, d_act.astype(BF16))

        small[:, pl.ds(0, 768)] = atom_grad[...].astype(BF16)

    need(1, 2)
    token_product()
    pl.semaphore_wait(barrier, N_SAMPLE + N_TILE - 1)
    need(3, 4, 5)
    form_theirs(0)
    form_theirs(1)
    form_theirs(2)

    need(0, *range(6, 22))
    keep[0], inverse_z = norm_rows(pair[...].astype(F32), 1)
    normed_z = keep[0].astype(BF16)

    def project(block):
        return dot_t(in_w_t[pl.ds(block * 128, 128), :], normed_z)

    keep[1] = sigmoid(dot(normed_z, gate_w[...]))
    keep_p[...], inverse_p = norm_rows(product[...].reshape(128, 512).astype(F32), 0)
    normed_p = keep_p[...].astype(BF16)
    keep[2] = t_dot(normed_p, out_w[...])
    keep[3], inverse_n = norm_rows(following[...], 1)
    normed_n = keep[3].astype(BF16)

    for part in range(4):
        rows = [bias_block[:, part * 4 + i] for i in range(4)]
        for h in range(4):
            head_rows[part, pl.ds(h, 4, stride=4), :] = place_lanes(rows, h)
    d_heads = jnp.concatenate([head_rows[part] for part in range(4)], axis=1)
    high = d_heads.astype(BF16)
    low = (d_heads - high.astype(F32)).astype(BF16)
    d_normed_n = t_dot(high, bias_w_t[...]) + t_dot(low, bias_w_t[...])
    d_next = cot_pair[...].astype(F32) + norm_back_rows(keep[3], inverse_n, d_normed_n, 1)
    tri_gate = keep[1]
    d_linear = (d_next * tri_gate).astype(BF16)
    d_product = norm_back_rows(keep_p[...], inverse_p, dot_t(out_w[...], d_linear), 0).astype(BF16)
    for d in range(N_SAMPLE):
        x1[d] = d_product[d * 16 : d * 16 + 16]
    for d in sample_peers:
        send(x1.at[d], mid.at[s], send_sem.at[3], recv_sem.at[3], t, d)
    mid[s] = x1[s]
    small[...] = jnp.zeros((128, SMALL), BF16)
    small_mid[...] = jnp.zeros((16, N_TILE * 128), BF16)
    d_gate = (d_next * keep[2] * tri_gate * (1.0 - tri_gate)).astype(BF16)
    keep[4] = d_next
    small[:, pl.ds(768, 128)] = t_dot(normed_z, d_gate).astype(BF16)
    small[:, pl.ds(896, 128)] = dot(normed_p, d_linear).astype(BF16)
    small[pl.ds(0, 16), pl.ds(1024, 128)] = (dot(high, normed_n) + dot(low, normed_n)).astype(BF16)
    keep[5] = dot_t(d_gate, gate_w[...])
    form_mine(0)
    add_cores(0)
    wait_bytes(mid.at[pl.ds(0, N_SAMPLE - 1)], recv_sem.at[3])
    split_lanes(mid[...].reshape(128, 512).astype(F32), mid_rows)
    for d in range(N_TILE):
        for part in range(4):
            x2[d, :, pl.ds(part * 128, 128)] = mid_rows[part, pl.ds(d, 8, stride=16), :]
    for d in tile_peers:
        send(x2.at[d], arrived.at[t], send_sem.at[4], recv_sem.at[4], d, s)
    arrived[t] = x2[t]
    form_mine(1)
    add_cores(1)
    form_mine(2)
    add_cores(2)
    for side in range(2):
        gate_side = sigmoid(project(2 * side))
        masked = gate_side * mask[...]
        coefficient[2 * side] = masked * (1.0 - gate_side) * project(2 * side + 1)
        coefficient[2 * side + 1] = masked
    wait_bytes(arrived.at[pl.ds(0, N_TILE - 1)], recv_sem.at[4])
    split_lanes(arrived[...].reshape(128, 512), arrived_rows)
    panel_of(arrived_rows, 0, 8, panel)
    d_panel = joined(panel).astype(BF16)
    x3[:, 0] = dot(d_panel, right[...]).astype(BF16).reshape(N_TILE, 16, 256)
    x3[:, 1] = t_dot(d_panel, left[...]).astype(BF16).reshape(N_TILE, 16, 256)
    for d in tile_peers:
        send(x3.at[d], back.at[t], send_sem.at[5], recv_sem.at[5], d, s)
    back[t] = x3[t]
    token_norm()
    atom_sums()
    for k in range(1, N_SAMPLE):
        d = sample_peers[k - 1]
        rows = pl.ds(pl.multiple_of(d * 16, 16), 16)
        send(small.at[rows], small_part.at[k - 1], send_sem.at[7], recv_sem.at[7], t, d)
    own = pl.ds(pl.multiple_of(s * 16, 16), 16)
    wait_bytes(back.at[pl.ds(0, N_TILE - 1)], recv_sem.at[5])
    for side in range(2):
        split_lanes(back[:, side].reshape(256, 256).astype(F32), back_rows)

        def store(d, lanes, rows, side=side):
            x4[d, side, :, lanes] = rows.astype(BF16)

        blocks_of(back_rows, store)
    for d in sample_peers:
        send(x4.at[d], final.at[s], send_sem.at[6], recv_sem.at[6], t, d)
    final[s] = x4[s]
    add_first(0)
    add_first(1)
    add_first(2)
    wait_bytes(small_part, recv_sem.at[7])
    total = small[own, :].astype(F32)
    for k in range(N_SAMPLE - 1):
        total = total + small_part[k].astype(F32)
    small_mid[:, pl.ds(0, SMALL)] = total.astype(BF16)
    for k in range(1, N_TILE):
        d = tile_peers[k - 1]
        lanes = pl.ds(pl.multiple_of(d * 128, 128), 128)
        send(small_mid.at[:, lanes], small_last.at[k - 1], send_sem.at[8], recv_sem.at[8], d, s)
    wait_bytes(final.at[pl.ds(0, N_SAMPLE - 1)], recv_sem.at[6])
    d_normed_z = keep[5]
    for block in range(4):
        incoming = final[:, block // 2].reshape(128, 512).astype(F32)
        d_proj = (incoming * coefficient[block]).astype(BF16)
        tri[:, pl.ds(block * 128, 128)] = dot(d_proj, normed_z).astype(BF16)
        d_normed_z = d_normed_z + t_dot(d_proj, in_w_t[pl.ds(block * 128, 128), :])
    for k in range(1, N_SAMPLE):
        d = sample_peers[k - 1]
        rows = pl.ds(pl.multiple_of(d * 16, 16), 16)
        send(tri.at[rows], tri_part.at[k - 1], send_sem.at[11], recv_sem.at[11], t, d)
    add_second(0)
    add_second(1)
    add_second(2)
    grad_pair[...] = keep[4] + norm_back_rows(keep[0], inverse_z, d_normed_z, 1)
    wait_bytes(small_last, recv_sem.at[8])
    lanes = pl.ds(pl.multiple_of(t * 128, 128), 128)
    total = small_mid[:, lanes].astype(F32)
    for k in range(N_TILE - 1):
        total = total + small_last[k].astype(F32)
    small_sum[own, lanes] = total.astype(BF16)
    block = small_sum.at[own, lanes]
    for d in tile_peers:
        send(block, block, send_sem.at[9], recv_sem.at[9], d, s)
    wait_bytes(tri_part, recv_sem.at[11])
    total = tri[own, :].astype(F32)
    for k in range(N_SAMPLE - 1):
        total = total + tri_part[k].astype(F32)
    tri_all[t] = total.astype(BF16)
    for d in tile_peers:
        send(tri_all.at[t], tri_all.at[t], send_sem.at[12], recv_sem.at[12], d, s)
    for g in range(3):
        add_third(g)
    for g in range(3):
        gather_second(g)
    wait_bytes(tri_all.at[pl.ds(0, N_TILE - 1)], recv_sem.at[12])
    tri_sum[own, :] = jnp.sum(tri_all[...].astype(F32), axis=0).astype(BF16)
    for d in sample_peers:
        send(tri_sum.at[own], tri_sum.at[own], send_sem.at[13], recv_sem.at[13], t, d)
    wait_bytes(small_last, recv_sem.at[9])
    known = small_sum.at[own, pl.ds(0, SMALL)]
    for d in sample_peers:
        send(known, known, send_sem.at[10], recv_sem.at[10], t, d)
    for g in range(3):
        gather_first(g)
        unpack(full, g, core)
    wait_bytes(small_part, recv_sem.at[10])
    wait_bytes(tri_part, recv_sem.at[13])
    for g in range(3):
        wait_bytes(other.at[g], w_recv.at[g, 6])
        unpack(other, g, 1 - core)

    wait_bytes(mid.at[pl.ds(0, N_SAMPLE - 1)], send_sem.at[3])
    wait_bytes(arrived.at[pl.ds(0, N_TILE - 1)], send_sem.at[4])
    wait_bytes(back.at[pl.ds(0, N_TILE - 1)], send_sem.at[5])
    wait_bytes(final.at[pl.ds(0, N_SAMPLE - 1)], send_sem.at[6])
    wait_bytes(small_part, send_sem.at[7])
    wait_bytes(small_last, send_sem.at[8])
    wait_bytes(small_last, send_sem.at[9])
    wait_bytes(small_part, send_sem.at[10])
    wait_bytes(tri_part, send_sem.at[11])
    wait_bytes(tri_all.at[pl.ds(0, N_TILE - 1)], send_sem.at[12])
    wait_bytes(tri_part, send_sem.at[13])
    wait_bytes(theirs, w_send.at[0])
    wait_bytes(part1, w_send.at[1])
    wait_bytes(part2, w_send.at[2])
    wait_bytes(part3.at[:, pl.ds(0, 3)], w_send.at[3])
    wait_bytes(part2, w_send.at[4])
    wait_bytes(part1, w_send.at[5])
    wait_bytes(theirs, w_send.at[6])


def backward(collective_id, *operands):
    vmem = pl.BlockSpec(memory_space=pltpu.VMEM)
    chunk = (3, 4, ROWS, WIDTH)
    return pl.pallas_call(
        fetching(backward_kernel, len(operands)),
        out_shape=[
            jax.ShapeDtypeStruct((512, 128), F32),
            jax.ShapeDtypeStruct((512, 768), F32),
            jax.ShapeDtypeStruct((768, 3072), BF16),
            jax.ShapeDtypeStruct((768, 768), BF16),
            jax.ShapeDtypeStruct((128, N_TILE * 128), BF16),
            jax.ShapeDtypeStruct((128, 512), BF16),
        ],
        in_specs=[pl.BlockSpec(memory_space=pl.ANY)] * len(operands),
        out_specs=[vmem] * 6,
        scratch_shapes=[
            pltpu.VMEM((4, 16, 128), F32),
            pltpu.VMEM((4, 128, 512), F32),
            pltpu.VMEM((6, 512, 128), F32),
            pltpu.VMEM((128, 512), F32),
            pltpu.VMEM((N_SAMPLE, 16, 512), BF16),
            pltpu.VMEM((N_SAMPLE, 16, 512), BF16),
            pltpu.VMEM((4, 128, 128), F32),
            pltpu.VMEM((N_TILE, 8, 512), F32),
            pltpu.VMEM((N_TILE, 8, 512), F32),
            pltpu.VMEM((4, 128, 128), F32),
            pltpu.VMEM((2, 256, 128), F32),
            pltpu.VMEM((N_TILE, 2, 16, 256), BF16),
            pltpu.VMEM((N_TILE, 2, 16, 256), BF16),
            pltpu.VMEM((2, 256, 128), F32),
            pltpu.VMEM((N_SAMPLE, 2, 16, 512), BF16),
            pltpu.VMEM((N_SAMPLE, 2, 16, 512), BF16),
            pltpu.VMEM((128, SMALL), BF16),
            pltpu.VMEM((N_SAMPLE - 1, 16, SMALL), BF16),
            pltpu.VMEM((16, N_TILE * 128), BF16),
            pltpu.VMEM((N_TILE - 1, 16, 128), BF16),
            pltpu.VMEM((128, 512), BF16),
            pltpu.VMEM((N_SAMPLE - 1, 16, 512), BF16),
            pltpu.VMEM((N_TILE, 16, 512), BF16),
            pltpu.VMEM(chunk, BF16),
            pltpu.VMEM(chunk, BF16),
            pltpu.VMEM(chunk, BF16),
            pltpu.VMEM((3, 3, ROWS, WIDTH), BF16),
            pltpu.VMEM((3, ROWS, WIDTH), BF16),
            pltpu.VMEM((3, 3, 48, WIDTH), BF16),
            pltpu.VMEM((3, 48, WIDTH), BF16),
            pltpu.VMEM((3, 4, 48, WIDTH), BF16),
            pltpu.VMEM(chunk, BF16),
            pltpu.VMEM(chunk, BF16),
            pltpu.VMEM((768, 512), F32),
            pltpu.VMEM((256, 768), BF16),
            pltpu.VMEM((128, 768), F32),
            pltpu.SemaphoreType.DMA((14,)),
            pltpu.SemaphoreType.DMA((14,)),
            pltpu.SemaphoreType.DMA((7,)),
            pltpu.SemaphoreType.DMA((3, 7)),
        ]
        + fetch_scratch(operands),
        compiler_params=pltpu.CompilerParams(
            collective_id=collective_id, has_side_effects=True, vmem_limit_bytes=60 << 20
        ),
    )(*operands)


def widen_kernel(wide, narrow, wide_out, narrow_out):
    wide_out[...] = wide[...].astype(F32)
    narrow_out[...] = narrow[...].astype(F32)


def widen(wide, narrow):
    steps = 6
    specs = [
        pl.BlockSpec((x.shape[0] // steps, x.shape[1]), lambda i: (i, 0)) for x in (wide, narrow)
    ]
    return pl.pallas_call(
        widen_kernel,
        grid=(steps,),
        in_specs=specs,
        out_specs=specs,
        out_shape=[jax.ShapeDtypeStruct(x.shape, F32) for x in (wide, narrow)],
        compiler_params=pltpu.CompilerParams(vmem_limit_bytes=32 << 20),
    )(wide, narrow)


def shards(
    pair,
    pair_mask,
    tri_in_w,
    tri_gate_w,
    tri_out_w,
    bias_w,
    atom_feats,
    atom_to_token,
    atom_w,
    tokens,
    attention_input_weight,
    attention_output_weight,
    cot_pair,
    token_output_cotangent,
):
    hidden = tri_in_w.shape[1] // 4
    token_width = attention_input_weight.shape[0]
    head_count = bias_w.shape[1]
    total_tokens = tokens.shape[1]
    pair_rows = pair.reshape(-1, hidden)
    mask_row = pair_mask.astype(F32).reshape(1, -1)
    in_w_t, bias_w_t = tri_in_w.T, bias_w.T
    token_rows = tokens.reshape(-1, token_width)
    cot_rows = token_output_cotangent.reshape(-1, token_width)
    (
        following,
        left_panel,
        right_panel,
        product,
        every_feat,
        every_atom,
        token_cond,
        token_counts,
        hidden_t,
        inverse_h,
        gated_t,
        d_every_t,
        bias_block,
    ) = forward(
        0,
        pair_rows,
        in_w_t,
        mask_row,
        atom_feats,
        atom_to_token[None],
        tri_gate_w,
        tri_out_w,
        bias_w_t,
        atom_w,
        token_rows,
        attention_input_weight,
        dot_t(attention_output_weight, cot_rows),
    )
    d_every_t = d_every_t.reshape(4 * token_width, -1)
    token_output_rows = (
        tokens.astype(F32)
        + token_cond[None]
        + t_dot(gated_t, attention_output_weight).reshape(tokens.shape)
    )
    grad_pair, grad_tokens, in_sum, out_sum, small_sum, tri_sum = backward(
        1,
        bias_block,
        d_every_t,
        attention_input_weight,
        hidden_t,
        gated_t,
        cot_rows,
        pair_rows,
        in_w_t,
        mask_row,
        tri_gate_w,
        tri_out_w,
        bias_w_t,
        following,
        product,
        left_panel,
        right_panel,
        cot_pair.reshape(-1, hidden),
        inverse_h,
        token_counts,
        every_feat,
        every_atom,
        atom_w,
    )
    grad_tokens = grad_tokens.reshape(tokens.shape)
    small_sum = small_sum.astype(F32)
    at = token_width
    summed = (
        tri_sum.astype(F32)
        .reshape(hidden, 4, hidden)
        .transpose(2, 1, 0)
        .reshape(hidden, 4 * hidden),
        small_sum[:, at : at + hidden],
        small_sum[:, at + hidden : at + 2 * hidden],
        small_sum[:head_count, at + 2 * hidden : at + 3 * hidden].T,
        small_sum[:, :at],
        *widen(in_sum, out_sum),
    )
    pair_next, grad_pair = following.reshape(pair.shape), grad_pair.reshape(pair.shape)
    return (pair_next, token_output_rows, grad_pair, grad_tokens) + summed


def solution(mesh):
    in_specs = (
        P("tile", "sample", None),
        P("tile", "sample"),
        P(),
        P(),
        P(),
        P(),
        P("tile", None),
        P("tile"),
        P(),
        P(("tile", "sample"), None, None),
        P(),
        P(),
        P("tile", "sample", None),
        P(("tile", "sample"), None, None),
    )
    out_specs = (
        P("tile", "sample", None),
        P(("tile", "sample"), None, None),
        P("tile", "sample", None),
        P(("tile", "sample"), None, None),
        P(),
        P(),
        P(),
        P(),
        P(),
        P(),
        P(),
    )
    return jax.shard_map(shards, mesh=mesh, in_specs=in_specs, out_specs=out_specs, check_vma=False)
```

```python
import functools
import math

import jax
import jax.numpy as jnp
from jax import lax
from jax.experimental import pallas as pl
from jax.experimental.pallas import tpu as pltpu
from jax.sharding import PartitionSpec as P

EPSILON = 1e-05
N_TILE = 16
N_SAMPLE = 8
N_CHIP = 8
MESH = pl.DeviceIdType.MESH
BF16 = jnp.bfloat16
F32 = jnp.float32
HIGHEST = lax.Precision.HIGHEST


def wait_bytes(ref, sem):
    pltpu.make_async_copy(ref, ref, sem).wait()


def send(src, dst, send_sem, recv_sem, t, s):
    pltpu.make_async_remote_copy(
        src, dst, send_sem, recv_sem, device_id=(t, s), device_id_type=MESH
    ).start()


def dot(a, b):
    return jnp.dot(a, b, preferred_element_type=F32)


def dot_t(a, b):
    return lax.dot_general(a, b, (((1,), (1,)), ((), ())), preferred_element_type=F32)


def t_dot(a, b):
    return lax.dot_general(a, b, (((0,), (0,)), ((), ())), preferred_element_type=F32)


HEAD = 48
GROUP = 4
LANES = 32


def fetching(kernel, count):
    def run(*refs):
        sources, rest, buffers, sem = refs[:count], refs[count : -count - 1], refs[-count - 1 : -1], refs[-1]
        copies = [
            pltpu.make_async_copy(source, buffer, sem.at[i])
            for i, (source, buffer) in enumerate(zip(sources, buffers))
        ]
        for copy in copies:
            copy.start()

        def need(*which):
            for i in which:
                copies[i].wait()

        kernel(need, *buffers, *rest)

    return run


def fetch_scratch(operands):
    return [pltpu.VMEM(x.shape, x.dtype) for x in operands] + [
        pltpu.SemaphoreType.DMA((len(operands),))
    ]


def place_lanes(parts, first):
    group_of = lax.broadcasted_iota(jnp.int32, parts[0].shape, 1) // LANES
    result = None
    for i in range(4):
        shift = (i - first) % 4 * LANES
        moved = pltpu.roll(parts[i], shift, 1) if shift else parts[i]
        result = moved if result is None else jnp.where(group_of == i, moved, result)
    return result


def panel_of(arrived, first, step, panel):
    for part in range(4):
        rows = [
            arrived[part, pl.ds(first + s * (step // 8), 16, stride=step), :] for s in range(8)
        ]
        for i in range(4):
            for half in range(2):
                panel[half, pl.ds(part * 4 + i, 16, stride=16), :] = place_lanes(
                    rows[half * 4 : half * 4 + 4], i
                )


def blocks_of(panel, store):
    for half in range(2):
        for part in range(4):
            rows = [panel[half, pl.ds(part * 4 + i, 16, stride=16), :] for i in range(4)]
            for q in range(4):
                store(half * 4 + q, pl.ds(part * 128, 128), place_lanes(rows, q))


def split_lanes(values, ref):
    for part in range(ref.shape[0]):
        ref[part] = values[:, part * 128 : part * 128 + 128]


def joined(ref):
    return jnp.concatenate([ref[0], ref[1]], axis=1)


def norm_rows(values, axis):
    centered = values - jnp.mean(values, axis=axis, keepdims=True)
    inverse = lax.rsqrt(jnp.mean(centered * centered, axis=axis, keepdims=True) + EPSILON)
    return centered * inverse, inverse


def sigmoid(values):
    return 1.0 / (1.0 + jnp.exp(-values))


def attend(group, q, k, v, gate, up, bias, gated, d_every, d_bias, bias_rows, bias_total):
    tokens = bias_rows.shape[1]
    scale = 1.0 / math.sqrt(HEAD)
    group_of = lax.broadcasted_iota(jnp.int32, (tokens, 128), 1) // LANES

    for half in range(2):
        parts = [
            bias[:, :, half * 4 + i, group].reshape(tokens, 128).astype(F32) for i in range(4)
        ]
        for h in range(GROUP):
            row = parts[0] if h == 0 else pltpu.roll(parts[0], (-h) % 4 * LANES, 1)
            for i in range(1, 4):
                shift = (i - h) % 4 * LANES
                moved = pltpu.roll(parts[i], shift, 1) if shift else parts[i]
                row = jnp.where(group_of == i, moved, row)
            bias_rows[h, :, pl.ds(half * 128, 128)] = row

    @pl.loop(0, GROUP)
    def _(h):
        rows = pl.ds(pl.multiple_of(group * GROUP * HEAD + h * HEAD, 16), HEAD)
        for sample in range(2):
            columns = pl.ds(sample * tokens, tokens)
            qh, kh, vh = q[rows, columns], k[rows, columns], v[rows, columns]
            scores = t_dot(qh, kh) * scale + bias_rows[h]
            weights = jnp.exp(scores - jnp.max(scores, axis=1, keepdims=True))
            probs = weights * (1.0 / jnp.sum(weights, axis=1, keepdims=True))
            probs_b = probs.astype(BF16)
            attended = dot_t(vh, probs_b)
            gate_h, up_h = gate[rows, columns], up[rows, columns]
            gated[rows, columns] = (gate_h * attended).astype(BF16)
            d_att = (up_h * gate_h).astype(BF16)
            d_every[1, rows, columns] = (up_h * attended * gate_h * (1.0 - gate_h)).astype(BF16)
            d_probs = t_dot(d_att, vh)
            inner = jnp.sum(probs * d_probs, axis=1, keepdims=True)
            d_scores = probs * (d_probs - inner)
            d_scores_b = d_scores.astype(BF16)
            d_every[0, rows, columns] = (dot_t(kh, d_scores_b) * scale).astype(BF16)
            d_every[2, rows, columns] = (dot(qh, d_scores_b) * scale).astype(BF16)
            d_every[3, rows, columns] = dot(d_att, probs_b).astype(BF16)
            if sample == 0:
                bias_total[h] = d_scores
            else:
                bias_total[h] = bias_total[h] + d_scores

    for half in range(2):
        parts = [bias_total[h, :, pl.ds(half * 128, 128)] for h in range(GROUP)]
        for i in range(4):
            row = parts[0] if i == 0 else pltpu.roll(parts[0], (-i) % 4 * LANES, 1)
            for h in range(1, GROUP):
                shift = (h - i) % 4 * LANES
                moved = pltpu.roll(parts[h], shift, 1) if shift else parts[h]
                row = jnp.where(group_of == h, moved, row)
            d_bias[:, :, half * 4 + i, group] = row.astype(BF16).reshape(N_CHIP, 2, 16, 128)


def forward_kernel(
    need,
    pair,
    in_w_t,
    mask,
    feats,
    atoms,
    gate_w,
    out_w,
    bias_w_t,
    atom_w,
    tokens,
    in_w,
    out_weight,
    cot,
    pair_next,
    left,
    right,
    product,
    every_feat,
    every_atom,
    token_cond,
    counts,
    hidden_t,
    inverse_h,
    gated,
    d_every,
    bias_block,
    grad_tokens,
    atom_grad,
    x1,
    mid,
    mid_rows,
    x2,
    arrived,
    arrived_rows,
    panel,
    x3,
    back,
    back_rows,
    x4,
    packed,
    mine,
    bias,
    q,
    keys,
    v,
    gate,
    bias_rows,
    bias_total,
    d_bias,
    pair_sum,
    by_chip,
    by_sample,
    up,
    d_hidden,
    cond_grad,
    atom_total,
    send_sem,
    recv_sem,
    chip_in,
    core_in,
    core_back,
    chip_back,
):
    t, s = lax.axis_index("tile"), lax.axis_index("sample")
    m, c = t // 2, lax.rem(t, 2)
    barrier = pltpu.get_barrier_semaphore()
    tile_peers = [lax.rem(t + k, N_TILE) for k in range(1, N_TILE)]
    sample_peers = [lax.rem(s + k, N_SAMPLE) for k in range(1, N_SAMPLE)]
    for d in sample_peers:
        pl.semaphore_signal(barrier, inc=1, device_id=(t, d), device_id_type=MESH)
    for d in tile_peers:
        pl.semaphore_signal(barrier, inc=1, device_id=(d, s), device_id_type=MESH)

    def token_sums():
        token_cond[...] = jnp.zeros_like(token_cond)
        counts[...] = jnp.zeros_like(counts)

        @pl.loop(0, N_TILE)
        def _(a):
            pre = dot(every_feat[a], atom_w[...])
            token = lax.broadcasted_iota(jnp.int32, (256, 128), 0)
            one_hot = jnp.where(token == every_atom[a], 1.0, 0.0)
            token_cond[...] += dot(one_hot.astype(BF16), (pre * sigmoid(pre)).astype(BF16))
            counts[...] += jnp.sum(one_hot, axis=1, keepdims=True)

        token_cond[...] = token_cond[...] / counts[...]

    def token_norm():
        @pl.loop(0, 4)
        def _(a):
            lanes = pl.ds(pl.multiple_of(a * 128, 128), 128)
            of_token = pl.ds(pl.multiple_of(lax.rem(a, 2) * 128, 128), 128)
            state = tokens[lanes, :].astype(F32) + token_cond[of_token, :]
            normed, inverse = norm_rows(state.T, 0)
            hidden_t[:, lanes] = normed.astype(BF16)
            inverse_h[:, lanes] = inverse

    def token_project(block, out):
        @pl.loop(0, 3)
        def _(a):
            rows = pl.ds(pl.multiple_of(a * 256, 256), 256)
            columns = pl.ds(pl.multiple_of(block * 768 + a * 256, 256), 256)
            result = t_dot(in_w[:, columns], hidden_t[...])
            out[rows, :] = (sigmoid(result) if block == 1 else result).astype(out.dtype)

    def token_upstream():
        @pl.loop(0, 3)
        def _(a):
            rows = pl.ds(pl.multiple_of(a * 256, 256), 256)
            up[rows, :] = dot_t(out_weight[rows, :], cot[...])

    def back_product():
        @pl.loop(0, 2)
        def _(a):
            rows = pl.ds(pl.multiple_of(a * 384, 128), 384)
            d_hidden[rows, :] = dot(in_w[rows, :], d_every[...].reshape(3072, 512))

    def back_norm():
        @pl.loop(0, 4)
        def _(a):
            lanes = pl.ds(pl.multiple_of(a * 128, 128), 128)
            back_t = norm_back_rows(
                hidden_t[:, lanes].astype(F32), inverse_h[:, lanes], d_hidden[:, lanes], 0
            )
            grad_tokens[lanes, :] = cot[lanes, :].astype(F32) + back_t.T

        both = grad_tokens[pl.ds(0, 256), :] + grad_tokens[pl.ds(256, 256), :]
        cond_grad[...] = (both / counts[...]).astype(BF16)

    def back_atoms():
        atom_total[...] = jnp.zeros_like(atom_total)

        @pl.loop(0, N_TILE)
        def _(a):
            feat = every_feat[a]
            pre = dot(feat, atom_w[...])
            part = sigmoid(pre)
            token = lax.broadcasted_iota(jnp.int32, (256, 128), 0)
            one_hot = jnp.where(token == every_atom[a], 1.0, 0.0).astype(BF16)
            d_act = t_dot(one_hot, cond_grad[...]) * (part * (1.0 + pre * (1.0 - part)))
            atom_total[...] += t_dot(feat, d_act.astype(BF16))

        atom_grad[...] = atom_total[...].astype(BF16)

    need(0)
    normed_z = norm_rows(pair[...].astype(F32), 1)[0].astype(BF16)
    need(1, 2)

    def project(block):
        return dot_t(in_w_t[pl.ds(block * 128, 128), :], normed_z)

    for side in range(2):
        value = (sigmoid(project(2 * side)) * project(2 * side + 1) * mask[...]).astype(BF16)
        for d in range(N_SAMPLE):
            x1[d, side] = value[d * 16 : d * 16 + 16]
    need(3, 4)
    pl.semaphore_wait(barrier, N_SAMPLE + N_TILE - 2)
    for d in sample_peers:
        send(x1.at[d], mid.at[s], send_sem.at[0], recv_sem.at[0], t, d)
    for d in tile_peers:
        send(feats, every_feat.at[t], send_sem.at[1], recv_sem.at[1], d, s)
        send(atoms, every_atom.at[t], send_sem.at[2], recv_sem.at[2], d, s)
    every_feat[t] = feats[...]
    every_atom[t] = atoms[...]
    mid[s] = x1[s]
    need(5, 6, 7, 8, 9, 10, 11, 12)
    tri_gate = sigmoid(dot(normed_z, gate_w[...]))
    token_upstream()
    wait_bytes(mid.at[pl.ds(0, N_SAMPLE - 1)], recv_sem.at[0])
    split_lanes(mid[...].reshape(256, 512).astype(F32), mid_rows)
    for d in range(N_TILE):
        for part in range(4):
            x2[d, :, pl.ds(part * 128, 128)] = mid_rows[part, pl.ds(d, 16, stride=16), :].astype(
                BF16
            )
    for d in tile_peers:
        send(x2.at[d], arrived.at[t], send_sem.at[3], recv_sem.at[3], d, s)
    arrived[t] = x2[t]
    wait_bytes(every_feat.at[pl.ds(0, N_TILE - 1)], recv_sem.at[1])
    wait_bytes(every_atom.at[pl.ds(0, N_TILE - 1)], recv_sem.at[2])
    token_sums()
    wait_bytes(arrived.at[pl.ds(0, N_TILE - 1)], recv_sem.at[3])
    split_lanes(arrived[...].reshape(256, 512).astype(F32), arrived_rows)
    panel_of(arrived_rows, 0, 16, panel)
    left[...] = joined(panel).astype(BF16)
    panel_of(arrived_rows, 1, 16, panel)
    right[...] = joined(panel).astype(BF16)
    x3[...] = dot_t(left[...], right[...]).astype(BF16).reshape(N_TILE, 16, 256)
    for d in tile_peers:
        send(x3.at[d], back.at[t], send_sem.at[4], recv_sem.at[4], d, s)
    back[t] = x3[t]
    token_norm()
    wait_bytes(back.at[pl.ds(0, N_TILE - 1)], recv_sem.at[4])
    split_lanes(back[...].reshape(256, 256).astype(F32), back_rows)

    def store(d, lanes, rows):
        x4[d, :, lanes] = rows.astype(BF16)

    blocks_of(back_rows, store)
    for d in sample_peers:
        send(x4.at[d], product.at[s], send_sem.at[5], recv_sem.at[5], t, d)
    product[s] = x4[s]
    token_project(0, q)
    wait_bytes(product.at[pl.ds(0, N_SAMPLE - 1)], recv_sem.at[5])
    normed_p = norm_rows(product[...].reshape(128, 512).astype(F32), 0)[0].astype(BF16)
    linear = t_dot(normed_p, out_w[...])
    following = pair[...].astype(F32) + tri_gate * linear
    pair_next[...] = following
    normed_n = norm_rows(following, 1)[0].astype(BF16)
    head_rows = dot_t(bias_w_t[...], normed_n)
    split_lanes(head_rows, packed)
    for part in range(4):
        rows = [packed[part, pl.ds(h, 4, stride=4), :] for h in range(4)]
        for i in range(4):
            mine[:, part * 4 + i] = place_lanes(rows, i)
    bias[m, c, s] = mine[...].astype(BF16)

    own = bias.at[m, c, s]
    for d in sample_peers:
        send(own, own, send_sem.at[6], recv_sem.at[6], t, d)
    token_project(2, keys)
    wait_bytes(bias.at[m, c, pl.ds(0, N_SAMPLE - 1)], recv_sem.at[6])
    other = m * 2 + 1 - c
    for g in range(4):
        for k in range(1, N_CHIP):
            d = lax.rem(m + k, N_CHIP) * 2 + c
            send(bias.at[m, c, :, g], bias.at[m, c, :, g], send_sem.at[7], chip_in.at[g], d, s)
    token_project(3, v)
    token_project(1, gate)

    def pass_bias(g):
        wait_bytes(bias.at[pl.ds(0, N_CHIP - 1), 0, :, g], chip_in.at[g])
        send(bias.at[:, c, :, g], bias.at[:, c, :, g], send_sem.at[8], core_in.at[g], other, s)

    def add_cores(g):
        wait_bytes(pair_sum.at[:, :, g], core_back.at[g])
        for k in range(1, N_CHIP + 1):
            d = lax.rem(m + k, N_CHIP)
            total = pair_sum[d, :, g].astype(F32) + d_bias[d, c, :, g].astype(F32)
            pair_sum[d, :, g] = total.astype(BF16)
            if k < N_CHIP:
                send(
                    pair_sum.at[d, :, g],
                    by_chip.at[k - 1, :, g],
                    send_sem.at[10],
                    chip_back.at[g],
                    d * 2 + c,
                    s,
                )

    def add_chips(g):
        wait_bytes(by_chip.at[:, :, g], chip_back.at[g])
        total = pair_sum[m, :, g].astype(F32)
        for k in range(N_CHIP - 1):
            total = total + by_chip[k, :, g].astype(F32)
        pair_sum[m, :, g] = total.astype(BF16)
        for k in range(1, N_SAMPLE):
            d = sample_peers[k - 1]
            send(
                pair_sum.at[m, d, g], by_sample.at[k - 1, g], send_sem.at[11], recv_sem.at[7], t, d
            )

    pass_bias(0)
    pass_bias(1)

    @pl.loop(0, 4)
    def _(g):
        wait_bytes(bias.at[:, 0, :, g], core_in.at[g])
        attend(g, q, keys, v, gate, up, bias, gated, d_every, d_bias, bias_rows, bias_total)
        send(d_bias.at[:, 1 - c, :, g], pair_sum.at[:, :, g], send_sem.at[9], core_back.at[g], other, s)

        @pl.when(g < 2)
        def _():
            pass_bias(g + 2)

        @pl.when(g >= 1)
        def _():
            add_cores(g - 1)

        @pl.when(g >= 2)
        def _():
            add_chips(g - 2)

    back_product()
    add_cores(3)
    add_chips(2)
    back_norm()
    add_chips(3)
    back_atoms()
    wait_bytes(by_sample, recv_sem.at[7])
    bias_block[...] = pair_sum[m, s].astype(F32) + jnp.sum(by_sample[...].astype(F32), axis=0)
    wait_bytes(mid.at[pl.ds(0, N_SAMPLE - 1)], send_sem.at[0])
    wait_bytes(every_feat.at[pl.ds(0, N_TILE - 1)], send_sem.at[1])
    wait_bytes(every_atom.at[pl.ds(0, N_TILE - 1)], send_sem.at[2])
    wait_bytes(arrived.at[pl.ds(0, N_TILE - 1)], send_sem.at[3])
    wait_bytes(back.at[pl.ds(0, N_TILE - 1)], send_sem.at[4])
    wait_bytes(product.at[pl.ds(0, N_SAMPLE - 1)], send_sem.at[5])
    wait_bytes(bias.at[m, c, pl.ds(0, N_SAMPLE - 1)], send_sem.at[6])
    wait_bytes(bias.at[pl.ds(0, N_CHIP - 1), 0], send_sem.at[7])
    wait_bytes(bias.at[:, 0], send_sem.at[8])
    wait_bytes(pair_sum, send_sem.at[9])
    wait_bytes(by_chip, send_sem.at[10])
    wait_bytes(by_sample, send_sem.at[11])


def forward(collective_id, *operands):
    vmem = pl.BlockSpec(memory_space=pltpu.VMEM)
    feats, atoms = operands[3:5]
    return pl.pallas_call(
        fetching(forward_kernel, len(operands)),
        out_shape=[
            jax.ShapeDtypeStruct((512, 128), F32),
            jax.ShapeDtypeStruct((256, 256), BF16),
            jax.ShapeDtypeStruct((256, 256), BF16),
            jax.ShapeDtypeStruct((N_SAMPLE, 16, 512), BF16),
            jax.ShapeDtypeStruct((N_TILE,) + feats.shape, feats.dtype),
            jax.ShapeDtypeStruct((N_TILE,) + atoms.shape, atoms.dtype),
            jax.ShapeDtypeStruct((256, 768), F32),
            jax.ShapeDtypeStruct((256, 1), F32),
            jax.ShapeDtypeStruct((768, 512), BF16),
            jax.ShapeDtypeStruct((1, 512), F32),
            jax.ShapeDtypeStruct((768, 512), BF16),
            jax.ShapeDtypeStruct((4, 768, 512), BF16),
            jax.ShapeDtypeStruct((4, 16, 128), F32),
            jax.ShapeDtypeStruct((512, 768), F32),
            jax.ShapeDtypeStruct((128, 768), BF16),
        ],
        in_specs=[pl.BlockSpec(memory_space=pl.ANY)] * len(operands),
        out_specs=[vmem] * 15,
        scratch_shapes=[
            pltpu.VMEM((N_SAMPLE, 2, 16, 512), BF16),
            pltpu.VMEM((N_SAMPLE, 2, 16, 512), BF16),
            pltpu.VMEM((4, 256, 128), F32),
            pltpu.VMEM((N_TILE, 16, 512), BF16),
            pltpu.VMEM((N_TILE, 16, 512), BF16),
            pltpu.VMEM((4, 256, 128), F32),
            pltpu.VMEM((2, 256, 128), F32),
            pltpu.VMEM((N_TILE, 16, 256), BF16),
            pltpu.VMEM((N_TILE, 16, 256), BF16),
            pltpu.VMEM((2, 256, 128), F32),
            pltpu.VMEM((N_SAMPLE, 16, 512), BF16),
            pltpu.VMEM((4, 16, 128), F32),
            pltpu.VMEM((4, 16, 128), F32),
            pltpu.VMEM((N_CHIP, 2, N_SAMPLE, 4, 16, 128), BF16),
            pltpu.VMEM((768, 512), BF16),
            pltpu.VMEM((768, 512), BF16),
            pltpu.VMEM((768, 512), BF16),
            pltpu.VMEM((768, 512), F32),
            pltpu.VMEM((GROUP, 256, 256), F32),
            pltpu.VMEM((GROUP, 256, 256), F32),
            pltpu.VMEM((N_CHIP, 2, N_SAMPLE, 4, 16, 128), BF16),
            pltpu.VMEM((N_CHIP, N_SAMPLE, 4, 16, 128), BF16),
            pltpu.VMEM((N_CHIP - 1, N_SAMPLE, 4, 16, 128), BF16),
            pltpu.VMEM((N_SAMPLE - 1, 4, 16, 128), BF16),
            pltpu.VMEM((768, 512), F32),
            pltpu.VMEM((768, 512), F32),
            pltpu.VMEM((256, 768), BF16),
            pltpu.VMEM((128, 768), F32),
            pltpu.SemaphoreType.DMA((12,)),
            pltpu.SemaphoreType.DMA((8,)),
            pltpu.SemaphoreType.DMA((4,)),
            pltpu.SemaphoreType.DMA((4,)),
            pltpu.SemaphoreType.DMA((4,)),
            pltpu.SemaphoreType.DMA((4,)),
        ]
        + fetch_scratch(operands),
        compiler_params=pltpu.CompilerParams(
            collective_id=collective_id, has_side_effects=True, vmem_limit_bytes=60 << 20
        ),
    )(*operands)


ROWS = 192
WIDTH = 640
SMALL = 1152


def norm_back_rows(normed, inverse, incoming, axis):
    first = jnp.mean(incoming, axis=axis, keepdims=True)
    second = jnp.mean(incoming * normed, axis=axis, keepdims=True)
    return (incoming - first - normed * second) * inverse


def backward_kernel(
    need,
    bias_block,
    right_in,
    left_in,
    left_out,
    right_out,
    pair,
    in_w_t,
    mask,
    gate_w,
    out_w,
    bias_w_t,
    following,
    product,
    left,
    right,
    cot_pair,
    atom_grad,
    grad_pair,
    in_sum,
    out_sum,
    small_sum,
    tri_sum,
    head_rows,
    coefficient,
    keep,
    keep_p,
    x1,
    mid,
    mid_rows,
    x2,
    arrived,
    arrived_rows,
    panel,
    x3,
    back,
    back_rows,
    x4,
    final,
    small,
    small_part,
    small_mid,
    small_last,
    tri,
    tri_part,
    tri_all,
    theirs,
    mine,
    from_core,
    part1,
    sum1,
    part2,
    sum2,
    part3,
    full,
    other,
    send_sem,
    recv_sem,
    w_send,
    w_recv,
):
    t, s = lax.axis_index("tile"), lax.axis_index("sample")
    m, core = t // 2, lax.rem(t, 2)
    partner_t = m * 2 + 1 - core
    place = [lax.rem(s, 2) * 2 + t // 8, lax.rem(t // 2, 4), s // 2]
    tile_peers = [lax.rem(t + k, N_TILE) for k in range(1, N_TILE)]
    sample_peers = [lax.rem(s + k, N_SAMPLE) for k in range(1, N_SAMPLE)]

    def peer(axis, k):
        where = list(place)
        where[axis] = lax.rem(place[axis] + k, 4)
        x, y, z = where
        return where[axis], (lax.rem(x, 2) * 8 + y * 2 + core, z * 2 + x // 2)

    barrier = pltpu.get_barrier_semaphore()
    for d in sample_peers:
        pl.semaphore_signal(barrier, inc=1, device_id=(t, d), device_id_type=MESH)
    for d in tile_peers:
        pl.semaphore_signal(barrier, inc=1, device_id=(d, s), device_id_type=MESH)
    diagonal = (lax.rem(t + 8, N_TILE), s + 1 - 2 * lax.rem(s, 2))
    pl.semaphore_signal(barrier, inc=1, device_id=diagonal, device_id_type=MESH)

    def form(g, c, target):
        wide = pl.ds(pl.multiple_of(g * 1024 + c * 512, 512), 512)
        narrow = pl.ds(pl.multiple_of(g * 256 + c * 128, 128), 128)

        @pl.loop(0, 4)
        def _(a):
            rows = pl.ds(pl.multiple_of(a * ROWS, 64), ROWS)
            target[g, a, :, pl.ds(0, 512)] = dot_t(left_in[rows, :], right_in[wide, :]).astype(BF16)
            target[g, a, :, pl.ds(512, 128)] = dot(left_out[rows, :], right_out[:, narrow]).astype(
                BF16
            )

    def form_mine(g):
        form(g, core, mine)

    def add_cores(g):
        wait_bytes(from_core.at[g], w_recv.at[g, 0])

        @pl.loop(0, 4)
        def _(a):
            @pl.loop(0, ROWS // 16)
            def _(r):
                rows = pl.ds(pl.multiple_of(r * 16, 16), 16)
                total = mine[g, a, rows, :].astype(F32) + from_core[g, a, rows, :].astype(F32)
                mine[g, a, rows, :] = total.astype(BF16)

        for k in range(1, 4):
            d, to = peer(g, k)
            send(mine.at[g, d], part1.at[g, k - 1], w_send.at[1], w_recv.at[g, 1], *to)

    def add_first(g):
        p1 = place[g]
        wait_bytes(part1.at[g], w_recv.at[g, 1])

        @pl.loop(0, ROWS // 16)
        def _(r):
            rows = pl.ds(pl.multiple_of(r * 16, 16), 16)
            total = mine[g, p1, rows, :].astype(F32)
            for k in range(3):
                total = total + part1[g, k, rows, :].astype(F32)
            sum1[g, rows, :] = total.astype(BF16)

        for k in range(1, 4):
            d, to = peer((g + 1) % 3, k)
            rows = pl.ds(pl.multiple_of(d * 48, 16), 48)
            send(sum1.at[g, rows], part2.at[g, k - 1], w_send.at[2], w_recv.at[g, 2], *to)

    def add_second(g):
        p2, p3 = place[(g + 1) % 3], place[(g + 2) % 3]
        wait_bytes(part2.at[g], w_recv.at[g, 2])
        total = sum1[g, pl.ds(pl.multiple_of(p2 * 48, 16), 48), :].astype(F32)
        for k in range(3):
            total = total + part2[g, k].astype(F32)
        sum2[g] = total.astype(BF16)
        for k in range(1, 4):
            _, to = peer((g + 2) % 3, k)
            send(sum2.at[g], part3.at[g, p3], w_send.at[3], w_recv.at[g, 3], *to)
        part3[g, p3] = sum2[g]

    def add_third(g):
        p1, p2 = place[g], place[(g + 1) % 3]
        wait_bytes(part3.at[g, pl.ds(0, 3)], w_recv.at[g, 3])
        total = part3[g, 0].astype(F32)
        for k in range(1, 4):
            total = total + part3[g, k].astype(F32)
        rows = pl.ds(pl.multiple_of(p2 * 48, 16), 48)
        full[g, p1, rows, :] = total.astype(BF16)
        block = full.at[g, p1, rows]
        for k in range(1, 4):
            _, to = peer((g + 1) % 3, k)
            send(block, block, w_send.at[4], w_recv.at[g, 4], *to)

    def gather_second(g):
        p1 = place[g]
        wait_bytes(full.at[g, p1, pl.ds(0, 144)], w_recv.at[g, 4])
        block = full.at[g, p1]
        for k in range(1, 4):
            _, to = peer(g, k)
            send(block, block, w_send.at[5], w_recv.at[g, 5], *to)
        send(block, other.at[g, p1], w_send.at[6], w_recv.at[g, 6], partner_t, s)

    def unpack(source, g, c):
        wide = pl.ds(pl.multiple_of(g * 1024 + c * 512, 512), 512)
        narrow = pl.ds(pl.multiple_of(g * 256 + c * 128, 128), 128)

        @pl.loop(0, 4)
        def _(a):
            @pl.loop(0, ROWS // 16)
            def _(r):
                rows = pl.ds(pl.multiple_of(r * 16, 16), 16)
                to_rows = pl.ds(pl.multiple_of(a * ROWS + r * 16, 16), 16)
                in_sum[to_rows, wide] = source[g, a, rows, pl.ds(0, 512)]
                out_sum[to_rows, narrow] = source[g, a, rows, pl.ds(512, 128)]

    def gather_first(g):
        wait_bytes(full.at[g, pl.ds(0, 3)], w_recv.at[g, 5])
        for k in range(1, 4):
            p1 = lax.rem(place[g] + k, 4)
            send(full.at[g, p1], other.at[g, p1], w_send.at[6], w_recv.at[g, 6], partner_t, s)

    need(1, 2, 3, 4)
    for g in range(3):
        form(g, 1 - core, theirs)
    pl.semaphore_wait(barrier, N_SAMPLE + N_TILE - 1)
    for g in range(3):
        send(theirs.at[g], from_core.at[g], w_send.at[0], w_recv.at[g, 0], partner_t, s)

    need(0, *range(5, 17))
    keep[0], inverse_z = norm_rows(pair[...].astype(F32), 1)
    normed_z = keep[0].astype(BF16)

    def project(block):
        return dot_t(in_w_t[pl.ds(block * 128, 128), :], normed_z)

    keep[1] = sigmoid(dot(normed_z, gate_w[...]))
    keep_p[...], inverse_p = norm_rows(product[...].reshape(128, 512).astype(F32), 0)
    normed_p = keep_p[...].astype(BF16)
    keep[2] = t_dot(normed_p, out_w[...])
    keep[3], inverse_n = norm_rows(following[...], 1)
    normed_n = keep[3].astype(BF16)

    for part in range(4):
        rows = [bias_block[:, part * 4 + i] for i in range(4)]
        for h in range(4):
            head_rows[part, pl.ds(h, 4, stride=4), :] = place_lanes(rows, h)
    d_heads = jnp.concatenate([head_rows[part] for part in range(4)], axis=1)
    high = d_heads.astype(BF16)
    low = (d_heads - high.astype(F32)).astype(BF16)
    d_normed_n = t_dot(high, bias_w_t[...]) + t_dot(low, bias_w_t[...])
    d_next = cot_pair[...].astype(F32) + norm_back_rows(keep[3], inverse_n, d_normed_n, 1)
    tri_gate = keep[1]
    d_linear = (d_next * tri_gate).astype(BF16)
    d_product = norm_back_rows(keep_p[...], inverse_p, dot_t(out_w[...], d_linear), 0).astype(BF16)
    for d in range(N_SAMPLE):
        x1[d] = d_product[d * 16 : d * 16 + 16]
    for d in sample_peers:
        send(x1.at[d], mid.at[s], send_sem.at[3], recv_sem.at[3], t, d)
    mid[s] = x1[s]
    small[...] = jnp.zeros((128, SMALL), BF16)
    small[:, pl.ds(0, 768)] = atom_grad[...]
    small_mid[...] = jnp.zeros((16, N_TILE * 128), BF16)
    d_gate = (d_next * keep[2] * tri_gate * (1.0 - tri_gate)).astype(BF16)
    keep[4] = d_next
    small[:, pl.ds(768, 128)] = t_dot(normed_z, d_gate).astype(BF16)
    small[:, pl.ds(896, 128)] = dot(normed_p, d_linear).astype(BF16)
    small[pl.ds(0, 16), pl.ds(1024, 128)] = (dot(high, normed_n) + dot(low, normed_n)).astype(BF16)
    keep[5] = dot_t(d_gate, gate_w[...])
    form_mine(0)
    add_cores(0)
    wait_bytes(mid.at[pl.ds(0, N_SAMPLE - 1)], recv_sem.at[3])
    split_lanes(mid[...].reshape(128, 512).astype(F32), mid_rows)
    for d in range(N_TILE):
        for part in range(4):
            x2[d, :, pl.ds(part * 128, 128)] = mid_rows[part, pl.ds(d, 8, stride=16), :]
    for d in tile_peers:
        send(x2.at[d], arrived.at[t], send_sem.at[4], recv_sem.at[4], d, s)
    arrived[t] = x2[t]
    form_mine(1)
    add_cores(1)
    form_mine(2)
    add_cores(2)
    for side in range(2):
        gate_side = sigmoid(project(2 * side))
        masked = gate_side * mask[...]
        coefficient[2 * side] = masked * (1.0 - gate_side) * project(2 * side + 1)
        coefficient[2 * side + 1] = masked
    wait_bytes(arrived.at[pl.ds(0, N_TILE - 1)], recv_sem.at[4])
    split_lanes(arrived[...].reshape(128, 512), arrived_rows)
    panel_of(arrived_rows, 0, 8, panel)
    d_panel = joined(panel).astype(BF16)
    x3[:, 0] = dot(d_panel, right[...]).astype(BF16).reshape(N_TILE, 16, 256)
    x3[:, 1] = t_dot(d_panel, left[...]).astype(BF16).reshape(N_TILE, 16, 256)
    for d in tile_peers:
        send(x3.at[d], back.at[t], send_sem.at[5], recv_sem.at[5], d, s)
    back[t] = x3[t]
    add_first(0)
    for k in range(1, N_SAMPLE):
        d = sample_peers[k - 1]
        rows = pl.ds(pl.multiple_of(d * 16, 16), 16)
        send(small.at[rows], small_part.at[k - 1], send_sem.at[7], recv_sem.at[7], t, d)
    own = pl.ds(pl.multiple_of(s * 16, 16), 16)
    wait_bytes(back.at[pl.ds(0, N_TILE - 1)], recv_sem.at[5])
    for side in range(2):
        split_lanes(back[:, side].reshape(256, 256).astype(F32), back_rows)

        def store(d, lanes, rows, side=side):
            x4[d, side, :, lanes] = rows.astype(BF16)

        blocks_of(back_rows, store)
    for d in sample_peers:
        send(x4.at[d], final.at[s], send_sem.at[6], recv_sem.at[6], t, d)
    final[s] = x4[s]
    add_first(1)
    add_first(2)
    wait_bytes(small_part, recv_sem.at[7])
    total = small[own, :].astype(F32)
    for k in range(N_SAMPLE - 1):
        total = total + small_part[k].astype(F32)
    small_mid[:, pl.ds(0, SMALL)] = total.astype(BF16)
    for k in range(1, N_TILE):
        d = tile_peers[k - 1]
        lanes = pl.ds(pl.multiple_of(d * 128, 128), 128)
        send(small_mid.at[:, lanes], small_last.at[k - 1], send_sem.at[8], recv_sem.at[8], d, s)
    wait_bytes(final.at[pl.ds(0, N_SAMPLE - 1)], recv_sem.at[6])
    d_normed_z = keep[5]
    for block in range(4):
        incoming = final[:, block // 2].reshape(128, 512).astype(F32)
        d_proj = (incoming * coefficient[block]).astype(BF16)
        tri[:, pl.ds(block * 128, 128)] = dot(d_proj, normed_z).astype(BF16)
        d_normed_z = d_normed_z + t_dot(d_proj, in_w_t[pl.ds(block * 128, 128), :])
    for k in range(1, N_SAMPLE):
        d = sample_peers[k - 1]
        rows = pl.ds(pl.multiple_of(d * 16, 16), 16)
        send(tri.at[rows], tri_part.at[k - 1], send_sem.at[11], recv_sem.at[11], t, d)
    add_second(0)
    add_second(1)
    add_second(2)
    grad_pair[...] = keep[4] + norm_back_rows(keep[0], inverse_z, d_normed_z, 1)
    wait_bytes(small_last, recv_sem.at[8])
    lanes = pl.ds(pl.multiple_of(t * 128, 128), 128)
    total = small_mid[:, lanes].astype(F32)
    for k in range(N_TILE - 1):
        total = total + small_last[k].astype(F32)
    small_sum[own, lanes] = total.astype(BF16)
    block = small_sum.at[own, lanes]
    for d in tile_peers:
        send(block, block, send_sem.at[9], recv_sem.at[9], d, s)
    wait_bytes(tri_part, recv_sem.at[11])
    total = tri[own, :].astype(F32)
    for k in range(N_SAMPLE - 1):
        total = total + tri_part[k].astype(F32)
    tri_all[t] = total.astype(BF16)
    for d in tile_peers:
        send(tri_all.at[t], tri_all.at[t], send_sem.at[12], recv_sem.at[12], d, s)
    for g in range(3):
        add_third(g)
    for g in range(3):
        gather_second(g)
    wait_bytes(tri_all.at[pl.ds(0, N_TILE - 1)], recv_sem.at[12])
    tri_sum[own, :] = jnp.sum(tri_all[...].astype(F32), axis=0).astype(BF16)
    for d in sample_peers:
        send(tri_sum.at[own], tri_sum.at[own], send_sem.at[13], recv_sem.at[13], t, d)
    wait_bytes(small_last, recv_sem.at[9])
    known = small_sum.at[own, pl.ds(0, SMALL)]
    for d in sample_peers:
        send(known, known, send_sem.at[10], recv_sem.at[10], t, d)
    for g in range(3):
        gather_first(g)
        unpack(full, g, core)
    wait_bytes(small_part, recv_sem.at[10])
    wait_bytes(tri_part, recv_sem.at[13])
    for g in range(3):
        wait_bytes(other.at[g], w_recv.at[g, 6])
        unpack(other, g, 1 - core)

    wait_bytes(mid.at[pl.ds(0, N_SAMPLE - 1)], send_sem.at[3])
    wait_bytes(arrived.at[pl.ds(0, N_TILE - 1)], send_sem.at[4])
    wait_bytes(back.at[pl.ds(0, N_TILE - 1)], send_sem.at[5])
    wait_bytes(final.at[pl.ds(0, N_SAMPLE - 1)], send_sem.at[6])
    wait_bytes(small_part, send_sem.at[7])
    wait_bytes(small_last, send_sem.at[8])
    wait_bytes(small_last, send_sem.at[9])
    wait_bytes(small_part, send_sem.at[10])
    wait_bytes(tri_part, send_sem.at[11])
    wait_bytes(tri_all.at[pl.ds(0, N_TILE - 1)], send_sem.at[12])
    wait_bytes(tri_part, send_sem.at[13])
    wait_bytes(theirs, w_send.at[0])
    wait_bytes(part1, w_send.at[1])
    wait_bytes(part2, w_send.at[2])
    wait_bytes(part3.at[:, pl.ds(0, 3)], w_send.at[3])
    wait_bytes(part2, w_send.at[4])
    wait_bytes(part1, w_send.at[5])
    wait_bytes(theirs, w_send.at[6])


def backward(collective_id, *operands):
    vmem = pl.BlockSpec(memory_space=pltpu.VMEM)
    chunk = (3, 4, ROWS, WIDTH)
    return pl.pallas_call(
        fetching(backward_kernel, len(operands)),
        out_shape=[
            jax.ShapeDtypeStruct((512, 128), F32),
            jax.ShapeDtypeStruct((768, 3072), BF16),
            jax.ShapeDtypeStruct((768, 768), BF16),
            jax.ShapeDtypeStruct((128, N_TILE * 128), BF16),
            jax.ShapeDtypeStruct((128, 512), BF16),
        ],
        in_specs=[pl.BlockSpec(memory_space=pl.ANY)] * len(operands),
        out_specs=[vmem] * 5,
        scratch_shapes=[
            pltpu.VMEM((4, 16, 128), F32),
            pltpu.VMEM((4, 128, 512), F32),
            pltpu.VMEM((6, 512, 128), F32),
            pltpu.VMEM((128, 512), F32),
            pltpu.VMEM((N_SAMPLE, 16, 512), BF16),
            pltpu.VMEM((N_SAMPLE, 16, 512), BF16),
            pltpu.VMEM((4, 128, 128), F32),
            pltpu.VMEM((N_TILE, 8, 512), F32),
            pltpu.VMEM((N_TILE, 8, 512), F32),
            pltpu.VMEM((4, 128, 128), F32),
            pltpu.VMEM((2, 256, 128), F32),
            pltpu.VMEM((N_TILE, 2, 16, 256), BF16),
            pltpu.VMEM((N_TILE, 2, 16, 256), BF16),
            pltpu.VMEM((2, 256, 128), F32),
            pltpu.VMEM((N_SAMPLE, 2, 16, 512), BF16),
            pltpu.VMEM((N_SAMPLE, 2, 16, 512), BF16),
            pltpu.VMEM((128, SMALL), BF16),
            pltpu.VMEM((N_SAMPLE - 1, 16, SMALL), BF16),
            pltpu.VMEM((16, N_TILE * 128), BF16),
            pltpu.VMEM((N_TILE - 1, 16, 128), BF16),
            pltpu.VMEM((128, 512), BF16),
            pltpu.VMEM((N_SAMPLE - 1, 16, 512), BF16),
            pltpu.VMEM((N_TILE, 16, 512), BF16),
            pltpu.VMEM(chunk, BF16),
            pltpu.VMEM(chunk, BF16),
            pltpu.VMEM(chunk, BF16),
            pltpu.VMEM((3, 3, ROWS, WIDTH), BF16),
            pltpu.VMEM((3, ROWS, WIDTH), BF16),
            pltpu.VMEM((3, 3, 48, WIDTH), BF16),
            pltpu.VMEM((3, 48, WIDTH), BF16),
            pltpu.VMEM((3, 4, 48, WIDTH), BF16),
            pltpu.VMEM(chunk, BF16),
            pltpu.VMEM(chunk, BF16),
            pltpu.SemaphoreType.DMA((14,)),
            pltpu.SemaphoreType.DMA((14,)),
            pltpu.SemaphoreType.DMA((7,)),
            pltpu.SemaphoreType.DMA((3, 7)),
        ]
        + fetch_scratch(operands),
        compiler_params=pltpu.CompilerParams(
            collective_id=collective_id, has_side_effects=True, vmem_limit_bytes=60 << 20
        ),
    )(*operands)


def widen_kernel(wide, narrow, wide_out, narrow_out):
    wide_out[...] = wide[...].astype(F32)
    narrow_out[...] = narrow[...].astype(F32)


def widen(wide, narrow):
    steps = 6
    specs = [
        pl.BlockSpec((x.shape[0] // steps, x.shape[1]), lambda i: (i, 0)) for x in (wide, narrow)
    ]
    return pl.pallas_call(
        widen_kernel,
        grid=(steps,),
        in_specs=specs,
        out_specs=specs,
        out_shape=[jax.ShapeDtypeStruct(x.shape, F32) for x in (wide, narrow)],
        compiler_params=pltpu.CompilerParams(vmem_limit_bytes=62 << 20),
    )(wide, narrow)


def shards(
    pair,
    pair_mask,
    tri_in_w,
    tri_gate_w,
    tri_out_w,
    bias_w,
    atom_feats,
    atom_to_token,
    atom_w,
    tokens,
    attention_input_weight,
    attention_output_weight,
    cot_pair,
    token_output_cotangent,
):
    hidden = tri_in_w.shape[1] // 4
    token_width = attention_input_weight.shape[0]
    head_count = bias_w.shape[1]
    total_tokens = tokens.shape[1]
    pair_rows = pair.reshape(-1, hidden)
    mask_row = pair_mask.astype(F32).reshape(1, -1)
    in_w_t, bias_w_t = tri_in_w.T, bias_w.T
    token_rows = tokens.reshape(-1, token_width)
    cot_rows = token_output_cotangent.reshape(-1, token_width)
    (
        following,
        left_panel,
        right_panel,
        product,
        every_feat,
        every_atom,
        token_cond,
        token_counts,
        hidden_t,
        inverse_h,
        gated_t,
        d_every_t,
        bias_block,
        grad_tokens,
        atom_grad,
    ) = forward(
        0,
        pair_rows,
        in_w_t,
        mask_row,
        atom_feats,
        atom_to_token[None],
        tri_gate_w,
        tri_out_w,
        bias_w_t,
        atom_w,
        token_rows,
        attention_input_weight,
        attention_output_weight,
        cot_rows,
    )
    d_every_t = d_every_t.reshape(4 * token_width, -1)
    token_output_rows = (
        tokens.astype(F32)
        + token_cond[None]
        + t_dot(gated_t, attention_output_weight).reshape(tokens.shape)
    )
    grad_pair, in_sum, out_sum, small_sum, tri_sum = backward(
        1,
        bias_block,
        d_every_t,
        hidden_t,
        gated_t,
        cot_rows,
        pair_rows,
        in_w_t,
        mask_row,
        tri_gate_w,
        tri_out_w,
        bias_w_t,
        following,
        product,
        left_panel,
        right_panel,
        cot_pair.reshape(-1, hidden),
        atom_grad,
    )
    grad_tokens = grad_tokens.reshape(tokens.shape)
    small_sum = small_sum.astype(F32)
    at = token_width
    summed = (
        tri_sum.astype(F32)
        .reshape(hidden, 4, hidden)
        .transpose(2, 1, 0)
        .reshape(hidden, 4 * hidden),
        small_sum[:, at : at + hidden],
        small_sum[:, at + hidden : at + 2 * hidden],
        small_sum[:head_count, at + 2 * hidden : at + 3 * hidden].T,
        small_sum[:, :at],
        *widen(in_sum, out_sum),
    )
    pair_next, grad_pair = following.reshape(pair.shape), grad_pair.reshape(pair.shape)
    return (pair_next, token_output_rows, grad_pair, grad_tokens) + summed


def solution(mesh):
    in_specs = (
        P("tile", "sample", None),
        P("tile", "sample"),
        P(),
        P(),
        P(),
        P(),
        P("tile", None),
        P("tile"),
        P(),
        P(("tile", "sample"), None, None),
        P(),
        P(),
        P("tile", "sample", None),
        P(("tile", "sample"), None, None),
    )
    out_specs = (
        P("tile", "sample", None),
        P(("tile", "sample"), None, None),
        P("tile", "sample", None),
        P(("tile", "sample"), None, None),
        P(),
        P(),
        P(),
        P(),
        P(),
        P(),
        P(),
    )
    return jax.shard_map(shards, mesh=mesh, in_specs=in_specs, out_specs=out_specs, check_vma=False)
```

```python
import functools
import math

import jax
import jax.numpy as jnp
from jax import lax
from jax.experimental import pallas as pl
from jax.experimental.pallas import tpu as pltpu
from jax.sharding import PartitionSpec as P

EPSILON = 1e-05
N_TILE = 16
N_SAMPLE = 8
N_CHIP = 8
MESH = pl.DeviceIdType.MESH
BF16 = jnp.bfloat16
F32 = jnp.float32
HIGHEST = lax.Precision.HIGHEST


def wait_bytes(ref, sem):
    pltpu.make_async_copy(ref, ref, sem).wait()


def send(src, dst, send_sem, recv_sem, t, s):
    pltpu.make_async_remote_copy(
        src, dst, send_sem, recv_sem, device_id=(t, s), device_id_type=MESH
    ).start()


def dot(a, b):
    return jnp.dot(a, b, preferred_element_type=F32)


def dot_t(a, b):
    return lax.dot_general(a, b, (((1,), (1,)), ((), ())), preferred_element_type=F32)


def t_dot(a, b):
    return lax.dot_general(a, b, (((0,), (0,)), ((), ())), preferred_element_type=F32)


HEAD = 48
GROUP = 4
LANES = 32


def fetching(kernel, count):
    def run(*refs):
        sources, rest, buffers, sem = refs[:count], refs[count : -count - 1], refs[-count - 1 : -1], refs[-1]
        copies = [
            pltpu.make_async_copy(source, buffer, sem.at[i])
            for i, (source, buffer) in enumerate(zip(sources, buffers))
        ]
        for copy in copies:
            copy.start()

        def need(*which):
            for i in which:
                copies[i].wait()

        kernel(need, *buffers, *rest)

    return run


def fetch_scratch(operands):
    return [pltpu.VMEM(x.shape, x.dtype) for x in operands] + [
        pltpu.SemaphoreType.DMA((len(operands),))
    ]


def place_lanes(parts, first):
    group_of = lax.broadcasted_iota(jnp.int32, parts[0].shape, 1) // LANES
    result = None
    for i in range(4):
        shift = (i - first) % 4 * LANES
        moved = pltpu.roll(parts[i], shift, 1) if shift else parts[i]
        result = moved if result is None else jnp.where(group_of == i, moved, result)
    return result


def panel_of(arrived, first, step, panel):
    for part in range(4):
        rows = [
            arrived[part, pl.ds(first + s * (step // 8), 16, stride=step), :] for s in range(8)
        ]
        for i in range(4):
            for half in range(2):
                panel[half, pl.ds(part * 4 + i, 16, stride=16), :] = place_lanes(
                    rows[half * 4 : half * 4 + 4], i
                )


def blocks_of(panel, store):
    for half in range(2):
        for part in range(4):
            rows = [panel[half, pl.ds(part * 4 + i, 16, stride=16), :] for i in range(4)]
            for q in range(4):
                store(half * 4 + q, pl.ds(part * 128, 128), place_lanes(rows, q))


def split_lanes(values, ref):
    for part in range(ref.shape[0]):
        ref[part] = values[:, part * 128 : part * 128 + 128]


def joined(ref):
    return jnp.concatenate([ref[0], ref[1]], axis=1)


def norm_rows(values, axis):
    centered = values - jnp.mean(values, axis=axis, keepdims=True)
    inverse = lax.rsqrt(jnp.mean(centered * centered, axis=axis, keepdims=True) + EPSILON)
    return centered * inverse, inverse


def sigmoid(values):
    return 1.0 / (1.0 + jnp.exp(-values))


def attend(group, q, k, v, gate, up, bias, gated, d_every, d_bias, bias_rows, bias_total):
    tokens = bias_rows.shape[1]
    scale = 1.0 / math.sqrt(HEAD)
    group_of = lax.broadcasted_iota(jnp.int32, (tokens, 128), 1) // LANES

    for half in range(2):
        parts = [
            bias[:, :, half * 4 + i, group].reshape(tokens, 128).astype(F32) for i in range(4)
        ]
        for h in range(GROUP):
            row = parts[0] if h == 0 else pltpu.roll(parts[0], (-h) % 4 * LANES, 1)
            for i in range(1, 4):
                shift = (i - h) % 4 * LANES
                moved = pltpu.roll(parts[i], shift, 1) if shift else parts[i]
                row = jnp.where(group_of == i, moved, row)
            bias_rows[h, :, pl.ds(half * 128, 128)] = row

    @pl.loop(0, GROUP)
    def _(h):
        rows = pl.ds(pl.multiple_of(group * GROUP * HEAD + h * HEAD, 16), HEAD)
        for sample in range(2):
            columns = pl.ds(sample * tokens, tokens)
            qh, kh, vh = q[rows, columns], k[rows, columns], v[rows, columns]
            scores = t_dot(qh, kh) * scale + bias_rows[h]
            weights = jnp.exp(scores - jnp.max(scores, axis=1, keepdims=True))
            probs = weights * (1.0 / jnp.sum(weights, axis=1, keepdims=True))
            probs_b = probs.astype(BF16)
            attended = dot_t(vh, probs_b)
            gate_h, up_h = gate[rows, columns], up[rows, columns]
            gated[rows, columns] = (gate_h * attended).astype(BF16)
            d_att = (up_h * gate_h).astype(BF16)
            d_every[1, rows, columns] = (up_h * attended * gate_h * (1.0 - gate_h)).astype(BF16)
            d_probs = t_dot(d_att, vh)
            inner = jnp.sum(probs * d_probs, axis=1, keepdims=True)
            d_scores = probs * (d_probs - inner)
            d_scores_b = d_scores.astype(BF16)
            d_every[0, rows, columns] = (dot_t(kh, d_scores_b) * scale).astype(BF16)
            d_every[2, rows, columns] = (dot(qh, d_scores_b) * scale).astype(BF16)
            d_every[3, rows, columns] = dot(d_att, probs_b).astype(BF16)
            if sample == 0:
                bias_total[h] = d_scores
            else:
                bias_total[h] = bias_total[h] + d_scores

    for half in range(2):
        parts = [bias_total[h, :, pl.ds(half * 128, 128)] for h in range(GROUP)]
        for i in range(4):
            row = parts[0] if i == 0 else pltpu.roll(parts[0], (-i) % 4 * LANES, 1)
            for h in range(1, GROUP):
                shift = (h - i) % 4 * LANES
                moved = pltpu.roll(parts[h], shift, 1) if shift else parts[h]
                row = jnp.where(group_of == h, moved, row)
            d_bias[:, :, half * 4 + i, group] = row.astype(BF16).reshape(N_CHIP, 2, 16, 128)


def forward_kernel(
    need,
    pair,
    in_w_t,
    mask,
    feats,
    atoms,
    gate_w,
    out_w,
    bias_w_t,
    atom_w,
    tokens,
    in_w,
    out_weight,
    cot,
    pair_next,
    left,
    right,
    product,
    every_feat,
    every_atom,
    token_cond,
    counts,
    hidden_t,
    inverse_h,
    gated,
    d_every,
    bias_block,
    grad_tokens,
    atom_grad,
    x1,
    mid,
    mid_rows,
    x2,
    arrived,
    arrived_rows,
    panel,
    x3,
    back,
    back_rows,
    x4,
    packed,
    mine,
    bias,
    q,
    keys,
    v,
    gate,
    bias_rows,
    bias_total,
    d_bias,
    pair_sum,
    by_chip,
    by_sample,
    up,
    d_hidden,
    cond_grad,
    atom_total,
    send_sem,
    recv_sem,
    chip_in,
    core_in,
    core_back,
    chip_back,
):
    t, s = lax.axis_index("tile"), lax.axis_index("sample")
    m, c = t // 2, lax.rem(t, 2)
    barrier = pltpu.get_barrier_semaphore()
    tile_peers = [lax.rem(t + k, N_TILE) for k in range(1, N_TILE)]
    sample_peers = [lax.rem(s + k, N_SAMPLE) for k in range(1, N_SAMPLE)]
    for d in sample_peers:
        pl.semaphore_signal(barrier, inc=1, device_id=(t, d), device_id_type=MESH)
    for d in tile_peers:
        pl.semaphore_signal(barrier, inc=1, device_id=(d, s), device_id_type=MESH)

    def token_sums():
        token_cond[...] = jnp.zeros_like(token_cond)
        counts[...] = jnp.zeros_like(counts)

        @pl.loop(0, N_TILE)
        def _(a):
            pre = dot(every_feat[a], atom_w[...])
            token = lax.broadcasted_iota(jnp.int32, (256, 128), 0)
            one_hot = jnp.where(token == every_atom[a], 1.0, 0.0)
            token_cond[...] += dot(one_hot.astype(BF16), (pre * sigmoid(pre)).astype(BF16))
            counts[...] += jnp.sum(one_hot, axis=1, keepdims=True)

        token_cond[...] = token_cond[...] / counts[...]

    def token_norm():
        @pl.loop(0, 4)
        def _(a):
            lanes = pl.ds(pl.multiple_of(a * 128, 128), 128)
            of_token = pl.ds(pl.multiple_of(lax.rem(a, 2) * 128, 128), 128)
            state = tokens[lanes, :].astype(F32) + token_cond[of_token, :]
            normed, inverse = norm_rows(state.T, 0)
            hidden_t[:, lanes] = normed.astype(BF16)
            inverse_h[:, lanes] = inverse

    def token_project(block, out):
        @pl.loop(0, 3)
        def _(a):
            rows = pl.ds(pl.multiple_of(a * 256, 256), 256)
            columns = pl.ds(pl.multiple_of(block * 768 + a * 256, 256), 256)
            result = t_dot(in_w[:, columns], hidden_t[...])
            out[rows, :] = (sigmoid(result) if block == 1 else result).astype(out.dtype)

    def token_upstream():
        @pl.loop(0, 3)
        def _(a):
            rows = pl.ds(pl.multiple_of(a * 256, 256), 256)
            up[rows, :] = dot_t(out_weight[rows, :], cot[...])

    def back_product():
        @pl.loop(0, 2)
        def _(a):
            rows = pl.ds(pl.multiple_of(a * 384, 128), 384)
            d_hidden[rows, :] = dot(in_w[rows, :], d_every[...].reshape(3072, 512))

    def back_norm():
        @pl.loop(0, 4)
        def _(a):
            lanes = pl.ds(pl.multiple_of(a * 128, 128), 128)
            back_t = norm_back_rows(
                hidden_t[:, lanes].astype(F32), inverse_h[:, lanes], d_hidden[:, lanes], 0
            )
            grad_tokens[lanes, :] = cot[lanes, :].astype(F32) + back_t.T

        both = grad_tokens[pl.ds(0, 256), :] + grad_tokens[pl.ds(256, 256), :]
        cond_grad[...] = (both / counts[...]).astype(BF16)

    def back_atoms():
        atom_total[...] = jnp.zeros_like(atom_total)

        @pl.loop(0, N_TILE)
        def _(a):
            feat = every_feat[a]
            pre = dot(feat, atom_w[...])
            part = sigmoid(pre)
            token = lax.broadcasted_iota(jnp.int32, (256, 128), 0)
            one_hot = jnp.where(token == every_atom[a], 1.0, 0.0).astype(BF16)
            d_act = t_dot(one_hot, cond_grad[...]) * (part * (1.0 + pre * (1.0 - part)))
            atom_total[...] += t_dot(feat, d_act.astype(BF16))

        atom_grad[...] = atom_total[...].astype(BF16)

    need(0)
    normed_z = norm_rows(pair[...].astype(F32), 1)[0].astype(BF16)
    need(1, 2)

    def project(block):
        return dot_t(in_w_t[pl.ds(block * 128, 128), :], normed_z)

    for side in range(2):
        value = (sigmoid(project(2 * side)) * project(2 * side + 1) * mask[...]).astype(BF16)
        for d in range(N_SAMPLE):
            x1[d, side] = value[d * 16 : d * 16 + 16]
    need(3, 4)
    pl.semaphore_wait(barrier, N_SAMPLE + N_TILE - 2)
    for d in sample_peers:
        send(x1.at[d], mid.at[s], send_sem.at[0], recv_sem.at[0], t, d)
    for d in tile_peers:
        send(feats, every_feat.at[t], send_sem.at[1], recv_sem.at[1], d, s)
        send(atoms, every_atom.at[t], send_sem.at[2], recv_sem.at[2], d, s)
    every_feat[t] = feats[...]
    every_atom[t] = atoms[...]
    mid[s] = x1[s]
    need(5, 6, 7, 8, 9, 10, 11, 12)
    tri_gate = sigmoid(dot(normed_z, gate_w[...]))
    token_upstream()
    wait_bytes(mid.at[pl.ds(0, N_SAMPLE - 1)], recv_sem.at[0])
    split_lanes(mid[...].reshape(256, 512).astype(F32), mid_rows)
    for d in range(N_TILE):
        for part in range(4):
            x2[d, :, pl.ds(part * 128, 128)] = mid_rows[part, pl.ds(d, 16, stride=16), :].astype(
                BF16
            )
    for d in tile_peers:
        send(x2.at[d], arrived.at[t], send_sem.at[3], recv_sem.at[3], d, s)
    arrived[t] = x2[t]
    wait_bytes(every_feat.at[pl.ds(0, N_TILE - 1)], recv_sem.at[1])
    wait_bytes(every_atom.at[pl.ds(0, N_TILE - 1)], recv_sem.at[2])
    token_sums()
    wait_bytes(arrived.at[pl.ds(0, N_TILE - 1)], recv_sem.at[3])
    split_lanes(arrived[...].reshape(256, 512).astype(F32), arrived_rows)
    panel_of(arrived_rows, 0, 16, panel)
    left[...] = joined(panel).astype(BF16)
    panel_of(arrived_rows, 1, 16, panel)
    right[...] = joined(panel).astype(BF16)
    x3[...] = dot_t(left[...], right[...]).astype(BF16).reshape(N_TILE, 16, 256)
    for d in tile_peers:
        send(x3.at[d], back.at[t], send_sem.at[4], recv_sem.at[4], d, s)
    back[t] = x3[t]
    token_norm()
    wait_bytes(back.at[pl.ds(0, N_TILE - 1)], recv_sem.at[4])
    split_lanes(back[...].reshape(256, 256).astype(F32), back_rows)

    def store(d, lanes, rows):
        x4[d, :, lanes] = rows.astype(BF16)

    blocks_of(back_rows, store)
    for d in sample_peers:
        send(x4.at[d], product.at[s], send_sem.at[5], recv_sem.at[5], t, d)
    product[s] = x4[s]
    token_project(0, q)
    wait_bytes(product.at[pl.ds(0, N_SAMPLE - 1)], recv_sem.at[5])
    normed_p = norm_rows(product[...].reshape(128, 512).astype(F32), 0)[0].astype(BF16)
    linear = t_dot(normed_p, out_w[...])
    following = pair[...].astype(F32) + tri_gate * linear
    pair_next[...] = following
    normed_n = norm_rows(following, 1)[0].astype(BF16)
    head_rows = dot_t(bias_w_t[...], normed_n)
    split_lanes(head_rows, packed)
    for part in range(4):
        rows = [packed[part, pl.ds(h, 4, stride=4), :] for h in range(4)]
        for i in range(4):
            mine[:, part * 4 + i] = place_lanes(rows, i)
    bias[m, c, s] = mine[...].astype(BF16)

    own = bias.at[m, c, s]
    for d in sample_peers:
        send(own, own, send_sem.at[6], recv_sem.at[6], t, d)
    token_project(2, keys)
    wait_bytes(bias.at[m, c, pl.ds(0, N_SAMPLE - 1)], recv_sem.at[6])
    other = m * 2 + 1 - c
    for g in range(4):
        for k in range(1, N_CHIP):
            d = lax.rem(m + k, N_CHIP) * 2 + c
            send(bias.at[m, c, :, g], bias.at[m, c, :, g], send_sem.at[7], chip_in.at[g], d, s)
    token_project(3, v)

    def pass_bias(g):
        wait_bytes(bias.at[pl.ds(0, N_CHIP - 1), 0, :, g], chip_in.at[g])
        send(bias.at[:, c, :, g], bias.at[:, c, :, g], send_sem.at[8], core_in.at[g], other, s)

    def add_cores(g):
        wait_bytes(pair_sum.at[:, :, g], core_back.at[g])
        for k in range(1, N_CHIP + 1):
            d = lax.rem(m + k, N_CHIP)
            total = pair_sum[d, :, g].astype(F32) + d_bias[d, c, :, g].astype(F32)
            pair_sum[d, :, g] = total.astype(BF16)
            if k < N_CHIP:
                send(
                    pair_sum.at[d, :, g],
                    by_chip.at[k - 1, :, g],
                    send_sem.at[10],
                    chip_back.at[g],
                    d * 2 + c,
                    s,
                )

    def add_chips(g):
        wait_bytes(by_chip.at[:, :, g], chip_back.at[g])
        total = pair_sum[m, :, g].astype(F32)
        for k in range(N_CHIP - 1):
            total = total + by_chip[k, :, g].astype(F32)
        pair_sum[m, :, g] = total.astype(BF16)
        for k in range(1, N_SAMPLE):
            d = sample_peers[k - 1]
            send(
                pair_sum.at[m, d, g], by_sample.at[k - 1, g], send_sem.at[11], recv_sem.at[7], t, d
            )

    pass_bias(0)
    token_project(1, gate)
    pass_bias(1)

    @pl.loop(0, 4)
    def _(g):
        wait_bytes(bias.at[:, 0, :, g], core_in.at[g])
        attend(g, q, keys, v, gate, up, bias, gated, d_every, d_bias, bias_rows, bias_total)
        send(d_bias.at[:, 1 - c, :, g], pair_sum.at[:, :, g], send_sem.at[9], core_back.at[g], other, s)

        @pl.when(g < 2)
        def _():
            pass_bias(g + 2)

        @pl.when(g >= 1)
        def _():
            add_cores(g - 1)

        @pl.when(g >= 2)
        def _():
            add_chips(g - 2)

    back_product()
    add_cores(3)
    add_chips(2)
    back_norm()
    add_chips(3)
    back_atoms()
    wait_bytes(by_sample, recv_sem.at[7])
    bias_block[...] = pair_sum[m, s].astype(F32) + jnp.sum(by_sample[...].astype(F32), axis=0)
    wait_bytes(mid.at[pl.ds(0, N_SAMPLE - 1)], send_sem.at[0])
    wait_bytes(every_feat.at[pl.ds(0, N_TILE - 1)], send_sem.at[1])
    wait_bytes(every_atom.at[pl.ds(0, N_TILE - 1)], send_sem.at[2])
    wait_bytes(arrived.at[pl.ds(0, N_TILE - 1)], send_sem.at[3])
    wait_bytes(back.at[pl.ds(0, N_TILE - 1)], send_sem.at[4])
    wait_bytes(product.at[pl.ds(0, N_SAMPLE - 1)], send_sem.at[5])
    wait_bytes(bias.at[m, c, pl.ds(0, N_SAMPLE - 1)], send_sem.at[6])
    wait_bytes(bias.at[pl.ds(0, N_CHIP - 1), 0], send_sem.at[7])
    wait_bytes(bias.at[:, 0], send_sem.at[8])
    wait_bytes(pair_sum, send_sem.at[9])
    wait_bytes(by_chip, send_sem.at[10])
    wait_bytes(by_sample, send_sem.at[11])


def forward(collective_id, *operands):
    vmem = pl.BlockSpec(memory_space=pltpu.VMEM)
    feats, atoms = operands[3:5]
    return pl.pallas_call(
        fetching(forward_kernel, len(operands)),
        out_shape=[
            jax.ShapeDtypeStruct((512, 128), F32),
            jax.ShapeDtypeStruct((256, 256), BF16),
            jax.ShapeDtypeStruct((256, 256), BF16),
            jax.ShapeDtypeStruct((N_SAMPLE, 16, 512), BF16),
            jax.ShapeDtypeStruct((N_TILE,) + feats.shape, feats.dtype),
            jax.ShapeDtypeStruct((N_TILE,) + atoms.shape, atoms.dtype),
            jax.ShapeDtypeStruct((256, 768), F32),
            jax.ShapeDtypeStruct((256, 1), F32),
            jax.ShapeDtypeStruct((768, 512), BF16),
            jax.ShapeDtypeStruct((1, 512), F32),
            jax.ShapeDtypeStruct((768, 512), BF16),
            jax.ShapeDtypeStruct((4, 768, 512), BF16),
            jax.ShapeDtypeStruct((4, 16, 128), F32),
            jax.ShapeDtypeStruct((512, 768), F32),
            jax.ShapeDtypeStruct((128, 768), BF16),
        ],
        in_specs=[pl.BlockSpec(memory_space=pl.ANY)] * len(operands),
        out_specs=[vmem] * 15,
        scratch_shapes=[
            pltpu.VMEM((N_SAMPLE, 2, 16, 512), BF16),
            pltpu.VMEM((N_SAMPLE, 2, 16, 512), BF16),
            pltpu.VMEM((4, 256, 128), F32),
            pltpu.VMEM((N_TILE, 16, 512), BF16),
            pltpu.VMEM((N_TILE, 16, 512), BF16),
            pltpu.VMEM((4, 256, 128), F32),
            pltpu.VMEM((2, 256, 128), F32),
            pltpu.VMEM((N_TILE, 16, 256), BF16),
            pltpu.VMEM((N_TILE, 16, 256), BF16),
            pltpu.VMEM((2, 256, 128), F32),
            pltpu.VMEM((N_SAMPLE, 16, 512), BF16),
            pltpu.VMEM((4, 16, 128), F32),
            pltpu.VMEM((4, 16, 128), F32),
            pltpu.VMEM((N_CHIP, 2, N_SAMPLE, 4, 16, 128), BF16),
            pltpu.VMEM((768, 512), BF16),
            pltpu.VMEM((768, 512), BF16),
            pltpu.VMEM((768, 512), BF16),
            pltpu.VMEM((768, 512), F32),
            pltpu.VMEM((GROUP, 256, 256), F32),
            pltpu.VMEM((GROUP, 256, 256), F32),
            pltpu.VMEM((N_CHIP, 2, N_SAMPLE, 4, 16, 128), BF16),
            pltpu.VMEM((N_CHIP, N_SAMPLE, 4, 16, 128), BF16),
            pltpu.VMEM((N_CHIP - 1, N_SAMPLE, 4, 16, 128), BF16),
            pltpu.VMEM((N_SAMPLE - 1, 4, 16, 128), BF16),
            pltpu.VMEM((768, 512), F32),
            pltpu.VMEM((768, 512), F32),
            pltpu.VMEM((256, 768), BF16),
            pltpu.VMEM((128, 768), F32),
            pltpu.SemaphoreType.DMA((12,)),
            pltpu.SemaphoreType.DMA((8,)),
            pltpu.SemaphoreType.DMA((4,)),
            pltpu.SemaphoreType.DMA((4,)),
            pltpu.SemaphoreType.DMA((4,)),
            pltpu.SemaphoreType.DMA((4,)),
        ]
        + fetch_scratch(operands),
        compiler_params=pltpu.CompilerParams(
            collective_id=collective_id, has_side_effects=True, vmem_limit_bytes=60 << 20
        ),
    )(*operands)


ROWS = 192
WIDTH = 640
SMALL = 1152


def norm_back_rows(normed, inverse, incoming, axis):
    first = jnp.mean(incoming, axis=axis, keepdims=True)
    second = jnp.mean(incoming * normed, axis=axis, keepdims=True)
    return (incoming - first - normed * second) * inverse


def backward_kernel(
    need,
    bias_block,
    right_in,
    left_in,
    left_out,
    right_out,
    pair,
    in_w_t,
    mask,
    gate_w,
    out_w,
    bias_w_t,
    following,
    product,
    left,
    right,
    cot_pair,
    atom_grad,
    grad_pair,
    in_sum,
    out_sum,
    small_sum,
    tri_sum,
    head_rows,
    coefficient,
    keep,
    keep_p,
    x1,
    mid,
    mid_rows,
    x2,
    arrived,
    arrived_rows,
    panel,
    x3,
    back,
    back_rows,
    x4,
    final,
    small,
    small_part,
    small_mid,
    small_last,
    tri,
    tri_part,
    tri_all,
    theirs,
    mine,
    from_core,
    part1,
    sum1,
    part2,
    sum2,
    part3,
    full,
    other,
    send_sem,
    recv_sem,
    w_send,
    w_recv,
):
    t, s = lax.axis_index("tile"), lax.axis_index("sample")
    m, core = t // 2, lax.rem(t, 2)
    partner_t = m * 2 + 1 - core
    place = [lax.rem(s, 2) * 2 + t // 8, lax.rem(t // 2, 4), s // 2]
    tile_peers = [lax.rem(t + k, N_TILE) for k in range(1, N_TILE)]
    sample_peers = [lax.rem(s + k, N_SAMPLE) for k in range(1, N_SAMPLE)]

    def peer(axis, k):
        where = list(place)
        where[axis] = lax.rem(place[axis] + k, 4)
        x, y, z = where
        return where[axis], (lax.rem(x, 2) * 8 + y * 2 + core, z * 2 + x // 2)

    barrier = pltpu.get_barrier_semaphore()
    for d in sample_peers:
        pl.semaphore_signal(barrier, inc=1, device_id=(t, d), device_id_type=MESH)
    for d in tile_peers:
        pl.semaphore_signal(barrier, inc=1, device_id=(d, s), device_id_type=MESH)
    diagonal = (lax.rem(t + 8, N_TILE), s + 1 - 2 * lax.rem(s, 2))
    pl.semaphore_signal(barrier, inc=1, device_id=diagonal, device_id_type=MESH)

    def form(g, c, target):
        wide = pl.ds(pl.multiple_of(g * 1024 + c * 512, 512), 512)
        narrow = pl.ds(pl.multiple_of(g * 256 + c * 128, 128), 128)

        @pl.loop(0, 4)
        def _(a):
            rows = pl.ds(pl.multiple_of(a * ROWS, 64), ROWS)
            target[g, a, :, pl.ds(0, 512)] = dot_t(left_in[rows, :], right_in[wide, :]).astype(BF16)
            target[g, a, :, pl.ds(512, 128)] = dot(left_out[rows, :], right_out[:, narrow]).astype(
                BF16
            )

    def form_mine(g):
        form(g, core, mine)

    def add_cores(g):
        wait_bytes(from_core.at[g], w_recv.at[g, 0])

        @pl.loop(0, 4)
        def _(a):
            @pl.loop(0, ROWS // 16)
            def _(r):
                rows = pl.ds(pl.multiple_of(r * 16, 16), 16)
                total = mine[g, a, rows, :].astype(F32) + from_core[g, a, rows, :].astype(F32)
                mine[g, a, rows, :] = total.astype(BF16)

        for k in range(1, 4):
            d, to = peer(g, k)
            send(mine.at[g, d], part1.at[g, k - 1], w_send.at[1], w_recv.at[g, 1], *to)

    def add_first(g):
        p1 = place[g]
        wait_bytes(part1.at[g], w_recv.at[g, 1])

        @pl.loop(0, ROWS // 16)
        def _(r):
            rows = pl.ds(pl.multiple_of(r * 16, 16), 16)
            total = mine[g, p1, rows, :].astype(F32)
            for k in range(3):
                total = total + part1[g, k, rows, :].astype(F32)
            sum1[g, rows, :] = total.astype(BF16)

        for k in range(1, 4):
            d, to = peer((g + 1) % 3, k)
            rows = pl.ds(pl.multiple_of(d * 48, 16), 48)
            send(sum1.at[g, rows], part2.at[g, k - 1], w_send.at[2], w_recv.at[g, 2], *to)

    def add_second(g):
        p2, p3 = place[(g + 1) % 3], place[(g + 2) % 3]
        wait_bytes(part2.at[g], w_recv.at[g, 2])
        total = sum1[g, pl.ds(pl.multiple_of(p2 * 48, 16), 48), :].astype(F32)
        for k in range(3):
            total = total + part2[g, k].astype(F32)
        sum2[g] = total.astype(BF16)
        for k in range(1, 4):
            _, to = peer((g + 2) % 3, k)
            send(sum2.at[g], part3.at[g, p3], w_send.at[3], w_recv.at[g, 3], *to)
        part3[g, p3] = sum2[g]

    def add_third(g):
        p1, p2 = place[g], place[(g + 1) % 3]
        wait_bytes(part3.at[g, pl.ds(0, 3)], w_recv.at[g, 3])
        total = part3[g, 0].astype(F32)
        for k in range(1, 4):
            total = total + part3[g, k].astype(F32)
        rows = pl.ds(pl.multiple_of(p2 * 48, 16), 48)
        full[g, p1, rows, :] = total.astype(BF16)
        block = full.at[g, p1, rows]
        for k in range(1, 4):
            _, to = peer((g + 1) % 3, k)
            send(block, block, w_send.at[4], w_recv.at[g, 4], *to)

    def gather_second(g):
        p1 = place[g]
        wait_bytes(full.at[g, p1, pl.ds(0, 144)], w_recv.at[g, 4])
        block = full.at[g, p1]
        for k in range(1, 4):
            _, to = peer(g, k)
            send(block, block, w_send.at[5], w_recv.at[g, 5], *to)
        send(block, other.at[g, p1], w_send.at[6], w_recv.at[g, 6], partner_t, s)

    def unpack(source, g, c):
        wide = pl.ds(pl.multiple_of(g * 1024 + c * 512, 512), 512)
        narrow = pl.ds(pl.multiple_of(g * 256 + c * 128, 128), 128)

        @pl.loop(0, 4)
        def _(a):
            @pl.loop(0, ROWS // 16)
            def _(r):
                rows = pl.ds(pl.multiple_of(r * 16, 16), 16)
                to_rows = pl.ds(pl.multiple_of(a * ROWS + r * 16, 16), 16)
                in_sum[to_rows, wide] = source[g, a, rows, pl.ds(0, 512)]
                out_sum[to_rows, narrow] = source[g, a, rows, pl.ds(512, 128)]

    def gather_first(g):
        wait_bytes(full.at[g, pl.ds(0, 3)], w_recv.at[g, 5])
        for k in range(1, 4):
            p1 = lax.rem(place[g] + k, 4)
            send(full.at[g, p1], other.at[g, p1], w_send.at[6], w_recv.at[g, 6], partner_t, s)

    need(1, 2, 3, 4)
    for g in range(3):
        form(g, 1 - core, theirs)
    pl.semaphore_wait(barrier, N_SAMPLE + N_TILE - 1)
    for g in range(3):
        send(theirs.at[g], from_core.at[g], w_send.at[0], w_recv.at[g, 0], partner_t, s)

    need(0, *range(5, 17))
    keep[0], inverse_z = norm_rows(pair[...].astype(F32), 1)
    normed_z = keep[0].astype(BF16)

    def project(block):
        return dot_t(in_w_t[pl.ds(block * 128, 128), :], normed_z)

    keep[1] = sigmoid(dot(normed_z, gate_w[...]))
    keep_p[...], inverse_p = norm_rows(product[...].reshape(128, 512).astype(F32), 0)
    normed_p = keep_p[...].astype(BF16)
    keep[2] = t_dot(normed_p, out_w[...])
    keep[3], inverse_n = norm_rows(following[...], 1)
    normed_n = keep[3].astype(BF16)

    for part in range(4):
        rows = [bias_block[:, part * 4 + i] for i in range(4)]
        for h in range(4):
            head_rows[part, pl.ds(h, 4, stride=4), :] = place_lanes(rows, h)
    d_heads = jnp.concatenate([head_rows[part] for part in range(4)], axis=1)
    high = d_heads.astype(BF16)
    low = (d_heads - high.astype(F32)).astype(BF16)
    d_normed_n = t_dot(high, bias_w_t[...]) + t_dot(low, bias_w_t[...])
    d_next = cot_pair[...].astype(F32) + norm_back_rows(keep[3], inverse_n, d_normed_n, 1)
    tri_gate = keep[1]
    d_linear = (d_next * tri_gate).astype(BF16)
    d_product = norm_back_rows(keep_p[...], inverse_p, dot_t(out_w[...], d_linear), 0).astype(BF16)
    for d in range(N_SAMPLE):
        x1[d] = d_product[d * 16 : d * 16 + 16]
    for d in sample_peers:
        send(x1.at[d], mid.at[s], send_sem.at[3], recv_sem.at[3], t, d)
    mid[s] = x1[s]
    small[...] = jnp.zeros((128, SMALL), BF16)
    small[:, pl.ds(0, 768)] = atom_grad[...]
    small_mid[...] = jnp.zeros((16, N_TILE * 128), BF16)
    d_gate = (d_next * keep[2] * tri_gate * (1.0 - tri_gate)).astype(BF16)
    keep[4] = d_next
    small[:, pl.ds(768, 128)] = t_dot(normed_z, d_gate).astype(BF16)
    small[:, pl.ds(896, 128)] = dot(normed_p, d_linear).astype(BF16)
    small[pl.ds(0, 16), pl.ds(1024, 128)] = (dot(high, normed_n) + dot(low, normed_n)).astype(BF16)
    keep[5] = dot_t(d_gate, gate_w[...])
    form_mine(0)
    add_cores(0)
    form_mine(1)
    wait_bytes(mid.at[pl.ds(0, N_SAMPLE - 1)], recv_sem.at[3])
    split_lanes(mid[...].reshape(128, 512).astype(F32), mid_rows)
    for d in range(N_TILE):
        for part in range(4):
            x2[d, :, pl.ds(part * 128, 128)] = mid_rows[part, pl.ds(d, 8, stride=16), :]
    for d in tile_peers:
        send(x2.at[d], arrived.at[t], send_sem.at[4], recv_sem.at[4], d, s)
    arrived[t] = x2[t]
    add_cores(1)
    form_mine(2)
    add_cores(2)
    for side in range(2):
        gate_side = sigmoid(project(2 * side))
        masked = gate_side * mask[...]
        coefficient[2 * side] = masked * (1.0 - gate_side) * project(2 * side + 1)
        coefficient[2 * side + 1] = masked
    wait_bytes(arrived.at[pl.ds(0, N_TILE - 1)], recv_sem.at[4])
    split_lanes(arrived[...].reshape(128, 512), arrived_rows)
    panel_of(arrived_rows, 0, 8, panel)
    d_panel = joined(panel).astype(BF16)
    x3[:, 0] = dot(d_panel, right[...]).astype(BF16).reshape(N_TILE, 16, 256)
    x3[:, 1] = t_dot(d_panel, left[...]).astype(BF16).reshape(N_TILE, 16, 256)
    for d in tile_peers:
        send(x3.at[d], back.at[t], send_sem.at[5], recv_sem.at[5], d, s)
    back[t] = x3[t]
    add_first(0)
    add_first(1)
    for k in range(1, N_SAMPLE):
        d = sample_peers[k - 1]
        rows = pl.ds(pl.multiple_of(d * 16, 16), 16)
        send(small.at[rows], small_part.at[k - 1], send_sem.at[7], recv_sem.at[7], t, d)
    own = pl.ds(pl.multiple_of(s * 16, 16), 16)
    wait_bytes(back.at[pl.ds(0, N_TILE - 1)], recv_sem.at[5])
    for side in range(2):
        split_lanes(back[:, side].reshape(256, 256).astype(F32), back_rows)

        def store(d, lanes, rows, side=side):
            x4[d, side, :, lanes] = rows.astype(BF16)

        blocks_of(back_rows, store)
    for d in sample_peers:
        send(x4.at[d], final.at[s], send_sem.at[6], recv_sem.at[6], t, d)
    final[s] = x4[s]
    add_first(2)
    add_second(0)
    wait_bytes(small_part, recv_sem.at[7])
    total = small[own, :].astype(F32)
    for k in range(N_SAMPLE - 1):
        total = total + small_part[k].astype(F32)
    small_mid[:, pl.ds(0, SMALL)] = total.astype(BF16)
    for k in range(1, N_TILE):
        d = tile_peers[k - 1]
        lanes = pl.ds(pl.multiple_of(d * 128, 128), 128)
        send(small_mid.at[:, lanes], small_last.at[k - 1], send_sem.at[8], recv_sem.at[8], d, s)
    wait_bytes(final.at[pl.ds(0, N_SAMPLE - 1)], recv_sem.at[6])
    d_normed_z = keep[5]
    for block in range(4):
        incoming = final[:, block // 2].reshape(128, 512).astype(F32)
        d_proj = (incoming * coefficient[block]).astype(BF16)
        tri[:, pl.ds(block * 128, 128)] = dot(d_proj, normed_z).astype(BF16)
        d_normed_z = d_normed_z + t_dot(d_proj, in_w_t[pl.ds(block * 128, 128), :])
    for k in range(1, N_SAMPLE):
        d = sample_peers[k - 1]
        rows = pl.ds(pl.multiple_of(d * 16, 16), 16)
        send(tri.at[rows], tri_part.at[k - 1], send_sem.at[11], recv_sem.at[11], t, d)
    add_second(1)
    add_second(2)
    grad_pair[...] = keep[4] + norm_back_rows(keep[0], inverse_z, d_normed_z, 1)
    wait_bytes(small_last, recv_sem.at[8])
    lanes = pl.ds(pl.multiple_of(t * 128, 128), 128)
    total = small_mid[:, lanes].astype(F32)
    for k in range(N_TILE - 1):
        total = total + small_last[k].astype(F32)
    small_sum[own, lanes] = total.astype(BF16)
    block = small_sum.at[own, lanes]
    for d in tile_peers:
        send(block, block, send_sem.at[9], recv_sem.at[9], d, s)
    for g in range(3):
        add_third(g)
    wait_bytes(tri_part, recv_sem.at[11])
    total = tri[own, :].astype(F32)
    for k in range(N_SAMPLE - 1):
        total = total + tri_part[k].astype(F32)
    tri_all[t] = total.astype(BF16)
    for d in tile_peers:
        send(tri_all.at[t], tri_all.at[t], send_sem.at[12], recv_sem.at[12], d, s)
    for g in range(3):
        gather_second(g)
    wait_bytes(tri_all.at[pl.ds(0, N_TILE - 1)], recv_sem.at[12])
    tri_sum[own, :] = jnp.sum(tri_all[...].astype(F32), axis=0).astype(BF16)
    for d in sample_peers:
        send(tri_sum.at[own], tri_sum.at[own], send_sem.at[13], recv_sem.at[13], t, d)
    wait_bytes(small_last, recv_sem.at[9])
    known = small_sum.at[own, pl.ds(0, SMALL)]
    for d in sample_peers:
        send(known, known, send_sem.at[10], recv_sem.at[10], t, d)
    for g in range(3):
        gather_first(g)
        unpack(full, g, core)
    wait_bytes(small_part, recv_sem.at[10])
    wait_bytes(tri_part, recv_sem.at[13])
    for g in range(3):
        wait_bytes(other.at[g], w_recv.at[g, 6])
        unpack(other, g, 1 - core)

    wait_bytes(mid.at[pl.ds(0, N_SAMPLE - 1)], send_sem.at[3])
    wait_bytes(arrived.at[pl.ds(0, N_TILE - 1)], send_sem.at[4])
    wait_bytes(back.at[pl.ds(0, N_TILE - 1)], send_sem.at[5])
    wait_bytes(final.at[pl.ds(0, N_SAMPLE - 1)], send_sem.at[6])
    wait_bytes(small_part, send_sem.at[7])
    wait_bytes(small_last, send_sem.at[8])
    wait_bytes(small_last, send_sem.at[9])
    wait_bytes(small_part, send_sem.at[10])
    wait_bytes(tri_part, send_sem.at[11])
    wait_bytes(tri_all.at[pl.ds(0, N_TILE - 1)], send_sem.at[12])
    wait_bytes(tri_part, send_sem.at[13])
    wait_bytes(theirs, w_send.at[0])
    wait_bytes(part1, w_send.at[1])
    wait_bytes(part2, w_send.at[2])
    wait_bytes(part3.at[:, pl.ds(0, 3)], w_send.at[3])
    wait_bytes(part2, w_send.at[4])
    wait_bytes(part1, w_send.at[5])
    wait_bytes(theirs, w_send.at[6])


def backward(collective_id, *operands):
    vmem = pl.BlockSpec(memory_space=pltpu.VMEM)
    chunk = (3, 4, ROWS, WIDTH)
    return pl.pallas_call(
        fetching(backward_kernel, len(operands)),
        out_shape=[
            jax.ShapeDtypeStruct((512, 128), F32),
            jax.ShapeDtypeStruct((768, 3072), BF16),
            jax.ShapeDtypeStruct((768, 768), BF16),
            jax.ShapeDtypeStruct((128, N_TILE * 128), BF16),
            jax.ShapeDtypeStruct((128, 512), BF16),
        ],
        in_specs=[pl.BlockSpec(memory_space=pl.ANY)] * len(operands),
        out_specs=[vmem] * 5,
        scratch_shapes=[
            pltpu.VMEM((4, 16, 128), F32),
            pltpu.VMEM((4, 128, 512), F32),
            pltpu.VMEM((6, 512, 128), F32),
            pltpu.VMEM((128, 512), F32),
            pltpu.VMEM((N_SAMPLE, 16, 512), BF16),
            pltpu.VMEM((N_SAMPLE, 16, 512), BF16),
            pltpu.VMEM((4, 128, 128), F32),
            pltpu.VMEM((N_TILE, 8, 512), F32),
            pltpu.VMEM((N_TILE, 8, 512), F32),
            pltpu.VMEM((4, 128, 128), F32),
            pltpu.VMEM((2, 256, 128), F32),
            pltpu.VMEM((N_TILE, 2, 16, 256), BF16),
            pltpu.VMEM((N_TILE, 2, 16, 256), BF16),
            pltpu.VMEM((2, 256, 128), F32),
            pltpu.VMEM((N_SAMPLE, 2, 16, 512), BF16),
            pltpu.VMEM((N_SAMPLE, 2, 16, 512), BF16),
            pltpu.VMEM((128, SMALL), BF16),
            pltpu.VMEM((N_SAMPLE - 1, 16, SMALL), BF16),
            pltpu.VMEM((16, N_TILE * 128), BF16),
            pltpu.VMEM((N_TILE - 1, 16, 128), BF16),
            pltpu.VMEM((128, 512), BF16),
            pltpu.VMEM((N_SAMPLE - 1, 16, 512), BF16),
            pltpu.VMEM((N_TILE, 16, 512), BF16),
            pltpu.VMEM(chunk, BF16),
            pltpu.VMEM(chunk, BF16),
            pltpu.VMEM(chunk, BF16),
            pltpu.VMEM((3, 3, ROWS, WIDTH), BF16),
            pltpu.VMEM((3, ROWS, WIDTH), BF16),
            pltpu.VMEM((3, 3, 48, WIDTH), BF16),
            pltpu.VMEM((3, 48, WIDTH), BF16),
            pltpu.VMEM((3, 4, 48, WIDTH), BF16),
            pltpu.VMEM(chunk, BF16),
            pltpu.VMEM(chunk, BF16),
            pltpu.SemaphoreType.DMA((14,)),
            pltpu.SemaphoreType.DMA((14,)),
            pltpu.SemaphoreType.DMA((7,)),
            pltpu.SemaphoreType.DMA((3, 7)),
        ]
        + fetch_scratch(operands),
        compiler_params=pltpu.CompilerParams(
            collective_id=collective_id, has_side_effects=True, vmem_limit_bytes=60 << 20
        ),
    )(*operands)


def finish_kernel(
    wide,
    narrow,
    small,
    tri,
    gated,
    weight,
    tokens,
    cond,
    wide_out,
    narrow_out,
    tri_out,
    gate_out,
    linear_out,
    bias_out,
    atom_out,
    token_out,
):
    step = pl.program_id(0)
    wide_out[...] = wide[...].astype(F32)
    narrow_out[...] = narrow[...].astype(F32)

    @pl.when(step == 0)
    def _():
        for block in range(4):
            lanes = pl.ds(block * 128, 128)
            tri_out[:, lanes] = tri[:, lanes].astype(F32).T
        atom_out[...] = small[:, pl.ds(0, 768)].astype(F32)
        gate_out[...] = small[:, pl.ds(768, 128)].astype(F32)
        linear_out[...] = small[:, pl.ds(896, 128)].astype(F32)
        bias_out[...] = small[:, pl.ds(1024, 128)].astype(F32).T[:, 0 : bias_out.shape[1]]

    @pl.when(lax.rem(step, 3) == 0)
    def _():
        token_out[...] = tokens[...].astype(F32) + cond[...] + t_dot(gated[...], weight[...])


def finish(head_count, wide, narrow, small, tri, gated, weight, tokens, cond):
    steps = 12
    split = [
        pl.BlockSpec((x.shape[0] // steps, x.shape[1]), lambda i: (i, 0)) for x in (wide, narrow)
    ]

    def whole(shape):
        return pl.BlockSpec(shape, lambda i: (0, 0))

    rows = pl.BlockSpec((128, 768), lambda i: (i // 3, 0))
    one = [(128, 512), (128, 128), (128, 128), (128, head_count), (128, 768)]
    return pl.pallas_call(
        finish_kernel,
        grid=(steps,),
        in_specs=split
        + [whole(small.shape), whole(tri.shape)]
        + [
            pl.BlockSpec((768, 128), lambda i: (0, i // 3)),
            whole(weight.shape),
            rows,
            pl.BlockSpec((128, 768), lambda i: (lax.rem(i // 3, 2), 0)),
        ],
        out_specs=split + [whole(shape) for shape in one] + [rows],
        out_shape=[
            jax.ShapeDtypeStruct(shape, F32)
            for shape in [wide.shape, narrow.shape] + one + [tokens.shape]
        ],
        compiler_params=pltpu.CompilerParams(vmem_limit_bytes=60 << 20),
    )(wide, narrow, small, tri, gated, weight, tokens, cond)


def shards(
    pair,
    pair_mask,
    tri_in_w,
    tri_gate_w,
    tri_out_w,
    bias_w,
    atom_feats,
    atom_to_token,
    atom_w,
    tokens,
    attention_input_weight,
    attention_output_weight,
    cot_pair,
    token_output_cotangent,
):
    hidden = tri_in_w.shape[1] // 4
    token_width = attention_input_weight.shape[0]
    head_count = bias_w.shape[1]
    total_tokens = tokens.shape[1]
    pair_rows = pair.reshape(-1, hidden)
    mask_row = pair_mask.astype(F32).reshape(1, -1)
    in_w_t, bias_w_t = tri_in_w.T, bias_w.T
    token_rows = tokens.reshape(-1, token_width)
    cot_rows = token_output_cotangent.reshape(-1, token_width)
    (
        following,
        left_panel,
        right_panel,
        product,
        every_feat,
        every_atom,
        token_cond,
        token_counts,
        hidden_t,
        inverse_h,
        gated_t,
        d_every_t,
        bias_block,
        grad_tokens,
        atom_grad,
    ) = forward(
        0,
        pair_rows,
        in_w_t,
        mask_row,
        atom_feats,
        atom_to_token[None],
        tri_gate_w,
        tri_out_w,
        bias_w_t,
        atom_w,
        token_rows,
        attention_input_weight,
        attention_output_weight,
        cot_rows,
    )
    d_every_t = d_every_t.reshape(4 * token_width, -1)
    grad_pair, in_sum, out_sum, small_sum, tri_sum = backward(
        1,
        bias_block,
        d_every_t,
        hidden_t,
        gated_t,
        cot_rows,
        pair_rows,
        in_w_t,
        mask_row,
        tri_gate_w,
        tri_out_w,
        bias_w_t,
        following,
        product,
        left_panel,
        right_panel,
        cot_pair.reshape(-1, hidden),
        atom_grad,
    )
    grad_tokens = grad_tokens.reshape(tokens.shape)
    in_grad, out_grad, *others, token_output_rows = finish(
        head_count,
        in_sum,
        out_sum,
        small_sum,
        tri_sum,
        gated_t,
        attention_output_weight,
        token_rows,
        token_cond,
    )
    summed = (*others, in_grad, out_grad)
    token_output_rows = token_output_rows.reshape(tokens.shape)
    pair_next, grad_pair = following.reshape(pair.shape), grad_pair.reshape(pair.shape)
    return (pair_next, token_output_rows, grad_pair, grad_tokens) + summed


def solution(mesh):
    in_specs = (
        P("tile", "sample", None),
        P("tile", "sample"),
        P(),
        P(),
        P(),
        P(),
        P("tile", None),
        P("tile"),
        P(),
        P(("tile", "sample"), None, None),
        P(),
        P(),
        P("tile", "sample", None),
        P(("tile", "sample"), None, None),
    )
    out_specs = (
        P("tile", "sample", None),
        P(("tile", "sample"), None, None),
        P("tile", "sample", None),
        P(("tile", "sample"), None, None),
        P(),
        P(),
        P(),
        P(),
        P(),
        P(),
        P(),
    )
    return jax.shard_map(shards, mesh=mesh, in_specs=in_specs, out_specs=out_specs, check_vma=False)
```

```python
import functools
import math

import jax
import jax.numpy as jnp
from jax import lax
from jax.experimental import pallas as pl
from jax.experimental.pallas import tpu as pltpu
from jax.sharding import PartitionSpec as P

EPSILON = 1e-05
N_TILE = 16
N_SAMPLE = 8
N_CHIP = 8
MESH = pl.DeviceIdType.MESH
BF16 = jnp.bfloat16
F32 = jnp.float32
HIGHEST = lax.Precision.HIGHEST


def wait_bytes(ref, sem):
    pltpu.make_async_copy(ref, ref, sem).wait()


def send(src, dst, send_sem, recv_sem, t, s):
    pltpu.make_async_remote_copy(
        src, dst, send_sem, recv_sem, device_id=(t, s), device_id_type=MESH
    ).start()


def dot(a, b):
    return jnp.dot(a, b, preferred_element_type=F32)


def dot_t(a, b):
    return lax.dot_general(a, b, (((1,), (1,)), ((), ())), preferred_element_type=F32)


def t_dot(a, b):
    return lax.dot_general(a, b, (((0,), (0,)), ((), ())), preferred_element_type=F32)


HEAD = 48
GROUP = 4
LANES = 32


def fetching(kernel, count):
    def run(*refs):
        sources, rest, buffers, sem = refs[:count], refs[count : -count - 1], refs[-count - 1 : -1], refs[-1]
        copies = [
            pltpu.make_async_copy(source, buffer, sem.at[i])
            for i, (source, buffer) in enumerate(zip(sources, buffers))
        ]
        for copy in copies:
            copy.start()

        def need(*which):
            for i in which:
                copies[i].wait()

        kernel(need, *buffers, *rest)

    return run


def fetch_scratch(operands):
    return [pltpu.VMEM(x.shape, x.dtype) for x in operands] + [
        pltpu.SemaphoreType.DMA((len(operands),))
    ]


def place_lanes(parts, first):
    group_of = lax.broadcasted_iota(jnp.int32, parts[0].shape, 1) // LANES
    result = None
    for i in range(4):
        shift = (i - first) % 4 * LANES
        moved = pltpu.roll(parts[i], shift, 1) if shift else parts[i]
        result = moved if result is None else jnp.where(group_of == i, moved, result)
    return result


def panel_of(arrived, first, step, panel):
    for part in range(4):
        rows = [
            arrived[part, pl.ds(first + s * (step // 8), 16, stride=step), :] for s in range(8)
        ]
        for i in range(4):
            for half in range(2):
                panel[half, pl.ds(part * 4 + i, 16, stride=16), :] = place_lanes(
                    rows[half * 4 : half * 4 + 4], i
                )


def blocks_of(panel, store):
    for half in range(2):
        for part in range(4):
            rows = [panel[half, pl.ds(part * 4 + i, 16, stride=16), :] for i in range(4)]
            for q in range(4):
                store(half * 4 + q, pl.ds(part * 128, 128), place_lanes(rows, q))


def split_lanes(values, ref):
    for part in range(ref.shape[0]):
        ref[part] = values[:, part * 128 : part * 128 + 128]


def joined(ref):
    return jnp.concatenate([ref[0], ref[1]], axis=1)


def norm_rows(values, axis):
    centered = values - jnp.mean(values, axis=axis, keepdims=True)
    inverse = lax.rsqrt(jnp.mean(centered * centered, axis=axis, keepdims=True) + EPSILON)
    return centered * inverse, inverse


def sigmoid(values):
    return 1.0 / (1.0 + jnp.exp(-values))


def attend(group, q, k, v, gate, up, bias, gated, d_every, d_bias, bias_rows, bias_total):
    tokens = bias_rows.shape[1]
    scale = 1.0 / math.sqrt(HEAD)
    group_of = lax.broadcasted_iota(jnp.int32, (tokens, 128), 1) // LANES

    for half in range(2):
        parts = [
            bias[:, :, half * 4 + i, group].reshape(tokens, 128).astype(F32) for i in range(4)
        ]
        for h in range(GROUP):
            row = parts[0] if h == 0 else pltpu.roll(parts[0], (-h) % 4 * LANES, 1)
            for i in range(1, 4):
                shift = (i - h) % 4 * LANES
                moved = pltpu.roll(parts[i], shift, 1) if shift else parts[i]
                row = jnp.where(group_of == i, moved, row)
            bias_rows[h, :, pl.ds(half * 128, 128)] = row

    @pl.loop(0, GROUP)
    def _(h):
        rows = pl.ds(pl.multiple_of(group * GROUP * HEAD + h * HEAD, 16), HEAD)
        for sample in range(2):
            columns = pl.ds(sample * tokens, tokens)
            qh, kh, vh = q[rows, columns], k[rows, columns], v[rows, columns]
            scores = t_dot(qh, kh) * scale + bias_rows[h]
            weights = jnp.exp(scores - jnp.max(scores, axis=1, keepdims=True))
            probs = weights * (1.0 / jnp.sum(weights, axis=1, keepdims=True))
            probs_b = probs.astype(BF16)
            attended = dot_t(vh, probs_b)
            gate_h, up_h = gate[rows, columns], up[rows, columns]
            gated[rows, columns] = (gate_h * attended).astype(BF16)
            d_att = (up_h * gate_h).astype(BF16)
            d_every[1, rows, columns] = (up_h * attended * gate_h * (1.0 - gate_h)).astype(BF16)
            d_probs = t_dot(d_att, vh)
            inner = jnp.sum(probs * d_probs, axis=1, keepdims=True)
            d_scores = probs * (d_probs - inner)
            d_scores_b = d_scores.astype(BF16)
            d_every[0, rows, columns] = (dot_t(kh, d_scores_b) * scale).astype(BF16)
            d_every[2, rows, columns] = (dot(qh, d_scores_b) * scale).astype(BF16)
            d_every[3, rows, columns] = dot(d_att, probs_b).astype(BF16)
            if sample == 0:
                bias_total[h] = d_scores
            else:
                bias_total[h] = bias_total[h] + d_scores

    for half in range(2):
        parts = [bias_total[h, :, pl.ds(half * 128, 128)] for h in range(GROUP)]
        for i in range(4):
            row = parts[0] if i == 0 else pltpu.roll(parts[0], (-i) % 4 * LANES, 1)
            for h in range(1, GROUP):
                shift = (h - i) % 4 * LANES
                moved = pltpu.roll(parts[h], shift, 1) if shift else parts[h]
                row = jnp.where(group_of == h, moved, row)
            d_bias[:, :, half * 4 + i, group] = row.astype(BF16).reshape(N_CHIP, 2, 16, 128)


def forward_kernel(
    need,
    pair,
    in_w_t,
    mask,
    feats,
    atoms,
    gate_w,
    out_w,
    bias_w_t,
    atom_w,
    tokens,
    in_w,
    out_weight,
    cot,
    pair_next,
    left,
    right,
    product,
    every_feat,
    every_atom,
    token_cond,
    counts,
    hidden_t,
    inverse_h,
    gated,
    d_every,
    bias_block,
    grad_tokens,
    atom_grad,
    x1,
    mid,
    mid_rows,
    x2,
    arrived,
    arrived_rows,
    panel,
    x3,
    back,
    back_rows,
    x4,
    packed,
    mine,
    bias,
    q,
    keys,
    v,
    gate,
    bias_rows,
    bias_total,
    d_bias,
    pair_sum,
    by_chip,
    by_sample,
    up,
    d_hidden,
    cond_grad,
    atom_total,
    send_sem,
    recv_sem,
    chip_in,
    core_in,
    core_back,
    chip_back,
):
    t, s = lax.axis_index("tile"), lax.axis_index("sample")
    m, c = t // 2, lax.rem(t, 2)
    barrier = pltpu.get_barrier_semaphore()
    tile_peers = [lax.rem(t + k, N_TILE) for k in range(1, N_TILE)]
    sample_peers = [lax.rem(s + k, N_SAMPLE) for k in range(1, N_SAMPLE)]
    for d in sample_peers:
        pl.semaphore_signal(barrier, inc=1, device_id=(t, d), device_id_type=MESH)
    for d in tile_peers:
        pl.semaphore_signal(barrier, inc=1, device_id=(d, s), device_id_type=MESH)

    def token_sums():
        token_cond[...] = jnp.zeros_like(token_cond)
        counts[...] = jnp.zeros_like(counts)

        @pl.loop(0, N_TILE)
        def _(a):
            pre = dot(every_feat[a], atom_w[...])
            token = lax.broadcasted_iota(jnp.int32, (256, 128), 0)
            one_hot = jnp.where(token == every_atom[a], 1.0, 0.0)
            token_cond[...] += dot(one_hot.astype(BF16), (pre * sigmoid(pre)).astype(BF16))
            counts[...] += jnp.sum(one_hot, axis=1, keepdims=True)

        token_cond[...] = token_cond[...] / counts[...]

    def token_norm():
        @pl.loop(0, 4)
        def _(a):
            lanes = pl.ds(pl.multiple_of(a * 128, 128), 128)
            of_token = pl.ds(pl.multiple_of(lax.rem(a, 2) * 128, 128), 128)
            state = tokens[lanes, :].astype(F32) + token_cond[of_token, :]
            normed, inverse = norm_rows(state.T, 0)
            hidden_t[:, lanes] = normed.astype(BF16)
            inverse_h[:, lanes] = inverse

    def token_project(block, out):
        @pl.loop(0, 3)
        def _(a):
            rows = pl.ds(pl.multiple_of(a * 256, 256), 256)
            columns = pl.ds(pl.multiple_of(block * 768 + a * 256, 256), 256)
            result = t_dot(in_w[:, columns], hidden_t[...])
            out[rows, :] = (sigmoid(result) if block == 1 else result).astype(out.dtype)

    def token_upstream():
        @pl.loop(0, 3)
        def _(a):
            rows = pl.ds(pl.multiple_of(a * 256, 256), 256)
            up[rows, :] = dot_t(out_weight[rows, :], cot[...])

    def back_product():
        @pl.loop(0, 2)
        def _(a):
            rows = pl.ds(pl.multiple_of(a * 384, 128), 384)
            d_hidden[rows, :] = dot(in_w[rows, :], d_every[...].reshape(3072, 512))

    def back_norm():
        @pl.loop(0, 4)
        def _(a):
            lanes = pl.ds(pl.multiple_of(a * 128, 128), 128)
            back_t = norm_back_rows(
                hidden_t[:, lanes].astype(F32), inverse_h[:, lanes], d_hidden[:, lanes], 0
            )
            grad_tokens[lanes, :] = cot[lanes, :].astype(F32) + back_t.T

        both = grad_tokens[pl.ds(0, 256), :] + grad_tokens[pl.ds(256, 256), :]
        cond_grad[...] = (both / counts[...]).astype(BF16)

    def back_atoms():
        atom_total[...] = jnp.zeros_like(atom_total)

        @pl.loop(0, N_TILE)
        def _(a):
            feat = every_feat[a]
            pre = dot(feat, atom_w[...])
            part = sigmoid(pre)
            token = lax.broadcasted_iota(jnp.int32, (256, 128), 0)
            one_hot = jnp.where(token == every_atom[a], 1.0, 0.0).astype(BF16)
            d_act = t_dot(one_hot, cond_grad[...]) * (part * (1.0 + pre * (1.0 - part)))
            atom_total[...] += t_dot(feat, d_act.astype(BF16))

        atom_grad[...] = atom_total[...].astype(BF16)

    need(0)
    normed_z = norm_rows(pair[...].astype(F32), 1)[0].astype(BF16)
    need(1, 2)

    def project(block):
        return dot_t(in_w_t[pl.ds(block * 128, 128), :], normed_z)

    for side in range(2):
        value = (sigmoid(project(2 * side)) * project(2 * side + 1) * mask[...]).astype(BF16)
        for d in range(N_SAMPLE):
            x1[d, side] = value[d * 16 : d * 16 + 16]
    need(3, 4)
    pl.semaphore_wait(barrier, N_SAMPLE + N_TILE - 2)
    for d in sample_peers:
        send(x1.at[d], mid.at[s], send_sem.at[0], recv_sem.at[0], t, d)
    for d in tile_peers:
        send(feats, every_feat.at[t], send_sem.at[1], recv_sem.at[1], d, s)
        send(atoms, every_atom.at[t], send_sem.at[2], recv_sem.at[2], d, s)
    every_feat[t] = feats[...]
    every_atom[t] = atoms[...]
    mid[s] = x1[s]
    need(5, 6, 7, 8, 9, 10, 11, 12)
    tri_gate = sigmoid(dot(normed_z, gate_w[...]))
    token_upstream()
    wait_bytes(mid.at[pl.ds(0, N_SAMPLE - 1)], recv_sem.at[0])
    split_lanes(mid[...].reshape(256, 512).astype(F32), mid_rows)
    for d in range(N_TILE):
        for part in range(4):
            x2[d, :, pl.ds(part * 128, 128)] = mid_rows[part, pl.ds(d, 16, stride=16), :].astype(
                BF16
            )
    for d in tile_peers:
        send(x2.at[d], arrived.at[t], send_sem.at[3], recv_sem.at[3], d, s)
    arrived[t] = x2[t]
    wait_bytes(every_feat.at[pl.ds(0, N_TILE - 1)], recv_sem.at[1])
    wait_bytes(every_atom.at[pl.ds(0, N_TILE - 1)], recv_sem.at[2])
    token_sums()
    wait_bytes(arrived.at[pl.ds(0, N_TILE - 1)], recv_sem.at[3])
    split_lanes(arrived[...].reshape(256, 512).astype(F32), arrived_rows)
    panel_of(arrived_rows, 0, 16, panel)
    left[...] = joined(panel).astype(BF16)
    panel_of(arrived_rows, 1, 16, panel)
    right[...] = joined(panel).astype(BF16)
    x3[...] = dot_t(left[...], right[...]).astype(BF16).reshape(N_TILE, 16, 256)
    for d in tile_peers:
        send(x3.at[d], back.at[t], send_sem.at[4], recv_sem.at[4], d, s)
    back[t] = x3[t]
    token_norm()
    wait_bytes(back.at[pl.ds(0, N_TILE - 1)], recv_sem.at[4])
    split_lanes(back[...].reshape(256, 256).astype(F32), back_rows)

    def store(d, lanes, rows):
        x4[d, :, lanes] = rows.astype(BF16)

    blocks_of(back_rows, store)
    for d in sample_peers:
        send(x4.at[d], product.at[s], send_sem.at[5], recv_sem.at[5], t, d)
    product[s] = x4[s]
    token_project(0, q)
    wait_bytes(product.at[pl.ds(0, N_SAMPLE - 1)], recv_sem.at[5])
    normed_p = norm_rows(product[...].reshape(128, 512).astype(F32), 0)[0].astype(BF16)
    linear = t_dot(normed_p, out_w[...])
    following = pair[...].astype(F32) + tri_gate * linear
    pair_next[...] = following
    normed_n = norm_rows(following, 1)[0].astype(BF16)
    head_rows = dot_t(bias_w_t[...], normed_n)
    split_lanes(head_rows, packed)
    for part in range(4):
        rows = [packed[part, pl.ds(h, 4, stride=4), :] for h in range(4)]
        for i in range(4):
            mine[:, part * 4 + i] = place_lanes(rows, i)
    bias[m, c, s] = mine[...].astype(BF16)

    own = bias.at[m, c, s]
    for d in sample_peers:
        send(own, own, send_sem.at[6], recv_sem.at[6], t, d)
    token_project(2, keys)
    wait_bytes(bias.at[m, c, pl.ds(0, N_SAMPLE - 1)], recv_sem.at[6])
    other = m * 2 + 1 - c
    for g in range(4):
        for k in range(1, N_CHIP):
            d = lax.rem(m + k, N_CHIP) * 2 + c
            send(bias.at[m, c, :, g], bias.at[m, c, :, g], send_sem.at[7], chip_in.at[g], d, s)
    token_project(3, v)

    def pass_bias(g):
        wait_bytes(bias.at[pl.ds(0, N_CHIP - 1), 0, :, g], chip_in.at[g])
        send(bias.at[:, c, :, g], bias.at[:, c, :, g], send_sem.at[8], core_in.at[g], other, s)

    def add_cores(g):
        wait_bytes(pair_sum.at[:, :, g], core_back.at[g])
        for k in range(1, N_CHIP + 1):
            d = lax.rem(m + k, N_CHIP)
            total = pair_sum[d, :, g].astype(F32) + d_bias[d, c, :, g].astype(F32)
            pair_sum[d, :, g] = total.astype(BF16)
            if k < N_CHIP:
                send(
                    pair_sum.at[d, :, g],
                    by_chip.at[k - 1, :, g],
                    send_sem.at[10],
                    chip_back.at[g],
                    d * 2 + c,
                    s,
                )

    def add_chips(g):
        wait_bytes(by_chip.at[:, :, g], chip_back.at[g])
        total = pair_sum[m, :, g].astype(F32)
        for k in range(N_CHIP - 1):
            total = total + by_chip[k, :, g].astype(F32)
        pair_sum[m, :, g] = total.astype(BF16)
        for k in range(1, N_SAMPLE):
            d = sample_peers[k - 1]
            send(
                pair_sum.at[m, d, g], by_sample.at[k - 1, g], send_sem.at[11], recv_sem.at[7], t, d
            )

    pass_bias(0)
    token_project(1, gate)
    pass_bias(1)

    @pl.loop(0, 4)
    def _(g):
        wait_bytes(bias.at[:, 0, :, g], core_in.at[g])
        attend(g, q, keys, v, gate, up, bias, gated, d_every, d_bias, bias_rows, bias_total)
        send(d_bias.at[:, 1 - c, :, g], pair_sum.at[:, :, g], send_sem.at[9], core_back.at[g], other, s)

        @pl.when(g < 2)
        def _():
            pass_bias(g + 2)

        @pl.when(g >= 1)
        def _():
            add_cores(g - 1)

        @pl.when(g >= 2)
        def _():
            add_chips(g - 2)

    back_product()
    add_cores(3)
    add_chips(2)
    back_norm()
    add_chips(3)
    back_atoms()
    wait_bytes(by_sample, recv_sem.at[7])
    bias_block[...] = pair_sum[m, s].astype(F32) + jnp.sum(by_sample[...].astype(F32), axis=0)
    wait_bytes(mid.at[pl.ds(0, N_SAMPLE - 1)], send_sem.at[0])
    wait_bytes(every_feat.at[pl.ds(0, N_TILE - 1)], send_sem.at[1])
    wait_bytes(every_atom.at[pl.ds(0, N_TILE - 1)], send_sem.at[2])
    wait_bytes(arrived.at[pl.ds(0, N_TILE - 1)], send_sem.at[3])
    wait_bytes(back.at[pl.ds(0, N_TILE - 1)], send_sem.at[4])
    wait_bytes(product.at[pl.ds(0, N_SAMPLE - 1)], send_sem.at[5])
    wait_bytes(bias.at[m, c, pl.ds(0, N_SAMPLE - 1)], send_sem.at[6])
    wait_bytes(bias.at[pl.ds(0, N_CHIP - 1), 0], send_sem.at[7])
    wait_bytes(bias.at[:, 0], send_sem.at[8])
    wait_bytes(pair_sum, send_sem.at[9])
    wait_bytes(by_chip, send_sem.at[10])
    wait_bytes(by_sample, send_sem.at[11])


def forward(collective_id, *operands):
    vmem = pl.BlockSpec(memory_space=pltpu.VMEM)
    feats, atoms = operands[3:5]
    return pl.pallas_call(
        fetching(forward_kernel, len(operands)),
        out_shape=[
            jax.ShapeDtypeStruct((512, 128), F32),
            jax.ShapeDtypeStruct((256, 256), BF16),
            jax.ShapeDtypeStruct((256, 256), BF16),
            jax.ShapeDtypeStruct((N_SAMPLE, 16, 512), BF16),
            jax.ShapeDtypeStruct((N_TILE,) + feats.shape, feats.dtype),
            jax.ShapeDtypeStruct((N_TILE,) + atoms.shape, atoms.dtype),
            jax.ShapeDtypeStruct((256, 768), F32),
            jax.ShapeDtypeStruct((256, 1), F32),
            jax.ShapeDtypeStruct((768, 512), BF16),
            jax.ShapeDtypeStruct((1, 512), F32),
            jax.ShapeDtypeStruct((768, 512), BF16),
            jax.ShapeDtypeStruct((4, 768, 512), BF16),
            jax.ShapeDtypeStruct((4, 16, 128), F32),
            jax.ShapeDtypeStruct((512, 768), F32),
            jax.ShapeDtypeStruct((128, 768), BF16),
        ],
        in_specs=[pl.BlockSpec(memory_space=pl.ANY)] * len(operands),
        out_specs=[vmem] * 15,
        scratch_shapes=[
            pltpu.VMEM((N_SAMPLE, 2, 16, 512), BF16),
            pltpu.VMEM((N_SAMPLE, 2, 16, 512), BF16),
            pltpu.VMEM((4, 256, 128), F32),
            pltpu.VMEM((N_TILE, 16, 512), BF16),
            pltpu.VMEM((N_TILE, 16, 512), BF16),
            pltpu.VMEM((4, 256, 128), F32),
            pltpu.VMEM((2, 256, 128), F32),
            pltpu.VMEM((N_TILE, 16, 256), BF16),
            pltpu.VMEM((N_TILE, 16, 256), BF16),
            pltpu.VMEM((2, 256, 128), F32),
            pltpu.VMEM((N_SAMPLE, 16, 512), BF16),
            pltpu.VMEM((4, 16, 128), F32),
            pltpu.VMEM((4, 16, 128), F32),
            pltpu.VMEM((N_CHIP, 2, N_SAMPLE, 4, 16, 128), BF16),
            pltpu.VMEM((768, 512), BF16),
            pltpu.VMEM((768, 512), BF16),
            pltpu.VMEM((768, 512), BF16),
            pltpu.VMEM((768, 512), F32),
            pltpu.VMEM((GROUP, 256, 256), F32),
            pltpu.VMEM((GROUP, 256, 256), F32),
            pltpu.VMEM((N_CHIP, 2, N_SAMPLE, 4, 16, 128), BF16),
            pltpu.VMEM((N_CHIP, N_SAMPLE, 4, 16, 128), BF16),
            pltpu.VMEM((N_CHIP - 1, N_SAMPLE, 4, 16, 128), BF16),
            pltpu.VMEM((N_SAMPLE - 1, 4, 16, 128), BF16),
            pltpu.VMEM((768, 512), F32),
            pltpu.VMEM((768, 512), F32),
            pltpu.VMEM((256, 768), BF16),
            pltpu.VMEM((128, 768), F32),
            pltpu.SemaphoreType.DMA((12,)),
            pltpu.SemaphoreType.DMA((8,)),
            pltpu.SemaphoreType.DMA((4,)),
            pltpu.SemaphoreType.DMA((4,)),
            pltpu.SemaphoreType.DMA((4,)),
            pltpu.SemaphoreType.DMA((4,)),
        ]
        + fetch_scratch(operands),
        compiler_params=pltpu.CompilerParams(
            collective_id=collective_id, has_side_effects=True, vmem_limit_bytes=60 << 20
        ),
    )(*operands)


ROWS = 192
WIDTH = 640
SMALL = 1152


def norm_back_rows(normed, inverse, incoming, axis):
    first = jnp.mean(incoming, axis=axis, keepdims=True)
    second = jnp.mean(incoming * normed, axis=axis, keepdims=True)
    return (incoming - first - normed * second) * inverse


def backward_kernel(
    need,
    bias_block,
    right_in,
    left_in,
    left_out,
    right_out,
    pair,
    in_w_t,
    mask,
    gate_w,
    out_w,
    bias_w_t,
    following,
    product,
    left,
    right,
    cot_pair,
    atom_grad,
    grad_pair,
    in_sum,
    out_sum,
    small_sum,
    tri_sum,
    head_rows,
    coefficient,
    keep,
    keep_p,
    x1,
    mid,
    mid_rows,
    x2,
    arrived,
    arrived_rows,
    panel,
    x3,
    back,
    back_rows,
    x4,
    final,
    small,
    small_part,
    small_mid,
    small_last,
    tri,
    tri_part,
    tri_all,
    theirs,
    mine,
    from_core,
    part1,
    sum1,
    part2,
    sum2,
    part3,
    full,
    other,
    send_sem,
    recv_sem,
    w_send,
    w_recv,
):
    t, s = lax.axis_index("tile"), lax.axis_index("sample")
    m, core = t // 2, lax.rem(t, 2)
    partner_t = m * 2 + 1 - core
    place = [lax.rem(s, 2) * 2 + t // 8, lax.rem(t // 2, 4), s // 2]
    tile_peers = [lax.rem(t + k, N_TILE) for k in range(1, N_TILE)]
    sample_peers = [lax.rem(s + k, N_SAMPLE) for k in range(1, N_SAMPLE)]

    def peer(axis, k):
        where = list(place)
        where[axis] = lax.rem(place[axis] + k, 4)
        x, y, z = where
        return where[axis], (lax.rem(x, 2) * 8 + y * 2 + core, z * 2 + x // 2)

    barrier = pltpu.get_barrier_semaphore()
    for d in sample_peers:
        pl.semaphore_signal(barrier, inc=1, device_id=(t, d), device_id_type=MESH)
    for d in tile_peers:
        pl.semaphore_signal(barrier, inc=1, device_id=(d, s), device_id_type=MESH)
    diagonal = (lax.rem(t + 8, N_TILE), s + 1 - 2 * lax.rem(s, 2))
    pl.semaphore_signal(barrier, inc=1, device_id=diagonal, device_id_type=MESH)

    def form(g, c, target):
        wide = pl.ds(pl.multiple_of(g * 1024 + c * 512, 512), 512)
        narrow = pl.ds(pl.multiple_of(g * 256 + c * 128, 128), 128)

        @pl.loop(0, 4)
        def _(a):
            rows = pl.ds(pl.multiple_of(a * ROWS, 64), ROWS)
            target[g, a, :, pl.ds(0, 512)] = dot_t(left_in[rows, :], right_in[wide, :]).astype(BF16)
            target[g, a, :, pl.ds(512, 128)] = dot(left_out[rows, :], right_out[:, narrow]).astype(
                BF16
            )

    def form_mine(g):
        form(g, core, mine)

    def add_cores(g):
        wait_bytes(from_core.at[g], w_recv.at[g, 0])

        @pl.loop(0, 4)
        def _(a):
            @pl.loop(0, ROWS // 16)
            def _(r):
                rows = pl.ds(pl.multiple_of(r * 16, 16), 16)
                total = mine[g, a, rows, :].astype(F32) + from_core[g, a, rows, :].astype(F32)
                mine[g, a, rows, :] = total.astype(BF16)

        for k in range(1, 4):
            d, to = peer(g, k)
            send(mine.at[g, d], part1.at[g, k - 1], w_send.at[1], w_recv.at[g, 1], *to)

    def add_first(g):
        p1 = place[g]
        wait_bytes(part1.at[g], w_recv.at[g, 1])

        @pl.loop(0, ROWS // 16)
        def _(r):
            rows = pl.ds(pl.multiple_of(r * 16, 16), 16)
            total = mine[g, p1, rows, :].astype(F32)
            for k in range(3):
                total = total + part1[g, k, rows, :].astype(F32)
            sum1[g, rows, :] = total.astype(BF16)

        for k in range(1, 4):
            d, to = peer((g + 1) % 3, k)
            rows = pl.ds(pl.multiple_of(d * 48, 16), 48)
            send(sum1.at[g, rows], part2.at[g, k - 1], w_send.at[2], w_recv.at[g, 2], *to)

    def add_second(g):
        p2, p3 = place[(g + 1) % 3], place[(g + 2) % 3]
        wait_bytes(part2.at[g], w_recv.at[g, 2])
        total = sum1[g, pl.ds(pl.multiple_of(p2 * 48, 16), 48), :].astype(F32)
        for k in range(3):
            total = total + part2[g, k].astype(F32)
        sum2[g] = total.astype(BF16)
        for k in range(1, 4):
            _, to = peer((g + 2) % 3, k)
            send(sum2.at[g], part3.at[g, p3], w_send.at[3], w_recv.at[g, 3], *to)
        part3[g, p3] = sum2[g]

    def add_third(g):
        p1, p2 = place[g], place[(g + 1) % 3]
        wait_bytes(part3.at[g, pl.ds(0, 3)], w_recv.at[g, 3])
        total = part3[g, 0].astype(F32)
        for k in range(1, 4):
            total = total + part3[g, k].astype(F32)
        rows = pl.ds(pl.multiple_of(p2 * 48, 16), 48)
        full[g, p1, rows, :] = total.astype(BF16)
        block = full.at[g, p1, rows]
        for k in range(1, 4):
            _, to = peer((g + 1) % 3, k)
            send(block, block, w_send.at[4], w_recv.at[g, 4], *to)

    def gather_second(g):
        p1 = place[g]
        wait_bytes(full.at[g, p1, pl.ds(0, 144)], w_recv.at[g, 4])
        block = full.at[g, p1]
        for k in range(1, 4):
            _, to = peer(g, k)
            send(block, block, w_send.at[5], w_recv.at[g, 5], *to)
        send(block, other.at[g, p1], w_send.at[6], w_recv.at[g, 6], partner_t, s)

    def unpack(source, g, c):
        wide = pl.ds(pl.multiple_of(g * 1024 + c * 512, 512), 512)
        narrow = pl.ds(pl.multiple_of(g * 256 + c * 128, 128), 128)

        @pl.loop(0, 4)
        def _(a):
            @pl.loop(0, ROWS // 16)
            def _(r):
                rows = pl.ds(pl.multiple_of(r * 16, 16), 16)
                to_rows = pl.ds(pl.multiple_of(a * ROWS + r * 16, 16), 16)
                in_sum[to_rows, wide] = source[g, a, rows, pl.ds(0, 512)]
                out_sum[to_rows, narrow] = source[g, a, rows, pl.ds(512, 128)]

    def gather_first(g):
        wait_bytes(full.at[g, pl.ds(0, 3)], w_recv.at[g, 5])
        for k in range(1, 4):
            p1 = lax.rem(place[g] + k, 4)
            send(full.at[g, p1], other.at[g, p1], w_send.at[6], w_recv.at[g, 6], partner_t, s)

    need(1, 2, 3, 4)
    for g in range(3):
        form(g, 1 - core, theirs)
    pl.semaphore_wait(barrier, N_SAMPLE + N_TILE - 1)
    for g in range(3):
        send(theirs.at[g], from_core.at[g], w_send.at[0], w_recv.at[g, 0], partner_t, s)

    need(0, *range(5, 17))
    keep[0], inverse_z = norm_rows(pair[...].astype(F32), 1)
    normed_z = keep[0].astype(BF16)

    def project(block):
        return dot_t(in_w_t[pl.ds(block * 128, 128), :], normed_z)

    keep[1] = sigmoid(dot(normed_z, gate_w[...]))
    keep_p[...], inverse_p = norm_rows(product[...].reshape(128, 512).astype(F32), 0)
    normed_p = keep_p[...].astype(BF16)
    keep[2] = t_dot(normed_p, out_w[...])
    keep[3], inverse_n = norm_rows(following[...], 1)
    normed_n = keep[3].astype(BF16)

    for part in range(4):
        rows = [bias_block[:, part * 4 + i] for i in range(4)]
        for h in range(4):
            head_rows[part, pl.ds(h, 4, stride=4), :] = place_lanes(rows, h)
    d_heads = jnp.concatenate([head_rows[part] for part in range(4)], axis=1)
    high = d_heads.astype(BF16)
    low = (d_heads - high.astype(F32)).astype(BF16)
    d_normed_n = t_dot(high, bias_w_t[...]) + t_dot(low, bias_w_t[...])
    d_next = cot_pair[...].astype(F32) + norm_back_rows(keep[3], inverse_n, d_normed_n, 1)
    tri_gate = keep[1]
    d_linear = (d_next * tri_gate).astype(BF16)
    d_product = norm_back_rows(keep_p[...], inverse_p, dot_t(out_w[...], d_linear), 0).astype(BF16)
    for d in range(N_SAMPLE):
        x1[d] = d_product[d * 16 : d * 16 + 16]
    for d in sample_peers:
        send(x1.at[d], mid.at[s], send_sem.at[3], recv_sem.at[3], t, d)
    mid[s] = x1[s]
    small[...] = jnp.zeros((128, SMALL), BF16)
    small[:, pl.ds(0, 768)] = atom_grad[...]
    small_mid[...] = jnp.zeros((16, N_TILE * 128), BF16)
    d_gate = (d_next * keep[2] * tri_gate * (1.0 - tri_gate)).astype(BF16)
    keep[4] = d_next
    small[:, pl.ds(768, 128)] = t_dot(normed_z, d_gate).astype(BF16)
    small[:, pl.ds(896, 128)] = dot(normed_p, d_linear).astype(BF16)
    small[pl.ds(0, 16), pl.ds(1024, 128)] = (dot(high, normed_n) + dot(low, normed_n)).astype(BF16)
    keep[5] = dot_t(d_gate, gate_w[...])
    form_mine(0)
    add_cores(0)
    form_mine(1)
    wait_bytes(mid.at[pl.ds(0, N_SAMPLE - 1)], recv_sem.at[3])
    split_lanes(mid[...].reshape(128, 512).astype(F32), mid_rows)
    for d in range(N_TILE):
        for part in range(4):
            x2[d, :, pl.ds(part * 128, 128)] = mid_rows[part, pl.ds(d, 8, stride=16), :]
    for d in tile_peers:
        send(x2.at[d], arrived.at[t], send_sem.at[4], recv_sem.at[4], d, s)
    arrived[t] = x2[t]
    add_cores(1)
    form_mine(2)
    add_cores(2)
    for side in range(2):
        gate_side = sigmoid(project(2 * side))
        masked = gate_side * mask[...]
        coefficient[2 * side] = masked * (1.0 - gate_side) * project(2 * side + 1)
        coefficient[2 * side + 1] = masked
    wait_bytes(arrived.at[pl.ds(0, N_TILE - 1)], recv_sem.at[4])
    split_lanes(arrived[...].reshape(128, 512), arrived_rows)
    panel_of(arrived_rows, 0, 8, panel)
    d_panel = joined(panel).astype(BF16)
    x3[:, 0] = dot(d_panel, right[...]).astype(BF16).reshape(N_TILE, 16, 256)
    x3[:, 1] = t_dot(d_panel, left[...]).astype(BF16).reshape(N_TILE, 16, 256)
    for d in tile_peers:
        send(x3.at[d], back.at[t], send_sem.at[5], recv_sem.at[5], d, s)
    back[t] = x3[t]
    add_first(0)
    add_first(1)
    for k in range(1, N_SAMPLE):
        d = sample_peers[k - 1]
        rows = pl.ds(pl.multiple_of(d * 16, 16), 16)
        send(small.at[rows], small_part.at[k - 1], send_sem.at[7], recv_sem.at[7], t, d)
    own = pl.ds(pl.multiple_of(s * 16, 16), 16)
    wait_bytes(back.at[pl.ds(0, N_TILE - 1)], recv_sem.at[5])
    for side in range(2):
        split_lanes(back[:, side].reshape(256, 256).astype(F32), back_rows)

        def store(d, lanes, rows, side=side):
            x4[d, side, :, lanes] = rows.astype(BF16)

        blocks_of(back_rows, store)
    for d in sample_peers:
        send(x4.at[d], final.at[s], send_sem.at[6], recv_sem.at[6], t, d)
    final[s] = x4[s]
    add_first(2)
    add_second(0)
    wait_bytes(small_part, recv_sem.at[7])
    total = small[own, :].astype(F32)
    for k in range(N_SAMPLE - 1):
        total = total + small_part[k].astype(F32)
    small_mid[:, pl.ds(0, SMALL)] = total.astype(BF16)
    for k in range(1, N_TILE):
        d = tile_peers[k - 1]
        lanes = pl.ds(pl.multiple_of(d * 128, 128), 128)
        send(small_mid.at[:, lanes], small_last.at[k - 1], send_sem.at[8], recv_sem.at[8], d, s)
    wait_bytes(final.at[pl.ds(0, N_SAMPLE - 1)], recv_sem.at[6])
    d_normed_z = keep[5]
    for block in range(4):
        incoming = final[:, block // 2].reshape(128, 512).astype(F32)
        d_proj = (incoming * coefficient[block]).astype(BF16)
        tri[:, pl.ds(block * 128, 128)] = dot(d_proj, normed_z).astype(BF16)
        d_normed_z = d_normed_z + t_dot(d_proj, in_w_t[pl.ds(block * 128, 128), :])
    for k in range(1, N_SAMPLE):
        d = sample_peers[k - 1]
        rows = pl.ds(pl.multiple_of(d * 16, 16), 16)
        send(tri.at[rows], tri_part.at[k - 1], send_sem.at[11], recv_sem.at[11], t, d)
    add_second(1)
    add_second(2)
    grad_pair[...] = keep[4] + norm_back_rows(keep[0], inverse_z, d_normed_z, 1)
    wait_bytes(small_last, recv_sem.at[8])
    lanes = pl.ds(pl.multiple_of(t * 128, 128), 128)
    total = small_mid[:, lanes].astype(F32)
    for k in range(N_TILE - 1):
        total = total + small_last[k].astype(F32)
    small_sum[own, lanes] = total.astype(BF16)
    block = small_sum.at[own, lanes]
    for d in tile_peers:
        send(block, block, send_sem.at[9], recv_sem.at[9], d, s)
    for g in range(3):
        add_third(g)
    wait_bytes(tri_part, recv_sem.at[11])
    total = tri[own, :].astype(F32)
    for k in range(N_SAMPLE - 1):
        total = total + tri_part[k].astype(F32)
    tri_all[t] = total.astype(BF16)
    for d in tile_peers:
        send(tri_all.at[t], tri_all.at[t], send_sem.at[12], recv_sem.at[12], d, s)
    for g in range(3):
        gather_second(g)
    wait_bytes(tri_all.at[pl.ds(0, N_TILE - 1)], recv_sem.at[12])
    tri_sum[own, :] = jnp.sum(tri_all[...].astype(F32), axis=0).astype(BF16)
    for d in sample_peers:
        send(tri_sum.at[own], tri_sum.at[own], send_sem.at[13], recv_sem.at[13], t, d)
    wait_bytes(small_last, recv_sem.at[9])
    known = small_sum.at[own, pl.ds(0, SMALL)]
    for d in sample_peers:
        send(known, known, send_sem.at[10], recv_sem.at[10], t, d)
    for g in range(3):
        gather_first(g)
        unpack(full, g, core)
    wait_bytes(small_part, recv_sem.at[10])
    wait_bytes(tri_part, recv_sem.at[13])
    for g in range(3):
        wait_bytes(other.at[g], w_recv.at[g, 6])
        unpack(other, g, 1 - core)

    wait_bytes(mid.at[pl.ds(0, N_SAMPLE - 1)], send_sem.at[3])
    wait_bytes(arrived.at[pl.ds(0, N_TILE - 1)], send_sem.at[4])
    wait_bytes(back.at[pl.ds(0, N_TILE - 1)], send_sem.at[5])
    wait_bytes(final.at[pl.ds(0, N_SAMPLE - 1)], send_sem.at[6])
    wait_bytes(small_part, send_sem.at[7])
    wait_bytes(small_last, send_sem.at[8])
    wait_bytes(small_last, send_sem.at[9])
    wait_bytes(small_part, send_sem.at[10])
    wait_bytes(tri_part, send_sem.at[11])
    wait_bytes(tri_all.at[pl.ds(0, N_TILE - 1)], send_sem.at[12])
    wait_bytes(tri_part, send_sem.at[13])
    wait_bytes(theirs, w_send.at[0])
    wait_bytes(part1, w_send.at[1])
    wait_bytes(part2, w_send.at[2])
    wait_bytes(part3.at[:, pl.ds(0, 3)], w_send.at[3])
    wait_bytes(part2, w_send.at[4])
    wait_bytes(part1, w_send.at[5])
    wait_bytes(theirs, w_send.at[6])


def backward(collective_id, *operands):
    vmem = pl.BlockSpec(memory_space=pltpu.VMEM)
    chunk = (3, 4, ROWS, WIDTH)
    return pl.pallas_call(
        fetching(backward_kernel, len(operands)),
        out_shape=[
            jax.ShapeDtypeStruct((512, 128), F32),
            jax.ShapeDtypeStruct((768, 3072), BF16),
            jax.ShapeDtypeStruct((768, 768), BF16),
            jax.ShapeDtypeStruct((128, N_TILE * 128), BF16),
            jax.ShapeDtypeStruct((128, 512), BF16),
        ],
        in_specs=[pl.BlockSpec(memory_space=pl.ANY)] * len(operands),
        out_specs=[vmem] * 5,
        scratch_shapes=[
            pltpu.VMEM((4, 16, 128), F32),
            pltpu.VMEM((4, 128, 512), F32),
            pltpu.VMEM((6, 512, 128), F32),
            pltpu.VMEM((128, 512), F32),
            pltpu.VMEM((N_SAMPLE, 16, 512), BF16),
            pltpu.VMEM((N_SAMPLE, 16, 512), BF16),
            pltpu.VMEM((4, 128, 128), F32),
            pltpu.VMEM((N_TILE, 8, 512), F32),
            pltpu.VMEM((N_TILE, 8, 512), F32),
            pltpu.VMEM((4, 128, 128), F32),
            pltpu.VMEM((2, 256, 128), F32),
            pltpu.VMEM((N_TILE, 2, 16, 256), BF16),
            pltpu.VMEM((N_TILE, 2, 16, 256), BF16),
            pltpu.VMEM((2, 256, 128), F32),
            pltpu.VMEM((N_SAMPLE, 2, 16, 512), BF16),
            pltpu.VMEM((N_SAMPLE, 2, 16, 512), BF16),
            pltpu.VMEM((128, SMALL), BF16),
            pltpu.VMEM((N_SAMPLE - 1, 16, SMALL), BF16),
            pltpu.VMEM((16, N_TILE * 128), BF16),
            pltpu.VMEM((N_TILE - 1, 16, 128), BF16),
            pltpu.VMEM((128, 512), BF16),
            pltpu.VMEM((N_SAMPLE - 1, 16, 512), BF16),
            pltpu.VMEM((N_TILE, 16, 512), BF16),
            pltpu.VMEM(chunk, BF16),
            pltpu.VMEM(chunk, BF16),
            pltpu.VMEM(chunk, BF16),
            pltpu.VMEM((3, 3, ROWS, WIDTH), BF16),
            pltpu.VMEM((3, ROWS, WIDTH), BF16),
            pltpu.VMEM((3, 3, 48, WIDTH), BF16),
            pltpu.VMEM((3, 48, WIDTH), BF16),
            pltpu.VMEM((3, 4, 48, WIDTH), BF16),
            pltpu.VMEM(chunk, BF16),
            pltpu.VMEM(chunk, BF16),
            pltpu.SemaphoreType.DMA((14,)),
            pltpu.SemaphoreType.DMA((14,)),
            pltpu.SemaphoreType.DMA((7,)),
            pltpu.SemaphoreType.DMA((3, 7)),
        ]
        + fetch_scratch(operands),
        compiler_params=pltpu.CompilerParams(
            collective_id=collective_id, has_side_effects=True, vmem_limit_bytes=60 << 20
        ),
    )(*operands)


def finish_kernel(
    wide,
    narrow,
    small,
    tri,
    gated,
    weight,
    tokens,
    cond,
    wide_out,
    narrow_out,
    tri_out,
    gate_out,
    linear_out,
    bias_out,
    atom_out,
    token_out,
):
    step = pl.program_id(0)
    wide_out[...] = wide[...].astype(F32)
    narrow_out[...] = narrow[...].astype(F32)

    @pl.when(step == 0)
    def _():
        for block in range(4):
            lanes = pl.ds(block * 128, 128)
            tri_out[:, lanes] = tri[:, lanes].astype(F32).T
        atom_out[...] = small[:, pl.ds(0, 768)].astype(F32)
        gate_out[...] = small[:, pl.ds(768, 128)].astype(F32)
        linear_out[...] = small[:, pl.ds(896, 128)].astype(F32)
        bias_out[...] = small[:, pl.ds(1024, 128)].astype(F32).T[:, 0 : bias_out.shape[1]]

    token_out[...] = tokens[...].astype(F32) + cond[...] + t_dot(gated[...], weight[...])


def finish(head_count, wide, narrow, small, tri, gated, weight, tokens, cond):
    steps = 4
    split = [
        pl.BlockSpec((x.shape[0] // steps, x.shape[1]), lambda i: (i, 0)) for x in (wide, narrow)
    ]

    def whole(shape):
        return pl.BlockSpec(shape, lambda i: (0, 0))

    rows = pl.BlockSpec((128, 768), lambda i: (i, 0))
    one = [(128, 512), (128, 128), (128, 128), (128, head_count), (128, 768)]
    return pl.pallas_call(
        finish_kernel,
        grid=(steps,),
        in_specs=split
        + [whole(small.shape), whole(tri.shape)]
        + [
            pl.BlockSpec((768, 128), lambda i: (0, i)),
            whole(weight.shape),
            rows,
            pl.BlockSpec((128, 768), lambda i: (lax.rem(i, 2), 0)),
        ],
        out_specs=split + [whole(shape) for shape in one] + [rows],
        out_shape=[
            jax.ShapeDtypeStruct(shape, F32)
            for shape in [wide.shape, narrow.shape] + one + [tokens.shape]
        ],
        compiler_params=pltpu.CompilerParams(vmem_limit_bytes=60 << 20),
    )(wide, narrow, small, tri, gated, weight, tokens, cond)


def shards(
    pair,
    pair_mask,
    tri_in_w,
    tri_gate_w,
    tri_out_w,
    bias_w,
    atom_feats,
    atom_to_token,
    atom_w,
    tokens,
    attention_input_weight,
    attention_output_weight,
    cot_pair,
    token_output_cotangent,
):
    hidden = tri_in_w.shape[1] // 4
    token_width = attention_input_weight.shape[0]
    head_count = bias_w.shape[1]
    total_tokens = tokens.shape[1]
    pair_rows = pair.reshape(-1, hidden)
    mask_row = pair_mask.astype(F32).reshape(1, -1)
    in_w_t, bias_w_t = tri_in_w.T, bias_w.T
    token_rows = tokens.reshape(-1, token_width)
    cot_rows = token_output_cotangent.reshape(-1, token_width)
    (
        following,
        left_panel,
        right_panel,
        product,
        every_feat,
        every_atom,
        token_cond,
        token_counts,
        hidden_t,
        inverse_h,
        gated_t,
        d_every_t,
        bias_block,
        grad_tokens,
        atom_grad,
    ) = forward(
        0,
        pair_rows,
        in_w_t,
        mask_row,
        atom_feats,
        atom_to_token[None],
        tri_gate_w,
        tri_out_w,
        bias_w_t,
        atom_w,
        token_rows,
        attention_input_weight,
        attention_output_weight,
        cot_rows,
    )
    d_every_t = d_every_t.reshape(4 * token_width, -1)
    grad_pair, in_sum, out_sum, small_sum, tri_sum = backward(
        1,
        bias_block,
        d_every_t,
        hidden_t,
        gated_t,
        cot_rows,
        pair_rows,
        in_w_t,
        mask_row,
        tri_gate_w,
        tri_out_w,
        bias_w_t,
        following,
        product,
        left_panel,
        right_panel,
        cot_pair.reshape(-1, hidden),
        atom_grad,
    )
    grad_tokens = grad_tokens.reshape(tokens.shape)
    in_grad, out_grad, *others, token_output_rows = finish(
        head_count,
        in_sum,
        out_sum,
        small_sum,
        tri_sum,
        gated_t,
        attention_output_weight,
        token_rows,
        token_cond,
    )
    summed = (*others, in_grad, out_grad)
    token_output_rows = token_output_rows.reshape(tokens.shape)
    pair_next, grad_pair = following.reshape(pair.shape), grad_pair.reshape(pair.shape)
    return (pair_next, token_output_rows, grad_pair, grad_tokens) + summed


def solution(mesh):
    in_specs = (
        P("tile", "sample", None),
        P("tile", "sample"),
        P(),
        P(),
        P(),
        P(),
        P("tile", None),
        P("tile"),
        P(),
        P(("tile", "sample"), None, None),
        P(),
        P(),
        P("tile", "sample", None),
        P(("tile", "sample"), None, None),
    )
    out_specs = (
        P("tile", "sample", None),
        P(("tile", "sample"), None, None),
        P("tile", "sample", None),
        P(("tile", "sample"), None, None),
        P(),
        P(),
        P(),
        P(),
        P(),
        P(),
        P(),
    )
    return jax.shard_map(shards, mesh=mesh, in_specs=in_specs, out_specs=out_specs, check_vma=False)
```
